256 devices in a mesh: expert: 64 (over y_lo, x, z), tensor: 4 (over y_hi, core).
Axes of the slice: x: 4, y: 4 (y_hi: 2, y_lo: 2; y = y_hi * 2 + y_lo), z: 8, core: 2. Of those that a mesh axis runs over, the one named last changes fastest.
Arguments:
- tokens: bfloat16 [4096, 2, 2880], P('expert', None, 'tensor'), may hold values from -40 to 40
- attn_gain: float32 [2880], replicated, may hold values from 0.25 to 1.75
- w_query: bfloat16 [2880, 2048], P(None, 'tensor'), may hold values from -0.109375 to 0.109375
- key_value_weight: bfloat16 [2880, 4, 128], P(None, 'tensor'), may hold values from -0.625 to 0.625
- w_out: bfloat16 [2048, 2880], P('tensor'), may hold values from -0.125 to 0.125
- cache_keyval: bfloat16 [12288, 2, 4, 128], P('expert', None, 'tensor'), may hold values from -130 to 130
- prefix_length: int32 [2], replicated, may hold values from 3072 to 12288, as said below
- routed_experts: int32 [4096, 2, 4], P('expert'), may hold values from 0 to 63, all different within a row; in each aligned block of 128 rows (0 to 127, 128 to 255, ..., all dimensions but the last counted through in order) at most 20 rows name the same one
- route_weights: float32 [4096, 2, 4], P('expert'), may hold values from 0.1 to 0.6
- expert_gain: float32 [2880], replicated, may hold values from 0.25 to 1.75
- w_gate_up: bfloat16 [64, 2880, 2, 1440], P('expert', None, None, 'tensor'), may hold values from -0.109375 to 0.109375
- w_down: bfloat16 [64, 1440, 2880], P('expert', 'tensor'), may hold values from -0.15625 to 0.15625
Outputs:
- layer_output: bfloat16 [4096, 2, 2880], P('expert', None, 'tensor')
- new_key_value_rows: bfloat16 [4096, 2, 4, 128], P('expert', None, 'tensor')
The draws below stay inside these ranges and needn't reach their ends.
Inputs may be any that keep to these rules, and one draw needn't show every extreme that they name: `prefix_length`: one sequence, drawn from the seed, has a full cache of 12288 positions; no sequence has fewer than 3072. `routed_experts`: each token names 4 different experts. Taking tokens in position-major order, in each aligned block of 128 tokens (the tokens of one index of expert) at most 20 name the same expert, and in some blocks one expert is named by exactly 20.
All inputs are finite; a program needn't handle non-finite values.
Results may differ from the reference program's by a relative error of at most 0.02.
Values may be sent and summed in bfloat16 or wider, within the bound.
A program may use at most 128 MiB of HBM per device.

```python
import math
import jax
import jax.numpy as jnp
import numpy as np
from jax import lax

MODEL_DIM = 2880
HEAD_SIZE = 64
TOP = 4
QUERY_HEADS = 32
KEY_VALUE_HEADS = 4
FFH = 1440
SEQUENCE_COUNT = 2
TOK_DEV = 128
EXPERTS = 64
NEW_POSITIONS = 4096
CACHE_POSITIONS = 12288
CAP = 20
N_EXPERT = 64
N_TENSOR = 4


def draw_tokens(key, part):
    key = jax.random.fold_in(key, 11)
    base_key, column_key, row_key = jax.random.split(key, 3)
    column_ramp = jnp.arange(MODEL_DIM, dtype=jnp.float32) / (MODEL_DIM - 1)
    roughness = jnp.exp(jax.random.uniform(column_key, (MODEL_DIM,), jnp.float32, -0.5, 0.5))
    base_draw = jax.random.normal(base_key, (NEW_POSITIONS, SEQUENCE_COUNT, MODEL_DIM), jnp.float32)
    row_scale = jnp.exp(jax.random.uniform(row_key, (NEW_POSITIONS, SEQUENCE_COUNT, 1), jnp.float32, math.log(0.6), math.log(1.6)))
    column = jnp.exp(column_ramp * math.log(3.0)) * roughness
    return jnp.clip(base_draw * row_scale * column * 0.55, -40.0, 40.0).astype(jnp.bfloat16)


def draw_cache_keyval(key, part):
    key = jax.random.fold_in(key, 12)
    complete_shape = (CACHE_POSITIONS, SEQUENCE_COUNT, KEY_VALUE_HEADS, 2 * HEAD_SIZE)
    base_key = jax.random.fold_in(key, 0)
    return jnp.clip(2.4 * jax.random.normal(base_key, complete_shape, jnp.float32), -14.0, 14.0).astype(jnp.bfloat16)


def draw_prefix_length(key, part):
    key = jax.random.fold_in(key, 13)
    length_key, full_key = jax.random.split(key)
    lengths = jax.random.randint(length_key, (SEQUENCE_COUNT,), CACHE_POSITIONS // 4, CACHE_POSITIONS + 1)
    chosen = jax.random.randint(full_key, (), 0, SEQUENCE_COUNT)
    return jnp.where(jnp.arange(SEQUENCE_COUNT) == chosen, CACHE_POSITIONS, lengths).astype(jnp.int32)


def shard_levels(key, extent, cuts, smallest, largest):
    level, own = 1.0, jax.random.fold_in(key, 6)
    for position, shards_of in cuts:
        heights = jnp.exp(jax.random.uniform(jax.random.fold_in(own, position), (shards_of,), jnp.float32, smallest / len(cuts), largest / len(cuts)))
        level = level * jnp.repeat(heights, extent[position] // shards_of).reshape([-1 if axis == position else 1 for axis in range(len(extent))])
    return level


def routed_block(stream_key, own, number, rows, amount, top, bound, skew):
    sequence = jax.random.permutation(stream_key, amount)
    crowded, ordinary = load_shares(amount, rows * top, bound, skew, True), load_shares(amount, rows * top, bound, skew, False)
    places = jnp.arange(amount)

    def named(sizes, rotation):
        used = int((sizes > 0).sum())
        fixed = max(1, used // 4)
        moved = fixed + (places - fixed + rotation * (used - fixed)) % max(1, amount - fixed)
        return jnp.zeros((amount,), jnp.int32).at[sequence[jnp.where(places < fixed, places, moved)]].set(jnp.asarray(sizes, jnp.int32))

    sizes = jnp.where(number % 4 == 0, named(crowded, number // 4), named(ordinary, number - number // 4 - 1))
    mixed = jax.random.permutation(jax.random.fold_in(own, 3), amount)
    giver, taker = mixed[0:amount // 2 * 2:2], mixed[1:amount // 2 * 2:2]
    room = jnp.minimum(sizes[giver] - 1, bound - sizes[taker]) // 2
    room = jnp.where((giver == sequence[0]) | (taker == sequence[0]) | (sizes[taker] == 0), 0, jnp.maximum(room, 0))
    moved = jax.random.randint(jax.random.fold_in(own, 4), (amount // 2,), 0, 1 << 20) % (room + 1)
    sizes = sizes.at[giver].add(-moved).at[taker].add(moved)
    members = jnp.searchsorted(jnp.cumsum(sizes), jnp.arange(rows * top), side="right").astype(jnp.int32)
    grid = members.reshape(top, rows).T
    grid = grid[jax.random.permutation(jax.random.fold_in(own, 1), rows)]
    rotation = jax.random.randint(jax.random.fold_in(own, 2), (rows, 1), 0, top)
    return jnp.take_along_axis(grid, (jnp.arange(top)[None, :] + rotation) % top, axis=1)


def load_shares(number_of, total, reach, slope, full):
    loads = [(1 << 20) // math.isqrt(rank ** slope) + 1 for rank in range(1, number_of + 1)]
    largest = reach if full else min(reach, max(-(-total // number_of), total * loads[0] // sum(loads)))
    least = 1 if total - largest >= number_of - 1 else 0
    holding, surplus = [largest] + [least] * (number_of - 1), total - largest - least * (number_of - 1)
    while surplus > 0:
        free = [i for i in range(1, number_of) if holding[i] < largest] or [i for i in range(1, number_of) if holding[i] < reach]
        pool, budget = sum([loads[i] for i in free]), surplus
        for i in free:
            more = min(reach - holding[i], max(1, budget * loads[i] // pool), surplus)
            holding[i] = holding[i] + more
            surplus = surplus - more
    return np.array(holding)


def normal_values(own_key, extent, deviation, bound, cuts=(), held_as=jnp.bfloat16):
    level = shard_levels(own_key, extent, cuts, -0.22, 0.18) if cuts else 1.0
    result = jax.random.normal(own_key, extent, jnp.float32) * deviation * level
    return jnp.minimum(jnp.maximum(result, -bound), bound).astype(held_as)


def setup_inputs(seed: int = 0) -> dict:
    keys = jax.random.split(jax.random.key(seed), 13)
    tokens = draw_tokens(jax.random.fold_in(keys[12], 71), 0)
    attn_gain = jnp.clip(1.0 + 0.15 * jax.random.normal(keys[1], (MODEL_DIM,), jnp.float32), 0.25, 1.75)
    w_query = normal_values(keys[2], (MODEL_DIM, QUERY_HEADS * HEAD_SIZE), MODEL_DIM ** -0.5, 0.109375, ((1, 4),))
    key_value_weight = normal_values(keys[3], (MODEL_DIM, KEY_VALUE_HEADS, 2 * HEAD_SIZE), (2.4 / MODEL_DIM ** 0.5), 0.625, ((1, 4),))
    w_out = normal_values(keys[4], (QUERY_HEADS * HEAD_SIZE, MODEL_DIM), (QUERY_HEADS * HEAD_SIZE) ** -0.5, 0.125, ((0, 4),))
    cache_keyval = draw_cache_keyval(jax.random.fold_in(keys[12], 71), 0)
    prefix_length = draw_prefix_length(jax.random.fold_in(keys[12], 71), 0)
    routed_experts_keys = jax.random.split(jax.random.fold_in(keys[7], 1), NEW_POSITIONS * SEQUENCE_COUNT // TOK_DEV)
    routed_experts_turns = jax.random.permutation(jax.random.fold_in(keys[7], 3), NEW_POSITIONS * SEQUENCE_COUNT // TOK_DEV)
    routed_experts = jax.vmap(lambda own, number: routed_block(jax.random.fold_in(keys[7], 2), own, number, TOK_DEV, EXPERTS, TOP, CAP, 2))(routed_experts_keys, routed_experts_turns).reshape((NEW_POSITIONS, SEQUENCE_COUNT, TOP))
    route_weights = jnp.clip(0.1 + 0.5 * jax.random.uniform(keys[8], (NEW_POSITIONS, SEQUENCE_COUNT, TOP), jnp.float32) ** shard_levels(keys[8], (NEW_POSITIONS, SEQUENCE_COUNT, TOP), ((0, 64),), -0.2, 0.2), 0.1, 0.6)
    expert_gain = jnp.clip(1.0 + 0.15 * jax.random.normal(keys[9], (MODEL_DIM,), jnp.float32), 0.25, 1.75)
    w_gate_up = normal_values(keys[10], (EXPERTS, MODEL_DIM, 2, FFH), MODEL_DIM ** -0.5, 0.109375, ((0, 64), (3, 4)))
    w_down = normal_values(keys[11], (EXPERTS, FFH, MODEL_DIM), FFH ** -0.5, 0.15625, ((0, 64), (1, 4)))
    return dict(tokens=tokens, attn_gain=attn_gain, w_query=w_query, key_value_weight=key_value_weight, w_out=w_out, cache_keyval=cache_keyval, prefix_length=prefix_length, routed_experts=routed_experts, route_weights=route_weights, expert_gain=expert_gain, w_gate_up=w_gate_up, w_down=w_down)


EPSILON = 1e-05
ROPE_BASE = 150000.0

def rotate(vectors, places):
    half_dim = vectors.shape[-1] // 2
    steps_up = jnp.arange(half_dim, dtype=jnp.float32)
    frequency = jnp.exp(steps_up * (-math.log(ROPE_BASE) / half_dim))
    angles = places[..., None] * frequency
    cosine = jnp.cos(angles)
    sine_part = jnp.sin(angles)
    first_half = vectors[..., :half_dim]
    second_half = vectors[..., half_dim:]
    return jnp.concatenate([first_half * cosine - second_half * sine_part, second_half * cosine + first_half * sine_part], axis=-1)

def attend_sequence(query_heads, keys_all, values_all, cache_ok):
    group_width = QUERY_HEADS // KEY_VALUE_HEADS
    qblock = math.gcd(NEW_POSITIONS, 512)

    def one_block(block_index):
        block_queries = lax.dynamic_slice_in_dim(query_heads, block_index * qblock, qblock, 0).reshape(qblock * group_width, HEAD_SIZE)
        scores = jnp.dot(block_queries, keys_all.T, preferred_element_type=jnp.float32) * HEAD_SIZE ** (-0.5)
        query_place = block_index * qblock + jnp.arange(qblock * group_width, dtype=jnp.int32) // group_width
        span_ok = jnp.arange(NEW_POSITIONS, dtype=jnp.int32)[None, :] <= query_place[:, None]
        allowed = jnp.concatenate([jnp.broadcast_to(cache_ok[None, :], (qblock * group_width, CACHE_POSITIONS)), span_ok], axis=1)
        masked = jnp.where(allowed, scores, -1e+30)
        top_score = lax.optimization_barrier(jnp.max(masked, axis=1, keepdims=True))
        weights = jnp.where(allowed, jnp.exp(masked - top_score), 0.0)
        denominator = lax.optimization_barrier(jnp.sum(weights, axis=1, keepdims=True))
        probabilities = weights.astype(jnp.bfloat16)
        mixed_values = jnp.dot(probabilities, values_all, preferred_element_type=jnp.float32) / denominator
        return mixed_values.astype(jnp.bfloat16).reshape(qblock, group_width, HEAD_SIZE)
    blocks = lax.map(one_block, jnp.arange(NEW_POSITIONS // qblock, dtype=jnp.int32))
    return blocks.reshape(NEW_POSITIONS, group_width, HEAD_SIZE)

def reference(tokens, attn_gain, w_query, key_value_weight, w_out, cache_keyval, prefix_length, routed_experts, route_weights, expert_gain, w_gate_up, w_down):
    token_total_count = NEW_POSITIONS * SEQUENCE_COUNT
    group_width = QUERY_HEADS // KEY_VALUE_HEADS
    flat_tokens = tokens.reshape(token_total_count, MODEL_DIM).astype(jnp.float32)
    inverse_square_root = lax.rsqrt(lax.optimization_barrier(jnp.sum(flat_tokens * flat_tokens, axis=1)) / MODEL_DIM + EPSILON)
    rescaled = (flat_tokens * attn_gain).astype(jnp.bfloat16)
    queries_raw = jnp.dot(rescaled, w_query, preferred_element_type=jnp.float32) * inverse_square_root[:, None]
    key_value_unprojected = jnp.dot(rescaled, key_value_weight.reshape(MODEL_DIM, KEY_VALUE_HEADS * 2 * HEAD_SIZE), preferred_element_type=jnp.float32) * inverse_square_root[:, None]
    places = (prefix_length[None, :] + jnp.arange(NEW_POSITIONS, dtype=jnp.int32)[:, None]).reshape(token_total_count).astype(jnp.float32)
    query_matrix = rotate(queries_raw.reshape(token_total_count, QUERY_HEADS, HEAD_SIZE), places[:, None]).astype(jnp.bfloat16)
    key_value_heads = key_value_unprojected.reshape(token_total_count, KEY_VALUE_HEADS, 2 * HEAD_SIZE)
    rotated_keys = rotate(key_value_heads[..., :HEAD_SIZE], places[:, None])
    new_key_value_rows = jnp.concatenate([rotated_keys, key_value_heads[..., HEAD_SIZE:]], axis=-1).astype(jnp.bfloat16)
    query_lattice = query_matrix.reshape(NEW_POSITIONS, SEQUENCE_COUNT, KEY_VALUE_HEADS, group_width, HEAD_SIZE)
    new_position_lattice = new_key_value_rows.reshape(NEW_POSITIONS, SEQUENCE_COUNT, KEY_VALUE_HEADS, 2 * HEAD_SIZE)
    per_sequence = []
    for seq_index in range(SEQUENCE_COUNT):
        cache_ok = jnp.arange(CACHE_POSITIONS, dtype=jnp.int32) < prefix_length[seq_index]
        per_head = []
        for head_number_index in range(KEY_VALUE_HEADS):
            keys_all = jnp.concatenate([cache_keyval[:, seq_index, head_number_index, :HEAD_SIZE], new_position_lattice[:, seq_index, head_number_index, :HEAD_SIZE]], axis=0)
            values_all = jnp.concatenate([cache_keyval[:, seq_index, head_number_index, HEAD_SIZE:], new_position_lattice[:, seq_index, head_number_index, HEAD_SIZE:]], axis=0)
            per_head.append(attend_sequence(query_lattice[:, seq_index, head_number_index], keys_all, values_all, cache_ok))
        per_sequence.append(jnp.stack(per_head, axis=1))
    attended = jnp.stack(per_sequence, axis=1).reshape(token_total_count, QUERY_HEADS * HEAD_SIZE)
    projected = jnp.dot(attended, w_out, preferred_element_type=jnp.float32)
    hidden = (flat_tokens + projected).astype(jnp.bfloat16)
    hidden_wide = lax.optimization_barrier(hidden).astype(jnp.float32)
    second_root = lax.rsqrt(lax.optimization_barrier(jnp.sum(hidden_wide * hidden_wide, axis=1)) / MODEL_DIM + EPSILON)
    normed = (hidden_wide * second_root[:, None] * expert_gain).astype(jnp.bfloat16)
    choices_flat = routed_experts.reshape(token_total_count, TOP)
    weights_flat = route_weights.reshape(token_total_count, TOP)
    slots_all = N_EXPERT * CAP
    group_units = FFH // N_TENSOR

    def expert_step(expert_mix, inputs):
        gate_up_weight, down_weight, expert_index = inputs
        hits = choices_flat == expert_index
        token_weight = lax.optimization_barrier(jnp.sum(jnp.where(hits, weights_flat, 0.0), axis=1))
        chosen = jnp.any(hits, axis=1)
        picked = jnp.nonzero(chosen, size=slots_all, fill_value=0)[0].astype(jnp.int32)
        live = (jnp.arange(slots_all, dtype=jnp.int32) < jnp.sum(chosen.astype(jnp.int32))).astype(jnp.float32)
        rows_in = normed[picked]
        gate_up = jnp.dot(rows_in, gate_up_weight.reshape(MODEL_DIM, 2 * FFH), preferred_element_type=jnp.float32)
        gate_part = gate_up[:, :FFH]
        up_part = gate_up[:, FFH:]
        activated = (gate_part * jax.nn.sigmoid(1.702 * gate_part) * (up_part + 1.0)).astype(jnp.bfloat16)
        grouped = lax.optimization_barrier(activated).astype(jnp.float32).reshape(slots_all, N_TENSOR, group_units)
        down_groups = down_weight.astype(jnp.float32).reshape(N_TENSOR, group_units, MODEL_DIM)
        partials = jnp.einsum('mtf,tfd->tmd', grouped, down_groups, precision=lax.Precision.HIGHEST)
        rounded = lax.optimization_barrier(partials.astype(jnp.bfloat16)).astype(jnp.float32)
        expert_out = lax.optimization_barrier(jnp.sum(rounded, axis=0))
        scale_rows = token_weight[picked] * live
        return (expert_mix.at[picked].add(scale_rows[:, None] * expert_out), None)
    start_mix = jnp.zeros((token_total_count, MODEL_DIM), jnp.float32)
    expert_mix, unused_out = lax.scan(expert_step, start_mix, (w_gate_up, w_down, jnp.arange(EXPERTS, dtype=jnp.int32)))
    layer_output = (hidden_wide + expert_mix).astype(jnp.bfloat16).reshape(NEW_POSITIONS, SEQUENCE_COUNT, MODEL_DIM)
    return (layer_output, new_key_value_rows.reshape(NEW_POSITIONS, SEQUENCE_COUNT, KEY_VALUE_HEADS, 2 * HEAD_SIZE))
```

```python
import functools
import math

import jax
import jax.numpy as jnp
from jax import lax
from jax.experimental import pallas as pl
from jax.experimental.pallas import tpu as pltpu
from jax.sharding import PartitionSpec as P

EPSILON = 1e-05
ROPE_BASE = 150000.0
NEG = -1e30
MESH = pl.DeviceIdType.MESH
NY, NX, NZ = 2, 4, 8
LOG2E = 1.4426950408889634


def place_of(expert_rank):
    return expert_rank // (NX * NZ), (expert_rank // NZ) % NX, expert_rank % NZ


def rank_of(y_lo, x, z):
    return (y_lo * NX + x) * NZ + z


def greet(devices):
    barrier = pltpu.get_barrier_semaphore()
    for device in devices:
        pl.semaphore_signal(barrier, inc=1, device_id=device, device_id_type=MESH)
    pl.semaphore_wait(barrier, len(devices))


def send(src, dst, send_sem, recv_sem, device):
    copy = pltpu.make_async_remote_copy(
        src_ref=src,
        dst_ref=dst,
        send_sem=send_sem,
        recv_sem=recv_sem,
        device_id=device,
        device_id_type=MESH,
    )
    copy.start()
    return copy


def arrived(dst, send_sem, recv_sem, device):
    pltpu.make_async_remote_copy(
        src_ref=dst,
        dst_ref=dst,
        send_sem=send_sem,
        recv_sem=recv_sem,
        device_id=device,
        device_id_type=MESH,
    ).wait_recv()


def exchange_kernel(kv, q, kv_all, q_all, own_sem, xs, xr, ys, yr, zs, zr):
    rank, tensor = lax.axis_index("expert"), lax.axis_index("tensor")
    y_lo, x, z = place_of(rank)
    other = 1 - y_lo
    x_peers = [(rank_of(y_lo, lax.rem(x + d, NX), z), tensor) for d in range(1, NX)]
    y_peer = (rank_of(other, x, z), tensor)
    ring = [
        (rank_of(y_lo, x, lax.rem(z + 1, NZ)), tensor),
        (rank_of(y_lo, x, lax.rem(z + NZ - 1, NZ)), tensor),
    ]
    greet(x_peers + [y_peer] + ring)
    own = [
        pltpu.make_async_copy(kv, kv_all.at[z * 2 + y_lo], own_sem.at[0]),
        pltpu.make_async_copy(q, q_all.at[x], own_sem.at[1]),
    ]
    for copy in own:
        copy.start()
    pending = [send(kv, kv_all.at[z * 2 + y_lo], ys.at[0], yr.at[0], y_peer)]

    def slot(direction, steps, piece):
        origin = lax.rem(z + (NZ - steps if direction == 0 else steps), NZ)
        return kv_all.at[origin * 2 + (y_lo if piece == 0 else other)]

    def sems(direction, step, piece):
        index = 2 * (step - 1) + piece
        return zs.at[direction, index], zr.at[direction, index]

    def pass_on(direction, step, piece):
        src = kv if step == 1 and piece == 0 else slot(direction, step - 1, piece)
        pending.append(
            send(src, slot(direction, step - 1, piece), *sems(direction, step, piece), ring[direction])
        )

    def got(direction, step, piece):
        arrived(slot(direction, step, piece), *sems(direction, step, piece), ring[direction])

    for direction in range(2):
        pass_on(direction, 1, 0)
    for d in range(1, NX):
        pending.append(send(q, q_all.at[x], xs.at[d - 1], xr.at[d - 1], x_peers[d - 1]))
    arrived(kv_all.at[z * 2 + other], ys.at[0], yr.at[0], y_peer)
    for direction in range(2):
        pass_on(direction, 1, 1)
    half = NZ // 2
    for step in range(2, half + 1):
        for piece in range(2):
            for direction in range(2):
                got(direction, step - 1, piece)
                if step < half or direction == piece:
                    pass_on(direction, step, piece)
    for direction in range(2):
        got(direction, half, direction)
    for d in range(1, NX):
        arrived(q_all.at[lax.rem(x + NX - d, NX)], xs.at[d - 1], xr.at[d - 1], x_peers[d - 1])
    for copy in own:
        copy.wait()
    for copy in pending:
        copy.wait_send()


def exchange(kv, q):
    return pl.pallas_call(
        exchange_kernel,
        out_shape=(
            jax.ShapeDtypeStruct((NY * NZ,) + kv.shape, kv.dtype),
            jax.ShapeDtypeStruct((NX,) + q.shape, q.dtype),
        ),
        in_specs=[pl.BlockSpec(memory_space=pl.ANY)] * 2,
        out_specs=(pl.BlockSpec(memory_space=pl.ANY),) * 2,
        scratch_shapes=[
            pltpu.SemaphoreType.DMA((2,)),
            pltpu.SemaphoreType.DMA((NX - 1,)),
            pltpu.SemaphoreType.DMA((NX - 1,)),
            pltpu.SemaphoreType.DMA((1,)),
            pltpu.SemaphoreType.DMA((1,)),
            pltpu.SemaphoreType.DMA((2, NZ)),
            pltpu.SemaphoreType.DMA((2, NZ)),
        ],
        compiler_params=pltpu.CompilerParams(collective_id=0, has_side_effects=True),
        name="exchange",
    )(kv, q)


def attend_kernel(my_x, q_ref, kv_ref, mask_ref, o_ref, stat_ref, vt_ref, qa_ref):
    xq = pl.program_id(1)
    chunks, _, chunk = vt_ref.shape
    shards, _, keys, width = kv_ref.shape
    per = chunk // keys
    head, cols = q_ref.shape[2:]

    @pl.when(xq == 0)
    def _():
        for j in range(chunks):
            rows = kv_ref[j * per : (j + 1) * per, 0].reshape(chunk, width)
            flipped = rows.astype(jnp.float32).T
            vt_ref[j, :16, :] = jnp.ones((16, chunk), jnp.bfloat16)
            vt_ref[j, 16:, :] = flipped[head:].astype(jnp.bfloat16)

    qa_ref[:head, :] = q_ref[0, 0]
    qa_ref[head:width, :] = jnp.zeros((width - head, cols), jnp.bfloat16)
    row = lax.broadcasted_iota(jnp.int32, (width, cols), 0)
    lane = lax.broadcasted_iota(jnp.int32, (width, cols), 1)
    span = head
    tri = jnp.where(xq == my_x[0], lane % span, -1)
    hot = (row == tri) | (row == span + xq) | (row == span + NX)
    qa_ref[width:, :] = jnp.where(hot, 1.0, 0.0).astype(jnp.bfloat16)
    qa = qa_ref[...]
    top = jnp.full((1, cols), -3e38, jnp.float32)
    acc = jnp.zeros((vt_ref.shape[1], cols), jnp.float32)
    for j in range(chunks):
        lhs = jnp.concatenate(
            [
                kv_ref[j * per : (j + 1) * per, 0].reshape(chunk, width),
                mask_ref[0, j * per : (j + 1) * per].reshape(chunk, width),
            ],
            axis=1,
        )
        scores = jnp.dot(lhs, qa, preferred_element_type=jnp.float32)
        new_top = jnp.maximum(top, jnp.max(scores, axis=0, keepdims=True))
        probs = jnp.exp2(scores - new_top).astype(jnp.bfloat16)
        acc = acc * jnp.exp2(top - new_top) + jnp.dot(
            vt_ref[j], probs, preferred_element_type=jnp.float32
        )
        top = new_top
    total = acc[0:1]
    o_ref[0, 0] = (acc[16:] / total).astype(jnp.bfloat16)
    stat_ref[0, 0, 0:1, :] = top
    stat_ref[0, 0, 1:2, :] = total
    stat_ref[0, 0, 2:, :] = jnp.zeros((6, cols), jnp.float32)


def attend(my_x, q_all, kv_all, mask):
    nx, seqs, head, cols = q_all.shape
    shards, _, keys, width = kv_all.shape
    chunk = 2 * keys
    chunks = shards * keys // chunk
    return pl.pallas_call(
        attend_kernel,
        grid=(seqs, nx),
        in_specs=[
            pl.BlockSpec(memory_space=pltpu.SMEM),
            pl.BlockSpec((1, 1, head, cols), lambda s, i: (i, s, 0, 0)),
            pl.BlockSpec((shards, 1, keys, width), lambda s, i: (0, s, 0, 0)),
            pl.BlockSpec((1, shards, keys, width), lambda s, i: (s, 0, 0, 0)),
        ],
        out_shape=(
            jax.ShapeDtypeStruct((nx, seqs, head, cols), jnp.bfloat16),
            jax.ShapeDtypeStruct((nx, seqs, 8, cols), jnp.float32),
        ),
        out_specs=(
            pl.BlockSpec((1, 1, head, cols), lambda s, i: (i, s, 0, 0)),
            pl.BlockSpec((1, 1, 8, cols), lambda s, i: (i, s, 0, 0)),
        ),
        scratch_shapes=[
            pltpu.VMEM((chunks, 16 + head, chunk), jnp.bfloat16),
            pltpu.VMEM((2 * width, cols), jnp.bfloat16),
        ],
        compiler_params=pltpu.CompilerParams(vmem_limit_bytes=48 * 1024 * 1024),
        name="attend",
    )(my_x, q_all, kv_all, mask)


def back_kernel(o, stat, o_in, stat_in, own_sem, os, orr, ss, sr):
    rank, tensor = lax.axis_index("expert"), lax.axis_index("tensor")
    y_lo, x, z = place_of(rank)
    peers = [(rank_of(y_lo, lax.rem(x + d, NX), z), tensor) for d in range(1, NX)]
    greet(peers)
    own = [
        pltpu.make_async_copy(o.at[x], o_in.at[x], own_sem.at[0]),
        pltpu.make_async_copy(stat.at[x], stat_in.at[x], own_sem.at[1]),
    ]
    for copy in own:
        copy.start()
    pending = []
    for d in range(1, NX):
        to = lax.rem(x + d, NX)
        pending.append(send(o.at[to], o_in.at[x], os.at[d - 1], orr.at[d - 1], peers[d - 1]))
        pending.append(send(stat.at[to], stat_in.at[x], ss.at[d - 1], sr.at[d - 1], peers[d - 1]))
    for d in range(1, NX):
        source = lax.rem(x + NX - d, NX)
        arrived(o_in.at[source], os.at[d - 1], orr.at[d - 1], peers[d - 1])
        arrived(stat_in.at[source], ss.at[d - 1], sr.at[d - 1], peers[d - 1])
    for copy in own:
        copy.wait()
    for copy in pending:
        copy.wait_send()


def send_back(o, stat):
    return pl.pallas_call(
        back_kernel,
        out_shape=(
            jax.ShapeDtypeStruct(o.shape, o.dtype),
            jax.ShapeDtypeStruct(stat.shape, stat.dtype),
        ),
        in_specs=[pl.BlockSpec(memory_space=pl.ANY)] * 2,
        out_specs=(pl.BlockSpec(memory_space=pl.ANY),) * 2,
        scratch_shapes=[pltpu.SemaphoreType.DMA((2,))]
        + [pltpu.SemaphoreType.DMA((NX - 1,))] * 4,
        compiler_params=pltpu.CompilerParams(collective_id=1, has_side_effects=True),
        name="send_back",
    )(o, stat)


def key_masks(prefix_length, expert_rank, cache_rows, span, width):
    y_lo, x, z = place_of(expert_rank)
    shape = (prefix_length.shape[0], NY * NZ, cache_rows + span, width)
    shard = lax.broadcasted_iota(jnp.int32, shape, 1)
    row = lax.broadcasted_iota(jnp.int32, shape, 2)
    col = lax.broadcasted_iota(jnp.int32, shape, 3)
    key_rank = rank_of(shard % 2, x, shard // 2)
    in_cache = row < cache_rows
    beyond = (key_rank * cache_rows + row >= prefix_length[:, None, None, None]) & (
        col == span + NX
    )
    later_block = (col >= span) & (col < span + NX) & (key_rank > rank_of(y_lo, col - span, z))
    later_key = (col < span) & (key_rank == expert_rank) & (row - cache_rows > col)
    blocked = jnp.where(in_cache, beyond, later_block | later_key)
    return jnp.where(blocked, NEG, 0.0).astype(jnp.bfloat16)


def rotate(vectors, places):
    half_dim = vectors.shape[-1] // 2
    steps_up = jnp.arange(half_dim, dtype=jnp.float32)
    frequency = jnp.exp(steps_up * (-math.log(ROPE_BASE) / half_dim))
    angles = places[..., None] * frequency
    cosine = jnp.cos(angles)
    sine_part = jnp.sin(angles)
    first_half = vectors[..., :half_dim]
    second_half = vectors[..., half_dim:]
    return jnp.concatenate(
        [
            first_half * cosine - second_half * sine_part,
            second_half * cosine + first_half * sine_part,
        ],
        axis=-1,
    )


def on_device(
    tokens,
    attn_gain,
    w_query,
    key_value_weight,
    w_out,
    cache_keyval,
    prefix_length,
    routed_experts,
    route_weights,
    expert_gain,
    w_gate_up,
    w_down,
):
    span_dev, seq_count, quarter = tokens.shape
    model_width = attn_gain.shape[0]
    row_count = span_dev * seq_count
    local_kv = key_value_weight.shape[1]
    head_dim = key_value_weight.shape[2] // 2
    query_cols = w_query.shape[1]
    group_width = query_cols // head_dim // local_kv
    cache_rows = cache_keyval.shape[0]
    tensor_rank = lax.axis_index("tensor")
    expert_rank = lax.axis_index("expert")
    shard_piece = lax.all_gather(tokens, "tensor", axis=2, tiled=True)
    col_count = shard_piece.shape[2]
    piece_rows = shard_piece.reshape(row_count, col_count).astype(jnp.float32)
    rescaled = (piece_rows * attn_gain).astype(jnp.bfloat16)
    keyval_rows = key_value_weight.reshape(col_count, local_kv * 2 * head_dim)
    query_acc = jnp.dot(rescaled, w_query, preferred_element_type=jnp.float32)
    keyval_acc = jnp.dot(rescaled, keyval_rows, preferred_element_type=jnp.float32)
    square_sum = jnp.sum(piece_rows * piece_rows, axis=1)
    inverse_square_root = lax.rsqrt(square_sum / model_width + EPSILON)
    span_place = expert_rank * span_dev + jnp.arange(span_dev, dtype=jnp.int32)
    places = (prefix_length[None, :] + span_place[:, None]).reshape(row_count).astype(jnp.float32)
    query_scale = head_dim ** (-0.5) * LOG2E
    query_matrix = (
        rotate(
            (query_acc * inverse_square_root[:, None]).reshape(
                row_count, query_cols // head_dim, head_dim
            ),
            places[:, None],
        )
        * query_scale
    ).astype(jnp.bfloat16)
    key_value_heads = (keyval_acc * inverse_square_root[:, None]).reshape(
        row_count, local_kv, 2 * head_dim
    )
    rotated_keys = rotate(key_value_heads[..., :head_dim], places[:, None])
    new_key_value_rows = jnp.concatenate(
        [rotated_keys, key_value_heads[..., head_dim:]], axis=-1
    ).astype(jnp.bfloat16)
    new_key_value_rows = new_key_value_rows.reshape(span_dev, seq_count, local_kv, 2 * head_dim)
    query_count = span_dev * group_width
    own_queries = query_matrix.reshape(span_dev, seq_count, group_width, head_dim).transpose(
        1, 3, 2, 0
    )
    own_queries = own_queries.reshape(seq_count, head_dim, query_count)
    joined = jnp.concatenate([cache_keyval, new_key_value_rows], axis=0)[:, :, 0, :]
    joined = joined.transpose(1, 0, 2)
    kv_all, q_all = exchange(joined, own_queries)
    mask = key_masks(prefix_length, expert_rank, cache_rows, span_dev, 2 * head_dim)
    my_x = place_of(expert_rank)[1].astype(jnp.int32).reshape(1)
    part, stat = attend(my_x, q_all, kv_all, mask)
    part, stat = send_back(part, stat)
    tops, sums = stat[:, :, 0, :], stat[:, :, 1, :]
    share = jnp.exp2(tops - jnp.max(tops, axis=0)) * sums
    share = share / jnp.sum(share, axis=0)
    attended = jnp.sum(part.astype(jnp.float32) * share[:, :, None, :], axis=0).astype(jnp.bfloat16)
    attended = (
        attended.reshape(seq_count, head_dim, group_width, span_dev)
        .transpose(3, 0, 2, 1)
        .reshape(row_count, query_cols)
    )
    projected = jnp.dot(attended, w_out, preferred_element_type=jnp.float32)
    own_cols = lax.dynamic_slice_in_dim(
        projected, tensor_rank * quarter, quarter, 1
    ) + tokens.reshape(row_count, quarter).astype(jnp.float32)
    residual_term = lax.dynamic_update_slice_in_dim(projected, own_cols, tensor_rank * quarter, 1)
    hidden_sum = lax.psum(residual_term.astype(jnp.bfloat16), "tensor")
    hidden_wide = lax.optimization_barrier(hidden_sum).astype(jnp.float32)
    second_root = lax.rsqrt(jnp.sum(hidden_wide * hidden_wide, axis=1) / model_width + EPSILON)
    normed = (hidden_wide * second_root[:, None] * expert_gain).astype(jnp.bfloat16)
    top_count = routed_experts.shape[2]
    expert_count = lax.axis_size("expert")
    capacity = min(row_count, max(2, 5 * row_count * top_count // (2 * expert_count)))
    expert_list = routed_experts.reshape(row_count * top_count)
    one_hot = (expert_list[:, None] == jnp.arange(expert_count, dtype=jnp.int32)[None, :]).astype(
        jnp.int32
    )
    earlier = jnp.cumsum(one_hot, axis=0) - one_hot
    arrival = jnp.sum(earlier * one_hot, axis=1)
    slot_index = expert_list * capacity + arrival
    ffn_local = w_down.shape[1]
    gate_up_rows = w_gate_up[0].reshape(model_width, 2 * ffn_local)
    outgoing = (
        jnp.zeros((expert_count * capacity, model_width), jnp.bfloat16)
        .at[slot_index]
        .set(jnp.repeat(normed, top_count, axis=0))
    )
    received = lax.all_to_all(
        outgoing.reshape(expert_count, capacity, model_width),
        "expert",
        split_axis=0,
        concat_axis=0,
        tiled=True,
    )
    gate_up = jnp.dot(
        received.reshape(expert_count * capacity, model_width),
        gate_up_rows,
        preferred_element_type=jnp.float32,
    )
    gate_part = gate_up[:, :ffn_local]
    up_part = gate_up[:, ffn_local:]
    activated = (gate_part * jax.nn.sigmoid(1.702 * gate_part) * (up_part + 1.0)).astype(
        jnp.bfloat16
    )
    partial_value = jnp.dot(activated, w_down[0], preferred_element_type=jnp.float32)
    weight_cols = route_weights.reshape(row_count, top_count, 1)
    owner_sums = lax.psum_scatter(
        partial_value.astype(jnp.bfloat16), "tensor", scatter_dimension=1, tiled=True
    ).astype(jnp.float32)
    returned_rows = lax.all_to_all(
        owner_sums.reshape(expert_count, capacity, quarter).astype(jnp.bfloat16),
        "expert",
        split_axis=0,
        concat_axis=0,
        tiled=True,
    ).astype(jnp.float32)
    picked = returned_rows.reshape(expert_count * capacity, quarter)[slot_index]
    expert_mix = jnp.sum(picked.reshape(row_count, top_count, quarter) * weight_cols, axis=1)
    hidden_quarter = lax.dynamic_slice_in_dim(hidden_wide, tensor_rank * quarter, quarter, 1)
    layer_output = (
        (hidden_quarter + expert_mix).astype(jnp.bfloat16).reshape(span_dev, seq_count, quarter)
    )
    return (layer_output, new_key_value_rows)


def solution(mesh):
    return jax.shard_map(
        on_device,
        mesh=mesh,
        in_specs=(
            P("expert", None, "tensor"),
            P(),
            P(None, "tensor"),
            P(None, "tensor", None),
            P("tensor", None),
            P("expert", None, "tensor", None),
            P(),
            P("expert", None, None),
            P("expert", None, None),
            P(),
            P("expert", None, None, "tensor"),
            P("expert", "tensor", None),
        ),
        out_specs=(P("expert", None, "tensor"), P("expert", None, "tensor", None)),
        check_vma=False,
    )
```

```python
import functools
import math

import jax
import jax.numpy as jnp
from jax import lax
from jax.experimental import pallas as pl
from jax.experimental.pallas import tpu as pltpu
from jax.sharding import PartitionSpec as P

EPSILON = 1e-05
ROPE_BASE = 150000.0
NEG = -1e30
MESH = pl.DeviceIdType.MESH
NY, NX, NZ = 2, 4, 8
LOG2E = 1.4426950408889634


def place_of(expert_rank):
    return expert_rank // (NX * NZ), (expert_rank // NZ) % NX, expert_rank % NZ


def rank_of(y_lo, x, z):
    return (y_lo * NX + x) * NZ + z


def greet(devices):
    barrier = pltpu.get_barrier_semaphore()
    for device in devices:
        pl.semaphore_signal(barrier, inc=1, device_id=device, device_id_type=MESH)
    pl.semaphore_wait(barrier, len(devices))


def send(src, dst, send_sem, recv_sem, device):
    copy = pltpu.make_async_remote_copy(
        src_ref=src,
        dst_ref=dst,
        send_sem=send_sem,
        recv_sem=recv_sem,
        device_id=device,
        device_id_type=MESH,
    )
    copy.start()
    return copy


def arrived(dst, send_sem, recv_sem, device):
    pltpu.make_async_remote_copy(
        src_ref=dst,
        dst_ref=dst,
        send_sem=send_sem,
        recv_sem=recv_sem,
        device_id=device,
        device_id_type=MESH,
    ).wait_recv()


def exchange_kernel(
    kv, q, slab, kv_all, q_all, slab_all, own_sem, xs, xr, ys, yr, zs, zr, ts, tr
):
    rank, tensor = lax.axis_index("expert"), lax.axis_index("tensor")
    y_lo, x, z = place_of(rank)
    other = 1 - y_lo
    x_peers = [(rank_of(y_lo, lax.rem(x + d, NX), z), tensor) for d in range(1, NX)]
    y_peer = (rank_of(other, x, z), tensor)
    z_peers = [(rank_of(y_lo, x, lax.rem(z + d, NZ)), tensor) for d in range(1, NZ)]
    ring = [z_peers[0], z_peers[-1]]
    greet(x_peers + [y_peer] + z_peers)
    own = [
        pltpu.make_async_copy(kv, kv_all.at[z * 2 + y_lo], own_sem.at[0]),
        pltpu.make_async_copy(q, q_all.at[x], own_sem.at[1]),
        pltpu.make_async_copy(slab.at[z], slab_all.at[z], own_sem.at[2]),
    ]
    for copy in own:
        copy.start()
    pending = [send(kv, kv_all.at[z * 2 + y_lo], ys.at[0], yr.at[0], y_peer)]

    def slot(direction, steps, piece):
        origin = lax.rem(z + (NZ - steps if direction == 0 else steps), NZ)
        return kv_all.at[origin * 2 + (y_lo if piece == 0 else other)]

    def sems(direction, step, piece):
        index = 2 * (step - 1) + piece
        return zs.at[direction, index], zr.at[direction, index]

    def pass_on(direction, step, piece):
        src = kv if step == 1 and piece == 0 else slot(direction, step - 1, piece)
        pending.append(
            send(src, slot(direction, step - 1, piece), *sems(direction, step, piece), ring[direction])
        )

    def got(direction, step, piece):
        arrived(slot(direction, step, piece), *sems(direction, step, piece), ring[direction])

    for direction in range(2):
        pass_on(direction, 1, 0)
    for d in range(1, NX):
        pending.append(send(q, q_all.at[x], xs.at[d - 1], xr.at[d - 1], x_peers[d - 1]))
    for d in range(1, NZ):
        to = lax.rem(z + d, NZ)
        pending.append(
            send(slab.at[to], slab_all.at[z], ts.at[d - 1], tr.at[d - 1], z_peers[d - 1])
        )
    arrived(kv_all.at[z * 2 + other], ys.at[0], yr.at[0], y_peer)
    for direction in range(2):
        pass_on(direction, 1, 1)
    half = NZ // 2
    for step in range(2, half + 1):
        for piece in range(2):
            for direction in range(2):
                got(direction, step - 1, piece)
                if step < half or direction == piece:
                    pass_on(direction, step, piece)
    for direction in range(2):
        got(direction, half, direction)
    for d in range(1, NX):
        arrived(q_all.at[lax.rem(x + NX - d, NX)], xs.at[d - 1], xr.at[d - 1], x_peers[d - 1])
    for d in range(1, NZ):
        arrived(
            slab_all.at[lax.rem(z + NZ - d, NZ)], ts.at[d - 1], tr.at[d - 1], z_peers[d - 1]
        )
    for copy in own:
        copy.wait()
    for copy in pending:
        copy.wait_send()


def exchange(kv, q, slab):
    return pl.pallas_call(
        exchange_kernel,
        out_shape=(
            jax.ShapeDtypeStruct((NY * NZ,) + kv.shape, kv.dtype),
            jax.ShapeDtypeStruct((NX,) + q.shape, q.dtype),
            jax.ShapeDtypeStruct(slab.shape, slab.dtype),
        ),
        in_specs=[pl.BlockSpec(memory_space=pl.ANY)] * 3,
        out_specs=(pl.BlockSpec(memory_space=pl.ANY),) * 3,
        scratch_shapes=[
            pltpu.SemaphoreType.DMA((3,)),
            pltpu.SemaphoreType.DMA((NX - 1,)),
            pltpu.SemaphoreType.DMA((NX - 1,)),
            pltpu.SemaphoreType.DMA((1,)),
            pltpu.SemaphoreType.DMA((1,)),
            pltpu.SemaphoreType.DMA((2, NZ)),
            pltpu.SemaphoreType.DMA((2, NZ)),
            pltpu.SemaphoreType.DMA((NZ - 1,)),
            pltpu.SemaphoreType.DMA((NZ - 1,)),
        ],
        compiler_params=pltpu.CompilerParams(collective_id=0, has_side_effects=True),
        name="exchange",
    )(kv, q, slab)


def attend_kernel(my_x, q_ref, kv_ref, mask_ref, o_ref, stat_ref, vt_ref, qa_ref):
    xq = pl.program_id(1)
    chunks, _, chunk = vt_ref.shape
    shards, _, keys, width = kv_ref.shape
    per = chunk // keys
    head, cols = q_ref.shape[2:]

    @pl.when(xq == 0)
    def _():
        for j in range(chunks):
            rows = kv_ref[j * per : (j + 1) * per, 0].reshape(chunk, width)
            flipped = rows.astype(jnp.float32).T
            vt_ref[j, :16, :] = jnp.ones((16, chunk), jnp.bfloat16)
            vt_ref[j, 16:, :] = flipped[head:].astype(jnp.bfloat16)

    qa_ref[:head, :] = q_ref[0, 0]
    qa_ref[head:width, :] = jnp.zeros((width - head, cols), jnp.bfloat16)
    row = lax.broadcasted_iota(jnp.int32, (width, cols), 0)
    lane = lax.broadcasted_iota(jnp.int32, (width, cols), 1)
    span = head
    tri = jnp.where(xq == my_x[0], lane % span, -1)
    hot = (row == tri) | (row == span + xq) | (row == span + NX)
    qa_ref[width:, :] = jnp.where(hot, 1.0, 0.0).astype(jnp.bfloat16)
    qa = qa_ref[...]
    top = jnp.full((1, cols), -3e38, jnp.float32)
    acc = jnp.zeros((vt_ref.shape[1], cols), jnp.float32)
    for j in range(chunks):
        lhs = jnp.concatenate(
            [
                kv_ref[j * per : (j + 1) * per, 0].reshape(chunk, width),
                mask_ref[0, j * per : (j + 1) * per].reshape(chunk, width),
            ],
            axis=1,
        )
        scores = jnp.dot(lhs, qa, preferred_element_type=jnp.float32)
        new_top = jnp.maximum(top, jnp.max(scores, axis=0, keepdims=True))
        probs = jnp.exp2(scores - new_top).astype(jnp.bfloat16)
        acc = acc * jnp.exp2(top - new_top) + jnp.dot(
            vt_ref[j], probs, preferred_element_type=jnp.float32
        )
        top = new_top
    total = acc[0:1]
    o_ref[0, 0] = (acc[16:] / total).astype(jnp.bfloat16)
    stat_ref[0, 0, 0:1, :] = top
    stat_ref[0, 0, 1:2, :] = total
    stat_ref[0, 0, 2:, :] = jnp.zeros((6, cols), jnp.float32)


def attend(my_x, q_all, kv_all, mask):
    nx, seqs, head, cols = q_all.shape
    shards, _, keys, width = kv_all.shape
    chunk = 2 * keys
    chunks = shards * keys // chunk
    return pl.pallas_call(
        attend_kernel,
        grid=(seqs, nx),
        in_specs=[
            pl.BlockSpec(memory_space=pltpu.SMEM),
            pl.BlockSpec((1, 1, head, cols), lambda s, i: (i, s, 0, 0)),
            pl.BlockSpec((shards, 1, keys, width), lambda s, i: (0, s, 0, 0)),
            pl.BlockSpec((1, shards, keys, width), lambda s, i: (s, 0, 0, 0)),
        ],
        out_shape=(
            jax.ShapeDtypeStruct((nx, seqs, head, cols), jnp.bfloat16),
            jax.ShapeDtypeStruct((nx, seqs, 8, cols), jnp.float32),
        ),
        out_specs=(
            pl.BlockSpec((1, 1, head, cols), lambda s, i: (i, s, 0, 0)),
            pl.BlockSpec((1, 1, 8, cols), lambda s, i: (i, s, 0, 0)),
        ),
        scratch_shapes=[
            pltpu.VMEM((chunks, 16 + head, chunk), jnp.bfloat16),
            pltpu.VMEM((2 * width, cols), jnp.bfloat16),
        ],
        compiler_params=pltpu.CompilerParams(vmem_limit_bytes=48 * 1024 * 1024),
        name="attend",
    )(my_x, q_all, kv_all, mask)


def back_kernel(o, stat, o_in, stat_in, own_sem, os, orr, ss, sr):
    rank, tensor = lax.axis_index("expert"), lax.axis_index("tensor")
    y_lo, x, z = place_of(rank)
    peers = [(rank_of(y_lo, lax.rem(x + d, NX), z), tensor) for d in range(1, NX)]
    greet(peers)
    own = [
        pltpu.make_async_copy(o.at[x], o_in.at[x], own_sem.at[0]),
        pltpu.make_async_copy(stat.at[x], stat_in.at[x], own_sem.at[1]),
    ]
    for copy in own:
        copy.start()
    pending = []
    for d in range(1, NX):
        to = lax.rem(x + d, NX)
        pending.append(send(o.at[to], o_in.at[x], os.at[d - 1], orr.at[d - 1], peers[d - 1]))
        pending.append(send(stat.at[to], stat_in.at[x], ss.at[d - 1], sr.at[d - 1], peers[d - 1]))
    for d in range(1, NX):
        source = lax.rem(x + NX - d, NX)
        arrived(o_in.at[source], os.at[d - 1], orr.at[d - 1], peers[d - 1])
        arrived(stat_in.at[source], ss.at[d - 1], sr.at[d - 1], peers[d - 1])
    for copy in own:
        copy.wait()
    for copy in pending:
        copy.wait_send()


def send_back(o, stat):
    return pl.pallas_call(
        back_kernel,
        out_shape=(
            jax.ShapeDtypeStruct(o.shape, o.dtype),
            jax.ShapeDtypeStruct(stat.shape, stat.dtype),
        ),
        in_specs=[pl.BlockSpec(memory_space=pl.ANY)] * 2,
        out_specs=(pl.BlockSpec(memory_space=pl.ANY),) * 2,
        scratch_shapes=[pltpu.SemaphoreType.DMA((2,))]
        + [pltpu.SemaphoreType.DMA((NX - 1,))] * 4,
        compiler_params=pltpu.CompilerParams(collective_id=1, has_side_effects=True),
        name="send_back",
    )(o, stat)


def corner(rank, tensor):
    y_lo, x, z = place_of(rank)
    y_hi, core = tensor // 2, lax.rem(tensor, 2)
    far = (rank, (1 - y_hi) * 2 + core)
    sides = [(rank_of(1 - y_lo, x, z), lax.rem(y_hi + r, 2) * 2 + core) for r in range(2)]
    mate = (rank, y_hi * 2 + 1 - core)
    return y_lo, x, z, y_hi, core, far, sides, mate


def f32(value):
    return value.astype(jnp.float32)


def norm_kernel(
    model_width, part, own_tokens, gain, hidden, spread,
    core_in, core_out, far_in, squares, squares_in, own_sem, cs, cr, fs, fr, qs, qr, zs, zr,
):
    rank, tensor = lax.axis_index("expert"), lax.axis_index("tensor")
    y_lo, x, z, y_hi, core, far, sides, mate = corner(rank, tensor)
    cross = (rank, (1 - y_hi) * 2 + 1 - core)
    ring = [
        (rank_of(y_lo, x, lax.rem(z + 1, NZ)), tensor),
        (rank_of(y_lo, x, lax.rem(z + NZ - 1, NZ)), tensor),
    ]
    greet([mate, far, cross] + ring)
    pending = []
    order = [1 - y_hi, y_hi]
    for i in range(2):
        src = part.at[order[i] * 2 + 1 - core]
        pending.append(send(src, core_in.at[i], cs.at[i], cr.at[i], mate))
    arrived(core_in.at[0], cs.at[0], cr.at[0], mate)
    core_out[...] = (f32(part[order[0] * 2 + core]) + f32(core_in[0])).astype(jnp.bfloat16)
    pending.append(send(core_out, far_in, fs.at[0], fr.at[0], far))
    arrived(core_in.at[1], cs.at[1], cr.at[1], mate)
    near = f32(own_tokens[...]) + (f32(part[order[1] * 2 + core]) + f32(core_in[1]))
    arrived(far_in, fs.at[0], fr.at[0], far)
    rounded = (near + f32(far_in[...])).astype(jnp.bfloat16)
    hidden[...] = rounded
    wide = f32(rounded)
    own_squares = jnp.sum(wide * wide, axis=1, keepdims=True)
    squares[...] = jnp.broadcast_to(own_squares, squares.shape)
    trio = [mate, far, cross]
    for i in range(3):
        pending.append(send(squares, squares_in.at[i], qs.at[i], qr.at[i], trio[i]))
    total = own_squares
    for i in range(3):
        arrived(squares_in.at[i], qs.at[i], qr.at[i], trio[i])
        total = total + squares_in[i, :, 0:1]
    root = lax.rsqrt(total / model_width + EPSILON)
    spread[z] = (wide * root * gain[...]).astype(jnp.bfloat16)
    rows = wide.shape[0] // 2

    def slot(direction, steps, piece):
        origin = lax.rem(z + (NZ - steps if direction == 0 else steps), NZ)
        return spread.at[origin, pl.ds(piece * rows, rows)]

    def sems(direction, step, piece):
        index = 2 * (step - 1) + piece
        return zs.at[direction, index], zr.at[direction, index]

    def pass_on(direction, step, piece):
        block = slot(direction, step - 1, piece)
        pending.append(send(block, block, *sems(direction, step, piece), ring[direction]))

    def got(direction, step, piece):
        arrived(slot(direction, step, piece), *sems(direction, step, piece), ring[direction])

    half = NZ // 2
    for piece in range(2):
        for direction in range(2):
            pass_on(direction, 1, piece)
    for step in range(2, half + 1):
        for piece in range(2):
            for direction in range(2):
                got(direction, step - 1, piece)
                if step < half or direction == piece:
                    pass_on(direction, step, piece)
    for direction in range(2):
        got(direction, half, direction)
    for copy in pending:
        copy.wait_send()


def norm_and_spread(part, own_tokens, gain, model_width):
    rows, quarter = own_tokens.shape
    block = (rows, quarter)
    vmem = pl.BlockSpec(memory_space=pltpu.VMEM)
    return pl.pallas_call(
        functools.partial(norm_kernel, model_width),
        out_shape=(
            jax.ShapeDtypeStruct(block, jnp.bfloat16),
            jax.ShapeDtypeStruct((NZ,) + block, jnp.bfloat16),
        ),
        in_specs=[vmem] * 3,
        out_specs=(vmem, vmem),
        scratch_shapes=[
            pltpu.VMEM((2,) + block, jnp.bfloat16),
            pltpu.VMEM(block, jnp.bfloat16),
            pltpu.VMEM(block, jnp.bfloat16),
            pltpu.VMEM((rows, 128), jnp.float32),
            pltpu.VMEM((3, rows, 128), jnp.float32),
            pltpu.SemaphoreType.DMA((1,)),
            pltpu.SemaphoreType.DMA((2,)),
            pltpu.SemaphoreType.DMA((2,)),
            pltpu.SemaphoreType.DMA((1,)),
            pltpu.SemaphoreType.DMA((1,)),
            pltpu.SemaphoreType.DMA((3,)),
            pltpu.SemaphoreType.DMA((3,)),
            pltpu.SemaphoreType.DMA((2, NZ)),
            pltpu.SemaphoreType.DMA((2, NZ)),
        ],
        compiler_params=pltpu.CompilerParams(
            collective_id=2, has_side_effects=True, vmem_limit_bytes=32 * 1024 * 1024
        ),
        name="norm_and_spread",
    )(part, own_tokens, gain)


def pick_kernel(slot_ref, rows_ref, out_ref):
    slots = slot_ref[0]
    count = rows_ref.shape[0]
    lane = lax.broadcasted_iota(jnp.int32, (slots.shape[0], count), 1)
    chosen = jnp.where(lane == slots, 1.0, 0.0).astype(jnp.bfloat16)
    out_ref[0] = jnp.dot(chosen, rows_ref[...], preferred_element_type=jnp.float32).astype(
        jnp.bfloat16
    )


def pick(slots, rows):
    groups, size, _ = slots.shape
    return pl.pallas_call(
        pick_kernel,
        grid=(groups,),
        in_specs=[
            pl.BlockSpec((1, size, 1), lambda i: (i, 0, 0)),
            pl.BlockSpec(rows.shape, lambda i: (0, 0)),
        ],
        out_shape=jax.ShapeDtypeStruct((groups, size, rows.shape[1]), jnp.bfloat16),
        out_specs=pl.BlockSpec((1, size, rows.shape[1]), lambda i: (i, 0, 0)),
        name="pick",
    )(slots, rows)


def dispatch_kernel(sel, rows, held, own_sem, xs, xr, ys, yr, cs, cr):
    rank, tensor = lax.axis_index("expert"), lax.axis_index("tensor")
    y_lo, x, z, y_hi, core, far, sides, mate = corner(rank, tensor)
    other = 1 - y_lo
    x_peers = [(rank_of(y_lo, lax.rem(x + d, NX), z), tensor) for d in range(1, NX)]
    greet(x_peers + [far] + sides + [mate])
    pending = []
    own = pltpu.make_async_copy(sel.at[y_lo, x], rows.at[tensor, y_lo, x], own_sem.at[0])
    own.start()

    def to_side(d, here, there):
        x_s = lax.rem(x + NX - d, NX)
        spot = rows.at[tensor, y_lo, x_s]
        for r in range(2):
            pending.append(send(there, spot, ys.at[d, r], yr.at[d, r], sides[r]))
        pending.append(send(here, spot, ys.at[d, 2], yr.at[d, 2], far))

    def forward(d, r, l):
        x_s = lax.rem(x + NX - d, NX)
        spot = rows.at[lax.rem(y_hi + r, 2) * 2 + core, lax.rem(y_lo + l, 2), x_s]
        index = 2 * r + l
        pending.append(send(spot, spot, cs.at[d, index], cr.at[d, index], mate))

    to_side(0, sel.at[y_lo, x], sel.at[other, x])
    for d in (2, 1, 3):
        to = lax.rem(x + d, NX)
        for i in range(2):
            src = sel.at[other if i == 0 else y_lo, to]
            dst = held.at[x] if i == 0 else rows.at[tensor, y_lo, x]
            pending.append(send(src, dst, xs.at[d - 1, i], xr.at[d - 1, i], x_peers[d - 1]))
    own.wait()
    forward(0, 0, 0)
    for d in (1, 3, 2):
        x_s = lax.rem(x + NX - d, NX)
        arrived(held.at[x_s], xs.at[d - 1, 0], xr.at[d - 1, 0], x_peers[d - 1])
        arrived(rows.at[tensor, y_lo, x_s], xs.at[d - 1, 1], xr.at[d - 1, 1], x_peers[d - 1])
        to_side(d, rows.at[tensor, y_lo, x_s], held.at[x_s])
        forward(d, 0, 0)
    for d in (0, 1, 3, 2):
        x_s = lax.rem(x + NX - d, NX)
        for r in range(2):
            spot = rows.at[lax.rem(y_hi + r, 2) * 2 + core, other, x_s]
            arrived(spot, ys.at[d, r], yr.at[d, r], sides[r])
            forward(d, r, 1)
        spot = rows.at[(1 - y_hi) * 2 + core, y_lo, x_s]
        arrived(spot, ys.at[d, 2], yr.at[d, 2], far)
        forward(d, 1, 0)
    for d in range(NX):
        x_s = lax.rem(x + NX - d, NX)
        for r in range(2):
            for l in range(2):
                spot = rows.at[lax.rem(y_hi + r, 2) * 2 + 1 - core, lax.rem(y_lo + l, 2), x_s]
                arrived(spot, cs.at[d, 2 * r + l], cr.at[d, 2 * r + l], mate)
    for copy in pending:
        copy.wait_send()


def dispatch(sel):
    any_space = pl.BlockSpec(memory_space=pl.ANY)
    return pl.pallas_call(
        dispatch_kernel,
        out_shape=(
            jax.ShapeDtypeStruct((4,) + sel.shape, sel.dtype),
            jax.ShapeDtypeStruct(sel.shape[1:], sel.dtype),
        ),
        in_specs=[any_space],
        out_specs=(any_space, any_space),
        scratch_shapes=[
            pltpu.SemaphoreType.DMA((1,)),
            pltpu.SemaphoreType.DMA((NX - 1, 2)),
            pltpu.SemaphoreType.DMA((NX - 1, 2)),
            pltpu.SemaphoreType.DMA((NX, 3)),
            pltpu.SemaphoreType.DMA((NX, 3)),
            pltpu.SemaphoreType.DMA((NX, 4)),
            pltpu.SemaphoreType.DMA((NX, 4)),
        ],
        compiler_params=pltpu.CompilerParams(collective_id=3, has_side_effects=True),
        name="dispatch",
    )(sel)[0]


def expert_kernel(rows_ref, up_ref, down_ref, out_ref):
    quarters, groups, size, width = rows_ref.shape
    count = groups * size
    units = down_ref.shape[1]
    total = jnp.zeros((count, up_ref.shape[2]), jnp.float32)
    for q in range(quarters):
        total += jnp.dot(
            rows_ref[q].reshape(count, width), up_ref[q], preferred_element_type=jnp.float32
        )
    gate, up = total[:, :units], total[:, units:]
    active = (gate * jax.nn.sigmoid(1.702 * gate) * (up + 1.0)).astype(jnp.bfloat16)
    for q in range(quarters):
        value = jnp.dot(active, down_ref[q], preferred_element_type=jnp.float32)
        out_ref[q] = value.astype(jnp.bfloat16).reshape(groups, size, width)


def run_expert(rows, up, down):
    quarters, groups, size, width = rows.shape
    step = 2
    block = pl.BlockSpec((quarters, step, size, width), lambda i: (0, i, 0, 0))
    return pl.pallas_call(
        expert_kernel,
        grid=(groups // step,),
        in_specs=[
            block,
            pl.BlockSpec(up.shape, lambda i: (0, 0, 0)),
            pl.BlockSpec(down.shape, lambda i: (0, 0, 0)),
        ],
        out_shape=jax.ShapeDtypeStruct(rows.shape, jnp.bfloat16),
        out_specs=block,
        compiler_params=pltpu.CompilerParams(vmem_limit_bytes=48 * 1024 * 1024),
        name="run_expert",
    )(rows, up, down)


def collect_kernel(part, out, mine, core_in, side_out, side_in, x_out, ms, cs, cr, ys, yr, xs, xr):
    rank, tensor = lax.axis_index("expert"), lax.axis_index("tensor")
    y_lo, x, z, y_hi, core, far, sides, mate = corner(rank, tensor)
    other = 1 - y_lo
    x_peers = [(rank_of(y_lo, lax.rem(x + d, NX), z), tensor) for d in range(1, NX)]
    greet(x_peers + [far] + sides + [mate])
    pending, loads = [], {}
    order = (2, 1, 3, 0)
    def where(kind):
        half = y_hi if kind in (0, 3) else 1 - y_hi
        return half, (other if kind < 2 else y_lo)

    for d in order:
        x_h = lax.rem(x + d, NX)
        for kind in range(4):
            half, side = where(kind)
            src = part.at[half * 2 + 1 - core, side, x_h]
            pending.append(
                send(src, core_in.at[d, kind], cs.at[d, kind], cr.at[d, kind], mate)
            )
            load = pltpu.make_async_copy(
                part.at[half * 2 + core, side, x_h], mine.at[d, kind], ms.at[d, kind]
            )
            load.start()
            loads[d, kind] = load
    for d in order:
        for kind in range(4):
            arrived(core_in.at[d, kind], cs.at[d, kind], cr.at[d, kind], mate)
            loads[d, kind].wait()
            both = f32(mine[d, kind]) + f32(core_in[d, kind])
            side_out[d, kind] = both.astype(jnp.bfloat16)
            if kind < 3:
                to = far if kind == 2 else sides[kind]
                pending.append(
                    send(
                        side_out.at[d, kind], side_in.at[d, kind], ys.at[d, kind], yr.at[d, kind], to
                    )
                )
    for d in order:
        for kind in range(3):
            to = far if kind == 2 else sides[kind]
            arrived(side_in.at[d, kind], ys.at[d, kind], yr.at[d, kind], to)
            if kind == 0:
                continue
            first = side_in[d, 0] if kind == 1 else side_out[d, 3]
            both = (f32(first) + f32(side_in[d, kind])).astype(jnp.bfloat16)
            i = kind - 1
            owner = other if kind == 1 else y_lo
            if d == 0:
                out[owner, x] = both
            else:
                x_out[d - 1, i] = both
                pending.append(
                    send(
                        x_out.at[d - 1, i], out.at[owner, x], xs.at[d - 1, i], xr.at[d - 1, i],
                        x_peers[d - 1],
                    )
                )
    for d in order[:-1]:
        x_e = lax.rem(x + NX - d, NX)
        for i in range(2):
            owner = other if i == 0 else y_lo
            arrived(out.at[owner, x_e], xs.at[d - 1, i], xr.at[d - 1, i], x_peers[d - 1])
    for copy in pending:
        copy.wait_send()


def collect(part):
    piece = part.shape[3:]
    return pl.pallas_call(
        collect_kernel,
        out_shape=jax.ShapeDtypeStruct(part.shape[1:], part.dtype),
        in_specs=[pl.BlockSpec(memory_space=pl.ANY)],
        out_specs=pl.BlockSpec(memory_space=pltpu.VMEM),
        scratch_shapes=[
            pltpu.VMEM((NX, 4) + piece, jnp.bfloat16),
            pltpu.VMEM((NX, 4) + piece, jnp.bfloat16),
            pltpu.VMEM((NX, 4) + piece, jnp.bfloat16),
            pltpu.VMEM((NX, 3) + piece, jnp.bfloat16),
            pltpu.VMEM((NX - 1, 2) + piece, jnp.bfloat16),
            pltpu.SemaphoreType.DMA((NX, 4)),
            pltpu.SemaphoreType.DMA((NX, 4)),
            pltpu.SemaphoreType.DMA((NX, 4)),
            pltpu.SemaphoreType.DMA((NX, 3)),
            pltpu.SemaphoreType.DMA((NX, 3)),
            pltpu.SemaphoreType.DMA((NX - 1, 2)),
            pltpu.SemaphoreType.DMA((NX - 1, 2)),
        ],
        compiler_params=pltpu.CompilerParams(
            collective_id=4, has_side_effects=True, vmem_limit_bytes=48 * 1024 * 1024
        ),
        name="collect",
    )(part)


def mix_kernel(slot_ref, weight_ref, rows_ref, out_ref):
    count = out_ref.shape[1]
    row = lax.broadcasted_iota(jnp.int32, (count, slot_ref.shape[1]), 0) + pl.program_id(0) * count
    share = jnp.where(row == slot_ref[...], weight_ref[...], 0.0).astype(jnp.bfloat16)
    out_ref[0] = jnp.dot(share, rows_ref[...], preferred_element_type=jnp.float32).astype(
        jnp.bfloat16
    )


def mix(slots, weights, rows, blocks, count):
    width = rows.shape[1]
    whole = lambda i: (0, 0)
    return pl.pallas_call(
        mix_kernel,
        grid=(blocks,),
        in_specs=[
            pl.BlockSpec(slots.shape, whole),
            pl.BlockSpec(weights.shape, whole),
            pl.BlockSpec(rows.shape, whole),
        ],
        out_shape=jax.ShapeDtypeStruct((blocks, count, width), jnp.bfloat16),
        out_specs=pl.BlockSpec((1, count, width), lambda i: (i, 0, 0)),
        name="mix",
    )(slots, weights, rows)


def home_kernel(sums, hidden, out, staged, landed, zs, zr):
    rank, tensor = lax.axis_index("expert"), lax.axis_index("tensor")
    y_lo, x, z = place_of(rank)
    ring = [
        (rank_of(y_lo, x, lax.rem(z + 1, NZ)), tensor),
        (rank_of(y_lo, x, lax.rem(z + NZ - 1, NZ)), tensor),
    ]
    greet(ring)
    rows = hidden.shape[0] // 2
    half = NZ // 2
    pending = []

    def reach(direction, piece):
        return half if direction == piece else half - 1

    def got(direction, steps, piece):
        index = 2 * steps + piece
        arrived(
            landed.at[direction, index], zs.at[direction, index], zr.at[direction, index],
            ring[direction],
        )
        return f32(landed[direction, index])

    for steps in range(half, 0, -1):
        for piece in range(2):
            for direction in range(2):
                if steps > reach(direction, piece):
                    continue
                home = lax.rem(z + (steps if direction == 0 else NZ - steps), NZ)
                mine = f32(sums[home, pl.ds(piece * rows, rows)])
                if steps < reach(direction, piece):
                    mine = mine + got(direction, steps, piece)
                index = 2 * (steps - 1) + piece
                staged[direction, index] = mine.astype(jnp.bfloat16)
                pending.append(
                    send(
                        staged.at[direction, index], landed.at[direction, index],
                        zs.at[direction, index], zr.at[direction, index], ring[direction],
                    )
                )
    for piece in range(2):
        span = pl.ds(piece * rows, rows)
        total = f32(sums[z, span])
        for direction in range(2):
            total = total + got(direction, 0, piece)
        out[span] = (f32(hidden[span]) + total).astype(jnp.bfloat16)
    for copy in pending:
        copy.wait_send()


def bring_home(sums, hidden):
    rows, width = hidden.shape
    vmem = pl.BlockSpec(memory_space=pltpu.VMEM)
    return pl.pallas_call(
        home_kernel,
        out_shape=jax.ShapeDtypeStruct(hidden.shape, hidden.dtype),
        in_specs=[vmem, vmem],
        out_specs=vmem,
        scratch_shapes=[
            pltpu.VMEM((2, NZ, rows // 2, width), jnp.bfloat16),
            pltpu.VMEM((2, NZ, rows // 2, width), jnp.bfloat16),
            pltpu.SemaphoreType.DMA((2, NZ)),
            pltpu.SemaphoreType.DMA((2, NZ)),
        ],
        compiler_params=pltpu.CompilerParams(
            collective_id=5, has_side_effects=True, vmem_limit_bytes=32 * 1024 * 1024
        ),
        name="bring_home",
    )(sums, hidden)


def routing_slab(routed_experts, route_weights, expert_count, capacity):
    row_count, top_count = routed_experts.shape
    expert_list = routed_experts.reshape(row_count * top_count)
    one_hot = (expert_list[:, None] == jnp.arange(expert_count, dtype=jnp.int32)[None, :]).astype(
        jnp.int32
    )
    earlier = jnp.cumsum(one_hot, axis=0) - one_hot
    arrival = jnp.sum(earlier * one_hot, axis=1)
    slot_index = expert_list * capacity + arrival
    hit = slot_index[:, None] == jnp.arange(expert_count * capacity, dtype=jnp.int32)[None, :]
    row = (jnp.arange(row_count * top_count, dtype=jnp.int32) // top_count + 1).astype(jnp.float32)
    token = jnp.sum(jnp.where(hit, row[:, None], 0.0), axis=0) - 1.0
    weight = jnp.sum(jnp.where(hit, route_weights.reshape(-1, 1), 0.0), axis=0)
    planes = [
        jnp.pad(
            value.reshape(NY * NX, NZ, capacity).transpose(1, 0, 2),
            ((0, 0), (0, 0), (0, 128 - capacity)),
        )
        for value in (token, weight)
    ]
    return jnp.concatenate(planes, axis=2)


def key_masks(prefix_length, expert_rank, cache_rows, span, width):
    y_lo, x, z = place_of(expert_rank)
    shape = (prefix_length.shape[0], NY * NZ, cache_rows + span, width)
    shard = lax.broadcasted_iota(jnp.int32, shape, 1)
    row = lax.broadcasted_iota(jnp.int32, shape, 2)
    col = lax.broadcasted_iota(jnp.int32, shape, 3)
    key_rank = rank_of(shard % 2, x, shard // 2)
    in_cache = row < cache_rows
    beyond = (key_rank * cache_rows + row >= prefix_length[:, None, None, None]) & (
        col == span + NX
    )
    later_block = (col >= span) & (col < span + NX) & (key_rank > rank_of(y_lo, col - span, z))
    later_key = (col < span) & (key_rank == expert_rank) & (row - cache_rows > col)
    blocked = jnp.where(in_cache, beyond, later_block | later_key)
    return jnp.where(blocked, NEG, 0.0).astype(jnp.bfloat16)


def rotate(vectors, places):
    half_dim = vectors.shape[-1] // 2
    steps_up = jnp.arange(half_dim, dtype=jnp.float32)
    frequency = jnp.exp(steps_up * (-math.log(ROPE_BASE) / half_dim))
    angles = places[..., None] * frequency
    cosine = jnp.cos(angles)
    sine_part = jnp.sin(angles)
    first_half = vectors[..., :half_dim]
    second_half = vectors[..., half_dim:]
    return jnp.concatenate(
        [
            first_half * cosine - second_half * sine_part,
            second_half * cosine + first_half * sine_part,
        ],
        axis=-1,
    )


def on_device(
    tokens,
    attn_gain,
    w_query,
    key_value_weight,
    w_out,
    cache_keyval,
    prefix_length,
    routed_experts,
    route_weights,
    expert_gain,
    w_gate_up,
    w_down,
):
    span_dev, seq_count, quarter = tokens.shape
    model_width = attn_gain.shape[0]
    row_count = span_dev * seq_count
    local_kv = key_value_weight.shape[1]
    head_dim = key_value_weight.shape[2] // 2
    query_cols = w_query.shape[1]
    group_width = query_cols // head_dim // local_kv
    cache_rows = cache_keyval.shape[0]
    tensor_rank = lax.axis_index("tensor")
    expert_rank = lax.axis_index("expert")
    shard_piece = lax.all_gather(tokens, "tensor", axis=2, tiled=True)
    col_count = shard_piece.shape[2]
    piece_rows = shard_piece.reshape(row_count, col_count).astype(jnp.float32)
    rescaled = (piece_rows * attn_gain).astype(jnp.bfloat16)
    keyval_rows = key_value_weight.reshape(col_count, local_kv * 2 * head_dim)
    query_acc = jnp.dot(rescaled, w_query, preferred_element_type=jnp.float32)
    keyval_acc = jnp.dot(rescaled, keyval_rows, preferred_element_type=jnp.float32)
    square_sum = jnp.sum(piece_rows * piece_rows, axis=1)
    inverse_square_root = lax.rsqrt(square_sum / model_width + EPSILON)
    span_place = expert_rank * span_dev + jnp.arange(span_dev, dtype=jnp.int32)
    places = (prefix_length[None, :] + span_place[:, None]).reshape(row_count).astype(jnp.float32)
    query_scale = head_dim ** (-0.5) * LOG2E
    query_matrix = (
        rotate(
            (query_acc * inverse_square_root[:, None]).reshape(
                row_count, query_cols // head_dim, head_dim
            ),
            places[:, None],
        )
        * query_scale
    ).astype(jnp.bfloat16)
    key_value_heads = (keyval_acc * inverse_square_root[:, None]).reshape(
        row_count, local_kv, 2 * head_dim
    )
    rotated_keys = rotate(key_value_heads[..., :head_dim], places[:, None])
    new_key_value_rows = jnp.concatenate(
        [rotated_keys, key_value_heads[..., head_dim:]], axis=-1
    ).astype(jnp.bfloat16)
    new_key_value_rows = new_key_value_rows.reshape(span_dev, seq_count, local_kv, 2 * head_dim)
    query_count = span_dev * group_width
    own_queries = query_matrix.reshape(span_dev, seq_count, group_width, head_dim).transpose(
        1, 3, 2, 0
    )
    own_queries = own_queries.reshape(seq_count, head_dim, query_count)
    joined = jnp.concatenate([cache_keyval, new_key_value_rows], axis=0)[:, :, 0, :]
    joined = joined.transpose(1, 0, 2)
    top_count = routed_experts.shape[2]
    expert_count = lax.axis_size("expert")
    capacity = min(row_count, max(2, 5 * row_count * top_count // (2 * expert_count)))
    slab = routing_slab(
        routed_experts.reshape(row_count, top_count),
        route_weights.reshape(row_count, top_count),
        expert_count,
        capacity,
    )
    kv_all, q_all, slab_all = exchange(joined, own_queries, slab)
    mask = key_masks(prefix_length, expert_rank, cache_rows, span_dev, 2 * head_dim)
    my_x = place_of(expert_rank)[1].astype(jnp.int32).reshape(1)
    part, stat = attend(my_x, q_all, kv_all, mask)
    part, stat = send_back(part, stat)
    tops, sums = stat[:, :, 0, :], stat[:, :, 1, :]
    share = jnp.exp2(tops - jnp.max(tops, axis=0)) * sums
    share = share / jnp.sum(share, axis=0)
    attended = jnp.sum(part.astype(jnp.float32) * share[:, :, None, :], axis=0).astype(jnp.bfloat16)
    attended = (
        attended.reshape(seq_count, head_dim, group_width, span_dev)
        .transpose(3, 0, 2, 1)
        .reshape(row_count, query_cols)
    )
    quarters = model_width // quarter
    projected = jnp.einsum(
        "rk,kqn->qrn",
        attended,
        w_out.reshape(query_cols, quarters, quarter),
        preferred_element_type=jnp.float32,
    ).astype(jnp.bfloat16)
    gain = lax.dynamic_slice_in_dim(expert_gain, tensor_rank * quarter, quarter, 0)
    hidden, spread = norm_and_spread(
        projected, tokens.reshape(row_count, quarter), gain.reshape(1, quarter), model_width
    )
    token = slab_all[:, :, :capacity].astype(jnp.int32)
    first = jnp.arange(NZ, dtype=jnp.int32)[:, None, None] * row_count
    slot_token = jnp.where(token >= 0, token + first, -1).transpose(1, 0, 2)
    slot_weight = slab_all[:, :, 128 : 128 + capacity].transpose(1, 0, 2)
    groups, size = NY * NX, NZ * capacity
    sel = pick(slot_token.reshape(groups, size, 1), spread.reshape(NZ * row_count, quarter))
    rows = dispatch(sel.reshape(NY, NX, size, quarter))
    ffn_local = w_down.shape[1]
    units = -(-ffn_local // 128) * 128
    up = jnp.pad(w_gate_up[0], ((0, 0), (0, 0), (0, units - ffn_local)))
    up = up.reshape(quarters, quarter, 2 * units)
    down = jnp.pad(w_down[0], ((0, units - ffn_local), (0, 0)))
    down = down.reshape(units, quarters, quarter).transpose(1, 0, 2)
    value = run_expert(rows.reshape(quarters, groups, size, quarter), up, down)
    returned = collect(value.reshape(quarters, NY, NX, size, quarter))
    sums = mix(
        slot_token.reshape(1, groups * size),
        slot_weight.reshape(1, groups * size),
        returned.reshape(groups * size, quarter),
        NZ,
        row_count,
    )
    layer_output = bring_home(sums, hidden).reshape(span_dev, seq_count, quarter)
    return (layer_output, new_key_value_rows)


def solution(mesh):
    return jax.shard_map(
        on_device,
        mesh=mesh,
        in_specs=(
            P("expert", None, "tensor"),
            P(),
            P(None, "tensor"),
            P(None, "tensor", None),
            P("tensor", None),
            P("expert", None, "tensor", None),
            P(),
            P("expert", None, None),
            P("expert", None, None),
            P(),
            P("expert", None, None, "tensor"),
            P("expert", "tensor", None),
        ),
        out_specs=(P("expert", None, "tensor"), P("expert", None, "tensor", None)),
        check_vma=False,
    )
```

```python
import functools
import math

import jax
import jax.numpy as jnp
from jax import lax
from jax.experimental import pallas as pl
from jax.experimental.pallas import tpu as pltpu
from jax.sharding import PartitionSpec as P

EPSILON = 1e-05
ROPE_BASE = 150000.0
NEG = -1e30
MESH = pl.DeviceIdType.MESH
NY, NX, NZ = 2, 4, 8
LOG2E = 1.4426950408889634


def place_of(expert_rank):
    return expert_rank // (NX * NZ), (expert_rank // NZ) % NX, expert_rank % NZ


def rank_of(y_lo, x, z):
    return (y_lo * NX + x) * NZ + z


def greet(devices):
    barrier = pltpu.get_barrier_semaphore()
    for device in devices:
        pl.semaphore_signal(barrier, inc=1, device_id=device, device_id_type=MESH)
    pl.semaphore_wait(barrier, len(devices))


def send(src, dst, send_sem, recv_sem, device):
    copy = pltpu.make_async_remote_copy(
        src_ref=src,
        dst_ref=dst,
        send_sem=send_sem,
        recv_sem=recv_sem,
        device_id=device,
        device_id_type=MESH,
    )
    copy.start()
    return copy


def arrived(dst, send_sem, recv_sem, device):
    pltpu.make_async_remote_copy(
        src_ref=dst,
        dst_ref=dst,
        send_sem=send_sem,
        recv_sem=recv_sem,
        device_id=device,
        device_id_type=MESH,
    ).wait_recv()


def swap_blocks(value):
    half = value.shape[0] // 2
    top, bottom = value[:half], value[half:]
    left = lax.broadcasted_iota(jnp.int32, top.shape, 1) < half
    return jnp.concatenate(
        [
            jnp.where(left, top, pltpu.roll(bottom, half, 1)),
            jnp.where(left, pltpu.roll(top, half, 1), bottom),
        ],
        axis=0,
    )


def turn(first, second, cosine, sine):
    return first * cosine - second * sine, second * cosine + first * sine


def front_kernel(
    scale, own_tokens, gain, w_query, w_keyval, cosine, sine, cache, slab,
    fresh, kv_all, q_all, slab_all,
    gathered, q_own, own_sem, gs, gr, xs, xr, ys, yr, zs, zr, ts, tr,
):
    rank, tensor = lax.axis_index("expert"), lax.axis_index("tensor")
    y_lo, x, z, y_hi, core, far, sides, mate = corner(rank, tensor)
    other = 1 - y_lo
    rows, quarter = own_tokens.shape
    cache_rows, head = cache.shape[1], fresh.shape[2] // 2
    span = fresh.shape[1]
    x_peers = [(rank_of(y_lo, lax.rem(x + d, NX), z), tensor) for d in range(1, NX)]
    y_peer = (rank_of(other, x, z), tensor)
    z_peers = [(rank_of(y_lo, x, lax.rem(z + d, NZ)), tensor) for d in range(1, NZ)]
    ring = [z_peers[0], z_peers[-1]]
    greet(x_peers + [y_peer] + z_peers + [far, mate])
    pending = []
    parts = (pl.ds(0, cache_rows), pl.ds(cache_rows, span))
    first = (cache, fresh)

    def slot(part, direction, steps, piece):
        origin = lax.rem(z + (NZ - steps if direction == 0 else steps), NZ)
        return kv_all.at[origin * 2 + (y_lo if piece == 0 else other), :, parts[part]]

    def sems(part, direction, step, piece):
        index = 2 * (step - 1) + piece
        return zs.at[part, direction, index], zr.at[part, direction, index]

    def pass_on(part, direction, step, piece):
        block = slot(part, direction, step - 1, piece)
        src = first[part] if step == 1 and piece == 0 else block
        pending.append(send(src, block, *sems(part, direction, step, piece), ring[direction]))

    def got(part, direction, step, piece):
        arrived(
            slot(part, direction, step, piece), *sems(part, direction, step, piece), ring[direction]
        )

    def begin(part):
        block = slot(part, 0, 0, 0)
        copy = pltpu.make_async_copy(first[part], block, own_sem.at[part])
        copy.start()
        pending.append(send(first[part], block, ys.at[part], yr.at[part], y_peer))
        for direction in range(2):
            pass_on(part, direction, 1, 0)
        return copy

    def begin_other(part):
        arrived(slot(part, 0, 0, 1), ys.at[part], yr.at[part], y_peer)
        for direction in range(2):
            pass_on(part, direction, 1, 1)

    half = NZ // 2

    def step_on(part, step):
        for piece in range(2):
            for direction in range(2):
                got(part, direction, step - 1, piece)
                if step < half or direction == piece:
                    pass_on(part, direction, step, piece)

    mine = gathered.at[tensor]
    pending.append(send(own_tokens, mine, gs.at[0], gr.at[0], far))
    pending.append(send(own_tokens, mine, gs.at[1], gr.at[1], mate))
    own = [begin(0), pltpu.make_async_copy(slab.at[z], slab_all.at[z], own_sem.at[2])]
    own[1].start()
    for d in range(1, NZ):
        to = lax.rem(z + d, NZ)
        pending.append(
            send(slab.at[to], slab_all.at[z], ts.at[d - 1], tr.at[d - 1], z_peers[d - 1])
        )
    far_index, mate_index = (1 - y_hi) * 2 + core, y_hi * 2 + 1 - core
    cross_index = (1 - y_hi) * 2 + 1 - core

    def project(index, block):
        wide = f32(block)
        scaled = (wide * gain[index]).astype(jnp.bfloat16)
        span_of = pl.ds(pl.multiple_of(index * quarter, 16), quarter)
        return (
            jnp.dot(scaled, w_query[span_of, :], preferred_element_type=jnp.float32),
            jnp.dot(scaled, w_keyval[span_of, :], preferred_element_type=jnp.float32),
            jnp.sum(wide * wide, axis=1, keepdims=True),
        )

    total = project(tensor, own_tokens[...])
    begin_other(0)
    arrived(gathered.at[far_index], gs.at[0], gr.at[0], far)
    block = gathered.at[far_index]
    pending.append(send(block, block, gs.at[2], gr.at[2], mate))
    total = [a + b for a, b in zip(total, project(far_index, gathered[far_index]))]
    arrived(gathered.at[mate_index], gs.at[1], gr.at[1], mate)
    total = [a + b for a, b in zip(total, project(mate_index, gathered[mate_index]))]
    step_on(0, 2)
    arrived(gathered.at[cross_index], gs.at[2], gr.at[2], mate)
    total = [a + b for a, b in zip(total, project(cross_index, gathered[cross_index]))]
    root = lax.rsqrt(total[2] / (4 * quarter) + EPSILON)
    cos, sin = cosine[...], sine[...]
    flipped = (total[1] * root).T
    keys = turn(flipped[: head // 2], flipped[head // 2 : head], cos, sin)
    whole = jnp.concatenate([keys[0], keys[1], flipped[head:]], axis=0).T
    fresh[...] = whole.astype(jnp.bfloat16).reshape(fresh.shape)
    own.append(begin(1))
    raw = total[0] * root
    width = 2 * head
    for j in range(raw.shape[1] // width):
        pair = raw[:, j * width : (j + 1) * width].T
        turned = []
        for h in range(2):
            block = pair[h * head : (h + 1) * head]
            turned += turn(block[: head // 2], block[head // 2 :], cos, sin)
        sides_first = swap_blocks(jnp.concatenate(turned, axis=0) * scale).astype(jnp.bfloat16)
        for s in range(2):
            q_own[s, :, j * width : (j + 1) * width] = sides_first[s * head : (s + 1) * head]
    copy = pltpu.make_async_copy(q_own, q_all.at[x], own_sem.at[3])
    copy.start()
    own.append(copy)
    for d in range(1, NX):
        pending.append(send(q_own, q_all.at[x], xs.at[d - 1], xr.at[d - 1], x_peers[d - 1]))
    begin_other(1)
    step_on(0, 3)
    step_on(1, 2)
    step_on(0, 4)
    step_on(1, 3)
    step_on(1, 4)
    for part in range(2):
        for direction in range(2):
            got(part, direction, half, direction)
    for d in range(1, NX):
        arrived(q_all.at[lax.rem(x + NX - d, NX)], xs.at[d - 1], xr.at[d - 1], x_peers[d - 1])
    for d in range(1, NZ):
        arrived(
            slab_all.at[lax.rem(z + NZ - d, NZ)], ts.at[d - 1], tr.at[d - 1], z_peers[d - 1]
        )
    for copy in own:
        copy.wait()
    for copy in pending:
        copy.wait_send()


def front(scale, own_tokens, gain, w_query, w_keyval, cosine, sine, cache, slab):
    seqs, cache_rows, width = cache.shape
    rows, quarter = own_tokens.shape
    span, cols = rows // seqs, w_query.shape[1] * rows // seqs // (width // 2)
    vmem = pl.BlockSpec(memory_space=pltpu.VMEM)
    any_space = pl.BlockSpec(memory_space=pl.ANY)
    return pl.pallas_call(
        functools.partial(front_kernel, scale),
        out_shape=(
            jax.ShapeDtypeStruct((seqs, span, width), jnp.bfloat16),
            jax.ShapeDtypeStruct((NY * NZ, seqs, cache_rows + span, width), jnp.bfloat16),
            jax.ShapeDtypeStruct((NX, seqs, width // 2, cols), jnp.bfloat16),
            jax.ShapeDtypeStruct(slab.shape, slab.dtype),
        ),
        in_specs=[vmem] * 6 + [any_space] * 2,
        out_specs=(vmem, any_space, any_space, any_space),
        scratch_shapes=[
            pltpu.VMEM((4, rows, quarter), jnp.bfloat16),
            pltpu.VMEM((seqs, width // 2, cols), jnp.bfloat16),
            pltpu.SemaphoreType.DMA((4,)),
            pltpu.SemaphoreType.DMA((3,)),
            pltpu.SemaphoreType.DMA((3,)),
            pltpu.SemaphoreType.DMA((NX - 1,)),
            pltpu.SemaphoreType.DMA((NX - 1,)),
            pltpu.SemaphoreType.DMA((2,)),
            pltpu.SemaphoreType.DMA((2,)),
            pltpu.SemaphoreType.DMA((2, 2, NZ)),
            pltpu.SemaphoreType.DMA((2, 2, NZ)),
            pltpu.SemaphoreType.DMA((NZ - 1,)),
            pltpu.SemaphoreType.DMA((NZ - 1,)),
        ],
        compiler_params=pltpu.CompilerParams(
            collective_id=0, has_side_effects=True, vmem_limit_bytes=32 * 1024 * 1024
        ),
        name="front",
    )(own_tokens, gain, w_query, w_keyval, cosine, sine, cache, slab)


def attend_kernel(cache_rows, place, q_ref, kv_ref, o_ref, stat_ref, vt_ref, qa_ref, mask_ref):
    xq = pl.program_id(1)
    prefix = place[pl.program_id(0)]
    my_rank = place[place.shape[0] - 1]
    y_lo, x, z = place_of(my_rank)
    chunks, _, chunk = vt_ref.shape
    shards, _, keys, width = kv_ref.shape
    per = chunk // keys
    head, cols = q_ref.shape[2:]

    @pl.when(xq == 0)
    def _():
        for j in range(chunks):
            rows = kv_ref[j * per : (j + 1) * per, 0].reshape(chunk, width)
            flipped = rows.astype(jnp.float32).T
            vt_ref[j, :16, :] = jnp.ones((16, chunk), jnp.bfloat16)
            vt_ref[j, 16:, :] = flipped[head:].astype(jnp.bfloat16)
        span = keys - cache_rows
        old_row = lax.broadcasted_iota(jnp.int32, (cache_rows, width), 0)
        old_col = lax.broadcasted_iota(jnp.int32, (cache_rows, width), 1)
        new_row = lax.broadcasted_iota(jnp.int32, (span, width), 0)
        new_col = lax.broadcasted_iota(jnp.int32, (span, width), 1)
        old_row = jnp.where(old_col == span + NX, old_row, -1)
        in_block = (new_col >= span) & (new_col < span + NX)
        query_rank = rank_of(y_lo, new_col - span, z)
        later = (new_col < span) & (new_row > new_col)
        for j in range(shards):
            key_rank = rank_of(j % 2, x, j // 2)
            valid = jnp.maximum(prefix - key_rank * cache_rows, 0)
            beyond = jnp.where(old_row >= valid, NEG, 0.0)
            mask_ref[j, :cache_rows, :] = beyond.astype(jnp.bfloat16)
            same = jnp.where(key_rank == my_rank, 1, 0)
            hidden_key = (in_block & (key_rank > query_rank)) | (later & (same > 0))
            mask_ref[j, cache_rows:, :] = jnp.where(hidden_key, NEG, 0.0).astype(jnp.bfloat16)

    qa_ref[:head, :] = q_ref[0, 0]
    qa_ref[head:width, :] = jnp.zeros((width - head, cols), jnp.bfloat16)
    row = lax.broadcasted_iota(jnp.int32, (width, cols), 0)
    lane = lax.broadcasted_iota(jnp.int32, (width, cols), 1)
    span = head
    tri = jnp.where(xq == x, lane % span, -1)
    hot = (row == tri) | (row == span + xq) | (row == span + NX)
    qa_ref[width:, :] = jnp.where(hot, 1.0, 0.0).astype(jnp.bfloat16)
    qa = qa_ref[...]
    top = jnp.full((1, cols), -3e38, jnp.float32)
    acc = jnp.zeros((vt_ref.shape[1], cols), jnp.float32)
    for j in range(chunks):
        lhs = jnp.concatenate(
            [
                kv_ref[j * per : (j + 1) * per, 0].reshape(chunk, width),
                mask_ref[j * per : (j + 1) * per].reshape(chunk, width),
            ],
            axis=1,
        )
        scores = jnp.dot(lhs, qa, preferred_element_type=jnp.float32)
        new_top = jnp.maximum(top, jnp.max(scores, axis=0, keepdims=True))
        probs = jnp.exp2(scores - new_top).astype(jnp.bfloat16)
        acc = acc * jnp.exp2(top - new_top) + jnp.dot(
            vt_ref[j], probs, preferred_element_type=jnp.float32
        )
        top = new_top
    total = acc[0:1]
    o_ref[0, 0] = (acc[16:] / total).astype(jnp.bfloat16)
    stat_ref[0, 0, 0:1, :] = top
    stat_ref[0, 0, 1:2, :] = total
    stat_ref[0, 0, 2:, :] = jnp.zeros((6, cols), jnp.float32)


def attend(place, q_all, kv_all, cache_rows):
    nx, seqs, head, cols = q_all.shape
    shards, _, keys, width = kv_all.shape
    chunk = 2 * keys
    chunks = shards * keys // chunk
    return pl.pallas_call(
        functools.partial(attend_kernel, cache_rows),
        grid=(seqs, nx),
        in_specs=[
            pl.BlockSpec(memory_space=pltpu.SMEM),
            pl.BlockSpec((1, 1, head, cols), lambda s, i: (i, s, 0, 0)),
            pl.BlockSpec((shards, 1, keys, width), lambda s, i: (0, s, 0, 0)),
        ],
        out_shape=(
            jax.ShapeDtypeStruct((nx, seqs, head, cols), jnp.bfloat16),
            jax.ShapeDtypeStruct((nx, seqs, 8, cols), jnp.float32),
        ),
        out_specs=(
            pl.BlockSpec((1, 1, head, cols), lambda s, i: (i, s, 0, 0)),
            pl.BlockSpec((1, 1, 8, cols), lambda s, i: (i, s, 0, 0)),
        ),
        scratch_shapes=[
            pltpu.VMEM((chunks, 16 + head, chunk), jnp.bfloat16),
            pltpu.VMEM((2 * width, cols), jnp.bfloat16),
            pltpu.VMEM((shards, keys, width), jnp.bfloat16),
        ],
        compiler_params=pltpu.CompilerParams(vmem_limit_bytes=48 * 1024 * 1024),
        name="attend",
    )(place, q_all, kv_all)


def corner(rank, tensor):
    y_lo, x, z = place_of(rank)
    y_hi, core = tensor // 2, lax.rem(tensor, 2)
    far = (rank, (1 - y_hi) * 2 + core)
    sides = [(rank_of(1 - y_lo, x, z), lax.rem(y_hi + r, 2) * 2 + core) for r in range(2)]
    mate = (rank, y_hi * 2 + 1 - core)
    return y_lo, x, z, y_hi, core, far, sides, mate


def f32(value):
    return value.astype(jnp.float32)


def norm_kernel(
    model_width, o, stat, w_out, own_tokens, gain, hidden, spread,
    o_in, stat_in, to_core, core_in, core_out, far_in, squares, squares_in,
    os, orr, ss, sr, cs, cr, fs, fr, qs, qr, zs, zr,
):
    rank, tensor = lax.axis_index("expert"), lax.axis_index("tensor")
    y_lo, x, z, y_hi, core, far, sides, mate = corner(rank, tensor)
    cross = (rank, (1 - y_hi) * 2 + 1 - core)
    ring = [
        (rank_of(y_lo, x, lax.rem(z + 1, NZ)), tensor),
        (rank_of(y_lo, x, lax.rem(z + NZ - 1, NZ)), tensor),
    ]
    x_peers = [(rank_of(y_lo, lax.rem(x + d, NX), z), tensor) for d in range(1, NX)]
    greet([mate, far, cross] + ring + x_peers)
    pending = []
    for d in range(1, NX):
        to, i = lax.rem(x + d, NX), d - 1
        pending.append(send(stat.at[to], stat_in.at[i], ss.at[i], sr.at[i], x_peers[i]))
        pending.append(send(o.at[to], o_in.at[i], os.at[i], orr.at[i], x_peers[i]))
    stats, values = [stat[x]], [o[x]]
    for i in range(NX - 1):
        arrived(stat_in.at[i], ss.at[i], sr.at[i], x_peers[i])
        arrived(o_in.at[i], os.at[i], orr.at[i], x_peers[i])
        stats.append(stat_in[i])
        values.append(o_in[i])
    seqs, head, cols = values[0].shape
    merged = []
    for s in range(seqs):
        tops = [value[s, 0:1] for value in stats]
        top = functools.reduce(jnp.maximum, tops)
        shares = [jnp.exp2(a - top) * value[s, 1:2] for a, value in zip(tops, stats)]
        whole = functools.reduce(jnp.add, shares)
        merged.append(
            functools.reduce(jnp.add, [f32(v[s]) * (a / whole) for v, a in zip(values, shares)])
        )
    both = jnp.concatenate(merged, axis=0)
    wide_head = seqs * head
    attended = jnp.concatenate(
        [
            swap_blocks(both[:, j * wide_head : (j + 1) * wide_head].T)
            for j in range(cols // wide_head)
        ],
        axis=1,
    ).astype(jnp.bfloat16)
    quarter = own_tokens.shape[1]

    def projected(index):
        span_of = pl.ds(pl.multiple_of(index * quarter, 16), quarter)
        return lax.dot_general(
            attended, w_out[span_of, :], (((1,), (1,)), ((), ())),
            preferred_element_type=jnp.float32,
        )

    order = [1 - y_hi, y_hi]
    for i in range(2):
        to_core[i] = projected(order[i] * 2 + 1 - core).astype(jnp.bfloat16)
        pending.append(send(to_core.at[i], core_in.at[i], cs.at[i], cr.at[i], mate))
    for_far = projected(order[0] * 2 + core)
    arrived(core_in.at[0], cs.at[0], cr.at[0], mate)
    core_out[...] = (for_far + f32(core_in[0])).astype(jnp.bfloat16)
    pending.append(send(core_out, far_in, fs.at[0], fr.at[0], far))
    near = f32(own_tokens[...]) + projected(order[1] * 2 + core)
    arrived(core_in.at[1], cs.at[1], cr.at[1], mate)
    near = near + f32(core_in[1])
    arrived(far_in, fs.at[0], fr.at[0], far)
    rounded = (near + f32(far_in[...])).astype(jnp.bfloat16)
    hidden[...] = rounded
    wide = f32(rounded)
    own_squares = jnp.sum(wide * wide, axis=1, keepdims=True)
    squares[...] = jnp.broadcast_to(own_squares, squares.shape)
    trio = [mate, far, cross]
    for i in range(3):
        pending.append(send(squares, squares_in.at[i], qs.at[i], qr.at[i], trio[i]))
    total = own_squares
    for i in range(3):
        arrived(squares_in.at[i], qs.at[i], qr.at[i], trio[i])
        total = total + squares_in[i, :, 0:1]
    root = lax.rsqrt(total / model_width + EPSILON)
    spread[z] = (wide * root * gain[...]).astype(jnp.bfloat16)
    rows = wide.shape[0] // 2

    def slot(direction, steps, piece):
        origin = lax.rem(z + (NZ - steps if direction == 0 else steps), NZ)
        return spread.at[origin, pl.ds(piece * rows, rows)]

    def sems(direction, step, piece):
        index = 2 * (step - 1) + piece
        return zs.at[direction, index], zr.at[direction, index]

    def pass_on(direction, step, piece):
        block = slot(direction, step - 1, piece)
        pending.append(send(block, block, *sems(direction, step, piece), ring[direction]))

    def got(direction, step, piece):
        arrived(slot(direction, step, piece), *sems(direction, step, piece), ring[direction])

    half = NZ // 2
    for piece in range(2):
        for direction in range(2):
            pass_on(direction, 1, piece)
    for step in range(2, half + 1):
        for piece in range(2):
            for direction in range(2):
                got(direction, step - 1, piece)
                if step < half or direction == piece:
                    pass_on(direction, step, piece)
    for direction in range(2):
        got(direction, half, direction)
    for copy in pending:
        copy.wait_send()


def norm_and_spread(o, stat, w_out, own_tokens, gain, model_width):
    rows, quarter = own_tokens.shape
    block = (rows, quarter)
    vmem = pl.BlockSpec(memory_space=pltpu.VMEM)
    return pl.pallas_call(
        functools.partial(norm_kernel, model_width),
        out_shape=(
            jax.ShapeDtypeStruct(block, jnp.bfloat16),
            jax.ShapeDtypeStruct((NZ,) + block, jnp.bfloat16),
        ),
        in_specs=[vmem] * 5,
        out_specs=(vmem, vmem),
        scratch_shapes=[
            pltpu.VMEM((NX - 1,) + o.shape[1:], o.dtype),
            pltpu.VMEM((NX - 1,) + stat.shape[1:], stat.dtype),
            pltpu.VMEM((2,) + block, jnp.bfloat16),
            pltpu.VMEM((2,) + block, jnp.bfloat16),
            pltpu.VMEM(block, jnp.bfloat16),
            pltpu.VMEM(block, jnp.bfloat16),
            pltpu.VMEM((rows, 128), jnp.float32),
            pltpu.VMEM((3, rows, 128), jnp.float32),
            pltpu.SemaphoreType.DMA((NX - 1,)),
            pltpu.SemaphoreType.DMA((NX - 1,)),
            pltpu.SemaphoreType.DMA((NX - 1,)),
            pltpu.SemaphoreType.DMA((NX - 1,)),
            pltpu.SemaphoreType.DMA((2,)),
            pltpu.SemaphoreType.DMA((2,)),
            pltpu.SemaphoreType.DMA((1,)),
            pltpu.SemaphoreType.DMA((1,)),
            pltpu.SemaphoreType.DMA((3,)),
            pltpu.SemaphoreType.DMA((3,)),
            pltpu.SemaphoreType.DMA((2, NZ)),
            pltpu.SemaphoreType.DMA((2, NZ)),
        ],
        compiler_params=pltpu.CompilerParams(
            collective_id=2, has_side_effects=True, vmem_limit_bytes=32 * 1024 * 1024
        ),
        name="norm_and_spread",
    )(o, stat, w_out, own_tokens, gain)


def dispatch_kernel(slots, source, rows, sel, held, own_sem, xs, xr, ys, yr, cs, cr):
    rank, tensor = lax.axis_index("expert"), lax.axis_index("tensor")
    y_lo, x, z, y_hi, core, far, sides, mate = corner(rank, tensor)
    other = 1 - y_lo
    x_peers = [(rank_of(y_lo, lax.rem(x + d, NX), z), tensor) for d in range(1, NX)]
    greet(x_peers + [far] + sides + [mate])
    pending = []
    lane = lax.broadcasted_iota(jnp.int32, (slots.shape[2], source.shape[0]), 1)

    def pick(side, to):
        chosen = jnp.where(lane == slots[side, to], 1.0, 0.0).astype(jnp.bfloat16)
        sel[side, to] = jnp.dot(
            chosen, source[...], preferred_element_type=jnp.float32
        ).astype(jnp.bfloat16)

    pick(other, x)
    pick(y_lo, x)
    own = pltpu.make_async_copy(sel.at[y_lo, x], rows.at[tensor, y_lo, x], own_sem.at[0])
    own.start()

    def to_side(d, here, there):
        x_s = lax.rem(x + NX - d, NX)
        spot = rows.at[tensor, y_lo, x_s]
        for r in range(2):
            pending.append(send(there, spot, ys.at[d, r], yr.at[d, r], sides[r]))
        pending.append(send(here, spot, ys.at[d, 2], yr.at[d, 2], far))

    def forward(d, r, l):
        x_s = lax.rem(x + NX - d, NX)
        spot = rows.at[lax.rem(y_hi + r, 2) * 2 + core, lax.rem(y_lo + l, 2), x_s]
        index = 2 * r + l
        pending.append(send(spot, spot, cs.at[d, index], cr.at[d, index], mate))

    to_side(0, sel.at[y_lo, x], sel.at[other, x])
    for d in (2, 1, 3):
        to = lax.rem(x + d, NX)
        for i in range(2):
            pick(other if i == 0 else y_lo, to)
            src = sel.at[other if i == 0 else y_lo, to]
            dst = held.at[x] if i == 0 else rows.at[tensor, y_lo, x]
            pending.append(send(src, dst, xs.at[d - 1, i], xr.at[d - 1, i], x_peers[d - 1]))
    own.wait()
    forward(0, 0, 0)
    for d in (1, 3, 2):
        x_s = lax.rem(x + NX - d, NX)
        arrived(held.at[x_s], xs.at[d - 1, 0], xr.at[d - 1, 0], x_peers[d - 1])
        arrived(rows.at[tensor, y_lo, x_s], xs.at[d - 1, 1], xr.at[d - 1, 1], x_peers[d - 1])
        to_side(d, rows.at[tensor, y_lo, x_s], held.at[x_s])
        forward(d, 0, 0)
    for d in (0, 1, 3, 2):
        x_s = lax.rem(x + NX - d, NX)
        for r in range(2):
            spot = rows.at[lax.rem(y_hi + r, 2) * 2 + core, other, x_s]
            arrived(spot, ys.at[d, r], yr.at[d, r], sides[r])
            forward(d, r, 1)
        spot = rows.at[(1 - y_hi) * 2 + core, y_lo, x_s]
        arrived(spot, ys.at[d, 2], yr.at[d, 2], far)
        forward(d, 1, 0)
    for d in range(NX):
        x_s = lax.rem(x + NX - d, NX)
        for r in range(2):
            for l in range(2):
                spot = rows.at[lax.rem(y_hi + r, 2) * 2 + 1 - core, lax.rem(y_lo + l, 2), x_s]
                arrived(spot, cs.at[d, 2 * r + l], cr.at[d, 2 * r + l], mate)
    for copy in pending:
        copy.wait_send()


def dispatch(slots, source):
    piece = (slots.shape[2], source.shape[1])
    vmem = pl.BlockSpec(memory_space=pltpu.VMEM)
    return pl.pallas_call(
        dispatch_kernel,
        out_shape=jax.ShapeDtypeStruct((4, NY, NX) + piece, source.dtype),
        in_specs=[vmem, vmem],
        out_specs=pl.BlockSpec(memory_space=pl.ANY),
        scratch_shapes=[
            pltpu.VMEM((NY, NX) + piece, source.dtype),
            pltpu.VMEM((NX,) + piece, source.dtype),
            pltpu.SemaphoreType.DMA((1,)),
            pltpu.SemaphoreType.DMA((NX - 1, 2)),
            pltpu.SemaphoreType.DMA((NX - 1, 2)),
            pltpu.SemaphoreType.DMA((NX, 3)),
            pltpu.SemaphoreType.DMA((NX, 3)),
            pltpu.SemaphoreType.DMA((NX, 4)),
            pltpu.SemaphoreType.DMA((NX, 4)),
        ],
        compiler_params=pltpu.CompilerParams(
            collective_id=3, has_side_effects=True, vmem_limit_bytes=32 * 1024 * 1024
        ),
        name="dispatch",
    )(slots, source)


def expert_kernel(rows_ref, up_ref, down_ref, out_ref, up, down):
    quarters, groups, size, width = rows_ref.shape
    count = groups * size
    units, real = down.shape[1], down_ref.shape[0]

    @pl.when(pl.program_id(0) == 0)
    def _():
        blank = jnp.zeros((units - real, width), jnp.bfloat16)
        for q in range(quarters):
            span = slice(q * width, (q + 1) * width)
            for i in range(2):
                up[q, i * units : i * units + real, :] = up_ref[i, :, span]
                up[q, i * units + real : (i + 1) * units, :] = blank
            down[q, :real, :] = down_ref[:, span]
            down[q, real:, :] = blank

    total = jnp.zeros((count, 2 * units), jnp.float32)
    for q in range(quarters):
        total += lax.dot_general(
            rows_ref[q].reshape(count, width), up[q], (((1,), (1,)), ((), ())),
            preferred_element_type=jnp.float32,
        )
    gate, raised = total[:, :units], total[:, units:]
    active = (gate * jax.nn.sigmoid(1.702 * gate) * (raised + 1.0)).astype(jnp.bfloat16)
    for q in range(quarters):
        value = jnp.dot(active, down[q], preferred_element_type=jnp.float32)
        out_ref[q] = value.astype(jnp.bfloat16).reshape(groups, size, width)


def run_expert(rows, up, down):
    quarters, groups, size, width = rows.shape
    step = 2
    units = -(-down.shape[0] // 128) * 128
    block = pl.BlockSpec((quarters, step, size, width), lambda i: (0, i, 0, 0))
    return pl.pallas_call(
        expert_kernel,
        grid=(groups // step,),
        in_specs=[
            block,
            pl.BlockSpec(up.shape, lambda i: (0, 0, 0)),
            pl.BlockSpec(down.shape, lambda i: (0, 0)),
        ],
        out_shape=jax.ShapeDtypeStruct(rows.shape, jnp.bfloat16),
        out_specs=block,
        scratch_shapes=[
            pltpu.VMEM((quarters, 2 * units, width), jnp.bfloat16),
            pltpu.VMEM((quarters, units, width), jnp.bfloat16),
        ],
        compiler_params=pltpu.CompilerParams(vmem_limit_bytes=56 * 1024 * 1024),
        name="run_expert",
    )(rows, up, down)


def collect_kernel(part, out, mine, core_in, side_out, side_in, x_out, ms, cs, cr, ys, yr, xs, xr):
    rank, tensor = lax.axis_index("expert"), lax.axis_index("tensor")
    y_lo, x, z, y_hi, core, far, sides, mate = corner(rank, tensor)
    other = 1 - y_lo
    x_peers = [(rank_of(y_lo, lax.rem(x + d, NX), z), tensor) for d in range(1, NX)]
    greet(x_peers + [far] + sides + [mate])
    pending, loads = [], {}
    order = (2, 1, 3, 0)
    def where(kind):
        half = y_hi if kind in (0, 3) else 1 - y_hi
        return half, (other if kind < 2 else y_lo)

    for d in order:
        x_h = lax.rem(x + d, NX)
        for kind in range(4):
            half, side = where(kind)
            src = part.at[half * 2 + 1 - core, side, x_h]
            pending.append(
                send(src, core_in.at[d, kind], cs.at[d, kind], cr.at[d, kind], mate)
            )
            load = pltpu.make_async_copy(
                part.at[half * 2 + core, side, x_h], mine.at[d, kind], ms.at[d, kind]
            )
            load.start()
            loads[d, kind] = load
    for d in order:
        for kind in range(4):
            arrived(core_in.at[d, kind], cs.at[d, kind], cr.at[d, kind], mate)
            loads[d, kind].wait()
            both = f32(mine[d, kind]) + f32(core_in[d, kind])
            side_out[d, kind] = both.astype(jnp.bfloat16)
            if kind < 3:
                to = far if kind == 2 else sides[kind]
                pending.append(
                    send(
                        side_out.at[d, kind], side_in.at[d, kind], ys.at[d, kind], yr.at[d, kind], to
                    )
                )
    for d in order:
        for kind in range(3):
            to = far if kind == 2 else sides[kind]
            arrived(side_in.at[d, kind], ys.at[d, kind], yr.at[d, kind], to)
            if kind == 0:
                continue
            first = side_in[d, 0] if kind == 1 else side_out[d, 3]
            both = (f32(first) + f32(side_in[d, kind])).astype(jnp.bfloat16)
            i = kind - 1
            owner = other if kind == 1 else y_lo
            if d == 0:
                out[owner, x] = both
            else:
                x_out[d - 1, i] = both
                pending.append(
                    send(
                        x_out.at[d - 1, i], out.at[owner, x], xs.at[d - 1, i], xr.at[d - 1, i],
                        x_peers[d - 1],
                    )
                )
    for d in order[:-1]:
        x_e = lax.rem(x + NX - d, NX)
        for i in range(2):
            owner = other if i == 0 else y_lo
            arrived(out.at[owner, x_e], xs.at[d - 1, i], xr.at[d - 1, i], x_peers[d - 1])
    for copy in pending:
        copy.wait_send()


def collect(part):
    piece = part.shape[3:]
    return pl.pallas_call(
        collect_kernel,
        out_shape=jax.ShapeDtypeStruct(part.shape[1:], part.dtype),
        in_specs=[pl.BlockSpec(memory_space=pl.ANY)],
        out_specs=pl.BlockSpec(memory_space=pltpu.VMEM),
        scratch_shapes=[
            pltpu.VMEM((NX, 4) + piece, jnp.bfloat16),
            pltpu.VMEM((NX, 4) + piece, jnp.bfloat16),
            pltpu.VMEM((NX, 4) + piece, jnp.bfloat16),
            pltpu.VMEM((NX, 3) + piece, jnp.bfloat16),
            pltpu.VMEM((NX - 1, 2) + piece, jnp.bfloat16),
            pltpu.SemaphoreType.DMA((NX, 4)),
            pltpu.SemaphoreType.DMA((NX, 4)),
            pltpu.SemaphoreType.DMA((NX, 4)),
            pltpu.SemaphoreType.DMA((NX, 3)),
            pltpu.SemaphoreType.DMA((NX, 3)),
            pltpu.SemaphoreType.DMA((NX - 1, 2)),
            pltpu.SemaphoreType.DMA((NX - 1, 2)),
        ],
        compiler_params=pltpu.CompilerParams(
            collective_id=4, has_side_effects=True, vmem_limit_bytes=48 * 1024 * 1024
        ),
        name="collect",
    )(part)


def home_kernel(slots, weights, rows_in, hidden, out, sums, staged, landed, zs, zr):
    rank, tensor = lax.axis_index("expert"), lax.axis_index("tensor")
    y_lo, x, z = place_of(rank)
    ring = [
        (rank_of(y_lo, x, lax.rem(z + 1, NZ)), tensor),
        (rank_of(y_lo, x, lax.rem(z + NZ - 1, NZ)), tensor),
    ]
    greet(ring)
    count = hidden.shape[0]
    rows = count // 2
    half = NZ // 2
    pending = []
    row = lax.broadcasted_iota(jnp.int32, (count, slots.shape[1]), 0)

    def add_up(home):
        share = jnp.where(row + home * count == slots[...], weights[...], 0.0)
        sums[home] = jnp.dot(
            share.astype(jnp.bfloat16), rows_in[...], preferred_element_type=jnp.float32
        ).astype(jnp.bfloat16)

    def reach(direction, piece):
        return half if direction == piece else half - 1

    def got(direction, steps, piece):
        index = 2 * steps + piece
        arrived(
            landed.at[direction, index], zs.at[direction, index], zr.at[direction, index],
            ring[direction],
        )
        return f32(landed[direction, index])

    for steps in range(half, 0, -1):
        add_up(lax.rem(z + steps, NZ))
        if steps < half:
            add_up(lax.rem(z + NZ - steps, NZ))
        for piece in range(2):
            for direction in range(2):
                if steps > reach(direction, piece):
                    continue
                home = lax.rem(z + (steps if direction == 0 else NZ - steps), NZ)
                mine = f32(sums[home, pl.ds(piece * rows, rows)])
                if steps < reach(direction, piece):
                    mine = mine + got(direction, steps, piece)
                index = 2 * (steps - 1) + piece
                staged[direction, index] = mine.astype(jnp.bfloat16)
                pending.append(
                    send(
                        staged.at[direction, index], landed.at[direction, index],
                        zs.at[direction, index], zr.at[direction, index], ring[direction],
                    )
                )
    add_up(z)
    for piece in range(2):
        span = pl.ds(piece * rows, rows)
        total = f32(sums[z, span])
        for direction in range(2):
            total = total + got(direction, 0, piece)
        out[span] = (f32(hidden[span]) + total).astype(jnp.bfloat16)
    for copy in pending:
        copy.wait_send()


def bring_home(slots, weights, rows_in, hidden):
    rows, width = hidden.shape
    vmem = pl.BlockSpec(memory_space=pltpu.VMEM)
    return pl.pallas_call(
        home_kernel,
        out_shape=jax.ShapeDtypeStruct(hidden.shape, hidden.dtype),
        in_specs=[vmem] * 4,
        out_specs=vmem,
        scratch_shapes=[
            pltpu.VMEM((NZ, rows, width), jnp.bfloat16),
            pltpu.VMEM((2, NZ, rows // 2, width), jnp.bfloat16),
            pltpu.VMEM((2, NZ, rows // 2, width), jnp.bfloat16),
            pltpu.SemaphoreType.DMA((2, NZ)),
            pltpu.SemaphoreType.DMA((2, NZ)),
        ],
        compiler_params=pltpu.CompilerParams(
            collective_id=5, has_side_effects=True, vmem_limit_bytes=32 * 1024 * 1024
        ),
        name="bring_home",
    )(slots, weights, rows_in, hidden)


def route_kernel(capacity, routed, weights, slab):
    experts, _ = slab.shape
    top_count, count = routed.shape
    row = lax.broadcasted_iota(jnp.int32, (experts, count), 0)
    lane = lax.broadcasted_iota(jnp.int32, (experts, count), 1)
    expert = lax.rem(row, experts // NZ) * NZ + row // (experts // NZ)
    before = jnp.where(
        lax.broadcasted_iota(jnp.int32, (count, count), 0)
        < lax.broadcasted_iota(jnp.int32, (count, count), 1),
        1.0,
        0.0,
    ).astype(jnp.bfloat16)
    token = f32(lane + 1)
    earlier = jnp.zeros((experts, 1), jnp.float32)
    arrivals, shares = [], []
    for k in range(top_count):
        hit = jnp.where(expert == routed[k : k + 1, :], 1.0, 0.0)
        ahead = jnp.dot(hit.astype(jnp.bfloat16), before, preferred_element_type=jnp.float32)
        arrivals.append(jnp.where(hit > 0.0, ahead + earlier, -1.0))
        shares.append(weights[k : k + 1, :])
        earlier = earlier + jnp.sum(hit, axis=1, keepdims=True)
    tokens, scales = jnp.full((experts, 128), -1.0, jnp.float32), jnp.zeros(
        (experts, 128), jnp.float32
    )
    slot = lax.broadcasted_iota(jnp.int32, (experts, 128), 1)
    for place in range(capacity):
        named = jnp.zeros((experts, count), jnp.float32)
        scale = jnp.zeros((experts, count), jnp.float32)
        for k in range(top_count):
            here = arrivals[k] == float(place)
            named = jnp.where(here, token, named)
            scale = jnp.where(here, shares[k], scale)
        tokens = jnp.where(slot == place, jnp.sum(named, axis=1, keepdims=True) - 1.0, tokens)
        scales = jnp.where(slot == place, jnp.sum(scale, axis=1, keepdims=True), scales)
    slab[:, :128] = tokens
    slab[:, 128:] = scales


def routing_slab(routed, weights, expert_count, capacity):
    vmem = pl.BlockSpec(memory_space=pltpu.VMEM)
    slab = pl.pallas_call(
        functools.partial(route_kernel, capacity),
        out_shape=jax.ShapeDtypeStruct((expert_count, 256), jnp.float32),
        in_specs=[vmem, vmem],
        out_specs=vmem,
        name="route",
    )(routed, weights)
    return slab.reshape(NZ, expert_count // NZ, 256)


def on_device(
    tokens,
    attn_gain,
    w_query,
    key_value_weight,
    w_out,
    cache_keyval,
    prefix_length,
    routed_experts,
    route_weights,
    expert_gain,
    w_gate_up,
    w_down,
):
    span_dev, seq_count, quarter = tokens.shape
    model_width = attn_gain.shape[0]
    row_count = span_dev * seq_count
    head_dim = key_value_weight.shape[2] // 2
    cache_rows = cache_keyval.shape[0]
    tensor_rank = lax.axis_index("tensor")
    expert_rank = lax.axis_index("expert")
    quarters = model_width // quarter
    top_count = routed_experts.shape[2]
    expert_count = lax.axis_size("expert")
    capacity = min(row_count, max(2, 5 * row_count * top_count // (2 * expert_count)))
    half_dim = head_dim // 2
    steps_up = jnp.arange(half_dim, dtype=jnp.float32)
    frequency = jnp.exp(steps_up * (-math.log(ROPE_BASE) / half_dim))
    span_place = expert_rank * span_dev + jnp.arange(span_dev, dtype=jnp.int32)
    places = (prefix_length[:, None] + span_place[None, :]).reshape(row_count).astype(jnp.float32)
    angles = frequency[:, None] * places[None, :]
    slab = routing_slab(
        routed_experts.transpose(2, 1, 0).reshape(top_count, row_count),
        route_weights.transpose(2, 1, 0).reshape(top_count, row_count),
        expert_count,
        capacity,
    )
    own_tokens = tokens.transpose(1, 0, 2).reshape(row_count, quarter)
    fresh, kv_all, q_all, slab_all = front(
        head_dim ** (-0.5) * LOG2E,
        own_tokens,
        attn_gain.reshape(quarters, 1, quarter),
        w_query,
        key_value_weight[:, 0, :],
        jnp.cos(angles),
        jnp.sin(angles),
        cache_keyval[:, :, 0, :].transpose(1, 0, 2),
        slab,
    )
    new_key_value_rows = fresh.transpose(1, 0, 2)[:, :, None, :]
    place = jnp.concatenate([prefix_length, expert_rank.astype(jnp.int32).reshape(1)])
    part, stat = attend(place, q_all, kv_all, cache_rows)
    gain = lax.dynamic_slice_in_dim(expert_gain, tensor_rank * quarter, quarter, 0)
    hidden, spread = norm_and_spread(
        part, stat, w_out.T, own_tokens, gain.reshape(1, quarter), model_width
    )
    token = slab_all[:, :, :capacity].astype(jnp.int32)
    first = jnp.arange(NZ, dtype=jnp.int32)[:, None, None] * row_count
    slot_token = jnp.where(token >= 0, token + first, -1).transpose(1, 0, 2)
    slot_weight = slab_all[:, :, 128 : 128 + capacity].transpose(1, 0, 2)
    groups, size = NY * NX, NZ * capacity
    rows = dispatch(
        slot_token.reshape(NY, NX, size, 1), spread.reshape(NZ * row_count, quarter)
    )
    value = run_expert(
        rows.reshape(quarters, groups, size, quarter),
        w_gate_up[0].transpose(1, 2, 0),
        w_down[0],
    )
    returned = collect(value.reshape(quarters, NY, NX, size, quarter))
    layer_output = bring_home(
        slot_token.reshape(1, groups * size),
        slot_weight.reshape(1, groups * size),
        returned.reshape(groups * size, quarter),
        hidden,
    )
    layer_output = layer_output.reshape(seq_count, span_dev, quarter).transpose(1, 0, 2)
    return (layer_output, new_key_value_rows)


def solution(mesh):
    return jax.shard_map(
        on_device,
        mesh=mesh,
        in_specs=(
            P("expert", None, "tensor"),
            P(),
            P(None, "tensor"),
            P(None, "tensor", None),
            P("tensor", None),
            P("expert", None, "tensor", None),
            P(),
            P("expert", None, None),
            P("expert", None, None),
            P(),
            P("expert", None, None, "tensor"),
            P("expert", "tensor", None),
        ),
        out_specs=(P("expert", None, "tensor"), P("expert", None, "tensor", None)),
        check_vma=False,
    )
```

```python
import functools
import math

import jax
import jax.numpy as jnp
from jax import lax
from jax.experimental import pallas as pl
from jax.experimental.pallas import tpu as pltpu
from jax.sharding import PartitionSpec as P

EPSILON = 1e-05
ROPE_BASE = 150000.0
NEG = -1e30
MESH = pl.DeviceIdType.MESH
NY, NX, NZ = 2, 4, 8
LOG2E = 1.4426950408889634


def place_of(expert_rank):
    return expert_rank // (NX * NZ), (expert_rank // NZ) % NX, expert_rank % NZ


def rank_of(y_lo, x, z):
    return (y_lo * NX + x) * NZ + z


def greet(devices):
    barrier = pltpu.get_barrier_semaphore()
    for device in devices:
        pl.semaphore_signal(barrier, inc=1, device_id=device, device_id_type=MESH)
    pl.semaphore_wait(barrier, len(devices))


def send(src, dst, send_sem, recv_sem, device):
    copy = pltpu.make_async_remote_copy(
        src_ref=src,
        dst_ref=dst,
        send_sem=send_sem,
        recv_sem=recv_sem,
        device_id=device,
        device_id_type=MESH,
    )
    copy.start()
    return copy


def arrived(dst, send_sem, recv_sem, device):
    pltpu.make_async_remote_copy(
        src_ref=dst,
        dst_ref=dst,
        send_sem=send_sem,
        recv_sem=recv_sem,
        device_id=device,
        device_id_type=MESH,
    ).wait_recv()


def swap_blocks(value):
    half = value.shape[0] // 2
    top, bottom = value[:half], value[half:]
    left = lax.broadcasted_iota(jnp.int32, top.shape, 1) < half
    return jnp.concatenate(
        [
            jnp.where(left, top, pltpu.roll(bottom, half, 1)),
            jnp.where(left, pltpu.roll(top, half, 1), bottom),
        ],
        axis=0,
    )


def turn(first, second, cosine, sine):
    return first * cosine - second * sine, second * cosine + first * sine


def front_kernel(
    scale, own_tokens, gain, w_query, w_keyval, cosine, sine, cache, slab,
    fresh, kv_all, q_all, slab_all,
    gathered, q_own, own_sem, gs, gr, xs, xr, ys, yr, zs, zr, ts, tr,
):
    rank, tensor = lax.axis_index("expert"), lax.axis_index("tensor")
    y_lo, x, z, y_hi, core, far, sides, mate = corner(rank, tensor)
    other = 1 - y_lo
    rows, quarter = own_tokens.shape
    cache_rows, head = cache.shape[1], fresh.shape[2] // 2
    span = fresh.shape[1]
    x_peers = [(rank_of(y_lo, lax.rem(x + d, NX), z), tensor) for d in range(1, NX)]
    y_peer = (rank_of(other, x, z), tensor)
    z_peers = [(rank_of(y_lo, x, lax.rem(z + d, NZ)), tensor) for d in range(1, NZ)]
    ring = [z_peers[0], z_peers[-1]]
    greet(x_peers + [y_peer] + z_peers + [far, mate])
    pending = []
    parts = (pl.ds(0, cache_rows), pl.ds(cache_rows, span))
    first = (cache, fresh)

    def slot(part, direction, steps, piece):
        origin = lax.rem(z + (NZ - steps if direction == 0 else steps), NZ)
        return kv_all.at[origin * 2 + (y_lo if piece == 0 else other), :, parts[part]]

    def sems(part, direction, step, piece):
        index = 2 * (step - 1) + piece
        return zs.at[part, direction, index], zr.at[part, direction, index]

    def pass_on(part, direction, step, piece):
        block = slot(part, direction, step - 1, piece)
        src = first[part] if step == 1 and piece == 0 else block
        pending.append(send(src, block, *sems(part, direction, step, piece), ring[direction]))

    def got(part, direction, step, piece):
        arrived(
            slot(part, direction, step, piece), *sems(part, direction, step, piece), ring[direction]
        )

    def begin(part):
        block = slot(part, 0, 0, 0)
        copy = pltpu.make_async_copy(first[part], block, own_sem.at[part])
        copy.start()
        pending.append(send(first[part], block, ys.at[part], yr.at[part], y_peer))
        for direction in range(2):
            pass_on(part, direction, 1, 0)
        return copy

    def begin_other(part):
        arrived(slot(part, 0, 0, 1), ys.at[part], yr.at[part], y_peer)
        for direction in range(2):
            pass_on(part, direction, 1, 1)

    half = NZ // 2

    def step_on(part, step):
        for piece in range(2):
            for direction in range(2):
                got(part, direction, step - 1, piece)
                if step < half or direction == piece:
                    pass_on(part, direction, step, piece)

    mine = gathered.at[tensor]
    pending.append(send(own_tokens, mine, gs.at[0], gr.at[0], far))
    pending.append(send(own_tokens, mine, gs.at[1], gr.at[1], mate))
    own = [begin(0), pltpu.make_async_copy(slab.at[z], slab_all.at[z], own_sem.at[2])]
    own[1].start()
    for d in range(1, NZ):
        to = lax.rem(z + d, NZ)
        pending.append(
            send(slab.at[to], slab_all.at[z], ts.at[d - 1], tr.at[d - 1], z_peers[d - 1])
        )
    far_index, mate_index = (1 - y_hi) * 2 + core, y_hi * 2 + 1 - core
    cross_index = (1 - y_hi) * 2 + 1 - core

    def project(index, block):
        wide = f32(block)
        scaled = (wide * gain[index]).astype(jnp.bfloat16)
        span_of = pl.ds(pl.multiple_of(index * quarter, 16), quarter)
        return (
            jnp.dot(scaled, w_query[span_of, :], preferred_element_type=jnp.float32),
            jnp.dot(scaled, w_keyval[span_of, :], preferred_element_type=jnp.float32),
            jnp.sum(wide * wide, axis=1, keepdims=True),
        )

    total = project(tensor, own_tokens[...])
    begin_other(0)
    arrived(gathered.at[far_index], gs.at[0], gr.at[0], far)
    block = gathered.at[far_index]
    pending.append(send(block, block, gs.at[2], gr.at[2], mate))
    total = [a + b for a, b in zip(total, project(far_index, gathered[far_index]))]
    arrived(gathered.at[mate_index], gs.at[1], gr.at[1], mate)
    total = [a + b for a, b in zip(total, project(mate_index, gathered[mate_index]))]
    step_on(0, 2)
    arrived(gathered.at[cross_index], gs.at[2], gr.at[2], mate)
    total = [a + b for a, b in zip(total, project(cross_index, gathered[cross_index]))]
    root = lax.rsqrt(total[2] / (4 * quarter) + EPSILON)
    cos, sin = cosine[...], sine[...]
    flipped = (total[1] * root).T
    keys = turn(flipped[: head // 2], flipped[head // 2 : head], cos, sin)
    whole = jnp.concatenate([keys[0], keys[1], flipped[head:]], axis=0).T
    fresh[...] = whole.astype(jnp.bfloat16).reshape(fresh.shape)
    own.append(begin(1))
    raw = total[0] * root
    width = 2 * head
    for j in range(raw.shape[1] // width):
        pair = raw[:, j * width : (j + 1) * width].T
        turned = []
        for h in range(2):
            block = pair[h * head : (h + 1) * head]
            turned += turn(block[: head // 2], block[head // 2 :], cos, sin)
        sides_first = swap_blocks(jnp.concatenate(turned, axis=0) * scale).astype(jnp.bfloat16)
        for s in range(2):
            q_own[s, :, j * width : (j + 1) * width] = sides_first[s * head : (s + 1) * head]
    copy = pltpu.make_async_copy(q_own, q_all.at[x], own_sem.at[3])
    copy.start()
    own.append(copy)
    for d in range(1, NX):
        pending.append(send(q_own, q_all.at[x], xs.at[d - 1], xr.at[d - 1], x_peers[d - 1]))
    begin_other(1)
    step_on(0, 3)
    step_on(1, 2)
    step_on(0, 4)
    step_on(1, 3)
    step_on(1, 4)
    for part in range(2):
        for direction in range(2):
            got(part, direction, half, direction)
    for d in range(1, NX):
        arrived(q_all.at[lax.rem(x + NX - d, NX)], xs.at[d - 1], xr.at[d - 1], x_peers[d - 1])
    for d in range(1, NZ):
        arrived(
            slab_all.at[lax.rem(z + NZ - d, NZ)], ts.at[d - 1], tr.at[d - 1], z_peers[d - 1]
        )
    for copy in own:
        copy.wait()
    for copy in pending:
        copy.wait_send()


def front(scale, own_tokens, gain, w_query, w_keyval, cosine, sine, cache, slab):
    seqs, cache_rows, width = cache.shape
    rows, quarter = own_tokens.shape
    span, cols = rows // seqs, w_query.shape[1] * rows // seqs // (width // 2)
    vmem = pl.BlockSpec(memory_space=pltpu.VMEM)
    any_space = pl.BlockSpec(memory_space=pl.ANY)
    return pl.pallas_call(
        functools.partial(front_kernel, scale),
        out_shape=(
            jax.ShapeDtypeStruct((seqs, span, width), jnp.bfloat16),
            jax.ShapeDtypeStruct((NY * NZ, seqs, cache_rows + span, width), jnp.bfloat16),
            jax.ShapeDtypeStruct((NX, seqs, width // 2, cols), jnp.bfloat16),
            jax.ShapeDtypeStruct(slab.shape, slab.dtype),
        ),
        in_specs=[vmem] * 6 + [any_space] * 2,
        out_specs=(vmem, any_space, any_space, any_space),
        scratch_shapes=[
            pltpu.VMEM((4, rows, quarter), jnp.bfloat16),
            pltpu.VMEM((seqs, width // 2, cols), jnp.bfloat16),
            pltpu.SemaphoreType.DMA((4,)),
            pltpu.SemaphoreType.DMA((3,)),
            pltpu.SemaphoreType.DMA((3,)),
            pltpu.SemaphoreType.DMA((NX - 1,)),
            pltpu.SemaphoreType.DMA((NX - 1,)),
            pltpu.SemaphoreType.DMA((2,)),
            pltpu.SemaphoreType.DMA((2,)),
            pltpu.SemaphoreType.DMA((2, 2, NZ)),
            pltpu.SemaphoreType.DMA((2, 2, NZ)),
            pltpu.SemaphoreType.DMA((NZ - 1,)),
            pltpu.SemaphoreType.DMA((NZ - 1,)),
        ],
        compiler_params=pltpu.CompilerParams(
            collective_id=0, has_side_effects=True, vmem_limit_bytes=32 * 1024 * 1024
        ),
        name="front",
    )(own_tokens, gain, w_query, w_keyval, cosine, sine, cache, slab)


def attend_kernel(cache_rows, place, q_ref, kv_ref, o_ref, stat_ref, vt_ref, qa_ref, mask_ref):
    xq = pl.program_id(1)
    prefix = place[pl.program_id(0)]
    my_rank = place[place.shape[0] - 1]
    y_lo, x, z = place_of(my_rank)
    chunks, _, chunk = vt_ref.shape
    shards, _, keys, width = kv_ref.shape
    per = chunk // keys
    head, cols = q_ref.shape[2:]

    @pl.when(xq == 0)
    def _():
        for j in range(chunks):
            rows = kv_ref[j * per : (j + 1) * per, 0].reshape(chunk, width)
            flipped = rows.astype(jnp.float32).T
            vt_ref[j, :16, :] = jnp.ones((16, chunk), jnp.bfloat16)
            vt_ref[j, 16:, :] = flipped[head:].astype(jnp.bfloat16)
        span = keys - cache_rows
        old_row = lax.broadcasted_iota(jnp.int32, (cache_rows, width), 0)
        old_col = lax.broadcasted_iota(jnp.int32, (cache_rows, width), 1)
        new_row = lax.broadcasted_iota(jnp.int32, (span, width), 0)
        new_col = lax.broadcasted_iota(jnp.int32, (span, width), 1)
        old_row = jnp.where(old_col == span + NX, old_row, -1)
        in_block = (new_col >= span) & (new_col < span + NX)
        query_rank = rank_of(y_lo, new_col - span, z)
        later = (new_col < span) & (new_row > new_col)
        for j in range(shards):
            key_rank = rank_of(j % 2, x, j // 2)
            valid = jnp.maximum(prefix - key_rank * cache_rows, 0)
            beyond = jnp.where(old_row >= valid, NEG, 0.0)
            mask_ref[j, :cache_rows, :] = beyond.astype(jnp.bfloat16)
            same = jnp.where(key_rank == my_rank, 1, 0)
            hidden_key = (in_block & (key_rank > query_rank)) | (later & (same > 0))
            mask_ref[j, cache_rows:, :] = jnp.where(hidden_key, NEG, 0.0).astype(jnp.bfloat16)

    qa_ref[:head, :] = q_ref[0, 0]
    qa_ref[head:width, :] = jnp.zeros((width - head, cols), jnp.bfloat16)
    row = lax.broadcasted_iota(jnp.int32, (width, cols), 0)
    lane = lax.broadcasted_iota(jnp.int32, (width, cols), 1)
    span = head
    tri = jnp.where(xq == x, lane % span, -1)
    hot = (row == tri) | (row == span + xq) | (row == span + NX)
    qa_ref[width:, :] = jnp.where(hot, 1.0, 0.0).astype(jnp.bfloat16)
    qa = qa_ref[...]
    top = jnp.full((1, cols), -3e38, jnp.float32)
    acc = jnp.zeros((vt_ref.shape[1], cols), jnp.float32)
    for j in range(chunks):
        lhs = jnp.concatenate(
            [
                kv_ref[j * per : (j + 1) * per, 0].reshape(chunk, width),
                mask_ref[j * per : (j + 1) * per].reshape(chunk, width),
            ],
            axis=1,
        )
        scores = jnp.dot(lhs, qa, preferred_element_type=jnp.float32)
        new_top = jnp.maximum(top, jnp.max(scores, axis=0, keepdims=True))
        probs = jnp.exp2(scores - new_top).astype(jnp.bfloat16)
        acc = acc * jnp.exp2(top - new_top) + jnp.dot(
            vt_ref[j], probs, preferred_element_type=jnp.float32
        )
        top = new_top
    total = acc[0:1]
    o_ref[0, 0] = (acc[16:] / total).astype(jnp.bfloat16)
    stat_ref[0, 0, 0:1, :] = top
    stat_ref[0, 0, 1:2, :] = total
    stat_ref[0, 0, 2:, :] = jnp.zeros((6, cols), jnp.float32)


def attend(place, q_all, kv_all, cache_rows):
    nx, seqs, head, cols = q_all.shape
    shards, _, keys, width = kv_all.shape
    chunk = 2 * keys
    chunks = shards * keys // chunk
    return pl.pallas_call(
        functools.partial(attend_kernel, cache_rows),
        grid=(seqs, nx),
        in_specs=[
            pl.BlockSpec(memory_space=pltpu.SMEM),
            pl.BlockSpec((1, 1, head, cols), lambda s, i: (i, s, 0, 0)),
            pl.BlockSpec((shards, 1, keys, width), lambda s, i: (0, s, 0, 0)),
        ],
        out_shape=(
            jax.ShapeDtypeStruct((nx, seqs, head, cols), jnp.bfloat16),
            jax.ShapeDtypeStruct((nx, seqs, 8, cols), jnp.float32),
        ),
        out_specs=(
            pl.BlockSpec((1, 1, head, cols), lambda s, i: (i, s, 0, 0)),
            pl.BlockSpec((1, 1, 8, cols), lambda s, i: (i, s, 0, 0)),
        ),
        scratch_shapes=[
            pltpu.VMEM((chunks, 16 + head, chunk), jnp.bfloat16),
            pltpu.VMEM((2 * width, cols), jnp.bfloat16),
            pltpu.VMEM((shards, keys, width), jnp.bfloat16),
        ],
        compiler_params=pltpu.CompilerParams(vmem_limit_bytes=48 * 1024 * 1024),
        name="attend",
    )(place, q_all, kv_all)


def corner(rank, tensor):
    y_lo, x, z = place_of(rank)
    y_hi, core = tensor // 2, lax.rem(tensor, 2)
    far = (rank, (1 - y_hi) * 2 + core)
    sides = [(rank_of(1 - y_lo, x, z), lax.rem(y_hi + r, 2) * 2 + core) for r in range(2)]
    mate = (rank, y_hi * 2 + 1 - core)
    return y_lo, x, z, y_hi, core, far, sides, mate


def f32(value):
    return value.astype(jnp.float32)


def norm_kernel(
    model_width, o, stat, w_out, own_tokens, gain, hidden, spread,
    o_in, stat_in, to_core, core_in, core_out, far_in, squares, squares_in,
    os, orr, ss, sr, cs, cr, fs, fr, qs, qr, zs, zr,
):
    rank, tensor = lax.axis_index("expert"), lax.axis_index("tensor")
    y_lo, x, z, y_hi, core, far, sides, mate = corner(rank, tensor)
    cross = (rank, (1 - y_hi) * 2 + 1 - core)
    ring = [
        (rank_of(y_lo, x, lax.rem(z + 1, NZ)), tensor),
        (rank_of(y_lo, x, lax.rem(z + NZ - 1, NZ)), tensor),
    ]
    x_peers = [(rank_of(y_lo, lax.rem(x + d, NX), z), tensor) for d in range(1, NX)]
    greet([mate, far, cross] + ring + x_peers)
    pending = []
    for d in range(1, NX):
        to, i = lax.rem(x + d, NX), d - 1
        pending.append(send(stat.at[to], stat_in.at[i], ss.at[i], sr.at[i], x_peers[i]))
        pending.append(send(o.at[to], o_in.at[i], os.at[i], orr.at[i], x_peers[i]))
    stats, values = [stat[x]], [o[x]]
    for i in range(NX - 1):
        arrived(stat_in.at[i], ss.at[i], sr.at[i], x_peers[i])
        arrived(o_in.at[i], os.at[i], orr.at[i], x_peers[i])
        stats.append(stat_in[i])
        values.append(o_in[i])
    seqs, head, cols = values[0].shape
    merged = []
    for s in range(seqs):
        tops = [value[s, 0:1] for value in stats]
        top = functools.reduce(jnp.maximum, tops)
        shares = [jnp.exp2(a - top) * value[s, 1:2] for a, value in zip(tops, stats)]
        whole = functools.reduce(jnp.add, shares)
        merged.append(
            functools.reduce(jnp.add, [f32(v[s]) * (a / whole) for v, a in zip(values, shares)])
        )
    both = jnp.concatenate(merged, axis=0)
    wide_head = seqs * head
    attended = jnp.concatenate(
        [
            swap_blocks(both[:, j * wide_head : (j + 1) * wide_head].T)
            for j in range(cols // wide_head)
        ],
        axis=1,
    ).astype(jnp.bfloat16)
    quarter = own_tokens.shape[1]

    def projected(index):
        span_of = pl.ds(pl.multiple_of(index * quarter, 16), quarter)
        return lax.dot_general(
            attended, w_out[span_of, :], (((1,), (1,)), ((), ())),
            preferred_element_type=jnp.float32,
        )

    order = [1 - y_hi, y_hi]
    for i in range(2):
        to_core[i] = projected(order[i] * 2 + 1 - core).astype(jnp.bfloat16)
        pending.append(send(to_core.at[i], core_in.at[i], cs.at[i], cr.at[i], mate))
    for_far = projected(order[0] * 2 + core)
    arrived(core_in.at[0], cs.at[0], cr.at[0], mate)
    core_out[...] = (for_far + f32(core_in[0])).astype(jnp.bfloat16)
    pending.append(send(core_out, far_in, fs.at[0], fr.at[0], far))
    near = f32(own_tokens[...]) + projected(order[1] * 2 + core)
    arrived(core_in.at[1], cs.at[1], cr.at[1], mate)
    near = near + f32(core_in[1])
    arrived(far_in, fs.at[0], fr.at[0], far)
    rounded = (near + f32(far_in[...])).astype(jnp.bfloat16)
    hidden[...] = rounded
    wide = f32(rounded)
    own_squares = jnp.sum(wide * wide, axis=1, keepdims=True)
    squares[...] = jnp.broadcast_to(own_squares, squares.shape)
    trio = [mate, far, cross]
    for i in range(3):
        pending.append(send(squares, squares_in.at[i], qs.at[i], qr.at[i], trio[i]))
    total = own_squares
    for i in range(3):
        arrived(squares_in.at[i], qs.at[i], qr.at[i], trio[i])
        total = total + squares_in[i, :, 0:1]
    root = lax.rsqrt(total / model_width + EPSILON)
    spread[z] = (wide * root * gain[...]).astype(jnp.bfloat16)
    rows = wide.shape[0] // 2

    def slot(direction, steps, piece):
        origin = lax.rem(z + (NZ - steps if direction == 0 else steps), NZ)
        return spread.at[origin, pl.ds(piece * rows, rows)]

    def sems(direction, step, piece):
        index = 2 * (step - 1) + piece
        return zs.at[direction, index], zr.at[direction, index]

    def pass_on(direction, step, piece):
        block = slot(direction, step - 1, piece)
        pending.append(send(block, block, *sems(direction, step, piece), ring[direction]))

    def got(direction, step, piece):
        arrived(slot(direction, step, piece), *sems(direction, step, piece), ring[direction])

    half = NZ // 2
    for piece in range(2):
        for direction in range(2):
            pass_on(direction, 1, piece)
    for step in range(2, half + 1):
        for piece in range(2):
            for direction in range(2):
                got(direction, step - 1, piece)
                if step < half or direction == piece:
                    pass_on(direction, step, piece)
    for direction in range(2):
        got(direction, half, direction)
    for copy in pending:
        copy.wait_send()


def norm_and_spread(o, stat, w_out, own_tokens, gain, model_width):
    rows, quarter = own_tokens.shape
    block = (rows, quarter)
    vmem = pl.BlockSpec(memory_space=pltpu.VMEM)
    return pl.pallas_call(
        functools.partial(norm_kernel, model_width),
        out_shape=(
            jax.ShapeDtypeStruct(block, jnp.bfloat16),
            jax.ShapeDtypeStruct((NZ,) + block, jnp.bfloat16),
        ),
        in_specs=[vmem] * 5,
        out_specs=(vmem, vmem),
        scratch_shapes=[
            pltpu.VMEM((NX - 1,) + o.shape[1:], o.dtype),
            pltpu.VMEM((NX - 1,) + stat.shape[1:], stat.dtype),
            pltpu.VMEM((2,) + block, jnp.bfloat16),
            pltpu.VMEM((2,) + block, jnp.bfloat16),
            pltpu.VMEM(block, jnp.bfloat16),
            pltpu.VMEM(block, jnp.bfloat16),
            pltpu.VMEM((rows, 128), jnp.float32),
            pltpu.VMEM((3, rows, 128), jnp.float32),
            pltpu.SemaphoreType.DMA((NX - 1,)),
            pltpu.SemaphoreType.DMA((NX - 1,)),
            pltpu.SemaphoreType.DMA((NX - 1,)),
            pltpu.SemaphoreType.DMA((NX - 1,)),
            pltpu.SemaphoreType.DMA((2,)),
            pltpu.SemaphoreType.DMA((2,)),
            pltpu.SemaphoreType.DMA((1,)),
            pltpu.SemaphoreType.DMA((1,)),
            pltpu.SemaphoreType.DMA((3,)),
            pltpu.SemaphoreType.DMA((3,)),
            pltpu.SemaphoreType.DMA((2, NZ)),
            pltpu.SemaphoreType.DMA((2, NZ)),
        ],
        compiler_params=pltpu.CompilerParams(
            collective_id=2, has_side_effects=True, vmem_limit_bytes=32 * 1024 * 1024
        ),
        name="norm_and_spread",
    )(o, stat, w_out, own_tokens, gain)


def expert_kernel(
    slots, source, up_hbm, down_hbm, out,
    rows, sel, held, up_raw, down_raw, up, down, mine, to_mate, core_in, side_in, x_out,
    ws, xs, xr, ys, yr, fs, fr, cs, cr, bs, br, es, er,
):
    rank, tensor = lax.axis_index("expert"), lax.axis_index("tensor")
    y_lo, x, z, y_hi, core, far, sides, mate = corner(rank, tensor)
    other = 1 - y_lo
    x_peers = [(rank_of(y_lo, lax.rem(x + d, NX), z), tensor) for d in range(1, NX)]
    greet(x_peers + [far] + sides + [mate])
    pending = []
    loads = [
        pltpu.make_async_copy(up_hbm, up_raw, ws.at[0]),
        pltpu.make_async_copy(down_hbm, down_raw, ws.at[1]),
    ]
    for load in loads:
        load.start()
    size, width = sel.shape[2:]
    quarters = rows.shape[0]
    lane = lax.broadcasted_iota(jnp.int32, (size, source.shape[0]), 1)

    def pick(side, to):
        chosen = jnp.where(lane == slots[side, to], 1.0, 0.0).astype(jnp.bfloat16)
        return jnp.dot(chosen, source[...], preferred_element_type=jnp.float32).astype(
            jnp.bfloat16
        )

    def to_side(d, here, there):
        spot = rows.at[tensor, y_lo, lax.rem(x + NX - d, NX)]
        for r in range(2):
            pending.append(send(there, spot, ys.at[d, r], yr.at[d, r], sides[r]))
        pending.append(send(here, spot, ys.at[d, 2], yr.at[d, 2], far))

    def forward(d, r, l):
        x_s = lax.rem(x + NX - d, NX)
        spot = rows.at[lax.rem(y_hi + r, 2) * 2 + core, lax.rem(y_lo + l, 2), x_s]
        index = 2 * r + l
        pending.append(send(spot, spot, fs.at[d, index], fr.at[d, index], mate))

    def from_sides(d):
        x_s = lax.rem(x + NX - d, NX)
        for r in range(2):
            spot = rows.at[lax.rem(y_hi + r, 2) * 2 + core, other, x_s]
            arrived(spot, ys.at[d, r], yr.at[d, r], sides[r])
            forward(d, r, 1)
        spot = rows.at[(1 - y_hi) * 2 + core, y_lo, x_s]
        arrived(spot, ys.at[d, 2], yr.at[d, 2], far)
        forward(d, 1, 0)

    def from_mate(d):
        x_s = lax.rem(x + NX - d, NX)
        for r in range(2):
            for l in range(2):
                spot = rows.at[lax.rem(y_hi + r, 2) * 2 + 1 - core, lax.rem(y_lo + l, 2), x_s]
                arrived(spot, fs.at[d, 2 * r + l], fr.at[d, 2 * r + l], mate)

    units, real = down.shape[1], down_raw.shape[0]

    def run(d):
        x_s = lax.rem(x + NX - d, NX)
        total = jnp.zeros((2 * size, 2 * units), jnp.float32)
        for q in range(quarters):
            block = jnp.concatenate([rows[q, other, x_s], rows[q, y_lo, x_s]], axis=0)
            total += lax.dot_general(
                block, up[q], (((1,), (1,)), ((), ())), preferred_element_type=jnp.float32
            )
        gate, raised = total[:, :units], total[:, units:]
        active = (gate * jax.nn.sigmoid(1.702 * gate) * (raised + 1.0)).astype(jnp.bfloat16)
        for h in range(2):
            half = lax.rem(y_hi + h, 2)
            for owner in range(2):
                index = half * 2 + (core if owner else 1 - core)
                value = jnp.dot(active, down[index], preferred_element_type=jnp.float32).astype(
                    jnp.bfloat16
                )
                into = mine if owner else to_mate
                into[d, h] = value[:size]
                into[d, 3 - h] = value[size:]
                if not owner:
                    for kind in (h, 3 - h):
                        pending.append(
                            send(
                                to_mate.at[d, kind], core_in.at[d, kind],
                                cs.at[d, kind], cr.at[d, kind], mate,
                            )
                        )

    def back_to_sides(d):
        for kind in range(4):
            arrived(core_in.at[d, kind], cs.at[d, kind], cr.at[d, kind], mate)
            both = f32(mine[d, kind]) + f32(core_in[d, kind])
            mine[d, kind] = both.astype(jnp.bfloat16)
            if kind < 3:
                to = far if kind == 2 else sides[kind]
                pending.append(
                    send(mine.at[d, kind], side_in.at[d, kind], bs.at[d, kind], br.at[d, kind], to)
                )

    def back_to_x(d):
        for kind in range(3):
            to = far if kind == 2 else sides[kind]
            arrived(side_in.at[d, kind], bs.at[d, kind], br.at[d, kind], to)
            if kind == 0:
                continue
            first = side_in[d, 0] if kind == 1 else mine[d, 3]
            both = (f32(first) + f32(side_in[d, kind])).astype(jnp.bfloat16)
            i = kind - 1
            owner = other if kind == 1 else y_lo
            if d == 0:
                out[owner, x] = both
            else:
                e = NX - d - 1
                x_out[d - 1, i] = both
                pending.append(
                    send(x_out.at[d - 1, i], out.at[owner, x], es.at[e, i], er.at[e, i], x_peers[e])
                )

    sel[other, x] = pick(other, x)
    rows[tensor, y_lo, x] = pick(y_lo, x)
    to_side(0, rows.at[tensor, y_lo, x], sel.at[other, x])
    for d in (1, 3, 2):
        to = lax.rem(x + d, NX)
        for i in range(2):
            side = other if i == 0 else y_lo
            sel[side, to] = pick(side, to)
            dst = held.at[x] if i == 0 else rows.at[tensor, y_lo, x]
            pending.append(
                send(sel.at[side, to], dst, xs.at[d - 1, i], xr.at[d - 1, i], x_peers[d - 1])
            )
    forward(0, 0, 0)
    blank = jnp.zeros((units - real, width), jnp.bfloat16)
    for load in loads:
        load.wait()
    for q in range(quarters):
        span = slice(q * width, (q + 1) * width)
        for i in range(2):
            up[q, i * units : i * units + real, :] = up_raw[i, :, span]
            up[q, i * units + real : (i + 1) * units, :] = blank
        down[q, :real, :] = down_raw[:, span]
        down[q, real:, :] = blank

    def from_x(d):
        x_s = lax.rem(x + NX - d, NX)
        arrived(held.at[x_s], xs.at[d - 1, 0], xr.at[d - 1, 0], x_peers[d - 1])
        arrived(rows.at[tensor, y_lo, x_s], xs.at[d - 1, 1], xr.at[d - 1, 1], x_peers[d - 1])
        to_side(d, rows.at[tensor, y_lo, x_s], held.at[x_s])
        forward(d, 0, 0)

    from_x(1)
    from_x(3)
    from_sides(0)
    from_x(2)
    for d in (0, 1, 3, 2):
        if d:
            from_sides(d)
        from_mate(d)
        run(d)
        if d in (1, 3):
            back_to_sides(d)
    back_to_sides(2)
    back_to_sides(0)
    for d in (1, 3, 2, 0):
        back_to_x(d)
    for d in range(1, NX):
        x_e = lax.rem(x + NX - d, NX)
        for i in range(2):
            owner = other if i == 0 else y_lo
            arrived(out.at[owner, x_e], es.at[d - 1, i], er.at[d - 1, i], x_peers[d - 1])
    for copy in pending:
        copy.wait_send()


def run_experts(slots, source, up, down):
    width = source.shape[1]
    piece = (slots.shape[2], width)
    quarters = down.shape[1] // width
    units = -(-down.shape[0] // 128) * 128
    vmem = pl.BlockSpec(memory_space=pltpu.VMEM)
    any_space = pl.BlockSpec(memory_space=pl.ANY)
    bf16, sem = jnp.bfloat16, pltpu.SemaphoreType.DMA
    return pl.pallas_call(
        expert_kernel,
        out_shape=jax.ShapeDtypeStruct((NY, NX) + piece, bf16),
        in_specs=[vmem, vmem, any_space, any_space],
        out_specs=vmem,
        scratch_shapes=[
            pltpu.VMEM((quarters, NY, NX) + piece, bf16),
            pltpu.VMEM((NY, NX) + piece, bf16),
            pltpu.VMEM((NX,) + piece, bf16),
            pltpu.VMEM(up.shape, bf16),
            pltpu.VMEM(down.shape, bf16),
            pltpu.VMEM((quarters, 2 * units, width), bf16),
            pltpu.VMEM((quarters, units, width), bf16),
            pltpu.VMEM((NX, 4) + piece, bf16),
            pltpu.VMEM((NX, 4) + piece, bf16),
            pltpu.VMEM((NX, 4) + piece, bf16),
            pltpu.VMEM((NX, 3) + piece, bf16),
            pltpu.VMEM((NX - 1, 2) + piece, bf16),
            sem((2,)),
            sem((NX - 1, 2)),
            sem((NX - 1, 2)),
            sem((NX, 3)),
            sem((NX, 3)),
            sem((NX, 4)),
            sem((NX, 4)),
            sem((NX, 4)),
            sem((NX, 4)),
            sem((NX, 3)),
            sem((NX, 3)),
            sem((NX - 1, 2)),
            sem((NX - 1, 2)),
        ],
        compiler_params=pltpu.CompilerParams(
            collective_id=3, has_side_effects=True, vmem_limit_bytes=58 * 1024 * 1024
        ),
        name="run_experts",
    )(slots, source, up, down)


def home_kernel(slots, weights, rows_in, hidden, out, sums, staged, landed, zs, zr):
    rank, tensor = lax.axis_index("expert"), lax.axis_index("tensor")
    y_lo, x, z = place_of(rank)
    ring = [
        (rank_of(y_lo, x, lax.rem(z + 1, NZ)), tensor),
        (rank_of(y_lo, x, lax.rem(z + NZ - 1, NZ)), tensor),
    ]
    greet(ring)
    count = hidden.shape[0]
    rows = count // 2
    half = NZ // 2
    pending = []
    row = lax.broadcasted_iota(jnp.int32, (count, slots.shape[1]), 0)

    def add_up(home):
        share = jnp.where(row + home * count == slots[...], weights[...], 0.0)
        sums[home] = jnp.dot(
            share.astype(jnp.bfloat16), rows_in[...], preferred_element_type=jnp.float32
        ).astype(jnp.bfloat16)

    def reach(direction, piece):
        return half if direction == piece else half - 1

    def got(direction, steps, piece):
        index = 2 * steps + piece
        arrived(
            landed.at[direction, index], zs.at[direction, index], zr.at[direction, index],
            ring[direction],
        )
        return f32(landed[direction, index])

    for steps in range(half, 0, -1):
        add_up(lax.rem(z + steps, NZ))
        if steps < half:
            add_up(lax.rem(z + NZ - steps, NZ))
        for piece in range(2):
            for direction in range(2):
                if steps > reach(direction, piece):
                    continue
                home = lax.rem(z + (steps if direction == 0 else NZ - steps), NZ)
                mine = f32(sums[home, pl.ds(piece * rows, rows)])
                if steps < reach(direction, piece):
                    mine = mine + got(direction, steps, piece)
                index = 2 * (steps - 1) + piece
                staged[direction, index] = mine.astype(jnp.bfloat16)
                pending.append(
                    send(
                        staged.at[direction, index], landed.at[direction, index],
                        zs.at[direction, index], zr.at[direction, index], ring[direction],
                    )
                )
    add_up(z)
    for piece in range(2):
        span = pl.ds(piece * rows, rows)
        total = f32(sums[z, span])
        for direction in range(2):
            total = total + got(direction, 0, piece)
        out[span] = (f32(hidden[span]) + total).astype(jnp.bfloat16)
    for copy in pending:
        copy.wait_send()


def bring_home(slots, weights, rows_in, hidden):
    rows, width = hidden.shape
    vmem = pl.BlockSpec(memory_space=pltpu.VMEM)
    return pl.pallas_call(
        home_kernel,
        out_shape=jax.ShapeDtypeStruct(hidden.shape, hidden.dtype),
        in_specs=[vmem] * 4,
        out_specs=vmem,
        scratch_shapes=[
            pltpu.VMEM((NZ, rows, width), jnp.bfloat16),
            pltpu.VMEM((2, NZ, rows // 2, width), jnp.bfloat16),
            pltpu.VMEM((2, NZ, rows // 2, width), jnp.bfloat16),
            pltpu.SemaphoreType.DMA((2, NZ)),
            pltpu.SemaphoreType.DMA((2, NZ)),
        ],
        compiler_params=pltpu.CompilerParams(
            collective_id=5, has_side_effects=True, vmem_limit_bytes=32 * 1024 * 1024
        ),
        name="bring_home",
    )(slots, weights, rows_in, hidden)


def route_kernel(capacity, routed, weights, slab):
    experts, _ = slab.shape
    top_count, count = routed.shape
    row = lax.broadcasted_iota(jnp.int32, (experts, count), 0)
    lane = lax.broadcasted_iota(jnp.int32, (experts, count), 1)
    expert = lax.rem(row, experts // NZ) * NZ + row // (experts // NZ)
    before = jnp.where(
        lax.broadcasted_iota(jnp.int32, (count, count), 0)
        < lax.broadcasted_iota(jnp.int32, (count, count), 1),
        1.0,
        0.0,
    ).astype(jnp.bfloat16)
    token = f32(lane + 1)
    earlier = jnp.zeros((experts, 1), jnp.float32)
    arrivals, shares = [], []
    for k in range(top_count):
        hit = jnp.where(expert == routed[k : k + 1, :], 1.0, 0.0)
        ahead = jnp.dot(hit.astype(jnp.bfloat16), before, preferred_element_type=jnp.float32)
        arrivals.append(jnp.where(hit > 0.0, ahead + earlier, -1.0))
        shares.append(weights[k : k + 1, :])
        earlier = earlier + jnp.sum(hit, axis=1, keepdims=True)
    tokens, scales = jnp.full((experts, 128), -1.0, jnp.float32), jnp.zeros(
        (experts, 128), jnp.float32
    )
    slot = lax.broadcasted_iota(jnp.int32, (experts, 128), 1)
    for place in range(capacity):
        named = jnp.zeros((experts, count), jnp.float32)
        scale = jnp.zeros((experts, count), jnp.float32)
        for k in range(top_count):
            here = arrivals[k] == float(place)
            named = jnp.where(here, token, named)
            scale = jnp.where(here, shares[k], scale)
        tokens = jnp.where(slot == place, jnp.sum(named, axis=1, keepdims=True) - 1.0, tokens)
        scales = jnp.where(slot == place, jnp.sum(scale, axis=1, keepdims=True), scales)
    slab[:, :128] = tokens
    slab[:, 128:] = scales


def routing_slab(routed, weights, expert_count, capacity):
    vmem = pl.BlockSpec(memory_space=pltpu.VMEM)
    slab = pl.pallas_call(
        functools.partial(route_kernel, capacity),
        out_shape=jax.ShapeDtypeStruct((expert_count, 256), jnp.float32),
        in_specs=[vmem, vmem],
        out_specs=vmem,
        name="route",
    )(routed, weights)
    return slab.reshape(NZ, expert_count // NZ, 256)


def on_device(
    tokens,
    attn_gain,
    w_query,
    key_value_weight,
    w_out,
    cache_keyval,
    prefix_length,
    routed_experts,
    route_weights,
    expert_gain,
    w_gate_up,
    w_down,
):
    span_dev, seq_count, quarter = tokens.shape
    model_width = attn_gain.shape[0]
    row_count = span_dev * seq_count
    head_dim = key_value_weight.shape[2] // 2
    cache_rows = cache_keyval.shape[0]
    tensor_rank = lax.axis_index("tensor")
    expert_rank = lax.axis_index("expert")
    quarters = model_width // quarter
    top_count = routed_experts.shape[2]
    expert_count = lax.axis_size("expert")
    capacity = min(row_count, max(2, 5 * row_count * top_count // (2 * expert_count)))
    half_dim = head_dim // 2
    steps_up = jnp.arange(half_dim, dtype=jnp.float32)
    frequency = jnp.exp(steps_up * (-math.log(ROPE_BASE) / half_dim))
    span_place = expert_rank * span_dev + jnp.arange(span_dev, dtype=jnp.int32)
    places = (prefix_length[:, None] + span_place[None, :]).reshape(row_count).astype(jnp.float32)
    angles = frequency[:, None] * places[None, :]
    slab = routing_slab(
        routed_experts.transpose(2, 1, 0).reshape(top_count, row_count),
        route_weights.transpose(2, 1, 0).reshape(top_count, row_count),
        expert_count,
        capacity,
    )
    own_tokens = tokens.transpose(1, 0, 2).reshape(row_count, quarter)
    fresh, kv_all, q_all, slab_all = front(
        head_dim ** (-0.5) * LOG2E,
        own_tokens,
        attn_gain.reshape(quarters, 1, quarter),
        w_query,
        key_value_weight[:, 0, :],
        jnp.cos(angles),
        jnp.sin(angles),
        cache_keyval[:, :, 0, :].transpose(1, 0, 2),
        slab,
    )
    new_key_value_rows = fresh.transpose(1, 0, 2)[:, :, None, :]
    place = jnp.concatenate([prefix_length, expert_rank.astype(jnp.int32).reshape(1)])
    part, stat = attend(place, q_all, kv_all, cache_rows)
    gain = lax.dynamic_slice_in_dim(expert_gain, tensor_rank * quarter, quarter, 0)
    hidden, spread = norm_and_spread(
        part, stat, w_out.T, own_tokens, gain.reshape(1, quarter), model_width
    )
    token = slab_all[:, :, :capacity].astype(jnp.int32)
    first = jnp.arange(NZ, dtype=jnp.int32)[:, None, None] * row_count
    slot_token = jnp.where(token >= 0, token + first, -1).transpose(1, 0, 2)
    slot_weight = slab_all[:, :, 128 : 128 + capacity].transpose(1, 0, 2)
    groups, size = NY * NX, NZ * capacity
    returned = run_experts(
        slot_token.reshape(NY, NX, size, 1),
        spread.reshape(NZ * row_count, quarter),
        w_gate_up[0].transpose(1, 2, 0),
        w_down[0],
    )
    layer_output = bring_home(
        slot_token.reshape(1, groups * size),
        slot_weight.reshape(1, groups * size),
        returned.reshape(groups * size, quarter),
        hidden,
    )
    layer_output = layer_output.reshape(seq_count, span_dev, quarter).transpose(1, 0, 2)
    return (layer_output, new_key_value_rows)


def solution(mesh):
    return jax.shard_map(
        on_device,
        mesh=mesh,
        in_specs=(
            P("expert", None, "tensor"),
            P(),
            P(None, "tensor"),
            P(None, "tensor", None),
            P("tensor", None),
            P("expert", None, "tensor", None),
            P(),
            P("expert", None, None),
            P("expert", None, None),
            P(),
            P("expert", None, None, "tensor"),
            P("expert", "tensor", None),
        ),
        out_specs=(P("expert", None, "tensor"), P("expert", None, "tensor", None)),
        check_vma=False,
    )
```

```python
import functools
import math

import jax
import jax.numpy as jnp
from jax import lax
from jax.experimental import pallas as pl
from jax.experimental.pallas import tpu as pltpu
from jax.sharding import PartitionSpec as P

EPSILON = 1e-05
ROPE_BASE = 150000.0
NEG = -1e30
MESH = pl.DeviceIdType.MESH
NY, NX, NZ = 2, 4, 8
LOG2E = 1.4426950408889634


def place_of(expert_rank):
    return expert_rank // (NX * NZ), (expert_rank // NZ) % NX, expert_rank % NZ


def rank_of(y_lo, x, z):
    return (y_lo * NX + x) * NZ + z


def greet(devices):
    barrier = pltpu.get_barrier_semaphore()
    for device in devices:
        pl.semaphore_signal(barrier, inc=1, device_id=device, device_id_type=MESH)
    pl.semaphore_wait(barrier, len(devices))


def send(src, dst, send_sem, recv_sem, device):
    copy = pltpu.make_async_remote_copy(
        src_ref=src,
        dst_ref=dst,
        send_sem=send_sem,
        recv_sem=recv_sem,
        device_id=device,
        device_id_type=MESH,
    )
    copy.start()
    return copy


def arrived(dst, send_sem, recv_sem, device):
    pltpu.make_async_remote_copy(
        src_ref=dst,
        dst_ref=dst,
        send_sem=send_sem,
        recv_sem=recv_sem,
        device_id=device,
        device_id_type=MESH,
    ).wait_recv()


def swap_blocks(value):
    half = value.shape[0] // 2
    top, bottom = value[:half], value[half:]
    left = lax.broadcasted_iota(jnp.int32, top.shape, 1) < half
    return jnp.concatenate(
        [
            jnp.where(left, top, pltpu.roll(bottom, half, 1)),
            jnp.where(left, pltpu.roll(top, half, 1), bottom),
        ],
        axis=0,
    )


def turn(first, second, cosine, sine):
    return first * cosine - second * sine, second * cosine + first * sine


def corner(rank, tensor):
    y_lo, x, z = place_of(rank)
    y_hi, core = tensor // 2, lax.rem(tensor, 2)
    far = (rank, (1 - y_hi) * 2 + core)
    sides = [(rank_of(1 - y_lo, x, z), lax.rem(y_hi + r, 2) * 2 + core) for r in range(2)]
    mate = (rank, y_hi * 2 + 1 - core)
    return y_lo, x, z, y_hi, core, far, sides, mate


def f32(value):
    return value.astype(jnp.float32)


def attention_kernel(
    scale, own_tokens, gain, cosine, sine, cache, prefix, out_gain, slab, w_query_hbm, w_keyval_hbm, w_out_hbm,
    fresh, hidden, spread, slab_all,
    w_query, w_keyval, w_out, gathered, kv_old, kv_new, q_all, qa, tops, sums, o_out, stat_out,
    o_in, stat_in, to_core, core_in, keep, far_out, far_in, squares, squares_in,
    ws, gs, gr, xs, xr, ys, yr, zs, zr, ts, tr, own_sem, os, orr, ss, sr, cs, cr, fs, fr, qs, qr, hs, hr,
):
    rank, tensor = lax.axis_index("expert"), lax.axis_index("tensor")
    y_lo, x, z, y_hi, core, far, sides, mate = corner(rank, tensor)
    other = 1 - y_lo
    rows, quarter = own_tokens.shape
    seqs, span, width = fresh.shape
    cache_rows, head = cache.shape[1], width // 2
    cols = q_all.shape[3]
    bf16 = jnp.bfloat16
    x_peers = [(rank_of(y_lo, lax.rem(x + d, NX), z), tensor) for d in range(1, NX)]
    y_peer = (rank_of(other, x, z), tensor)
    z_peers = [(rank_of(y_lo, x, lax.rem(z + d, NZ)), tensor) for d in range(1, NZ)]
    ring = [z_peers[0], z_peers[-1]]
    cross = (rank, (1 - y_hi) * 2 + 1 - core)
    greet(x_peers + [y_peer] + z_peers + [far, mate, cross])
    pending = []
    loads = [
        pltpu.make_async_copy(src, dst, ws.at[i])
        for i, (src, dst) in enumerate(
            [(w_query_hbm, w_query), (w_keyval_hbm, w_keyval), (w_out_hbm, w_out)]
        )
    ]
    for load in loads:
        load.start()
    half = NZ // 2
    stores = (kv_old, kv_new)

    def slot(part, direction, steps, piece):
        origin = lax.rem(z + (NZ - steps if direction == 0 else steps), NZ)
        return stores[part].at[origin * 2 + (y_lo if piece == 0 else other)]

    def sems(part, direction, step, piece):
        index = 2 * (step - 1) + piece
        return zs.at[part, direction, index], zr.at[part, direction, index]

    def pass_on(part, direction, step, piece):
        block = slot(part, direction, step - 1, piece)
        pending.append(send(block, block, *sems(part, direction, step, piece), ring[direction]))

    def got(part, direction, step, piece):
        arrived(
            slot(part, direction, step, piece), *sems(part, direction, step, piece), ring[direction]
        )

    def begin(part):
        block = slot(part, 0, 0, 0)
        pending.append(send(block, block, ys.at[part], yr.at[part], y_peer))
        for direction in range(2):
            pass_on(part, direction, 1, 0)

    def begin_other(part):
        arrived(slot(part, 0, 0, 1), ys.at[part], yr.at[part], y_peer)
        for direction in range(2):
            pass_on(part, direction, 1, 1)

    def step_on(part, step):
        for piece in range(2):
            for direction in range(2):
                got(part, direction, step - 1, piece)
                if step < half or direction == piece:
                    pass_on(part, direction, step, piece)

    mine = gathered.at[tensor]
    pending.append(send(own_tokens, mine, gs.at[0], gr.at[0], far))
    pending.append(send(own_tokens, mine, gs.at[1], gr.at[1], mate))
    kv_old[z * 2 + y_lo] = cache[...]
    begin(0)
    own_slab = pltpu.make_async_copy(slab.at[z], slab_all.at[z], own_sem.at[0])
    own_slab.start()
    for d in range(1, NZ):
        to = lax.rem(z + d, NZ)
        pending.append(
            send(slab.at[to], slab_all.at[z], ts.at[d - 1], tr.at[d - 1], z_peers[d - 1])
        )
    far_index, mate_index = (1 - y_hi) * 2 + core, y_hi * 2 + 1 - core
    cross_index = (1 - y_hi) * 2 + 1 - core

    def rows_of(index):
        return pl.ds(pl.multiple_of(index * quarter, 16), quarter)

    def project(index, block):
        wide = f32(block)
        scaled = (wide * gain[index]).astype(bf16)
        return (
            jnp.dot(scaled, w_query[rows_of(index), :], preferred_element_type=jnp.float32),
            jnp.dot(scaled, w_keyval[rows_of(index), :], preferred_element_type=jnp.float32),
            jnp.sum(wide * wide, axis=1, keepdims=True),
        )

    loads[0].wait()
    loads[1].wait()
    total = project(tensor, own_tokens[...])
    begin_other(0)
    arrived(gathered.at[far_index], gs.at[0], gr.at[0], far)
    block = gathered.at[far_index]
    pending.append(send(block, block, gs.at[2], gr.at[2], mate))
    total = [a + b for a, b in zip(total, project(far_index, gathered[far_index]))]
    arrived(gathered.at[mate_index], gs.at[1], gr.at[1], mate)
    total = [a + b for a, b in zip(total, project(mate_index, gathered[mate_index]))]
    step_on(0, 2)
    arrived(gathered.at[cross_index], gs.at[2], gr.at[2], mate)
    total = [a + b for a, b in zip(total, project(cross_index, gathered[cross_index]))]
    root = lax.rsqrt(total[2] / (4 * quarter) + EPSILON)
    cos, sin = cosine[...], sine[...]
    flipped = (total[1] * root).T
    keys = turn(flipped[: head // 2], flipped[head // 2 : head], cos, sin)
    whole = jnp.concatenate([keys[0], keys[1], flipped[head:]], axis=0).T
    own_rows = whole.astype(bf16).reshape(fresh.shape)
    fresh[...] = own_rows
    kv_new[z * 2 + y_lo] = own_rows
    begin(1)
    raw = total[0] * root
    for j in range(raw.shape[1] // width):
        pair = raw[:, j * width : (j + 1) * width].T
        turned = []
        for h in range(2):
            block = pair[h * head : (h + 1) * head]
            turned += turn(block[: head // 2], block[head // 2 :], cos, sin)
        first = swap_blocks(jnp.concatenate(turned, axis=0) * scale).astype(bf16)
        for s in range(seqs):
            q_all[0, s, :, j * width : (j + 1) * width] = first[s * head : (s + 1) * head]
    for d in (1, 3, 2):
        pending.append(
            send(q_all.at[0], q_all.at[NX - d], xs.at[d - 1], xr.at[d - 1], x_peers[d - 1])
        )
    begin_other(1)
    step_on(0, 3)

    row = lax.broadcasted_iota(jnp.int32, (width, cols), 0)
    lane = lax.broadcasted_iota(jnp.int32, (width, cols), 1)
    for k in range(NX):
        hot = (row == span + lax.rem(x + k, NX)) | (row == span + NX)
        if k == 0:
            hot = hot | (row == lax.rem(lane, span))
        qa[k, head:width, :] = jnp.zeros((width - head, cols), bf16)
        qa[k, width:, :] = jnp.where(hot, 1.0, 0.0).astype(bf16)

    def old_chunk(s, offsets):
        values, masks = [], []
        old_row = lax.broadcasted_iota(jnp.int32, (cache_rows, width), 0)
        marked = lax.broadcasted_iota(jnp.int32, (cache_rows, width), 1) == span + NX
        for offset in offsets:
            origin = lax.rem(z + offset, NZ)
            for side in range(NY):
                values.append(kv_old[origin * 2 + side, s])
                place = old_row + rank_of(side, x, origin) * cache_rows
                masks.append(
                    jnp.where(marked & (place >= prefix[s]), NEG, 0.0).astype(bf16)
                )
        return jnp.concatenate(values, axis=0), jnp.concatenate(masks, axis=0)

    def new_chunk(s):
        masks = []
        new_row = lax.broadcasted_iota(jnp.int32, (span, width), 0)
        new_col = lax.broadcasted_iota(jnp.int32, (span, width), 1)
        in_block = (new_col >= span) & (new_col < span + NX)
        query_rank = rank_of(y_lo, new_col - span, z)
        later = (new_col < span) & (new_row > new_col)
        for shard in range(NY * NZ):
            key_rank = rank_of(shard % 2, x, shard // 2)
            late = in_block & (key_rank > query_rank)
            same = later & (jnp.full(later.shape, key_rank, jnp.int32) == rank)
            masks.append(jnp.where(late | same, NEG, 0.0).astype(bf16))
        return kv_new[:, s].reshape(NY * NZ * span, width), jnp.concatenate(masks, axis=0)

    def attend(chunk, fresh_start):
        keyval, mask = chunk
        lhs = jnp.concatenate([keyval, mask], axis=1)
        flipped = f32(keyval).T[head:].astype(bf16)
        values = jnp.concatenate([jnp.ones((16, keyval.shape[0]), bf16), flipped], axis=0)
        for k in range(NX):
            scores = jnp.dot(lhs, qa[k], preferred_element_type=jnp.float32)
            top = jnp.max(scores, axis=0, keepdims=True)
            if not fresh_start:
                top = jnp.maximum(top, tops[k])
            probs = jnp.exp2(scores - top).astype(bf16)
            part = jnp.dot(values, probs, preferred_element_type=jnp.float32)
            if not fresh_start:
                part = part + sums[k] * jnp.exp2(tops[k] - top)
            sums[k] = part
            tops[k] = top

    def take_queries(s):
        for k in range(NX):
            qa[k, :head, :] = q_all[k, s]

    def finish(s):
        for k in (2, 1, 3, 0):
            value = sums[k]
            o_out[s, k] = (value[16:] / value[0:1]).astype(bf16)
            stat_out[s, k, 0:1, :] = tops[k]
            stat_out[s, k, 1:2, :] = value[0:1]
            stat_out[s, k, 2:, :] = jnp.zeros((6, cols), jnp.float32)
            if k:
                to, i = x_peers[k - 1], NX - k - 1
                pending.append(
                    send(stat_out.at[s, k], stat_in.at[s, i], ss.at[s, i], sr.at[s, i], to)
                )
                pending.append(send(o_out.at[s, k], o_in.at[s, i], os.at[s, i], orr.at[s, i], to))

    order = [1 - y_hi, y_hi]

    def combine(s):
        stats, values = [stat_out[s, 0]], [o_out[s, 0]]
        for i in (0, 2, 1):
            arrived(stat_in.at[s, i], ss.at[s, i], sr.at[s, i], x_peers[i])
            arrived(o_in.at[s, i], os.at[s, i], orr.at[s, i], x_peers[i])
            stats.append(stat_in[s, i])
            values.append(o_in[s, i])
        top = functools.reduce(jnp.maximum, [value[0:1] for value in stats])
        shares = [jnp.exp2(value[0:1] - top) * value[1:2] for value in stats]
        every = functools.reduce(jnp.add, shares)
        merged = functools.reduce(
            jnp.add, [f32(value) * (share / every) for value, share in zip(values, shares)]
        )
        blank = jnp.zeros((head, width), jnp.float32)
        attended = jnp.concatenate(
            [
                swap_blocks(
                    jnp.concatenate([merged[:, j * width : (j + 1) * width], blank], axis=0).T
                )[:span]
                for j in range(cols // width)
            ],
            axis=1,
        ).astype(bf16)

        def projected(index):
            return lax.dot_general(
                attended, w_out[rows_of(index), :], (((1,), (1,)), ((), ())),
                preferred_element_type=jnp.float32,
            )

        for i in range(2):
            to_core[s, i] = projected(order[i] * 2 + 1 - core).astype(bf16)
            pending.append(
                send(to_core.at[s, i], core_in.at[s, i], cs.at[s, i], cr.at[s, i], mate)
            )
        keep[s, 0] = projected(order[0] * 2 + core)
        keep[s, 1] = projected(order[1] * 2 + core)

    def across_core(s):
        arrived(core_in.at[s, 0], cs.at[s, 0], cr.at[s, 0], mate)
        far_out[s] = (keep[s, 0] + f32(core_in[s, 0])).astype(bf16)
        pending.append(send(far_out.at[s], far_in.at[s], fs.at[s], fr.at[s], far))

    trio = [mate, far, cross]

    def residual(s):
        mine = pl.ds(s * span, span)
        arrived(core_in.at[s, 1], cs.at[s, 1], cr.at[s, 1], mate)
        near = f32(own_tokens[mine]) + (keep[s, 1] + f32(core_in[s, 1]))
        arrived(far_in.at[s], fs.at[s], fr.at[s], far)
        rounded = (near + f32(far_in[s])).astype(bf16)
        hidden[mine] = rounded
        wide = f32(rounded)
        squares[s] = jnp.broadcast_to(jnp.sum(wide * wide, axis=1, keepdims=True), squares.shape[1:])
        for i in range(3):
            pending.append(
                send(squares.at[s], squares_in.at[s, i], qs.at[s, i], qr.at[s, i], trio[i])
            )

    def spot(direction, steps, s):
        origin = lax.rem(z + (NZ - steps if direction == 0 else steps), NZ)
        return spread.at[origin, pl.ds(s * span, span)]

    def ring_on(s, step):
        for direction in range(2):
            if 1 < step <= half or (step > half and direction == s):
                arrived(
                    spot(direction, step - 1, s), hs.at[direction, step - 1, s],
                    hr.at[direction, step - 1, s], ring[direction],
                )
            if step < half or (step == half and direction == s):
                block = spot(direction, step - 1, s)
                pending.append(
                    send(
                        block, block, hs.at[direction, step, s], hr.at[direction, step, s],
                        ring[direction],
                    )
                )

    def normalise(s):
        mine = pl.ds(s * span, span)
        total = squares[s, :, 0:1]
        for i in range(3):
            arrived(squares_in.at[s, i], qs.at[s, i], qr.at[s, i], trio[i])
            total = total + squares_in[s, i, :, 0:1]
        factor = lax.rsqrt(total / (4 * quarter) + EPSILON)
        spread[z, mine] = (f32(hidden[mine]) * factor * out_gain[...]).astype(bf16)
        ring_on(s, 1)

    near_first = [(0, NZ - 1), (1, NZ - 2), (2, NZ - 3), (3, 4)]
    for d in (1, 3, 2):
        arrived(q_all.at[NX - d], xs.at[d - 1], xr.at[d - 1], x_peers[d - 1])
    take_queries(0)
    step_on(1, 2)
    attend(old_chunk(0, near_first[0]), True)
    step_on(0, 4)
    step_on(1, 3)
    attend(old_chunk(0, near_first[1]), False)
    step_on(1, 4)
    attend(old_chunk(0, near_first[2]), False)
    for part in range(2):
        for direction in range(2):
            got(part, direction, half, direction)
    attend(old_chunk(0, near_first[3]), False)
    attend(new_chunk(0), False)
    finish(0)
    take_queries(1)
    attend(old_chunk(1, near_first[0]), True)
    loads[2].wait()
    attend(old_chunk(1, near_first[1]), False)
    combine(0)
    attend(old_chunk(1, near_first[2]), False)
    across_core(0)
    attend(old_chunk(1, near_first[3]), False)
    residual(0)
    attend(new_chunk(1), False)
    finish(1)
    normalise(0)
    ring_on(0, 2)
    combine(1)
    ring_on(0, 3)
    across_core(1)
    ring_on(0, 4)
    residual(1)
    ring_on(0, 5)
    normalise(1)
    for step in range(2, half + 2):
        ring_on(1, step)
    for d in range(1, NZ):
        arrived(
            slab_all.at[lax.rem(z + NZ - d, NZ)], ts.at[d - 1], tr.at[d - 1], z_peers[d - 1]
        )
    own_slab.wait()
    for copy in pending:
        copy.wait_send()


def attention(
    scale, own_tokens, gain, cosine, sine, cache, prefix, out_gain, slab, w_query, w_keyval, w_out
):
    seqs, cache_rows, width = cache.shape
    rows, quarter = own_tokens.shape
    span, head = rows // seqs, width // 2
    cols = w_query.shape[1] // head * span
    vmem = pl.BlockSpec(memory_space=pltpu.VMEM)
    any_space = pl.BlockSpec(memory_space=pl.ANY)
    bf16, wide, sem = jnp.bfloat16, jnp.float32, pltpu.SemaphoreType.DMA
    return pl.pallas_call(
        functools.partial(attention_kernel, scale),
        out_shape=(
            jax.ShapeDtypeStruct((seqs, span, width), bf16),
            jax.ShapeDtypeStruct((rows, quarter), bf16),
            jax.ShapeDtypeStruct((NZ, rows, quarter), bf16),
            jax.ShapeDtypeStruct(slab.shape, slab.dtype),
        ),
        in_specs=[vmem] * 7 + [any_space] * 4,
        out_specs=(vmem, vmem, vmem, any_space),
        scratch_shapes=[
            pltpu.VMEM(w_query.shape, bf16),
            pltpu.VMEM(w_keyval.shape, bf16),
            pltpu.VMEM(w_out.shape, bf16),
            pltpu.VMEM((4, rows, quarter), bf16),
            pltpu.VMEM((NY * NZ, seqs, cache_rows, width), bf16),
            pltpu.VMEM((NY * NZ, seqs, span, width), bf16),
            pltpu.VMEM((NX, seqs, head, cols), bf16),
            pltpu.VMEM((NX, 2 * width, cols), bf16),
            pltpu.VMEM((NX, 1, cols), wide),
            pltpu.VMEM((NX, 16 + head, cols), wide),
            pltpu.VMEM((seqs, NX, head, cols), bf16),
            pltpu.VMEM((seqs, NX, 8, cols), wide),
            pltpu.VMEM((seqs, NX - 1, head, cols), bf16),
            pltpu.VMEM((seqs, NX - 1, 8, cols), wide),
            pltpu.VMEM((seqs, 2, span, quarter), bf16),
            pltpu.VMEM((seqs, 2, span, quarter), bf16),
            pltpu.VMEM((seqs, 2, span, quarter), wide),
            pltpu.VMEM((seqs, span, quarter), bf16),
            pltpu.VMEM((seqs, span, quarter), bf16),
            pltpu.VMEM((seqs, span, 128), wide),
            pltpu.VMEM((seqs, 3, span, 128), wide),
            sem((3,)),
            sem((3,)),
            sem((3,)),
            sem((NX - 1,)),
            sem((NX - 1,)),
            sem((2,)),
            sem((2,)),
            sem((2, 2, NZ)),
            sem((2, 2, NZ)),
            sem((NZ - 1,)),
            sem((NZ - 1,)),
            sem((1,)),
            sem((seqs, NX - 1)),
            sem((seqs, NX - 1)),
            sem((seqs, NX - 1)),
            sem((seqs, NX - 1)),
            sem((seqs, 2)),
            sem((seqs, 2)),
            sem((seqs,)),
            sem((seqs,)),
            sem((seqs, 3)),
            sem((seqs, 3)),
            sem((2, NZ // 2 + 1, seqs)),
            sem((2, NZ // 2 + 1, seqs)),
        ],
        compiler_params=pltpu.CompilerParams(
            collective_id=0, has_side_effects=True, vmem_limit_bytes=48 * 1024 * 1024
        ),
        name="attention",
    )(own_tokens, gain, cosine, sine, cache, prefix, out_gain, slab, w_query, w_keyval, w_out)


def expert_kernel(
    slots, source, up_hbm, down_hbm, out,
    rows, sel, held, up_raw, down_raw, up, down, mine, to_mate, core_in, side_in, x_out,
    ws, xs, xr, ys, yr, fs, fr, cs, cr, bs, br, es, er,
):
    rank, tensor = lax.axis_index("expert"), lax.axis_index("tensor")
    y_lo, x, z, y_hi, core, far, sides, mate = corner(rank, tensor)
    other = 1 - y_lo
    x_peers = [(rank_of(y_lo, lax.rem(x + d, NX), z), tensor) for d in range(1, NX)]
    greet(x_peers + [far] + sides + [mate])
    pending = []
    loads = [
        pltpu.make_async_copy(up_hbm, up_raw, ws.at[0]),
        pltpu.make_async_copy(down_hbm, down_raw, ws.at[1]),
    ]
    for load in loads:
        load.start()
    size, width = sel.shape[2:]
    quarters = rows.shape[0]
    lane = lax.broadcasted_iota(jnp.int32, (size, source.shape[0]), 1)

    def pick(side, to):
        chosen = jnp.where(lane == slots[side, to], 1.0, 0.0).astype(jnp.bfloat16)
        return jnp.dot(chosen, source[...], preferred_element_type=jnp.float32).astype(
            jnp.bfloat16
        )

    def to_side(d, here, there):
        spot = rows.at[tensor, y_lo, lax.rem(x + NX - d, NX)]
        for r in range(2):
            pending.append(send(there, spot, ys.at[d, r], yr.at[d, r], sides[r]))
        pending.append(send(here, spot, ys.at[d, 2], yr.at[d, 2], far))

    def forward(d, r, l):
        x_s = lax.rem(x + NX - d, NX)
        spot = rows.at[lax.rem(y_hi + r, 2) * 2 + core, lax.rem(y_lo + l, 2), x_s]
        index = 2 * r + l
        pending.append(send(spot, spot, fs.at[d, index], fr.at[d, index], mate))

    def from_sides(d):
        x_s = lax.rem(x + NX - d, NX)
        for r in range(2):
            spot = rows.at[lax.rem(y_hi + r, 2) * 2 + core, other, x_s]
            arrived(spot, ys.at[d, r], yr.at[d, r], sides[r])
            forward(d, r, 1)
        spot = rows.at[(1 - y_hi) * 2 + core, y_lo, x_s]
        arrived(spot, ys.at[d, 2], yr.at[d, 2], far)
        forward(d, 1, 0)

    def from_mate(d):
        x_s = lax.rem(x + NX - d, NX)
        for r in range(2):
            for l in range(2):
                spot = rows.at[lax.rem(y_hi + r, 2) * 2 + 1 - core, lax.rem(y_lo + l, 2), x_s]
                arrived(spot, fs.at[d, 2 * r + l], fr.at[d, 2 * r + l], mate)

    units, real = down.shape[1], down_raw.shape[0]

    def run(d):
        x_s = lax.rem(x + NX - d, NX)
        total = jnp.zeros((2 * size, 2 * units), jnp.float32)
        for q in range(quarters):
            block = jnp.concatenate([rows[q, other, x_s], rows[q, y_lo, x_s]], axis=0)
            total += lax.dot_general(
                block, up[q], (((1,), (1,)), ((), ())), preferred_element_type=jnp.float32
            )
        gate, raised = total[:, :units], total[:, units:]
        active = (gate * jax.nn.sigmoid(1.702 * gate) * (raised + 1.0)).astype(jnp.bfloat16)
        for h in range(2):
            half = lax.rem(y_hi + h, 2)
            for owner in range(2):
                index = half * 2 + (core if owner else 1 - core)
                value = jnp.dot(active, down[index], preferred_element_type=jnp.float32).astype(
                    jnp.bfloat16
                )
                into = mine if owner else to_mate
                into[d, h] = value[:size]
                into[d, 3 - h] = value[size:]
                if not owner:
                    for kind in (h, 3 - h):
                        pending.append(
                            send(
                                to_mate.at[d, kind], core_in.at[d, kind],
                                cs.at[d, kind], cr.at[d, kind], mate,
                            )
                        )

    def back_to_sides(d):
        for kind in range(4):
            arrived(core_in.at[d, kind], cs.at[d, kind], cr.at[d, kind], mate)
            both = f32(mine[d, kind]) + f32(core_in[d, kind])
            mine[d, kind] = both.astype(jnp.bfloat16)
            if kind < 3:
                to = far if kind == 2 else sides[kind]
                pending.append(
                    send(mine.at[d, kind], side_in.at[d, kind], bs.at[d, kind], br.at[d, kind], to)
                )

    def back_to_x(d):
        for kind in range(3):
            to = far if kind == 2 else sides[kind]
            arrived(side_in.at[d, kind], bs.at[d, kind], br.at[d, kind], to)
            if kind == 0:
                continue
            first = side_in[d, 0] if kind == 1 else mine[d, 3]
            both = (f32(first) + f32(side_in[d, kind])).astype(jnp.bfloat16)
            i = kind - 1
            owner = other if kind == 1 else y_lo
            if d == 0:
                out[owner, x] = both
            else:
                e = NX - d - 1
                x_out[d - 1, i] = both
                pending.append(
                    send(x_out.at[d - 1, i], out.at[owner, x], es.at[e, i], er.at[e, i], x_peers[e])
                )

    sel[other, x] = pick(other, x)
    rows[tensor, y_lo, x] = pick(y_lo, x)
    to_side(0, rows.at[tensor, y_lo, x], sel.at[other, x])
    for d in (1, 3, 2):
        to = lax.rem(x + d, NX)
        for i in range(2):
            side = other if i == 0 else y_lo
            sel[side, to] = pick(side, to)
            dst = held.at[x] if i == 0 else rows.at[tensor, y_lo, x]
            pending.append(
                send(sel.at[side, to], dst, xs.at[d - 1, i], xr.at[d - 1, i], x_peers[d - 1])
            )
    forward(0, 0, 0)
    blank = jnp.zeros((units - real, width), jnp.bfloat16)
    for load in loads:
        load.wait()
    for q in range(quarters):
        span = slice(q * width, (q + 1) * width)
        for i in range(2):
            up[q, i * units : i * units + real, :] = up_raw[i, :, span]
            up[q, i * units + real : (i + 1) * units, :] = blank
        down[q, :real, :] = down_raw[:, span]
        down[q, real:, :] = blank

    def from_x(d):
        x_s = lax.rem(x + NX - d, NX)
        arrived(held.at[x_s], xs.at[d - 1, 0], xr.at[d - 1, 0], x_peers[d - 1])
        arrived(rows.at[tensor, y_lo, x_s], xs.at[d - 1, 1], xr.at[d - 1, 1], x_peers[d - 1])
        to_side(d, rows.at[tensor, y_lo, x_s], held.at[x_s])
        forward(d, 0, 0)

    from_x(1)
    from_x(3)
    from_sides(0)
    from_x(2)
    for d in (0, 1, 3, 2):
        if d:
            from_sides(d)
        from_mate(d)
        run(d)
        if d in (1, 3):
            back_to_sides(d)
    back_to_sides(2)
    back_to_sides(0)
    for d in (1, 3, 2, 0):
        back_to_x(d)
    for d in range(1, NX):
        x_e = lax.rem(x + NX - d, NX)
        for i in range(2):
            owner = other if i == 0 else y_lo
            arrived(out.at[owner, x_e], es.at[d - 1, i], er.at[d - 1, i], x_peers[d - 1])
    for copy in pending:
        copy.wait_send()


def run_experts(slots, source, up, down):
    width = source.shape[1]
    piece = (slots.shape[2], width)
    quarters = down.shape[1] // width
    units = -(-down.shape[0] // 128) * 128
    vmem = pl.BlockSpec(memory_space=pltpu.VMEM)
    any_space = pl.BlockSpec(memory_space=pl.ANY)
    bf16, sem = jnp.bfloat16, pltpu.SemaphoreType.DMA
    return pl.pallas_call(
        expert_kernel,
        out_shape=jax.ShapeDtypeStruct((NY, NX) + piece, bf16),
        in_specs=[vmem, vmem, any_space, any_space],
        out_specs=vmem,
        scratch_shapes=[
            pltpu.VMEM((quarters, NY, NX) + piece, bf16),
            pltpu.VMEM((NY, NX) + piece, bf16),
            pltpu.VMEM((NX,) + piece, bf16),
            pltpu.VMEM(up.shape, bf16),
            pltpu.VMEM(down.shape, bf16),
            pltpu.VMEM((quarters, 2 * units, width), bf16),
            pltpu.VMEM((quarters, units, width), bf16),
            pltpu.VMEM((NX, 4) + piece, bf16),
            pltpu.VMEM((NX, 4) + piece, bf16),
            pltpu.VMEM((NX, 4) + piece, bf16),
            pltpu.VMEM((NX, 3) + piece, bf16),
            pltpu.VMEM((NX - 1, 2) + piece, bf16),
            sem((2,)),
            sem((NX - 1, 2)),
            sem((NX - 1, 2)),
            sem((NX, 3)),
            sem((NX, 3)),
            sem((NX, 4)),
            sem((NX, 4)),
            sem((NX, 4)),
            sem((NX, 4)),
            sem((NX, 3)),
            sem((NX, 3)),
            sem((NX - 1, 2)),
            sem((NX - 1, 2)),
        ],
        compiler_params=pltpu.CompilerParams(
            collective_id=3, has_side_effects=True, vmem_limit_bytes=58 * 1024 * 1024
        ),
        name="run_experts",
    )(slots, source, up, down)


def home_kernel(slots, weights, rows_in, hidden, out, sums, staged, landed, zs, zr):
    rank, tensor = lax.axis_index("expert"), lax.axis_index("tensor")
    y_lo, x, z = place_of(rank)
    ring = [
        (rank_of(y_lo, x, lax.rem(z + 1, NZ)), tensor),
        (rank_of(y_lo, x, lax.rem(z + NZ - 1, NZ)), tensor),
    ]
    greet(ring)
    count = hidden.shape[0]
    rows = count // 2
    half = NZ // 2
    pending = []
    row = lax.broadcasted_iota(jnp.int32, (count, slots.shape[1]), 0)

    def add_up(home):
        share = jnp.where(row + home * count == slots[...], weights[...], 0.0)
        sums[home] = jnp.dot(
            share.astype(jnp.bfloat16), rows_in[...], preferred_element_type=jnp.float32
        ).astype(jnp.bfloat16)

    def reach(direction, piece):
        return half if direction == piece else half - 1

    def got(direction, steps, piece):
        index = 2 * steps + piece
        arrived(
            landed.at[direction, index], zs.at[direction, index], zr.at[direction, index],
            ring[direction],
        )
        return f32(landed[direction, index])

    for steps in range(half, 0, -1):
        add_up(lax.rem(z + steps, NZ))
        if steps < half:
            add_up(lax.rem(z + NZ - steps, NZ))
        for piece in range(2):
            for direction in range(2):
                if steps > reach(direction, piece):
                    continue
                home = lax.rem(z + (steps if direction == 0 else NZ - steps), NZ)
                mine = f32(sums[home, pl.ds(piece * rows, rows)])
                if steps < reach(direction, piece):
                    mine = mine + got(direction, steps, piece)
                index = 2 * (steps - 1) + piece
                staged[direction, index] = mine.astype(jnp.bfloat16)
                pending.append(
                    send(
                        staged.at[direction, index], landed.at[direction, index],
                        zs.at[direction, index], zr.at[direction, index], ring[direction],
                    )
                )
    add_up(z)
    for piece in range(2):
        span = pl.ds(piece * rows, rows)
        total = f32(sums[z, span])
        for direction in range(2):
            total = total + got(direction, 0, piece)
        out[span] = (f32(hidden[span]) + total).astype(jnp.bfloat16)
    for copy in pending:
        copy.wait_send()


def bring_home(slots, weights, rows_in, hidden):
    rows, width = hidden.shape
    vmem = pl.BlockSpec(memory_space=pltpu.VMEM)
    return pl.pallas_call(
        home_kernel,
        out_shape=jax.ShapeDtypeStruct(hidden.shape, hidden.dtype),
        in_specs=[vmem] * 4,
        out_specs=vmem,
        scratch_shapes=[
            pltpu.VMEM((NZ, rows, width), jnp.bfloat16),
            pltpu.VMEM((2, NZ, rows // 2, width), jnp.bfloat16),
            pltpu.VMEM((2, NZ, rows // 2, width), jnp.bfloat16),
            pltpu.SemaphoreType.DMA((2, NZ)),
            pltpu.SemaphoreType.DMA((2, NZ)),
        ],
        compiler_params=pltpu.CompilerParams(
            collective_id=5, has_side_effects=True, vmem_limit_bytes=32 * 1024 * 1024
        ),
        name="bring_home",
    )(slots, weights, rows_in, hidden)


def route_kernel(capacity, routed, weights, slab):
    experts, _ = slab.shape
    top_count, count = routed.shape
    row = lax.broadcasted_iota(jnp.int32, (experts, count), 0)
    lane = lax.broadcasted_iota(jnp.int32, (experts, count), 1)
    expert = lax.rem(row, experts // NZ) * NZ + row // (experts // NZ)
    before = jnp.where(
        lax.broadcasted_iota(jnp.int32, (count, count), 0)
        < lax.broadcasted_iota(jnp.int32, (count, count), 1),
        1.0,
        0.0,
    ).astype(jnp.bfloat16)
    token = f32(lane + 1)
    earlier = jnp.zeros((experts, 1), jnp.float32)
    arrivals, shares = [], []
    for k in range(top_count):
        hit = jnp.where(expert == routed[k : k + 1, :], 1.0, 0.0)
        ahead = jnp.dot(hit.astype(jnp.bfloat16), before, preferred_element_type=jnp.float32)
        arrivals.append(jnp.where(hit > 0.0, ahead + earlier, -1.0))
        shares.append(weights[k : k + 1, :])
        earlier = earlier + jnp.sum(hit, axis=1, keepdims=True)
    tokens, scales = jnp.full((experts, 128), -1.0, jnp.float32), jnp.zeros(
        (experts, 128), jnp.float32
    )
    slot = lax.broadcasted_iota(jnp.int32, (experts, 128), 1)
    for place in range(capacity):
        named = jnp.zeros((experts, count), jnp.float32)
        scale = jnp.zeros((experts, count), jnp.float32)
        for k in range(top_count):
            here = arrivals[k] == float(place)
            named = jnp.where(here, token, named)
            scale = jnp.where(here, shares[k], scale)
        tokens = jnp.where(slot == place, jnp.sum(named, axis=1, keepdims=True) - 1.0, tokens)
        scales = jnp.where(slot == place, jnp.sum(scale, axis=1, keepdims=True), scales)
    slab[:, :128] = tokens
    slab[:, 128:] = scales


def routing_slab(routed, weights, expert_count, capacity):
    vmem = pl.BlockSpec(memory_space=pltpu.VMEM)
    slab = pl.pallas_call(
        functools.partial(route_kernel, capacity),
        out_shape=jax.ShapeDtypeStruct((expert_count, 256), jnp.float32),
        in_specs=[vmem, vmem],
        out_specs=vmem,
        name="route",
    )(routed, weights)
    return slab.reshape(NZ, expert_count // NZ, 256)


def on_device(
    tokens,
    attn_gain,
    w_query,
    key_value_weight,
    w_out,
    cache_keyval,
    prefix_length,
    routed_experts,
    route_weights,
    expert_gain,
    w_gate_up,
    w_down,
):
    span_dev, seq_count, quarter = tokens.shape
    model_width = attn_gain.shape[0]
    row_count = span_dev * seq_count
    head_dim = key_value_weight.shape[2] // 2
    cache_rows = cache_keyval.shape[0]
    tensor_rank = lax.axis_index("tensor")
    expert_rank = lax.axis_index("expert")
    quarters = model_width // quarter
    top_count = routed_experts.shape[2]
    expert_count = lax.axis_size("expert")
    capacity = min(row_count, max(2, 5 * row_count * top_count // (2 * expert_count)))
    half_dim = head_dim // 2
    steps_up = jnp.arange(half_dim, dtype=jnp.float32)
    frequency = jnp.exp(steps_up * (-math.log(ROPE_BASE) / half_dim))
    span_place = expert_rank * span_dev + jnp.arange(span_dev, dtype=jnp.int32)
    places = (prefix_length[:, None] + span_place[None, :]).reshape(row_count).astype(jnp.float32)
    angles = frequency[:, None] * places[None, :]
    slab = routing_slab(
        routed_experts.transpose(2, 1, 0).reshape(top_count, row_count),
        route_weights.transpose(2, 1, 0).reshape(top_count, row_count),
        expert_count,
        capacity,
    )
    own_tokens = tokens.transpose(1, 0, 2).reshape(row_count, quarter)
    gain = lax.dynamic_slice_in_dim(expert_gain, tensor_rank * quarter, quarter, 0)
    fresh, hidden, spread, slab_all = attention(
        head_dim ** (-0.5) * LOG2E,
        own_tokens,
        attn_gain.reshape(quarters, 1, quarter),
        jnp.cos(angles),
        jnp.sin(angles),
        cache_keyval[:, :, 0, :].transpose(1, 0, 2),
        jnp.broadcast_to(prefix_length[:, None, None], (seq_count, 1, 2 * head_dim)),
        gain.reshape(1, quarter),
        slab,
        w_query,
        key_value_weight[:, 0, :],
        w_out.T,
    )
    new_key_value_rows = fresh.transpose(1, 0, 2)[:, :, None, :]
    token = slab_all[:, :, :capacity].astype(jnp.int32)
    first = jnp.arange(NZ, dtype=jnp.int32)[:, None, None] * row_count
    slot_token = jnp.where(token >= 0, token + first, -1).transpose(1, 0, 2)
    slot_weight = slab_all[:, :, 128 : 128 + capacity].transpose(1, 0, 2)
    groups, size = NY * NX, NZ * capacity
    returned = run_experts(
        slot_token.reshape(NY, NX, size, 1),
        spread.reshape(NZ * row_count, quarter),
        w_gate_up[0].transpose(1, 2, 0),
        w_down[0],
    )
    layer_output = bring_home(
        slot_token.reshape(1, groups * size),
        slot_weight.reshape(1, groups * size),
        returned.reshape(groups * size, quarter),
        hidden,
    )
    layer_output = layer_output.reshape(seq_count, span_dev, quarter).transpose(1, 0, 2)
    return (layer_output, new_key_value_rows)


def solution(mesh):
    return jax.shard_map(
        on_device,
        mesh=mesh,
        in_specs=(
            P("expert", None, "tensor"),
            P(),
            P(None, "tensor"),
            P(None, "tensor", None),
            P("tensor", None),
            P("expert", None, "tensor", None),
            P(),
            P("expert", None, None),
            P("expert", None, None),
            P(),
            P("expert", None, None, "tensor"),
            P("expert", "tensor", None),
        ),
        out_specs=(P("expert", None, "tensor"), P("expert", None, "tensor", None)),
        check_vma=False,
    )
```

```python
import functools
import math

import jax
import jax.numpy as jnp
from jax import lax
from jax.experimental import pallas as pl
from jax.experimental.pallas import tpu as pltpu
from jax.sharding import PartitionSpec as P

EPSILON = 1e-05
ROPE_BASE = 150000.0
NEG = -1e30
MESH = pl.DeviceIdType.MESH
NY, NX, NZ = 2, 4, 8
LOG2E = 1.4426950408889634


def place_of(expert_rank):
    return expert_rank // (NX * NZ), (expert_rank // NZ) % NX, expert_rank % NZ


def rank_of(y_lo, x, z):
    return (y_lo * NX + x) * NZ + z


def greet(devices):
    barrier = pltpu.get_barrier_semaphore()
    for device in devices:
        pl.semaphore_signal(barrier, inc=1, device_id=device, device_id_type=MESH)
    pl.semaphore_wait(barrier, len(devices))


def send(src, dst, send_sem, recv_sem, device):
    copy = pltpu.make_async_remote_copy(
        src_ref=src,
        dst_ref=dst,
        send_sem=send_sem,
        recv_sem=recv_sem,
        device_id=device,
        device_id_type=MESH,
    )
    copy.start()
    return copy


def arrived(dst, send_sem, recv_sem, device):
    pltpu.make_async_remote_copy(
        src_ref=dst,
        dst_ref=dst,
        send_sem=send_sem,
        recv_sem=recv_sem,
        device_id=device,
        device_id_type=MESH,
    ).wait_recv()


def swap_blocks(value):
    half = value.shape[0] // 2
    top, bottom = value[:half], value[half:]
    left = lax.broadcasted_iota(jnp.int32, top.shape, 1) < half
    return jnp.concatenate(
        [
            jnp.where(left, top, pltpu.roll(bottom, half, 1)),
            jnp.where(left, pltpu.roll(top, half, 1), bottom),
        ],
        axis=0,
    )


def turn(first, second, cosine, sine):
    return first * cosine - second * sine, second * cosine + first * sine


def corner(rank, tensor):
    y_lo, x, z = place_of(rank)
    y_hi, core = tensor // 2, lax.rem(tensor, 2)
    far = (rank, (1 - y_hi) * 2 + core)
    sides = [(rank_of(1 - y_lo, x, z), lax.rem(y_hi + r, 2) * 2 + core) for r in range(2)]
    mate = (rank, y_hi * 2 + 1 - core)
    return y_lo, x, z, y_hi, core, far, sides, mate


def f32(value):
    return value.astype(jnp.float32)


def attention_kernel(
    scale, own_tokens, gain, cosine, sine, cache, prefix, out_gain, slab, w_query_hbm, w_keyval_hbm, w_out_hbm,
    fresh, hidden, spread, roots, slab_all,
    w_query, w_keyval, w_out, gathered, kv_old, kv_new, q_all, qa, tops, sums, o_out, stat_out,
    o_in, stat_in, to_core, core_in, keep, far_out, far_in, squares, squares_in,
    ws, gs, gr, xs, xr, ys, yr, zs, zr, ts, tr, own_sem, os, orr, ss, sr, cs, cr, fs, fr, qs, qr, hs, hr, rs, rr,
):
    rank, tensor = lax.axis_index("expert"), lax.axis_index("tensor")
    y_lo, x, z, y_hi, core, far, sides, mate = corner(rank, tensor)
    other = 1 - y_lo
    rows, quarter = own_tokens.shape
    seqs, span, width = fresh.shape
    cache_rows, head = cache.shape[1], width // 2
    cols = q_all.shape[3]
    bf16 = jnp.bfloat16
    x_peers = [(rank_of(y_lo, lax.rem(x + d, NX), z), tensor) for d in range(1, NX)]
    y_peer = (rank_of(other, x, z), tensor)
    z_peers = [(rank_of(y_lo, x, lax.rem(z + d, NZ)), tensor) for d in range(1, NZ)]
    ring = [z_peers[0], z_peers[-1]]
    cross = (rank, (1 - y_hi) * 2 + 1 - core)
    greet(x_peers + [y_peer] + z_peers + [far, mate, cross])
    pending = []
    loads = [
        pltpu.make_async_copy(src, dst, ws.at[i])
        for i, (src, dst) in enumerate(
            [(w_query_hbm, w_query), (w_keyval_hbm, w_keyval), (w_out_hbm, w_out)]
        )
    ]
    for load in loads:
        load.start()
    half = NZ // 2
    stores = (kv_old, kv_new)

    def slot(part, direction, steps, piece):
        origin = lax.rem(z + (NZ - steps if direction == 0 else steps), NZ)
        return stores[part].at[origin * 2 + (y_lo if piece == 0 else other)]

    def sems(part, direction, step, piece):
        index = 2 * (step - 1) + piece
        return zs.at[part, direction, index], zr.at[part, direction, index]

    def pass_on(part, direction, step, piece):
        block = slot(part, direction, step - 1, piece)
        pending.append(send(block, block, *sems(part, direction, step, piece), ring[direction]))

    def got(part, direction, step, piece):
        arrived(
            slot(part, direction, step, piece), *sems(part, direction, step, piece), ring[direction]
        )

    def begin(part):
        block = slot(part, 0, 0, 0)
        pending.append(send(block, block, ys.at[part], yr.at[part], y_peer))
        for direction in range(2):
            pass_on(part, direction, 1, 0)

    def begin_other(part):
        arrived(slot(part, 0, 0, 1), ys.at[part], yr.at[part], y_peer)
        for direction in range(2):
            pass_on(part, direction, 1, 1)

    def step_on(part, step):
        for piece in range(2):
            for direction in range(2):
                got(part, direction, step - 1, piece)
                if step < half or direction == piece:
                    pass_on(part, direction, step, piece)

    mine = gathered.at[tensor]
    pending.append(send(own_tokens, mine, gs.at[0], gr.at[0], far))
    pending.append(send(own_tokens, mine, gs.at[1], gr.at[1], mate))
    kv_old[z * 2 + y_lo] = cache[...]
    begin(0)
    own_slab = pltpu.make_async_copy(slab.at[z], slab_all.at[z], own_sem.at[0])
    own_slab.start()
    for d in range(1, NZ):
        to = lax.rem(z + d, NZ)
        pending.append(
            send(slab.at[to], slab_all.at[z], ts.at[d - 1], tr.at[d - 1], z_peers[d - 1])
        )
    far_index, mate_index = (1 - y_hi) * 2 + core, y_hi * 2 + 1 - core
    cross_index = (1 - y_hi) * 2 + 1 - core

    def rows_of(index):
        return pl.ds(pl.multiple_of(index * quarter, 16), quarter)

    def project(index, block):
        wide = f32(block)
        scaled = (wide * gain[index]).astype(bf16)
        return (
            jnp.dot(scaled, w_query[rows_of(index), :], preferred_element_type=jnp.float32),
            jnp.dot(scaled, w_keyval[rows_of(index), :], preferred_element_type=jnp.float32),
            jnp.sum(wide * wide, axis=1, keepdims=True),
        )

    loads[0].wait()
    loads[1].wait()
    total = project(tensor, own_tokens[...])
    begin_other(0)
    arrived(gathered.at[far_index], gs.at[0], gr.at[0], far)
    block = gathered.at[far_index]
    pending.append(send(block, block, gs.at[2], gr.at[2], mate))
    total = [a + b for a, b in zip(total, project(far_index, gathered[far_index]))]
    arrived(gathered.at[mate_index], gs.at[1], gr.at[1], mate)
    total = [a + b for a, b in zip(total, project(mate_index, gathered[mate_index]))]
    step_on(0, 2)
    arrived(gathered.at[cross_index], gs.at[2], gr.at[2], mate)
    total = [a + b for a, b in zip(total, project(cross_index, gathered[cross_index]))]
    root = lax.rsqrt(total[2] / (4 * quarter) + EPSILON)
    cos, sin = cosine[...], sine[...]
    flipped = (total[1] * root).T
    keys = turn(flipped[: head // 2], flipped[head // 2 : head], cos, sin)
    whole = jnp.concatenate([keys[0], keys[1], flipped[head:]], axis=0).T
    own_rows = whole.astype(bf16).reshape(fresh.shape)
    fresh[...] = own_rows
    kv_new[z * 2 + y_lo] = own_rows
    begin(1)
    raw = total[0] * root
    for j in range(raw.shape[1] // width):
        pair = raw[:, j * width : (j + 1) * width].T
        turned = []
        for h in range(2):
            block = pair[h * head : (h + 1) * head]
            turned += turn(block[: head // 2], block[head // 2 :], cos, sin)
        first = swap_blocks(jnp.concatenate(turned, axis=0) * scale).astype(bf16)
        for s in range(seqs):
            q_all[0, s, :, j * width : (j + 1) * width] = first[s * head : (s + 1) * head]
    for d in (1, 3, 2):
        pending.append(
            send(q_all.at[0], q_all.at[NX - d], xs.at[d - 1], xr.at[d - 1], x_peers[d - 1])
        )
    begin_other(1)
    step_on(0, 3)

    row = lax.broadcasted_iota(jnp.int32, (width, cols), 0)
    lane = lax.broadcasted_iota(jnp.int32, (width, cols), 1)
    for k in range(NX):
        hot = (row == span + lax.rem(x + k, NX)) | (row == span + NX)
        if k == 0:
            hot = hot | (row == lax.rem(lane, span))
        for s in range(seqs):
            qa[s, k, head:width, :] = jnp.zeros((width - head, cols), bf16)
            qa[s, k, width:, :] = jnp.where(hot, 1.0, 0.0).astype(bf16)

    def old_chunk(s, offsets):
        values, masks = [], []
        old_row = lax.broadcasted_iota(jnp.int32, (cache_rows, width), 0)
        marked = lax.broadcasted_iota(jnp.int32, (cache_rows, width), 1) == span + NX
        for offset in offsets:
            origin = lax.rem(z + offset, NZ)
            for side in range(NY):
                values.append(kv_old[origin * 2 + side, s])
                place = old_row + rank_of(side, x, origin) * cache_rows
                masks.append(
                    jnp.where(marked & (place >= prefix[s]), NEG, 0.0).astype(bf16)
                )
        return jnp.concatenate(values, axis=0), jnp.concatenate(masks, axis=0)

    def new_chunk(s):
        masks = []
        new_row = lax.broadcasted_iota(jnp.int32, (span, width), 0)
        new_col = lax.broadcasted_iota(jnp.int32, (span, width), 1)
        in_block = (new_col >= span) & (new_col < span + NX)
        query_rank = rank_of(y_lo, new_col - span, z)
        later = (new_col < span) & (new_row > new_col)
        for shard in range(NY * NZ):
            key_rank = rank_of(shard % 2, x, shard // 2)
            late = in_block & (key_rank > query_rank)
            same = later & (jnp.full(later.shape, key_rank, jnp.int32) == rank)
            masks.append(jnp.where(late | same, NEG, 0.0).astype(bf16))
        return kv_new[:, s].reshape(NY * NZ * span, width), jnp.concatenate(masks, axis=0)

    def operands(keyval, mask):
        flipped = f32(keyval).T[head:].astype(bf16)
        ones = jnp.ones((16, keyval.shape[0]), bf16)
        return (
            jnp.concatenate([keyval, mask], axis=1),
            jnp.concatenate([ones, flipped], axis=0),
        )

    def attend(chunks, gates, ends):
        turns = [(s, c, k) for s in range(seqs) for c in range(len(chunks)) for k in range(NX)]
        held = {}

        def score(turn):
            s, c, k = turn
            if k == 0:
                gates[s][c]()
                held[s, c] = operands(*chunks[c](s))
            return jnp.dot(held[s, c][0], qa[s, k], preferred_element_type=jnp.float32)

        ahead = score(turns[0])
        for at, (s, c, k) in enumerate(turns):
            scores = ahead
            if at + 1 < len(turns):
                ahead = score(turns[at + 1])
            top = jnp.max(scores, axis=0, keepdims=True)
            if c:
                top = jnp.maximum(top, tops[k])
            probs = jnp.exp2(scores - top).astype(bf16)
            part = jnp.dot(held[s, c][1], probs, preferred_element_type=jnp.float32)
            if c:
                part = part + sums[k] * jnp.exp2(tops[k] - top)
            sums[k] = part
            tops[k] = top
            if c == len(chunks) - 1:
                ends(s, k)

    def finish(s, k):
        value = sums[k]
        o_out[s, k] = (value[16:] / value[0:1]).astype(bf16)
        stat_out[s, k, 0:1, :] = tops[k]
        stat_out[s, k, 1:2, :] = value[0:1]
        stat_out[s, k, 2:, :] = jnp.zeros((6, cols), jnp.float32)
        if k:
            to, i = x_peers[k - 1], NX - k - 1
            pending.append(send(stat_out.at[s, k], stat_in.at[s, i], ss.at[s, i], sr.at[s, i], to))
            pending.append(send(o_out.at[s, k], o_in.at[s, i], os.at[s, i], orr.at[s, i], to))

    order = [1 - y_hi, y_hi]

    def combine(s):
        stats, values = [stat_out[s, 0]], [o_out[s, 0]]
        for i in (0, 2, 1):
            arrived(stat_in.at[s, i], ss.at[s, i], sr.at[s, i], x_peers[i])
            arrived(o_in.at[s, i], os.at[s, i], orr.at[s, i], x_peers[i])
            stats.append(stat_in[s, i])
            values.append(o_in[s, i])
        top = functools.reduce(jnp.maximum, [value[0:1] for value in stats])
        shares = [jnp.exp2(value[0:1] - top) * value[1:2] for value in stats]
        every = functools.reduce(jnp.add, shares)
        merged = functools.reduce(
            jnp.add, [f32(value) * (share / every) for value, share in zip(values, shares)]
        )
        blank = jnp.zeros((head, width), jnp.float32)
        attended = jnp.concatenate(
            [
                swap_blocks(
                    jnp.concatenate([merged[:, j * width : (j + 1) * width], blank], axis=0).T
                )[:span]
                for j in range(cols // width)
            ],
            axis=1,
        ).astype(bf16)

        def projected(index):
            return lax.dot_general(
                attended, w_out[rows_of(index), :], (((1,), (1,)), ((), ())),
                preferred_element_type=jnp.float32,
            )

        for i in range(2):
            to_core[s, i] = projected(order[i] * 2 + 1 - core).astype(bf16)
            pending.append(
                send(to_core.at[s, i], core_in.at[s, i], cs.at[s, i], cr.at[s, i], mate)
            )
        keep[s, 0] = projected(order[0] * 2 + core)
        keep[s, 1] = projected(order[1] * 2 + core)

    def across_core(s):
        arrived(core_in.at[s, 0], cs.at[s, 0], cr.at[s, 0], mate)
        far_out[s] = (keep[s, 0] + f32(core_in[s, 0])).astype(bf16)
        pending.append(send(far_out.at[s], far_in.at[s], fs.at[s], fr.at[s], far))

    trio = [mate, far, cross]

    def residual(s):
        mine = pl.ds(s * span, span)
        arrived(core_in.at[s, 1], cs.at[s, 1], cr.at[s, 1], mate)
        near = f32(own_tokens[mine]) + (keep[s, 1] + f32(core_in[s, 1]))
        arrived(far_in.at[s], fs.at[s], fr.at[s], far)
        rounded = (near + f32(far_in[s])).astype(bf16)
        hidden[mine] = rounded
        wide = f32(rounded)
        own = jnp.broadcast_to(jnp.sum(wide * wide, axis=1, keepdims=True), (span, width))
        squares[s] = own.T[:8]
        for i in range(3):
            pending.append(
                send(squares.at[s], squares_in.at[s, i], qs.at[s, i], qr.at[s, i], trio[i])
            )
        spread[z, mine] = (wide * out_gain[tensor]).astype(bf16)
        ring_on(s, 1)

    def spot(direction, steps, s):
        origin = lax.rem(z + (NZ - steps if direction == 0 else steps), NZ)
        return spread.at[origin, pl.ds(s * span, span)]

    def ring_on(s, step):
        for direction in range(2):
            if 1 < step <= half or (step > half and direction == s):
                arrived(
                    spot(direction, step - 1, s), hs.at[direction, step - 1, s],
                    hr.at[direction, step - 1, s], ring[direction],
                )
            if step < half or (step == half and direction == s):
                block = spot(direction, step - 1, s)
                pending.append(
                    send(
                        block, block, hs.at[direction, step, s], hr.at[direction, step, s],
                        ring[direction],
                    )
                )

    def share_root(s):
        total = squares[s]
        for i in range(3):
            arrived(squares_in.at[s, i], qs.at[s, i], qr.at[s, i], trio[i])
            total = total + squares_in[s, i]
        roots[z, s] = lax.rsqrt(total / (4 * quarter) + EPSILON)
        block = roots.at[z, s]
        for d in range(1, NZ):
            pending.append(send(block, block, rs.at[s, d - 1], rr.at[s, d - 1], z_peers[d - 1]))

    near_first = [(0, NZ - 1), (1, NZ - 2), (2, NZ - 3), (3, 4)]
    for d in (1, 3, 2):
        arrived(q_all.at[NX - d], xs.at[d - 1], xr.at[d - 1], x_peers[d - 1])
    for s in range(seqs):
        for k in range(NX):
            qa[s, k, :head, :] = q_all[k, s]

    def last(part):
        for direction in range(2):
            got(part, direction, half, direction)

    def second():
        step_on(0, 4)
        step_on(1, 2)

    def fourth():
        last(0)
        step_on(1, 4)

    nothing = lambda: None
    chunks = [functools.partial(old_chunk, offsets=pair) for pair in near_first] + [new_chunk]
    gates = [
        [nothing, second, lambda: step_on(1, 3), fourth, lambda: last(1)],
        [
            nothing,
            loads[2].wait,
            lambda: combine(0),
            lambda: across_core(0),
            lambda: residual(0),
        ],
    ]
    attend(chunks, gates, finish)
    ring_on(0, 2)
    combine(1)
    ring_on(0, 3)
    across_core(1)
    ring_on(0, 4)
    share_root(0)
    residual(1)
    ring_on(0, 5)
    for step in range(2, half + 2):
        ring_on(1, step)
        if step == 3:
            share_root(1)
    for s in range(seqs):
        for d in range(1, NZ):
            arrived(
                roots.at[lax.rem(z + NZ - d, NZ), s], rs.at[s, d - 1], rr.at[s, d - 1], z_peers[d - 1]
            )
    for d in range(1, NZ):
        arrived(
            slab_all.at[lax.rem(z + NZ - d, NZ)], ts.at[d - 1], tr.at[d - 1], z_peers[d - 1]
        )
    own_slab.wait()
    for copy in pending:
        copy.wait_send()


def attention(
    scale, own_tokens, gain, cosine, sine, cache, prefix, out_gain, slab, w_query, w_keyval, w_out
):
    seqs, cache_rows, width = cache.shape
    rows, quarter = own_tokens.shape
    span, head = rows // seqs, width // 2
    cols = w_query.shape[1] // head * span
    vmem = pl.BlockSpec(memory_space=pltpu.VMEM)
    any_space = pl.BlockSpec(memory_space=pl.ANY)
    bf16, wide, sem = jnp.bfloat16, jnp.float32, pltpu.SemaphoreType.DMA
    return pl.pallas_call(
        functools.partial(attention_kernel, scale),
        out_shape=(
            jax.ShapeDtypeStruct((seqs, span, width), bf16),
            jax.ShapeDtypeStruct((rows, quarter), bf16),
            jax.ShapeDtypeStruct((NZ, rows, quarter), bf16),
            jax.ShapeDtypeStruct((NZ, seqs, 8, span), wide),
            jax.ShapeDtypeStruct(slab.shape, slab.dtype),
        ),
        in_specs=[vmem] * 5
        + [pl.BlockSpec(memory_space=pltpu.SMEM), vmem]
        + [any_space] * 4,
        out_specs=(vmem, vmem, vmem, vmem, any_space),
        scratch_shapes=[
            pltpu.VMEM(w_query.shape, bf16),
            pltpu.VMEM(w_keyval.shape, bf16),
            pltpu.VMEM(w_out.shape, bf16),
            pltpu.VMEM((4, rows, quarter), bf16),
            pltpu.VMEM((NY * NZ, seqs, cache_rows, width), bf16),
            pltpu.VMEM((NY * NZ, seqs, span, width), bf16),
            pltpu.VMEM((NX, seqs, head, cols), bf16),
            pltpu.VMEM((seqs, NX, 2 * width, cols), bf16),
            pltpu.VMEM((NX, 1, cols), wide),
            pltpu.VMEM((NX, 16 + head, cols), wide),
            pltpu.VMEM((seqs, NX, head, cols), bf16),
            pltpu.VMEM((seqs, NX, 8, cols), wide),
            pltpu.VMEM((seqs, NX - 1, head, cols), bf16),
            pltpu.VMEM((seqs, NX - 1, 8, cols), wide),
            pltpu.VMEM((seqs, 2, span, quarter), bf16),
            pltpu.VMEM((seqs, 2, span, quarter), bf16),
            pltpu.VMEM((seqs, 2, span, quarter), wide),
            pltpu.VMEM((seqs, span, quarter), bf16),
            pltpu.VMEM((seqs, span, quarter), bf16),
            pltpu.VMEM((seqs, 8, span), wide),
            pltpu.VMEM((seqs, 3, 8, span), wide),
            sem((3,)),
            sem((3,)),
            sem((3,)),
            sem((NX - 1,)),
            sem((NX - 1,)),
            sem((2,)),
            sem((2,)),
            sem((2, 2, NZ)),
            sem((2, 2, NZ)),
            sem((NZ - 1,)),
            sem((NZ - 1,)),
            sem((1,)),
            sem((seqs, NX - 1)),
            sem((seqs, NX - 1)),
            sem((seqs, NX - 1)),
            sem((seqs, NX - 1)),
            sem((seqs, 2)),
            sem((seqs, 2)),
            sem((seqs,)),
            sem((seqs,)),
            sem((seqs, 3)),
            sem((seqs, 3)),
            sem((2, NZ // 2 + 1, seqs)),
            sem((2, NZ // 2 + 1, seqs)),
            sem((seqs, NZ - 1)),
            sem((seqs, NZ - 1)),
        ],
        compiler_params=pltpu.CompilerParams(
            collective_id=0, has_side_effects=True, vmem_limit_bytes=60 * 1024 * 1024
        ),
        name="attention",
    )(own_tokens, gain, cosine, sine, cache, prefix, out_gain, slab, w_query, w_keyval, w_out)


def expert_kernel(
    slots, source, roots, up_hbm, down_hbm, out,
    rows, sel, held, up_raw, down_raw, up, down, mine, to_mate, core_in, side_in, x_out,
    ws, xs, xr, ys, yr, fs, fr, cs, cr, bs, br, es, er,
):
    rank, tensor = lax.axis_index("expert"), lax.axis_index("tensor")
    y_lo, x, z, y_hi, core, far, sides, mate = corner(rank, tensor)
    other = 1 - y_lo
    x_peers = [(rank_of(y_lo, lax.rem(x + d, NX), z), tensor) for d in range(1, NX)]
    greet(x_peers + [far] + sides + [mate])
    pending = []
    loads = [
        pltpu.make_async_copy(up_hbm, up_raw, ws.at[0]),
        pltpu.make_async_copy(down_hbm, down_raw, ws.at[1]),
    ]
    for load in loads:
        load.start()
    size, width = sel.shape[2:]
    quarters = rows.shape[0]
    lane = lax.broadcasted_iota(jnp.int32, (size, source.shape[0]), 1)

    def pick(side, to):
        named = lane == slots[side, to]
        chosen = jnp.where(named, 1.0, 0.0).astype(jnp.bfloat16)
        root = jnp.sum(jnp.where(named, roots[...], 0.0), axis=1, keepdims=True)
        picked = jnp.dot(chosen, source[...], preferred_element_type=jnp.float32)
        return (picked * root).astype(jnp.bfloat16)

    def to_side(d, here, there):
        spot = rows.at[tensor, y_lo, lax.rem(x + NX - d, NX)]
        for r in range(2):
            pending.append(send(there, spot, ys.at[d, r], yr.at[d, r], sides[r]))
        pending.append(send(here, spot, ys.at[d, 2], yr.at[d, 2], far))

    def forward(d, r, l):
        x_s = lax.rem(x + NX - d, NX)
        spot = rows.at[lax.rem(y_hi + r, 2) * 2 + core, lax.rem(y_lo + l, 2), x_s]
        index = 2 * r + l
        pending.append(send(spot, spot, fs.at[d, index], fr.at[d, index], mate))

    def from_sides(d):
        x_s = lax.rem(x + NX - d, NX)
        for r in range(2):
            spot = rows.at[lax.rem(y_hi + r, 2) * 2 + core, other, x_s]
            arrived(spot, ys.at[d, r], yr.at[d, r], sides[r])
            forward(d, r, 1)
        spot = rows.at[(1 - y_hi) * 2 + core, y_lo, x_s]
        arrived(spot, ys.at[d, 2], yr.at[d, 2], far)
        forward(d, 1, 0)

    def from_mate(d):
        x_s = lax.rem(x + NX - d, NX)
        for r in range(2):
            for l in range(2):
                spot = rows.at[lax.rem(y_hi + r, 2) * 2 + 1 - core, lax.rem(y_lo + l, 2), x_s]
                arrived(spot, fs.at[d, 2 * r + l], fr.at[d, 2 * r + l], mate)

    units, real = down.shape[1], down_raw.shape[0]

    def run(d):
        x_s = lax.rem(x + NX - d, NX)
        total = jnp.zeros((2 * size, 2 * units), jnp.float32)
        for q in range(quarters):
            block = jnp.concatenate([rows[q, other, x_s], rows[q, y_lo, x_s]], axis=0)
            total += lax.dot_general(
                block, up[q], (((1,), (1,)), ((), ())), preferred_element_type=jnp.float32
            )
        gate, raised = total[:, :units], total[:, units:]
        active = (gate * jax.nn.sigmoid(1.702 * gate) * (raised + 1.0)).astype(jnp.bfloat16)
        for h in range(2):
            half = lax.rem(y_hi + h, 2)
            for owner in range(2):
                index = half * 2 + (core if owner else 1 - core)
                value = jnp.dot(active, down[index], preferred_element_type=jnp.float32).astype(
                    jnp.bfloat16
                )
                into = mine if owner else to_mate
                into[d, h] = value[:size]
                into[d, 3 - h] = value[size:]
                if not owner:
                    for kind in (h, 3 - h):
                        pending.append(
                            send(
                                to_mate.at[d, kind], core_in.at[d, kind],
                                cs.at[d, kind], cr.at[d, kind], mate,
                            )
                        )

    def back_to_sides(d):
        for kind in range(4):
            arrived(core_in.at[d, kind], cs.at[d, kind], cr.at[d, kind], mate)
            both = f32(mine[d, kind]) + f32(core_in[d, kind])
            mine[d, kind] = both.astype(jnp.bfloat16)
            if kind < 3:
                to = far if kind == 2 else sides[kind]
                pending.append(
                    send(mine.at[d, kind], side_in.at[d, kind], bs.at[d, kind], br.at[d, kind], to)
                )

    def back_to_x(d):
        for kind in range(3):
            to = far if kind == 2 else sides[kind]
            arrived(side_in.at[d, kind], bs.at[d, kind], br.at[d, kind], to)
            if kind == 0:
                continue
            first = side_in[d, 0] if kind == 1 else mine[d, 3]
            both = (f32(first) + f32(side_in[d, kind])).astype(jnp.bfloat16)
            i = kind - 1
            owner = other if kind == 1 else y_lo
            if d == 0:
                out[owner, x] = both
            else:
                e = NX - d - 1
                x_out[d - 1, i] = both
                pending.append(
                    send(x_out.at[d - 1, i], out.at[owner, x], es.at[e, i], er.at[e, i], x_peers[e])
                )

    sel[other, x] = pick(other, x)
    rows[tensor, y_lo, x] = pick(y_lo, x)
    to_side(0, rows.at[tensor, y_lo, x], sel.at[other, x])
    for d in (1, 3, 2):
        to = lax.rem(x + d, NX)
        for i in range(2):
            side = other if i == 0 else y_lo
            sel[side, to] = pick(side, to)
            dst = held.at[x] if i == 0 else rows.at[tensor, y_lo, x]
            pending.append(
                send(sel.at[side, to], dst, xs.at[d - 1, i], xr.at[d - 1, i], x_peers[d - 1])
            )
    forward(0, 0, 0)
    blank = jnp.zeros((units - real, width), jnp.bfloat16)
    for load in loads:
        load.wait()
    for q in range(quarters):
        span = slice(q * width, (q + 1) * width)
        for i in range(2):
            up[q, i * units : i * units + real, :] = up_raw[i, :, span]
            up[q, i * units + real : (i + 1) * units, :] = blank
        down[q, :real, :] = down_raw[:, span]
        down[q, real:, :] = blank

    def from_x(d):
        x_s = lax.rem(x + NX - d, NX)
        arrived(held.at[x_s], xs.at[d - 1, 0], xr.at[d - 1, 0], x_peers[d - 1])
        arrived(rows.at[tensor, y_lo, x_s], xs.at[d - 1, 1], xr.at[d - 1, 1], x_peers[d - 1])
        to_side(d, rows.at[tensor, y_lo, x_s], held.at[x_s])
        forward(d, 0, 0)

    from_x(1)
    from_x(3)
    from_sides(0)
    from_x(2)
    for d in (0, 1, 3, 2):
        if d:
            from_sides(d)
        from_mate(d)
        run(d)
        if d in (1, 3):
            back_to_sides(d)
    back_to_sides(2)
    back_to_sides(0)
    for d in (1, 3, 2, 0):
        back_to_x(d)
    for d in range(1, NX):
        x_e = lax.rem(x + NX - d, NX)
        for i in range(2):
            owner = other if i == 0 else y_lo
            arrived(out.at[owner, x_e], es.at[d - 1, i], er.at[d - 1, i], x_peers[d - 1])
    for copy in pending:
        copy.wait_send()


def run_experts(slots, source, roots, up, down):
    width = source.shape[1]
    piece = (slots.shape[2], width)
    quarters = down.shape[1] // width
    units = -(-down.shape[0] // 128) * 128
    vmem = pl.BlockSpec(memory_space=pltpu.VMEM)
    any_space = pl.BlockSpec(memory_space=pl.ANY)
    bf16, sem = jnp.bfloat16, pltpu.SemaphoreType.DMA
    return pl.pallas_call(
        expert_kernel,
        out_shape=jax.ShapeDtypeStruct((NY, NX) + piece, bf16),
        in_specs=[vmem, vmem, vmem, any_space, any_space],
        out_specs=vmem,
        scratch_shapes=[
            pltpu.VMEM((quarters, NY, NX) + piece, bf16),
            pltpu.VMEM((NY, NX) + piece, bf16),
            pltpu.VMEM((NX,) + piece, bf16),
            pltpu.VMEM(up.shape, bf16),
            pltpu.VMEM(down.shape, bf16),
            pltpu.VMEM((quarters, 2 * units, width), bf16),
            pltpu.VMEM((quarters, units, width), bf16),
            pltpu.VMEM((NX, 4) + piece, bf16),
            pltpu.VMEM((NX, 4) + piece, bf16),
            pltpu.VMEM((NX, 4) + piece, bf16),
            pltpu.VMEM((NX, 3) + piece, bf16),
            pltpu.VMEM((NX - 1, 2) + piece, bf16),
            sem((2,)),
            sem((NX - 1, 2)),
            sem((NX - 1, 2)),
            sem((NX, 3)),
            sem((NX, 3)),
            sem((NX, 4)),
            sem((NX, 4)),
            sem((NX, 4)),
            sem((NX, 4)),
            sem((NX, 3)),
            sem((NX, 3)),
            sem((NX - 1, 2)),
            sem((NX - 1, 2)),
        ],
        compiler_params=pltpu.CompilerParams(
            collective_id=3, has_side_effects=True, vmem_limit_bytes=61 * 1024 * 1024
        ),
        name="run_experts",
    )(slots, source, roots, up, down)


def home_kernel(slots, weights, rows_in, hidden, out, sums, staged, landed, zs, zr):
    rank, tensor = lax.axis_index("expert"), lax.axis_index("tensor")
    y_lo, x, z = place_of(rank)
    ring = [
        (rank_of(y_lo, x, lax.rem(z + 1, NZ)), tensor),
        (rank_of(y_lo, x, lax.rem(z + NZ - 1, NZ)), tensor),
    ]
    greet(ring)
    count = hidden.shape[0]
    rows = count // 2
    half = NZ // 2
    pending = []
    row = lax.broadcasted_iota(jnp.int32, (count, slots.shape[1]), 0)

    def add_up(home):
        share = jnp.where(row + home * count == slots[...], weights[...], 0.0)
        sums[home] = jnp.dot(
            share.astype(jnp.bfloat16), rows_in[...], preferred_element_type=jnp.float32
        ).astype(jnp.bfloat16)

    def reach(direction, piece):
        return half if direction == piece else half - 1

    def got(direction, steps, piece):
        index = 2 * steps + piece
        arrived(
            landed.at[direction, index], zs.at[direction, index], zr.at[direction, index],
            ring[direction],
        )
        return f32(landed[direction, index])

    for steps in range(half, 0, -1):
        add_up(lax.rem(z + steps, NZ))
        if steps < half:
            add_up(lax.rem(z + NZ - steps, NZ))
        for piece in range(2):
            for direction in range(2):
                if steps > reach(direction, piece):
                    continue
                home = lax.rem(z + (steps if direction == 0 else NZ - steps), NZ)
                mine = f32(sums[home, pl.ds(piece * rows, rows)])
                if steps < reach(direction, piece):
                    mine = mine + got(direction, steps, piece)
                index = 2 * (steps - 1) + piece
                staged[direction, index] = mine.astype(jnp.bfloat16)
                pending.append(
                    send(
                        staged.at[direction, index], landed.at[direction, index],
                        zs.at[direction, index], zr.at[direction, index], ring[direction],
                    )
                )
    add_up(z)
    for piece in range(2):
        span = pl.ds(piece * rows, rows)
        total = f32(sums[z, span])
        for direction in range(2):
            total = total + got(direction, 0, piece)
        out[span] = (f32(hidden[span]) + total).astype(jnp.bfloat16)
    for copy in pending:
        copy.wait_send()


def bring_home(slots, weights, rows_in, hidden):
    rows, width = hidden.shape
    vmem = pl.BlockSpec(memory_space=pltpu.VMEM)
    return pl.pallas_call(
        home_kernel,
        out_shape=jax.ShapeDtypeStruct(hidden.shape, hidden.dtype),
        in_specs=[vmem] * 4,
        out_specs=vmem,
        scratch_shapes=[
            pltpu.VMEM((NZ, rows, width), jnp.bfloat16),
            pltpu.VMEM((2, NZ, rows // 2, width), jnp.bfloat16),
            pltpu.VMEM((2, NZ, rows // 2, width), jnp.bfloat16),
            pltpu.SemaphoreType.DMA((2, NZ)),
            pltpu.SemaphoreType.DMA((2, NZ)),
        ],
        compiler_params=pltpu.CompilerParams(
            collective_id=5, has_side_effects=True, vmem_limit_bytes=32 * 1024 * 1024
        ),
        name="bring_home",
    )(slots, weights, rows_in, hidden)


def route_kernel(capacity, routed, weights, slab):
    experts, _ = slab.shape
    seqs, top_count, count = routed.shape
    row = lax.broadcasted_iota(jnp.int32, (experts, count), 0)
    lane = lax.broadcasted_iota(jnp.int32, (experts, count), 1)
    expert = lax.rem(row, experts // NZ) * NZ + row // (experts // NZ)
    before = jnp.where(
        lax.broadcasted_iota(jnp.int32, (count, count), 0)
        < lax.broadcasted_iota(jnp.int32, (count, count), 1),
        1.0,
        0.0,
    ).astype(jnp.bfloat16)
    earlier = jnp.zeros((experts, 1), jnp.float32)
    named, shares = [], []
    for s in range(seqs):
        for k in range(top_count):
            hit = jnp.where(expert == routed[s, k : k + 1, :], 1.0, 0.0)
            ahead = jnp.dot(hit.astype(jnp.bfloat16), before, preferred_element_type=jnp.float32)
            named.append((jnp.where(hit > 0.0, ahead + earlier, -1.0), f32(lane + s * count + 1)))
            shares.append(weights[s, k : k + 1, :])
            earlier = earlier + jnp.sum(hit, axis=1, keepdims=True)
    tokens = jnp.full((experts, 128), -1.0, jnp.float32)
    scales = jnp.zeros((experts, 128), jnp.float32)
    slot = lax.broadcasted_iota(jnp.int32, (experts, 128), 1)
    for place in range(capacity):
        token = jnp.zeros((experts, count), jnp.float32)
        scale = jnp.zeros((experts, count), jnp.float32)
        for (arrival, number), share in zip(named, shares):
            here = arrival == float(place)
            token = jnp.where(here, number, token)
            scale = jnp.where(here, share, scale)
        tokens = jnp.where(slot == place, jnp.sum(token, axis=1, keepdims=True) - 1.0, tokens)
        scales = jnp.where(slot == place, jnp.sum(scale, axis=1, keepdims=True), scales)
    slab[:, :128] = tokens
    slab[:, 128:] = scales


def routing_slab(routed, weights, expert_count, capacity):
    vmem = pl.BlockSpec(memory_space=pltpu.VMEM)
    slab = pl.pallas_call(
        functools.partial(route_kernel, capacity),
        out_shape=jax.ShapeDtypeStruct((expert_count, 256), jnp.float32),
        in_specs=[vmem, vmem],
        out_specs=vmem,
        name="route",
    )(routed, weights)
    return slab.reshape(NZ, expert_count // NZ, 256)


def on_device(
    tokens,
    attn_gain,
    w_query,
    key_value_weight,
    w_out,
    cache_keyval,
    prefix_length,
    routed_experts,
    route_weights,
    expert_gain,
    w_gate_up,
    w_down,
):
    span_dev, seq_count, quarter = tokens.shape
    model_width = attn_gain.shape[0]
    row_count = span_dev * seq_count
    head_dim = key_value_weight.shape[2] // 2
    cache_rows = cache_keyval.shape[0]
    expert_rank = lax.axis_index("expert")
    quarters = model_width // quarter
    top_count = routed_experts.shape[2]
    expert_count = lax.axis_size("expert")
    capacity = min(row_count, max(2, 5 * row_count * top_count // (2 * expert_count)))
    half_dim = head_dim // 2
    steps_up = jnp.arange(half_dim, dtype=jnp.float32)
    frequency = jnp.exp(steps_up * (-math.log(ROPE_BASE) / half_dim))
    span_place = expert_rank * span_dev + jnp.arange(span_dev, dtype=jnp.int32)
    places = (prefix_length[:, None] + span_place[None, :]).reshape(row_count).astype(jnp.float32)
    angles = frequency[:, None] * places[None, :]
    slab = routing_slab(
        routed_experts.transpose(1, 2, 0),
        route_weights.transpose(1, 2, 0),
        expert_count,
        capacity,
    )
    own_tokens = tokens.transpose(1, 0, 2).reshape(row_count, quarter)
    fresh, hidden, spread, roots, slab_all = attention(
        head_dim ** (-0.5) * LOG2E,
        own_tokens,
        attn_gain.reshape(quarters, 1, quarter),
        jnp.cos(angles),
        jnp.sin(angles),
        cache_keyval[:, :, 0, :].transpose(1, 0, 2),
        prefix_length,
        expert_gain.reshape(quarters, 1, quarter),
        slab,
        w_query,
        key_value_weight[:, 0, :],
        w_out.T,
    )
    new_key_value_rows = fresh.transpose(1, 0, 2)[:, :, None, :]
    token = slab_all[:, :, :capacity].astype(jnp.int32)
    first = jnp.arange(NZ, dtype=jnp.int32)[:, None, None] * row_count
    slot_token = jnp.where(token >= 0, token + first, -1).transpose(1, 0, 2)
    slot_weight = slab_all[:, :, 128 : 128 + capacity].transpose(1, 0, 2)
    groups, size = NY * NX, NZ * capacity
    returned = run_experts(
        slot_token.reshape(NY, NX, size, 1),
        spread.reshape(NZ * row_count, quarter),
        roots[:, :, 0, :].reshape(1, NZ * row_count),
        w_gate_up[0].transpose(1, 2, 0),
        w_down[0],
    )
    layer_output = bring_home(
        slot_token.reshape(1, groups * size),
        slot_weight.reshape(1, groups * size),
        returned.reshape(groups * size, quarter),
        hidden,
    )
    layer_output = layer_output.reshape(seq_count, span_dev, quarter).transpose(1, 0, 2)
    return (layer_output, new_key_value_rows)


def solution(mesh):
    return jax.shard_map(
        on_device,
        mesh=mesh,
        in_specs=(
            P("expert", None, "tensor"),
            P(),
            P(None, "tensor"),
            P(None, "tensor", None),
            P("tensor", None),
            P("expert", None, "tensor", None),
            P(),
            P("expert", None, None),
            P("expert", None, None),
            P(),
            P("expert", None, None, "tensor"),
            P("expert", "tensor", None),
        ),
        out_specs=(P("expert", None, "tensor"), P("expert", None, "tensor", None)),
        check_vma=False,
    )
```

```python
import functools
import math

import jax
import jax.numpy as jnp
from jax import lax
from jax.experimental import pallas as pl
from jax.experimental.pallas import tpu as pltpu
from jax.sharding import PartitionSpec as P

EPSILON = 1e-05
ROPE_BASE = 150000.0
NEG = -1e30
MESH = pl.DeviceIdType.MESH
NY, NX, NZ = 2, 4, 8
LOG2E = 1.4426950408889634


def place_of(expert_rank):
    return expert_rank // (NX * NZ), (expert_rank // NZ) % NX, expert_rank % NZ


def rank_of(y_lo, x, z):
    return (y_lo * NX + x) * NZ + z


def greet(devices):
    barrier = pltpu.get_barrier_semaphore()
    for device in devices:
        pl.semaphore_signal(barrier, inc=1, device_id=device, device_id_type=MESH)
    pl.semaphore_wait(barrier, len(devices))


def send(src, dst, send_sem, recv_sem, device):
    copy = pltpu.make_async_remote_copy(
        src_ref=src,
        dst_ref=dst,
        send_sem=send_sem,
        recv_sem=recv_sem,
        device_id=device,
        device_id_type=MESH,
    )
    copy.start()
    return copy


def arrived(dst, send_sem, recv_sem, device):
    pltpu.make_async_remote_copy(
        src_ref=dst,
        dst_ref=dst,
        send_sem=send_sem,
        recv_sem=recv_sem,
        device_id=device,
        device_id_type=MESH,
    ).wait_recv()


def swap_blocks(value):
    half = value.shape[0] // 2
    top, bottom = value[:half], value[half:]
    left = lax.broadcasted_iota(jnp.int32, top.shape, 1) < half
    return jnp.concatenate(
        [
            jnp.where(left, top, pltpu.roll(bottom, half, 1)),
            jnp.where(left, pltpu.roll(top, half, 1), bottom),
        ],
        axis=0,
    )


def turn(first, second, cosine, sine):
    return first * cosine - second * sine, second * cosine + first * sine


def corner(rank, tensor):
    y_lo, x, z = place_of(rank)
    y_hi, core = tensor // 2, lax.rem(tensor, 2)
    far = (rank, (1 - y_hi) * 2 + core)
    sides = [(rank_of(1 - y_lo, x, z), lax.rem(y_hi + r, 2) * 2 + core) for r in range(2)]
    mate = (rank, y_hi * 2 + 1 - core)
    return y_lo, x, z, y_hi, core, far, sides, mate


def f32(value):
    return value.astype(jnp.float32)


def attention_kernel(
    scale, own_tokens, gain, cosine, sine, cache, prefix, out_gain, slab, w_query_hbm, w_keyval_hbm, w_out_hbm,
    fresh, hidden, spread, roots, slab_all,
    w_query, w_keyval, w_out, gathered, kv_old, kv_new, q_all, qa, tops, sums, o_out, stat_out,
    o_in, stat_in, to_core, core_in, keep, far_out, far_in, squares, squares_in,
    ws, gs, gr, xs, xr, ys, yr, zs, zr, ts, tr, own_sem, os, orr, ss, sr, cs, cr, fs, fr, qs, qr, hs, hr, rs, rr,
):
    rank, tensor = lax.axis_index("expert"), lax.axis_index("tensor")
    y_lo, x, z, y_hi, core, far, sides, mate = corner(rank, tensor)
    other = 1 - y_lo
    rows, quarter = own_tokens.shape
    seqs, span, width = fresh.shape
    cache_rows, head = cache.shape[1], width // 2
    cols = q_all.shape[3]
    bf16 = jnp.bfloat16
    x_peers = [(rank_of(y_lo, lax.rem(x + d, NX), z), tensor) for d in range(1, NX)]
    y_peer = (rank_of(other, x, z), tensor)
    z_peers = [(rank_of(y_lo, x, lax.rem(z + d, NZ)), tensor) for d in range(1, NZ)]
    ring = [z_peers[0], z_peers[-1]]
    cross = (rank, (1 - y_hi) * 2 + 1 - core)
    greet(x_peers + [y_peer] + z_peers + [far, mate, cross])
    pending = []
    loads = [
        pltpu.make_async_copy(src, dst, ws.at[i])
        for i, (src, dst) in enumerate(
            [(w_query_hbm, w_query), (w_keyval_hbm, w_keyval), (w_out_hbm, w_out)]
        )
    ]
    for load in loads:
        load.start()
    half = NZ // 2
    stores = (kv_old, kv_new)

    def slot(part, direction, steps, piece):
        origin = lax.rem(z + (NZ - steps if direction == 0 else steps), NZ)
        return stores[part].at[origin * 2 + (y_lo if piece == 0 else other)]

    def sems(part, direction, step, piece):
        index = 2 * (step - 1) + piece
        return zs.at[part, direction, index], zr.at[part, direction, index]

    def pass_on(part, direction, step, piece):
        block = slot(part, direction, step - 1, piece)
        pending.append(send(block, block, *sems(part, direction, step, piece), ring[direction]))

    def got(part, direction, step, piece):
        arrived(
            slot(part, direction, step, piece), *sems(part, direction, step, piece), ring[direction]
        )

    def begin(part):
        block = slot(part, 0, 0, 0)
        pending.append(send(block, block, ys.at[part], yr.at[part], y_peer))
        for direction in range(2):
            pass_on(part, direction, 1, 0)

    def begin_other(part):
        arrived(slot(part, 0, 0, 1), ys.at[part], yr.at[part], y_peer)
        for direction in range(2):
            pass_on(part, direction, 1, 1)

    def step_on(part, step):
        for piece in range(2):
            for direction in range(2):
                got(part, direction, step - 1, piece)
                if step < half or direction == piece:
                    pass_on(part, direction, step, piece)

    mine = gathered.at[tensor]
    pending.append(send(own_tokens, mine, gs.at[0], gr.at[0], far))
    pending.append(send(own_tokens, mine, gs.at[1], gr.at[1], mate))
    kv_old[z * 2 + y_lo] = cache[...]
    begin(0)
    own_slab = pltpu.make_async_copy(slab.at[z], slab_all.at[z], own_sem.at[0])
    own_slab.start()
    for d in range(1, NZ):
        to = lax.rem(z + d, NZ)
        pending.append(
            send(slab.at[to], slab_all.at[z], ts.at[d - 1], tr.at[d - 1], z_peers[d - 1])
        )
    far_index, mate_index = (1 - y_hi) * 2 + core, y_hi * 2 + 1 - core
    cross_index = (1 - y_hi) * 2 + 1 - core

    def rows_of(index):
        return pl.ds(pl.multiple_of(index * quarter, 16), quarter)

    def project(index, block):
        wide = f32(block)
        scaled = (wide * gain[index]).astype(bf16)
        return (
            jnp.dot(scaled, w_query[rows_of(index), :], preferred_element_type=jnp.float32),
            jnp.dot(scaled, w_keyval[rows_of(index), :], preferred_element_type=jnp.float32),
            jnp.sum(wide * wide, axis=1, keepdims=True),
        )

    loads[0].wait()
    loads[1].wait()
    total = project(tensor, own_tokens[...])
    begin_other(0)
    arrived(gathered.at[far_index], gs.at[0], gr.at[0], far)
    block = gathered.at[far_index]
    pending.append(send(block, block, gs.at[2], gr.at[2], mate))
    total = [a + b for a, b in zip(total, project(far_index, gathered[far_index]))]
    arrived(gathered.at[mate_index], gs.at[1], gr.at[1], mate)
    total = [a + b for a, b in zip(total, project(mate_index, gathered[mate_index]))]
    step_on(0, 2)
    arrived(gathered.at[cross_index], gs.at[2], gr.at[2], mate)
    total = [a + b for a, b in zip(total, project(cross_index, gathered[cross_index]))]
    root = lax.rsqrt(total[2] / (4 * quarter) + EPSILON)
    cos, sin = cosine[...], sine[...]
    flipped = (total[1] * root).T
    keys = turn(flipped[: head // 2], flipped[head // 2 : head], cos, sin)
    whole = jnp.concatenate([keys[0], keys[1], flipped[head:]], axis=0).T
    own_rows = whole.astype(bf16).reshape(fresh.shape)
    fresh[...] = own_rows
    kv_new[z * 2 + y_lo] = own_rows
    begin(1)
    raw = total[0] * root
    for j in range(raw.shape[1] // width):
        pair = raw[:, j * width : (j + 1) * width].T
        turned = []
        for h in range(2):
            block = pair[h * head : (h + 1) * head]
            turned += turn(block[: head // 2], block[head // 2 :], cos, sin)
        first = swap_blocks(jnp.concatenate(turned, axis=0) * scale).astype(bf16)
        for s in range(seqs):
            q_all[0, s, :, j * width : (j + 1) * width] = first[s * head : (s + 1) * head]
    for d in (1, 3, 2):
        pending.append(
            send(q_all.at[0], q_all.at[NX - d], xs.at[d - 1], xr.at[d - 1], x_peers[d - 1])
        )
    begin_other(1)
    step_on(0, 3)

    row = lax.broadcasted_iota(jnp.int32, (width, cols), 0)
    lane = lax.broadcasted_iota(jnp.int32, (width, cols), 1)
    for k in range(NX):
        hot = (row == span + lax.rem(x + k, NX)) | (row == span + NX)
        if k == 0:
            hot = hot | (row == lax.rem(lane, span))
        for s in range(seqs):
            qa[s, k, head:width, :] = jnp.zeros((width - head, cols), bf16)
            qa[s, k, width:, :] = jnp.where(hot, 1.0, 0.0).astype(bf16)

    def old_chunk(s, offsets):
        values, masks = [], []
        old_row = lax.broadcasted_iota(jnp.int32, (cache_rows, width), 0)
        marked = lax.broadcasted_iota(jnp.int32, (cache_rows, width), 1) == span + NX
        for offset in offsets:
            origin = lax.rem(z + offset, NZ)
            for side in range(NY):
                values.append(kv_old[origin * 2 + side, s])
                place = old_row + rank_of(side, x, origin) * cache_rows
                masks.append(
                    jnp.where(marked & (place >= prefix[s]), NEG, 0.0).astype(bf16)
                )
        return jnp.concatenate(values, axis=0), jnp.concatenate(masks, axis=0)

    def new_chunk(s):
        masks = []
        new_row = lax.broadcasted_iota(jnp.int32, (span, width), 0)
        new_col = lax.broadcasted_iota(jnp.int32, (span, width), 1)
        in_block = (new_col >= span) & (new_col < span + NX)
        query_rank = rank_of(y_lo, new_col - span, z)
        later = (new_col < span) & (new_row > new_col)
        for shard in range(NY * NZ):
            key_rank = rank_of(shard % 2, x, shard // 2)
            late = in_block & (key_rank > query_rank)
            same = later & (jnp.full(later.shape, key_rank, jnp.int32) == rank)
            masks.append(jnp.where(late | same, NEG, 0.0).astype(bf16))
        return kv_new[:, s].reshape(NY * NZ * span, width), jnp.concatenate(masks, axis=0)

    def operands(keyval, mask):
        flipped = f32(keyval).T[head:].astype(bf16)
        ones = jnp.ones((16, keyval.shape[0]), bf16)
        return (
            jnp.concatenate([keyval, mask], axis=1),
            jnp.concatenate([ones, flipped], axis=0),
        )

    def attend(chunks, gates, ends):
        turns = [(s, c, k) for s in range(seqs) for c in range(len(chunks)) for k in range(NX)]
        held = {}

        def score(turn):
            s, c, k = turn
            if k == 0:
                gates[s][c]()
                held[s, c] = operands(*chunks[c](s))
            return jnp.dot(held[s, c][0], qa[s, k], preferred_element_type=jnp.float32)

        ahead = score(turns[0])
        for at, (s, c, k) in enumerate(turns):
            scores = ahead
            if at + 1 < len(turns):
                ahead = score(turns[at + 1])
            top = jnp.max(scores, axis=0, keepdims=True)
            if c:
                top = jnp.maximum(top, tops[k])
            probs = jnp.exp2(scores - top).astype(bf16)
            part = jnp.dot(held[s, c][1], probs, preferred_element_type=jnp.float32)
            if c:
                part = part + sums[k] * jnp.exp2(tops[k] - top)
            sums[k] = part
            tops[k] = top
            if c == len(chunks) - 1:
                ends(s, k)

    def finish(s, k):
        value = sums[k]
        o_out[s, k] = (value[16:] / value[0:1]).astype(bf16)
        stat_out[s, k, 0:1, :] = tops[k]
        stat_out[s, k, 1:2, :] = value[0:1]
        stat_out[s, k, 2:, :] = jnp.zeros((6, cols), jnp.float32)
        if k:
            to, i = x_peers[k - 1], NX - k - 1
            pending.append(send(stat_out.at[s, k], stat_in.at[s, i], ss.at[s, i], sr.at[s, i], to))
            pending.append(send(o_out.at[s, k], o_in.at[s, i], os.at[s, i], orr.at[s, i], to))

    order = [1 - y_hi, y_hi]

    def combine(s):
        stats, values = [stat_out[s, 0]], [o_out[s, 0]]
        for i in (0, 2, 1):
            arrived(stat_in.at[s, i], ss.at[s, i], sr.at[s, i], x_peers[i])
            arrived(o_in.at[s, i], os.at[s, i], orr.at[s, i], x_peers[i])
            stats.append(stat_in[s, i])
            values.append(o_in[s, i])
        top = functools.reduce(jnp.maximum, [value[0:1] for value in stats])
        shares = [jnp.exp2(value[0:1] - top) * value[1:2] for value in stats]
        every = functools.reduce(jnp.add, shares)
        merged = functools.reduce(
            jnp.add, [f32(value) * (share / every) for value, share in zip(values, shares)]
        )
        blank = jnp.zeros((head, width), jnp.float32)
        attended = jnp.concatenate(
            [
                swap_blocks(
                    jnp.concatenate([merged[:, j * width : (j + 1) * width], blank], axis=0).T
                )[:span]
                for j in range(cols // width)
            ],
            axis=1,
        ).astype(bf16)

        def projected(index):
            return lax.dot_general(
                attended, w_out[rows_of(index), :], (((1,), (1,)), ((), ())),
                preferred_element_type=jnp.float32,
            )

        for i in range(2):
            to_core[s, i] = projected(order[i] * 2 + 1 - core).astype(bf16)
            pending.append(
                send(to_core.at[s, i], core_in.at[s, i], cs.at[s, i], cr.at[s, i], mate)
            )
        keep[s, 0] = projected(order[0] * 2 + core)
        keep[s, 1] = projected(order[1] * 2 + core)

    def across_core(s):
        arrived(core_in.at[s, 0], cs.at[s, 0], cr.at[s, 0], mate)
        far_out[s] = (keep[s, 0] + f32(core_in[s, 0])).astype(bf16)
        pending.append(send(far_out.at[s], far_in.at[s], fs.at[s], fr.at[s], far))

    trio = [mate, far, cross]

    def residual(s):
        mine = pl.ds(s * span, span)
        arrived(core_in.at[s, 1], cs.at[s, 1], cr.at[s, 1], mate)
        near = f32(own_tokens[mine]) + (keep[s, 1] + f32(core_in[s, 1]))
        arrived(far_in.at[s], fs.at[s], fr.at[s], far)
        rounded = (near + f32(far_in[s])).astype(bf16)
        hidden[mine] = rounded
        wide = f32(rounded)
        own = jnp.broadcast_to(jnp.sum(wide * wide, axis=1, keepdims=True), (span, width))
        blank = jnp.zeros((span, width), jnp.float32)
        squares[s] = jnp.concatenate([blank] * s + [own] + [blank] * (seqs - 1 - s), axis=0).T[:8]
        for i in range(3):
            pending.append(
                send(squares.at[s], squares_in.at[s, i], qs.at[s, i], qr.at[s, i], trio[i])
            )
        spread[z, mine] = (wide * out_gain[tensor]).astype(bf16)
        ring_on(s, 1)

    def spot(direction, steps, s):
        origin = lax.rem(z + (NZ - steps if direction == 0 else steps), NZ)
        return spread.at[origin, pl.ds(s * span, span)]

    def ring_on(s, step):
        for direction in range(2):
            if 1 < step <= half or (step > half and direction == s):
                arrived(
                    spot(direction, step - 1, s), hs.at[direction, step - 1, s],
                    hr.at[direction, step - 1, s], ring[direction],
                )
            if step < half or (step == half and direction == s):
                block = spot(direction, step - 1, s)
                pending.append(
                    send(
                        block, block, hs.at[direction, step, s], hr.at[direction, step, s],
                        ring[direction],
                    )
                )

    def share_root(s):
        total = squares[s]
        for i in range(3):
            arrived(squares_in.at[s, i], qs.at[s, i], qr.at[s, i], trio[i])
            total = total + squares_in[s, i]
        lane = lax.broadcasted_iota(jnp.int32, total.shape, 1)
        ours = (lane >= s * span) & (lane < (s + 1) * span)
        roots[z, s] = jnp.where(ours, lax.rsqrt(total / (4 * quarter) + EPSILON), 0.0)
        block = roots.at[z, s]
        for d in range(1, NZ):
            pending.append(send(block, block, rs.at[s, d - 1], rr.at[s, d - 1], z_peers[d - 1]))

    near_first = [(0, NZ - 1), (1, NZ - 2), (2, NZ - 3), (3, 4)]
    for d in (1, 3, 2):
        arrived(q_all.at[NX - d], xs.at[d - 1], xr.at[d - 1], x_peers[d - 1])
    for s in range(seqs):
        for k in range(NX):
            qa[s, k, :head, :] = q_all[k, s]

    def last(part):
        for direction in range(2):
            got(part, direction, half, direction)

    def second():
        step_on(0, 4)
        step_on(1, 2)

    def fourth():
        last(0)
        step_on(1, 4)

    nothing = lambda: None
    chunks = [functools.partial(old_chunk, offsets=pair) for pair in near_first] + [new_chunk]
    gates = [
        [nothing, second, lambda: step_on(1, 3), fourth, lambda: last(1)],
        [
            nothing,
            loads[2].wait,
            lambda: combine(0),
            lambda: across_core(0),
            lambda: residual(0),
        ],
    ]
    attend(chunks, gates, finish)
    ring_on(0, 2)
    combine(1)
    ring_on(0, 3)
    across_core(1)
    ring_on(0, 4)
    share_root(0)
    residual(1)
    ring_on(0, 5)
    for step in range(2, half + 2):
        ring_on(1, step)
        if step == 3:
            share_root(1)
    for s in range(seqs):
        for d in range(1, NZ):
            arrived(
                roots.at[lax.rem(z + NZ - d, NZ), s], rs.at[s, d - 1], rr.at[s, d - 1], z_peers[d - 1]
            )
    for d in range(1, NZ):
        arrived(
            slab_all.at[lax.rem(z + NZ - d, NZ)], ts.at[d - 1], tr.at[d - 1], z_peers[d - 1]
        )
    own_slab.wait()
    for copy in pending:
        copy.wait_send()


def attention(
    scale, own_tokens, gain, cosine, sine, cache, prefix, out_gain, slab, w_query, w_keyval, w_out
):
    seqs, cache_rows, width = cache.shape
    rows, quarter = own_tokens.shape
    span, head = rows // seqs, width // 2
    cols = w_query.shape[1] // head * span
    vmem = pl.BlockSpec(memory_space=pltpu.VMEM)
    any_space = pl.BlockSpec(memory_space=pl.ANY)
    bf16, wide, sem = jnp.bfloat16, jnp.float32, pltpu.SemaphoreType.DMA
    return pl.pallas_call(
        functools.partial(attention_kernel, scale),
        out_shape=(
            jax.ShapeDtypeStruct((seqs, span, width), bf16),
            jax.ShapeDtypeStruct((rows, quarter), bf16),
            jax.ShapeDtypeStruct((NZ, rows, quarter), bf16),
            jax.ShapeDtypeStruct((NZ, seqs, 8, rows), wide),
            jax.ShapeDtypeStruct(slab.shape, slab.dtype),
        ),
        in_specs=[vmem] * 5
        + [pl.BlockSpec(memory_space=pltpu.SMEM), vmem]
        + [any_space] * 4,
        out_specs=(vmem, vmem, vmem, vmem, any_space),
        scratch_shapes=[
            pltpu.VMEM(w_query.shape, bf16),
            pltpu.VMEM(w_keyval.shape, bf16),
            pltpu.VMEM(w_out.shape, bf16),
            pltpu.VMEM((4, rows, quarter), bf16),
            pltpu.VMEM((NY * NZ, seqs, cache_rows, width), bf16),
            pltpu.VMEM((NY * NZ, seqs, span, width), bf16),
            pltpu.VMEM((NX, seqs, head, cols), bf16),
            pltpu.VMEM((seqs, NX, 2 * width, cols), bf16),
            pltpu.VMEM((NX, 1, cols), wide),
            pltpu.VMEM((NX, 16 + head, cols), wide),
            pltpu.VMEM((seqs, NX, head, cols), bf16),
            pltpu.VMEM((seqs, NX, 8, cols), wide),
            pltpu.VMEM((seqs, NX - 1, head, cols), bf16),
            pltpu.VMEM((seqs, NX - 1, 8, cols), wide),
            pltpu.VMEM((seqs, 2, span, quarter), bf16),
            pltpu.VMEM((seqs, 2, span, quarter), bf16),
            pltpu.VMEM((seqs, 2, span, quarter), wide),
            pltpu.VMEM((seqs, span, quarter), bf16),
            pltpu.VMEM((seqs, span, quarter), bf16),
            pltpu.VMEM((seqs, 8, rows), wide),
            pltpu.VMEM((seqs, 3, 8, rows), wide),
            sem((3,)),
            sem((3,)),
            sem((3,)),
            sem((NX - 1,)),
            sem((NX - 1,)),
            sem((2,)),
            sem((2,)),
            sem((2, 2, NZ)),
            sem((2, 2, NZ)),
            sem((NZ - 1,)),
            sem((NZ - 1,)),
            sem((1,)),
            sem((seqs, NX - 1)),
            sem((seqs, NX - 1)),
            sem((seqs, NX - 1)),
            sem((seqs, NX - 1)),
            sem((seqs, 2)),
            sem((seqs, 2)),
            sem((seqs,)),
            sem((seqs,)),
            sem((seqs, 3)),
            sem((seqs, 3)),
            sem((2, NZ // 2 + 1, seqs)),
            sem((2, NZ // 2 + 1, seqs)),
            sem((seqs, NZ - 1)),
            sem((seqs, NZ - 1)),
        ],
        compiler_params=pltpu.CompilerParams(
            collective_id=0, has_side_effects=True, vmem_limit_bytes=60 * 1024 * 1024
        ),
        name="attention",
    )(own_tokens, gain, cosine, sine, cache, prefix, out_gain, slab, w_query, w_keyval, w_out)


def expert_kernel(
    capacity, slab, source, roots, hidden, up_hbm, down_hbm, out,
    rows, sel, held, up_raw, down_raw, up, down, slot_of, weight_of, root_of, shares,
    mine0, mine1, to_mate0, to_mate1, core_in0, core_in1, side_in0, side_in1, x_out0, x_out1,
    back0, back1, sums0, sums1, staged0, staged1, landed0, landed1,
    ws, xs, xr, ys, yr, fs, fr, cs, cr, bs, br, es, er, zs, zr,
):
    mine, to_mate, core_in = (mine0, mine1), (to_mate0, to_mate1), (core_in0, core_in1)
    side_in, x_out, back = (side_in0, side_in1), (x_out0, x_out1), (back0, back1)
    sums, staged, landed = (sums0, sums1), (staged0, staged1), (landed0, landed1)
    rank, tensor = lax.axis_index("expert"), lax.axis_index("tensor")
    y_lo, x, z, y_hi, core, far, sides, mate = corner(rank, tensor)
    other = 1 - y_lo
    x_peers = [(rank_of(y_lo, lax.rem(x + d, NX), z), tensor) for d in range(1, NX)]
    ring = [
        (rank_of(y_lo, x, lax.rem(z + 1, NZ)), tensor),
        (rank_of(y_lo, x, lax.rem(z + NZ - 1, NZ)), tensor),
    ]
    greet(x_peers + [far] + sides + [mate] + ring)
    pending = []
    loads = [
        pltpu.make_async_copy(up_hbm, up_raw, ws.at[0]),
        pltpu.make_async_copy(down_hbm, down_raw, ws.at[1]),
    ]
    for load in loads:
        load.start()
    size, width = sel.shape[2:]
    quarters = rows.shape[0]
    count = hidden.shape[0]
    bf16 = jnp.bfloat16
    cuts = (slice(0, mine0.shape[3]), slice(mine0.shape[3], width))

    at = lax.broadcasted_iota(jnp.int32, (size, count), 0)
    lane = lax.broadcasted_iota(jnp.int32, (size, count), 1)
    block_of = jnp.zeros((size, count), jnp.int32)
    for b in range(1, NZ):
        block_of = block_of + jnp.where(at >= b * capacity, 1, 0)
    ours = lane == at - block_of * capacity
    lane_f = f32(lane)

    def by_block(pieces):
        value = jnp.zeros((size, count), jnp.float32)
        for b in range(NZ):
            value = jnp.where(block_of == b, pieces[b], value)
        return value

    root_rows = by_block([roots[b, 0, 0:1, :] + roots[b, 1, 0:1, :] for b in range(NZ)])
    first = f32(block_of[:, 0:1] * count)

    def total_of(mask, value):
        return jnp.sum(jnp.where(mask, value, 0.0), axis=1, keepdims=True)

    for j in range(NY * NX):
        token = total_of(ours, by_block([slab[b, j : j + 1, :count] for b in range(NZ)]))
        weight_of[j] = total_of(ours, by_block([slab[b, j : j + 1, count:] for b in range(NZ)]))
        root_of[j] = total_of(lane_f == token, root_rows)
        slot_of[j] = jnp.where(token >= 0.0, token + first, -1.0)
    lanes = f32(lax.broadcasted_iota(jnp.int32, (size, source.shape[0]), 1))

    def pick(side, to):
        j = side * NX + to
        chosen = jnp.where(lanes == slot_of[j], 1.0, 0.0).astype(bf16)
        picked = jnp.dot(chosen, source[...], preferred_element_type=jnp.float32)
        return (picked * root_of[j]).astype(bf16)

    def to_side(d, here, there):
        spot = rows.at[tensor, y_lo, lax.rem(x + NX - d, NX)]
        for r in range(2):
            pending.append(send(there, spot, ys.at[d, r], yr.at[d, r], sides[r]))
        pending.append(send(here, spot, ys.at[d, 2], yr.at[d, 2], far))

    def forward(d, r, l):
        x_s = lax.rem(x + NX - d, NX)
        spot = rows.at[lax.rem(y_hi + r, 2) * 2 + core, lax.rem(y_lo + l, 2), x_s]
        index = 2 * r + l
        pending.append(send(spot, spot, fs.at[d, index], fr.at[d, index], mate))

    def from_sides(d):
        x_s = lax.rem(x + NX - d, NX)
        for r in range(2):
            spot = rows.at[lax.rem(y_hi + r, 2) * 2 + core, other, x_s]
            arrived(spot, ys.at[d, r], yr.at[d, r], sides[r])
            forward(d, r, 1)
        spot = rows.at[(1 - y_hi) * 2 + core, y_lo, x_s]
        arrived(spot, ys.at[d, 2], yr.at[d, 2], far)
        forward(d, 1, 0)

    def from_mate(d):
        x_s = lax.rem(x + NX - d, NX)
        for r in range(2):
            for l in range(2):
                spot = rows.at[lax.rem(y_hi + r, 2) * 2 + 1 - core, lax.rem(y_lo + l, 2), x_s]
                arrived(spot, fs.at[d, 2 * r + l], fr.at[d, 2 * r + l], mate)

    units, real = down.shape[1], down_raw.shape[0]

    def run(d):
        x_s = lax.rem(x + NX - d, NX)
        total = jnp.zeros((2 * size, 2 * units), jnp.float32)
        for q in range(quarters):
            block = jnp.concatenate([rows[q, other, x_s], rows[q, y_lo, x_s]], axis=0)
            total += lax.dot_general(
                block, up[q], (((1,), (1,)), ((), ())), preferred_element_type=jnp.float32
            )
        gate, raised = total[:, :units], total[:, units:]
        active = (gate * jax.nn.sigmoid(1.702 * gate) * (raised + 1.0)).astype(bf16)
        for f in range(2):
            for h in range(2):
                half = lax.rem(y_hi + h, 2)
                for owner in range(2):
                    index = half * 2 + (core if owner else 1 - core)
                    value = jnp.dot(
                        active, down[index, :, cuts[f]], preferred_element_type=jnp.float32
                    ).astype(bf16)
                    into = mine[f] if owner else to_mate[f]
                    into[d, h] = value[:size]
                    into[d, 3 - h] = value[size:]
                    if not owner:
                        for kind in (h, 3 - h):
                            pending.append(
                                send(
                                    into.at[d, kind], core_in[f].at[d, kind],
                                    cs.at[f, d, kind], cr.at[f, d, kind], mate,
                                )
                            )

    def back_to_sides(f, d):
        for kind in range(4):
            arrived(core_in[f].at[d, kind], cs.at[f, d, kind], cr.at[f, d, kind], mate)
            both = f32(mine[f][d, kind]) + f32(core_in[f][d, kind])
            mine[f][d, kind] = both.astype(bf16)
            if kind < 3:
                to = far if kind == 2 else sides[kind]
                pending.append(
                    send(
                        mine[f].at[d, kind], side_in[f].at[d, kind],
                        bs.at[f, d, kind], br.at[f, d, kind], to,
                    )
                )

    def spot_of(f, owner, at_x):
        return back[f].at[owner * NX + at_x]

    def back_to_x(f, d):
        for kind in range(3):
            to = far if kind == 2 else sides[kind]
            arrived(side_in[f].at[d, kind], bs.at[f, d, kind], br.at[f, d, kind], to)
            if kind == 0:
                continue
            near = side_in[f][d, 0] if kind == 1 else mine[f][d, 3]
            both = (f32(near) + f32(side_in[f][d, kind])).astype(bf16)
            i = kind - 1
            owner = other if kind == 1 else y_lo
            if d == 0:
                back[f][owner * NX + x] = both
            else:
                e = NX - d - 1
                x_out[f][d - 1, i] = both
                pending.append(
                    send(
                        x_out[f].at[d - 1, i], spot_of(f, owner, x),
                        es.at[f, e, i], er.at[f, e, i], x_peers[e],
                    )
                )

    def from_x_back(f):
        for d in range(1, NX):
            x_e = lax.rem(x + NX - d, NX)
            for i in range(2):
                owner = other if i == 0 else y_lo
                arrived(
                    spot_of(f, owner, x_e), es.at[f, d - 1, i], er.at[f, d - 1, i], x_peers[d - 1]
                )

    half_rows, half = count // 2, NZ // 2

    def add_up(f, steps):
        value = jnp.dot(
            shares[steps],
            back[f][...].reshape(NY * NX * size, back[f].shape[2]),
            preferred_element_type=jnp.float32,
        )
        sums[f][steps] = value.astype(bf16)

    def reach(direction, piece):
        return half if direction == piece else half - 1

    def got(f, direction, steps, piece):
        index = 2 * steps + piece
        arrived(
            landed[f].at[direction, index], zs.at[f, direction, index], zr.at[f, direction, index],
            ring[direction],
        )
        return f32(landed[f][direction, index])

    def toward(f, steps):
        add_up(f, steps)
        if steps < half:
            add_up(f, NZ - steps)
        for piece in range(2):
            for direction in range(2):
                if steps > reach(direction, piece):
                    continue
                home = steps if direction == 0 else NZ - steps
                value = f32(sums[f][home, pl.ds(piece * half_rows, half_rows)])
                if steps < reach(direction, piece):
                    value = value + got(f, direction, steps, piece)
                index = 2 * (steps - 1) + piece
                staged[f][direction, index] = value.astype(bf16)
                pending.append(
                    send(
                        staged[f].at[direction, index], landed[f].at[direction, index],
                        zs.at[f, direction, index], zr.at[f, direction, index], ring[direction],
                    )
                )
        if steps == 1:
            add_up(f, 0)

    def arrive_home(f):
        for piece in range(2):
            span = pl.ds(piece * half_rows, half_rows)
            value = f32(sums[f][0, span])
            for direction in range(2):
                value = value + got(f, direction, 0, piece)
            out[span, cuts[f]] = (f32(hidden[span, cuts[f]]) + value).astype(bf16)

    sel[other, x] = pick(other, x)
    rows[tensor, y_lo, x] = pick(y_lo, x)
    to_side(0, rows.at[tensor, y_lo, x], sel.at[other, x])
    for d in (1, 3, 2):
        to = lax.rem(x + d, NX)
        for i in range(2):
            side = other if i == 0 else y_lo
            sel[side, to] = pick(side, to)
            dst = held.at[x] if i == 0 else rows.at[tensor, y_lo, x]
            pending.append(
                send(sel.at[side, to], dst, xs.at[d - 1, i], xr.at[d - 1, i], x_peers[d - 1])
            )
    forward(0, 0, 0)
    blank = jnp.zeros((units - real, width), bf16)
    for load in loads:
        load.wait()
    for q in range(quarters):
        span = slice(q * width, (q + 1) * width)
        for i in range(2):
            up[q, i * units : i * units + real, :] = up_raw[i, :, span]
            up[q, i * units + real : (i + 1) * units, :] = blank
        down[q, :real, :] = down_raw[:, span]
        down[q, real:, :] = blank

    def from_x(d):
        x_s = lax.rem(x + NX - d, NX)
        arrived(held.at[x_s], xs.at[d - 1, 0], xr.at[d - 1, 0], x_peers[d - 1])
        arrived(rows.at[tensor, y_lo, x_s], xs.at[d - 1, 1], xr.at[d - 1, 1], x_peers[d - 1])
        to_side(d, rows.at[tensor, y_lo, x_s], held.at[x_s])
        forward(d, 0, 0)

    from_x(1)
    from_x(3)
    from_sides(0)
    from_x(2)
    wide_lane = f32(lax.broadcasted_iota(jnp.int32, (size, count), 1))
    for steps in range(NZ):
        start = f32(jnp.full((size, count), lax.rem(z + steps, NZ) * count, jnp.int32))
        flipped = [
            jnp.where(wide_lane + start == slot_of[j], weight_of[j], 0.0) for j in range(NY * NX)
        ]
        shares[steps] = jnp.concatenate(flipped, axis=0).T.astype(bf16)
    for d in (0, 1, 3, 2):
        if d:
            from_sides(d)
        from_mate(d)
        run(d)
        if d in (1, 3):
            back_to_sides(0, d)
    back_to_sides(0, 2)
    back_to_sides(0, 0)
    for d in (1, 3, 2, 0):
        back_to_sides(1, d)
    for d in (1, 3, 2, 0):
        back_to_x(0, d)
    from_x_back(0)
    for steps, d in zip(range(half, 0, -1), (1, 3, 2, 0)):
        toward(0, steps)
        back_to_x(1, d)
    arrive_home(0)
    from_x_back(1)
    for steps in range(half, 0, -1):
        toward(1, steps)
    arrive_home(1)
    for copy in pending:
        copy.wait_send()


def run_experts(capacity, slab, source, roots, hidden, up, down):
    count, width = hidden.shape
    size = NZ * capacity
    quarters = down.shape[1] // width
    units = -(-down.shape[0] // 128) * 128
    vmem = pl.BlockSpec(memory_space=pltpu.VMEM)
    any_space = pl.BlockSpec(memory_space=pl.ANY)
    bf16, sem, wide = jnp.bfloat16, pltpu.SemaphoreType.DMA, jnp.float32
    cut = -(-width // 256) * 128
    parts = (cut, width - cut)
    groups = NY * NX

    def pair(*lead):
        return [pltpu.VMEM(lead + (part,), bf16) for part in parts]

    return pl.pallas_call(
        functools.partial(expert_kernel, capacity),
        out_shape=jax.ShapeDtypeStruct((count, width), bf16),
        in_specs=[vmem] * 4 + [any_space] * 2,
        out_specs=vmem,
        scratch_shapes=[
            pltpu.VMEM((quarters, NY, NX, size, width), bf16),
            pltpu.VMEM((NY, NX, size, width), bf16),
            pltpu.VMEM((NX, size, width), bf16),
            pltpu.VMEM(up.shape, bf16),
            pltpu.VMEM(down.shape, bf16),
            pltpu.VMEM((quarters, 2 * units, width), bf16),
            pltpu.VMEM((quarters, units, width), bf16),
            pltpu.VMEM((groups, size, 1), wide),
            pltpu.VMEM((groups, size, 1), wide),
            pltpu.VMEM((groups, size, 1), wide),
            pltpu.VMEM((NZ, count, groups * size), bf16),
            *pair(NX, 4, size),
            *pair(NX, 4, size),
            *pair(NX, 4, size),
            *pair(NX, 3, size),
            *pair(NX - 1, 2, size),
            *pair(groups, size),
            *pair(NZ, count),
            *pair(2, NZ, count // 2),
            *pair(2, NZ, count // 2),
            sem((2,)),
            sem((NX - 1, 2)),
            sem((NX - 1, 2)),
            sem((NX, 3)),
            sem((NX, 3)),
            sem((NX, 4)),
            sem((NX, 4)),
            sem((2, NX, 4)),
            sem((2, NX, 4)),
            sem((2, NX, 3)),
            sem((2, NX, 3)),
            sem((2, NX - 1, 2)),
            sem((2, NX - 1, 2)),
            sem((2, 2, NZ)),
            sem((2, 2, NZ)),
        ],
        compiler_params=pltpu.CompilerParams(
            collective_id=3, has_side_effects=True, vmem_limit_bytes=62 * 1024 * 1024
        ),
        name="run_experts",
    )(slab, source, roots, hidden, up, down)


def route_kernel(capacity, routed, weights, slab):
    experts, _ = slab.shape
    seqs, top_count, count = routed.shape
    row = lax.broadcasted_iota(jnp.int32, (experts, count), 0)
    lane = lax.broadcasted_iota(jnp.int32, (experts, count), 1)
    expert = lax.rem(row, experts // NZ) * NZ + row // (experts // NZ)
    before = jnp.where(
        lax.broadcasted_iota(jnp.int32, (count, count), 0)
        < lax.broadcasted_iota(jnp.int32, (count, count), 1),
        1.0,
        0.0,
    ).astype(jnp.bfloat16)
    earlier = jnp.zeros((experts, 1), jnp.float32)
    named, shares = [], []
    for s in range(seqs):
        for k in range(top_count):
            hit = jnp.where(expert == routed[s, k : k + 1, :], 1.0, 0.0)
            ahead = jnp.dot(hit.astype(jnp.bfloat16), before, preferred_element_type=jnp.float32)
            named.append((jnp.where(hit > 0.0, ahead + earlier, -1.0), f32(lane + s * count + 1)))
            shares.append(weights[s, k : k + 1, :])
            earlier = earlier + jnp.sum(hit, axis=1, keepdims=True)
    tokens = jnp.full((experts, 128), -1.0, jnp.float32)
    scales = jnp.zeros((experts, 128), jnp.float32)
    slot = lax.broadcasted_iota(jnp.int32, (experts, 128), 1)
    for place in range(capacity):
        token = jnp.zeros((experts, count), jnp.float32)
        scale = jnp.zeros((experts, count), jnp.float32)
        for (arrival, number), share in zip(named, shares):
            here = arrival == float(place)
            token = jnp.where(here, number, token)
            scale = jnp.where(here, share, scale)
        tokens = jnp.where(slot == place, jnp.sum(token, axis=1, keepdims=True) - 1.0, tokens)
        scales = jnp.where(slot == place, jnp.sum(scale, axis=1, keepdims=True), scales)
    slab[:, :128] = tokens
    slab[:, 128:] = scales


def routing_slab(routed, weights, expert_count, capacity):
    vmem = pl.BlockSpec(memory_space=pltpu.VMEM)
    slab = pl.pallas_call(
        functools.partial(route_kernel, capacity),
        out_shape=jax.ShapeDtypeStruct((expert_count, 256), jnp.float32),
        in_specs=[vmem, vmem],
        out_specs=vmem,
        name="route",
    )(routed, weights)
    return slab.reshape(NZ, expert_count // NZ, 256)


def on_device(
    tokens,
    attn_gain,
    w_query,
    key_value_weight,
    w_out,
    cache_keyval,
    prefix_length,
    routed_experts,
    route_weights,
    expert_gain,
    w_gate_up,
    w_down,
):
    span_dev, seq_count, quarter = tokens.shape
    model_width = attn_gain.shape[0]
    row_count = span_dev * seq_count
    head_dim = key_value_weight.shape[2] // 2
    cache_rows = cache_keyval.shape[0]
    expert_rank = lax.axis_index("expert")
    quarters = model_width // quarter
    top_count = routed_experts.shape[2]
    expert_count = lax.axis_size("expert")
    capacity = min(row_count, max(2, 5 * row_count * top_count // (2 * expert_count)))
    half_dim = head_dim // 2
    steps_up = jnp.arange(half_dim, dtype=jnp.float32)
    frequency = jnp.exp(steps_up * (-math.log(ROPE_BASE) / half_dim))
    span_place = expert_rank * span_dev + jnp.arange(span_dev, dtype=jnp.int32)
    places = (prefix_length[:, None] + span_place[None, :]).reshape(row_count).astype(jnp.float32)
    angles = frequency[:, None] * places[None, :]
    slab = routing_slab(
        routed_experts.transpose(1, 2, 0),
        route_weights.transpose(1, 2, 0),
        expert_count,
        capacity,
    )
    own_tokens = tokens.transpose(1, 0, 2).reshape(row_count, quarter)
    fresh, hidden, spread, roots, slab_all = attention(
        head_dim ** (-0.5) * LOG2E,
        own_tokens,
        attn_gain.reshape(quarters, 1, quarter),
        jnp.cos(angles),
        jnp.sin(angles),
        cache_keyval[:, :, 0, :].transpose(1, 0, 2),
        prefix_length,
        expert_gain.reshape(quarters, 1, quarter),
        slab,
        w_query,
        key_value_weight[:, 0, :],
        w_out.T,
    )
    new_key_value_rows = fresh.transpose(1, 0, 2)[:, :, None, :]
    layer_output = run_experts(
        capacity,
        slab_all,
        spread.reshape(NZ * row_count, quarter),
        roots,
        hidden,
        w_gate_up[0].transpose(1, 2, 0),
        w_down[0],
    )
    layer_output = layer_output.reshape(seq_count, span_dev, quarter).transpose(1, 0, 2)
    return (layer_output, new_key_value_rows)


def solution(mesh):
    return jax.shard_map(
        on_device,
        mesh=mesh,
        in_specs=(
            P("expert", None, "tensor"),
            P(),
            P(None, "tensor"),
            P(None, "tensor", None),
            P("tensor", None),
            P("expert", None, "tensor", None),
            P(),
            P("expert", None, None),
            P("expert", None, None),
            P(),
            P("expert", None, None, "tensor"),
            P("expert", "tensor", None),
        ),
        out_specs=(P("expert", None, "tensor"), P("expert", None, "tensor", None)),
        check_vma=False,
    )
```

```python
import functools
import math

import jax
import jax.numpy as jnp
from jax import lax
from jax.experimental import pallas as pl
from jax.experimental.pallas import tpu as pltpu
from jax.sharding import PartitionSpec as P

EPSILON = 1e-05
ROPE_BASE = 150000.0
NEG = -1e30
MESH = pl.DeviceIdType.MESH
NY, NX, NZ = 2, 4, 8
LOG2E = 1.4426950408889634


def place_of(expert_rank):
    return expert_rank // (NX * NZ), (expert_rank // NZ) % NX, expert_rank % NZ


def rank_of(y_lo, x, z):
    return (y_lo * NX + x) * NZ + z


def greet(devices):
    barrier = pltpu.get_barrier_semaphore()
    for device in devices:
        pl.semaphore_signal(barrier, inc=1, device_id=device, device_id_type=MESH)
    pl.semaphore_wait(barrier, len(devices))


def send(src, dst, send_sem, recv_sem, device):
    copy = pltpu.make_async_remote_copy(
        src_ref=src,
        dst_ref=dst,
        send_sem=send_sem,
        recv_sem=recv_sem,
        device_id=device,
        device_id_type=MESH,
    )
    copy.start()
    return copy


def arrived(dst, send_sem, recv_sem, device):
    pltpu.make_async_remote_copy(
        src_ref=dst,
        dst_ref=dst,
        send_sem=send_sem,
        recv_sem=recv_sem,
        device_id=device,
        device_id_type=MESH,
    ).wait_recv()


def swap_blocks(value):
    half = value.shape[0] // 2
    top, bottom = value[:half], value[half:]
    left = lax.broadcasted_iota(jnp.int32, top.shape, 1) < half
    return jnp.concatenate(
        [
            jnp.where(left, top, pltpu.roll(bottom, half, 1)),
            jnp.where(left, pltpu.roll(top, half, 1), bottom),
        ],
        axis=0,
    )


def turn(first, second, cosine, sine):
    return first * cosine - second * sine, second * cosine + first * sine


def corner(rank, tensor):
    y_lo, x, z = place_of(rank)
    y_hi, core = tensor // 2, lax.rem(tensor, 2)
    far = (rank, (1 - y_hi) * 2 + core)
    sides = [(rank_of(1 - y_lo, x, z), lax.rem(y_hi + r, 2) * 2 + core) for r in range(2)]
    mate = (rank, y_hi * 2 + 1 - core)
    return y_lo, x, z, y_hi, core, far, sides, mate


def f32(value):
    return value.astype(jnp.float32)


def route(capacity, routed, weights, slab):
    planes, groups, _ = slab.shape
    experts = planes * groups
    seqs, top_count, count = routed.shape
    row = lax.broadcasted_iota(jnp.int32, (experts, count), 0)
    lane = lax.broadcasted_iota(jnp.int32, (experts, count), 1)
    expert = lax.rem(row, groups) * planes + row // groups
    before = jnp.where(
        lax.broadcasted_iota(jnp.int32, (count, count), 0)
        < lax.broadcasted_iota(jnp.int32, (count, count), 1),
        1.0,
        0.0,
    ).astype(jnp.bfloat16)
    earlier = jnp.zeros((experts, 1), jnp.float32)
    named = []
    for s in range(seqs):
        for k in range(top_count):
            hit = jnp.where(expert == routed[s, k : k + 1, :], 1.0, 0.0)
            ahead = jnp.dot(hit.astype(jnp.bfloat16), before, preferred_element_type=jnp.float32)
            arrival = jnp.where(hit > 0.0, ahead + earlier, -1.0)
            named.append((arrival, f32(lane + s * count + 1), weights[s, k : k + 1, :]))
            earlier = earlier + jnp.sum(hit, axis=1, keepdims=True)
    slot = lax.broadcasted_iota(jnp.int32, (experts, 128), 1)

    def fill(place, carry):
        tokens, scales = carry
        token = jnp.zeros((experts, count), jnp.float32)
        scale = jnp.zeros((experts, count), jnp.float32)
        for arrival, number, share in named:
            here = arrival == f32(place)
            token = jnp.where(here, number, token)
            scale = jnp.where(here, share, scale)
        return (
            jnp.where(slot == place, jnp.sum(token, axis=1, keepdims=True) - 1.0, tokens),
            jnp.where(slot == place, jnp.sum(scale, axis=1, keepdims=True), scales),
        )

    empty = jnp.full((experts, 128), -1.0, jnp.float32)
    tokens, scales = lax.fori_loop(0, capacity, fill, (empty, jnp.zeros_like(empty)))
    slab[:, :, :128] = tokens.reshape(planes, groups, 128)
    slab[:, :, 128:] = scales.reshape(planes, groups, 128)


def attention_kernel(
    scale, capacity, own_tokens, gain, cosine, sine, cache, routed, weights, prefix, w_query_hbm, w_keyval_hbm, w_out_hbm,
    fresh, hidden, spread, roots, slab_all,
    w_query, w_keyval, w_out, gathered, kv_old, kv_new, q_all, qa, tops, sums, o_out, stat_out,
    o_in, stat_in, to_core, core_in, keep, far_out, far_in, squares, squares_in,
    slab, ws, gs, gr, xs, xr, ys, yr, zs, zr, ts, tr, os, orr, ss, sr, cs, cr, fs, fr, qs, qr, hs, hr, rs, rr,
):
    rank, tensor = lax.axis_index("expert"), lax.axis_index("tensor")
    y_lo, x, z, y_hi, core, far, sides, mate = corner(rank, tensor)
    other = 1 - y_lo
    rows, quarter = own_tokens.shape
    seqs, span, width = fresh.shape
    cache_rows, head = cache.shape[1], width // 2
    cols = q_all.shape[3]
    bf16 = jnp.bfloat16
    x_peers = [(rank_of(y_lo, lax.rem(x + d, NX), z), tensor) for d in range(1, NX)]
    y_peer = (rank_of(other, x, z), tensor)
    z_peers = [(rank_of(y_lo, x, lax.rem(z + d, NZ)), tensor) for d in range(1, NZ)]
    ring = [z_peers[0], z_peers[-1]]
    cross = (rank, (1 - y_hi) * 2 + 1 - core)
    greet(x_peers + [y_peer] + z_peers + [far, mate, cross])
    pending = []
    loads = [
        pltpu.make_async_copy(src, dst, ws.at[i])
        for i, (src, dst) in enumerate(
            [(w_query_hbm, w_query), (w_keyval_hbm, w_keyval), (w_out_hbm, w_out)]
        )
    ]
    for load in loads:
        load.start()
    half = NZ // 2
    stores = (kv_old, kv_new)

    def slot(part, direction, steps, piece):
        origin = lax.rem(z + (NZ - steps if direction == 0 else steps), NZ)
        return stores[part].at[origin * 2 + (y_lo if piece == 0 else other)]

    def sems(part, direction, step, piece):
        index = 2 * (step - 1) + piece
        return zs.at[part, direction, index], zr.at[part, direction, index]

    def pass_on(part, direction, step, piece):
        block = slot(part, direction, step - 1, piece)
        pending.append(send(block, block, *sems(part, direction, step, piece), ring[direction]))

    def got(part, direction, step, piece):
        arrived(
            slot(part, direction, step, piece), *sems(part, direction, step, piece), ring[direction]
        )

    def begin(part):
        block = slot(part, 0, 0, 0)
        pending.append(send(block, block, ys.at[part], yr.at[part], y_peer))
        for direction in range(2):
            pass_on(part, direction, 1, 0)

    def begin_other(part):
        arrived(slot(part, 0, 0, 1), ys.at[part], yr.at[part], y_peer)
        for direction in range(2):
            pass_on(part, direction, 1, 1)

    def step_on(part, step):
        for piece in range(2):
            for direction in range(2):
                got(part, direction, step - 1, piece)
                if step < half or direction == piece:
                    pass_on(part, direction, step, piece)

    mine = gathered.at[tensor]
    pending.append(send(own_tokens, mine, gs.at[0], gr.at[0], far))
    pending.append(send(own_tokens, mine, gs.at[1], gr.at[1], mate))
    kv_old[z * 2 + y_lo] = cache[...]
    begin(0)
    far_index, mate_index = (1 - y_hi) * 2 + core, y_hi * 2 + 1 - core
    cross_index = (1 - y_hi) * 2 + 1 - core

    def rows_of(index):
        return pl.ds(pl.multiple_of(index * quarter, 16), quarter)

    def project(index, block):
        wide = f32(block)
        scaled = (wide * gain[0, index]).astype(bf16)
        return (
            jnp.dot(scaled, w_query[rows_of(index), :], preferred_element_type=jnp.float32),
            jnp.dot(scaled, w_keyval[rows_of(index), :], preferred_element_type=jnp.float32),
            jnp.sum(wide * wide, axis=1, keepdims=True),
        )

    loads[0].wait()
    loads[1].wait()
    def add_to(total, index):
        return [a + b for a, b in zip(total, project(index, gathered[index]))]

    total = project(tensor, own_tokens[...])
    arrived(gathered.at[mate_index], gs.at[1], gr.at[1], mate)
    total = add_to(total, mate_index)
    begin_other(0)
    route(capacity, routed, weights, slab)
    slab_all[z] = slab[z]
    arrived(gathered.at[far_index], gs.at[0], gr.at[0], far)
    block = gathered.at[far_index]
    pending.append(send(block, block, gs.at[2], gr.at[2], mate))
    for d in range(1, NZ):
        to = lax.rem(z + d, NZ)
        pending.append(
            send(slab.at[to], slab_all.at[z], ts.at[d - 1], tr.at[d - 1], z_peers[d - 1])
        )
    total = add_to(total, far_index)
    arrived(gathered.at[cross_index], gs.at[2], gr.at[2], mate)
    total = add_to(total, cross_index)
    root = lax.rsqrt(total[2] / (4 * quarter) + EPSILON)
    cos, sin = cosine[...], sine[...]
    flipped = (total[1] * root).T
    keys = turn(flipped[: head // 2], flipped[head // 2 : head], cos, sin)
    whole = jnp.concatenate([keys[0], keys[1], flipped[head:]], axis=0).T
    own_rows = whole.astype(bf16).reshape(fresh.shape)
    fresh[...] = own_rows
    kv_new[z * 2 + y_lo] = own_rows
    begin(1)
    step_on(0, 2)
    raw = total[0] * root
    for j in range(raw.shape[1] // width):
        pair = raw[:, j * width : (j + 1) * width].T
        turned = []
        for h in range(2):
            block = pair[h * head : (h + 1) * head]
            turned += turn(block[: head // 2], block[head // 2 :], cos, sin)
        first = swap_blocks(jnp.concatenate(turned, axis=0) * scale).astype(bf16)
        for s in range(seqs):
            q_all[0, s, :, j * width : (j + 1) * width] = first[s * head : (s + 1) * head]
    for s in range(seqs):
        for d in (1, 3, 2):
            src, dst = q_all.at[0, s], q_all.at[NX - d, s]
            pending.append(send(src, dst, xs.at[s, d - 1], xr.at[s, d - 1], x_peers[d - 1]))
    begin_other(1)
    step_on(0, 3)

    row = lax.broadcasted_iota(jnp.int32, (width, cols), 0)
    lane = lax.broadcasted_iota(jnp.int32, (width, cols), 1)
    for k in range(NX):
        hot = (row == span + lax.rem(x + k, NX)) | (row == span + NX)
        if k == 0:
            hot = hot | (row == lax.rem(lane, span))
        for s in range(seqs):
            qa[s, k, head:width, :] = jnp.zeros((width - head, cols), bf16)
            qa[s, k, width:, :] = jnp.where(hot, 1.0, 0.0).astype(bf16)

    def old_chunk(s, offsets):
        values, masks = [], []
        old_row = lax.broadcasted_iota(jnp.int32, (cache_rows, width), 0)
        marked = lax.broadcasted_iota(jnp.int32, (cache_rows, width), 1) == span + NX
        for offset in offsets:
            origin = lax.rem(z + offset, NZ)
            for side in range(NY):
                values.append(kv_old[origin * 2 + side, s])
                place = old_row + rank_of(side, x, origin) * cache_rows
                masks.append(
                    jnp.where(marked & (place >= prefix[s]), NEG, 0.0).astype(bf16)
                )
        return jnp.concatenate(values, axis=0), jnp.concatenate(masks, axis=0)

    def new_chunk(s):
        masks = []
        new_row = lax.broadcasted_iota(jnp.int32, (span, width), 0)
        new_col = lax.broadcasted_iota(jnp.int32, (span, width), 1)
        in_block = (new_col >= span) & (new_col < span + NX)
        query_rank = rank_of(y_lo, new_col - span, z)
        later = (new_col < span) & (new_row > new_col)
        for shard in range(NY * NZ):
            key_rank = rank_of(shard % 2, x, shard // 2)
            late = in_block & (key_rank > query_rank)
            same = later & (jnp.full(later.shape, key_rank, jnp.int32) == rank)
            masks.append(jnp.where(late | same, NEG, 0.0).astype(bf16))
        return kv_new[:, s].reshape(NY * NZ * span, width), jnp.concatenate(masks, axis=0)

    def operands(keyval, mask):
        flipped = f32(keyval).T[head:].astype(bf16)
        ones = jnp.ones((16, keyval.shape[0]), bf16)
        return (
            jnp.concatenate([keyval, mask], axis=1),
            jnp.concatenate([ones, flipped], axis=0),
        )

    def attend(chunks, gates, ends):
        turns = [
            (s, c, k)
            for s in range(seqs)
            for c in range(len(chunks))
            for k in ((0, 1, 3, 2) if c == 0 else (2, 1, 3, 0))
        ]
        held = {}

        def score(turn):
            s, c, k = turn
            if (s, c) not in held:
                gates[s][c]()
                held[s, c] = operands(*chunks[c](s))
            if c == 0:
                if k:
                    e = NX - k - 1
                    arrived(q_all.at[k, s], xs.at[s, e], xr.at[s, e], x_peers[e])
                qa[s, k, :head, :] = q_all[k, s]
            return jnp.dot(held[s, c][0], qa[s, k], preferred_element_type=jnp.float32)

        ahead = score(turns[0])
        for at, (s, c, k) in enumerate(turns):
            scores = ahead
            if at + 1 < len(turns):
                ahead = score(turns[at + 1])
            top = jnp.max(scores, axis=0, keepdims=True)
            if c:
                top = jnp.maximum(top, tops[k])
            probs = jnp.exp2(scores - top).astype(bf16)
            part = jnp.dot(held[s, c][1], probs, preferred_element_type=jnp.float32)
            if c:
                part = part + sums[k] * jnp.exp2(tops[k] - top)
            sums[k] = part
            tops[k] = top
            if c == len(chunks) - 1:
                ends(s, k)

    def finish(s, k):
        value = sums[k]
        o_out[s, k] = (value[16:] / value[0:1]).astype(bf16)
        stat_out[s, k, 0:1, :] = tops[k]
        stat_out[s, k, 1:2, :] = value[0:1]
        stat_out[s, k, 2:, :] = jnp.zeros((6, cols), jnp.float32)
        if k:
            to, i = x_peers[k - 1], NX - k - 1
            pending.append(send(stat_out.at[s, k], stat_in.at[s, i], ss.at[s, i], sr.at[s, i], to))
            pending.append(send(o_out.at[s, k], o_in.at[s, i], os.at[s, i], orr.at[s, i], to))

    order = [1 - y_hi, y_hi]

    def combine(s):
        stats, values = [stat_out[s, 0]], [o_out[s, 0]]
        for i in (0, 2, 1):
            arrived(stat_in.at[s, i], ss.at[s, i], sr.at[s, i], x_peers[i])
            arrived(o_in.at[s, i], os.at[s, i], orr.at[s, i], x_peers[i])
            stats.append(stat_in[s, i])
            values.append(o_in[s, i])
        top = functools.reduce(jnp.maximum, [value[0:1] for value in stats])
        shares = [jnp.exp2(value[0:1] - top) * value[1:2] for value in stats]
        every = functools.reduce(jnp.add, shares)
        merged = functools.reduce(
            jnp.add, [f32(value) * (share / every) for value, share in zip(values, shares)]
        )
        blank = jnp.zeros((head, width), jnp.float32)
        attended = jnp.concatenate(
            [
                swap_blocks(
                    jnp.concatenate([merged[:, j * width : (j + 1) * width], blank], axis=0).T
                )[:span]
                for j in range(cols // width)
            ],
            axis=1,
        ).astype(bf16)

        def projected(index):
            return lax.dot_general(
                attended, w_out[rows_of(index), :], (((1,), (1,)), ((), ())),
                preferred_element_type=jnp.float32,
            )

        for i in range(2):
            to_core[s, i] = projected(order[i] * 2 + 1 - core).astype(bf16)
            pending.append(
                send(to_core.at[s, i], core_in.at[s, i], cs.at[s, i], cr.at[s, i], mate)
            )
        keep[s, 0] = projected(order[0] * 2 + core)
        keep[s, 1] = projected(order[1] * 2 + core)

    def across_core(s):
        arrived(core_in.at[s, 0], cs.at[s, 0], cr.at[s, 0], mate)
        far_out[s] = (keep[s, 0] + f32(core_in[s, 0])).astype(bf16)
        pending.append(send(far_out.at[s], far_in.at[s], fs.at[s], fr.at[s], far))

    trio = [mate, far, cross]

    def residual(s):
        mine = pl.ds(s * span, span)
        arrived(core_in.at[s, 1], cs.at[s, 1], cr.at[s, 1], mate)
        near = f32(own_tokens[mine]) + (keep[s, 1] + f32(core_in[s, 1]))
        arrived(far_in.at[s], fs.at[s], fr.at[s], far)
        rounded = (near + f32(far_in[s])).astype(bf16)
        hidden[mine] = rounded
        wide = f32(rounded)
        own = jnp.broadcast_to(jnp.sum(wide * wide, axis=1, keepdims=True), (span, width))
        blank = jnp.zeros((span, width), jnp.float32)
        squares[s] = jnp.concatenate([blank] * s + [own] + [blank] * (seqs - 1 - s), axis=0).T[:8]
        for i in range(3):
            pending.append(
                send(squares.at[s], squares_in.at[s, i], qs.at[s, i], qr.at[s, i], trio[i])
            )
        spread[z, mine] = (wide * gain[1, tensor]).astype(bf16)
        ring_on(s, 1)

    bits = 2
    fine = span // bits

    def ring_on(s, step):
        for bit in range(bits):
            for direction in range(2):
                if 1 < step <= half or (step > half and direction == s):
                    block = spot(direction, step - 1, s, bit)
                    index = bits * (step - 2) + bit
                    arrived(
                        block, hs.at[direction, index, s], hr.at[direction, index, s],
                        ring[direction],
                    )
                if step < half or (step == half and direction == s):
                    block = spot(direction, step - 1, s, bit)
                    index = bits * (step - 1) + bit
                    pending.append(
                        send(
                            block, block, hs.at[direction, index, s], hr.at[direction, index, s],
                            ring[direction],
                        )
                    )

    def spot(direction, steps, s, bit):
        origin = lax.rem(z + (NZ - steps if direction == 0 else steps), NZ)
        return spread.at[origin, pl.ds(s * span + bit * fine, fine)]

    def share_root(s):
        total = squares[s]
        for i in range(3):
            arrived(squares_in.at[s, i], qs.at[s, i], qr.at[s, i], trio[i])
            total = total + squares_in[s, i]
        lane = lax.broadcasted_iota(jnp.int32, total.shape, 1)
        ours = (lane >= s * span) & (lane < (s + 1) * span)
        roots[z, s] = jnp.where(ours, lax.rsqrt(total / (4 * quarter) + EPSILON), 0.0)
        block = roots.at[z, s]
        for d in range(1, NZ):
            pending.append(send(block, block, rs.at[s, d - 1], rr.at[s, d - 1], z_peers[d - 1]))

    near_first = [(0, NZ - 1), (1, NZ - 2), (2, NZ - 3), (3, 4)]
    def last(part):
        for direction in range(2):
            got(part, direction, half, direction)

    def second():
        step_on(0, 4)
        step_on(1, 2)

    def fourth():
        last(0)
        step_on(1, 4)

    nothing = lambda: None
    chunks = [functools.partial(old_chunk, offsets=pair) for pair in near_first] + [new_chunk]
    gates = [
        [nothing, second, lambda: step_on(1, 3), fourth, lambda: last(1)],
        [
            nothing,
            loads[2].wait,
            lambda: combine(0),
            lambda: across_core(0),
            lambda: residual(0),
        ],
    ]
    attend(chunks, gates, finish)
    ring_on(0, 2)
    combine(1)
    ring_on(0, 3)
    across_core(1)
    ring_on(0, 4)
    share_root(0)
    residual(1)
    ring_on(0, 5)
    for step in range(2, half + 2):
        ring_on(1, step)
        if step == 3:
            share_root(1)
    for s in range(seqs):
        for d in range(1, NZ):
            arrived(
                roots.at[lax.rem(z + NZ - d, NZ), s], rs.at[s, d - 1], rr.at[s, d - 1], z_peers[d - 1]
            )
    for d in range(1, NZ):
        arrived(
            slab_all.at[lax.rem(z + NZ - d, NZ)], ts.at[d - 1], tr.at[d - 1], z_peers[d - 1]
        )
    for copy in pending:
        copy.wait_send()


def attention(
    scale, capacity, own_tokens, gain, cosine, sine, cache, routed, weights, prefix,
    w_query, w_keyval, w_out,
):
    seqs, cache_rows, width = cache.shape
    rows, quarter = own_tokens.shape
    span, head = rows // seqs, width // 2
    cols = w_query.shape[1] // head * span
    vmem = pl.BlockSpec(memory_space=pltpu.VMEM)
    any_space = pl.BlockSpec(memory_space=pl.ANY)
    bf16, wide, sem = jnp.bfloat16, jnp.float32, pltpu.SemaphoreType.DMA
    return pl.pallas_call(
        functools.partial(attention_kernel, scale, capacity),
        out_shape=(
            jax.ShapeDtypeStruct((seqs, span, width), bf16),
            jax.ShapeDtypeStruct((rows, quarter), bf16),
            jax.ShapeDtypeStruct((NZ, rows, quarter), bf16),
            jax.ShapeDtypeStruct((NZ, seqs, 8, rows), wide),
            jax.ShapeDtypeStruct((NZ, NY * NX, 256), wide),
        ),
        in_specs=[vmem] * 7 + [pl.BlockSpec(memory_space=pltpu.SMEM)] + [any_space] * 3,
        out_specs=(vmem,) * 5,
        scratch_shapes=[
            pltpu.VMEM(w_query.shape, bf16),
            pltpu.VMEM(w_keyval.shape, bf16),
            pltpu.VMEM(w_out.shape, bf16),
            pltpu.VMEM((4, rows, quarter), bf16),
            pltpu.VMEM((NY * NZ, seqs, cache_rows, width), bf16),
            pltpu.VMEM((NY * NZ, seqs, span, width), bf16),
            pltpu.VMEM((NX, seqs, head, cols), bf16),
            pltpu.VMEM((seqs, NX, 2 * width, cols), bf16),
            pltpu.VMEM((NX, 1, cols), wide),
            pltpu.VMEM((NX, 16 + head, cols), wide),
            pltpu.VMEM((seqs, NX, head, cols), bf16),
            pltpu.VMEM((seqs, NX, 8, cols), wide),
            pltpu.VMEM((seqs, NX - 1, head, cols), bf16),
            pltpu.VMEM((seqs, NX - 1, 8, cols), wide),
            pltpu.VMEM((seqs, 2, span, quarter), bf16),
            pltpu.VMEM((seqs, 2, span, quarter), bf16),
            pltpu.VMEM((seqs, 2, span, quarter), wide),
            pltpu.VMEM((seqs, span, quarter), bf16),
            pltpu.VMEM((seqs, span, quarter), bf16),
            pltpu.VMEM((seqs, 8, rows), wide),
            pltpu.VMEM((seqs, 3, 8, rows), wide),
            pltpu.VMEM((NZ, NY * NX, 256), wide),
            sem((3,)),
            sem((3,)),
            sem((3,)),
            sem((seqs, NX - 1)),
            sem((seqs, NX - 1)),
            sem((2,)),
            sem((2,)),
            sem((2, 2, NZ)),
            sem((2, 2, NZ)),
            sem((NZ - 1,)),
            sem((NZ - 1,)),
            sem((seqs, NX - 1)),
            sem((seqs, NX - 1)),
            sem((seqs, NX - 1)),
            sem((seqs, NX - 1)),
            sem((seqs, 2)),
            sem((seqs, 2)),
            sem((seqs,)),
            sem((seqs,)),
            sem((seqs, 3)),
            sem((seqs, 3)),
            sem((2, NZ, seqs)),
            sem((2, NZ, seqs)),
            sem((seqs, NZ - 1)),
            sem((seqs, NZ - 1)),
        ],
        compiler_params=pltpu.CompilerParams(
            collective_id=0, has_side_effects=True, vmem_limit_bytes=60 * 1024 * 1024
        ),
        name="attention",
    )(
        own_tokens, gain, cosine, sine, cache, routed, weights, prefix, w_query, w_keyval, w_out
    )


def expert_kernel(
    capacity, slab, source, roots, hidden, up_hbm, down_hbm, out,
    rows, sel, held, up_raw, down_raw, up, down, slot_of, weight_of, root_of, shares,
    mine0, mine1, to_mate0, to_mate1, core_in0, core_in1, side_in0, side_in1, x_out0, x_out1,
    back0, back1, sums0, sums1, staged0, staged1, landed0, landed1,
    ws, xs, xr, ys, yr, fs, fr, cs, cr, bs, br, es, er, zs, zr,
):
    mine, to_mate, core_in = (mine0, mine1), (to_mate0, to_mate1), (core_in0, core_in1)
    side_in, x_out, back = (side_in0, side_in1), (x_out0, x_out1), (back0, back1)
    sums, staged, landed = (sums0, sums1), (staged0, staged1), (landed0, landed1)
    rank, tensor = lax.axis_index("expert"), lax.axis_index("tensor")
    y_lo, x, z, y_hi, core, far, sides, mate = corner(rank, tensor)
    other = 1 - y_lo
    x_peers = [(rank_of(y_lo, lax.rem(x + d, NX), z), tensor) for d in range(1, NX)]
    ring = [
        (rank_of(y_lo, x, lax.rem(z + 1, NZ)), tensor),
        (rank_of(y_lo, x, lax.rem(z + NZ - 1, NZ)), tensor),
    ]
    greet(x_peers + [far] + sides + [mate] + ring)
    pending = []
    loads = [
        pltpu.make_async_copy(up_hbm, up_raw, ws.at[0]),
        pltpu.make_async_copy(down_hbm, down_raw, ws.at[1]),
    ]
    for load in loads:
        load.start()
    size, width = sel.shape[2:]
    quarters = rows.shape[0]
    count = hidden.shape[0]
    bf16 = jnp.bfloat16
    cuts = (slice(0, mine0.shape[3]), slice(mine0.shape[3], width))

    at = lax.broadcasted_iota(jnp.int32, (size, count), 0)
    lane = lax.broadcasted_iota(jnp.int32, (size, count), 1)
    block_of = jnp.zeros((size, count), jnp.int32)
    for b in range(1, NZ):
        block_of = block_of + jnp.where(at >= b * capacity, 1, 0)
    ours = lane == at - block_of * capacity
    lane_f = f32(lane)

    def by_block(pieces):
        value = jnp.zeros((size, count), jnp.float32)
        for b in range(NZ):
            value = jnp.where(block_of == b, pieces[b], value)
        return value

    root_rows = by_block([roots[b, 0, 0:1, :] + roots[b, 1, 0:1, :] for b in range(NZ)])
    first = f32(block_of[:, 0:1] * count)

    def total_of(mask, value):
        return jnp.sum(jnp.where(mask, value, 0.0), axis=1, keepdims=True)

    for j in range(NY * NX):
        token = total_of(ours, by_block([slab[b, j : j + 1, :count] for b in range(NZ)]))
        weight_of[j] = total_of(ours, by_block([slab[b, j : j + 1, count:] for b in range(NZ)]))
        root_of[j] = total_of(lane_f == token, root_rows)
        slot_of[j] = jnp.where(token >= 0.0, token + first, -1.0)
    lanes = f32(lax.broadcasted_iota(jnp.int32, (size, source.shape[0]), 1))

    def pick(side, to):
        j = side * NX + to
        chosen = jnp.where(lanes == slot_of[j], 1.0, 0.0).astype(bf16)
        picked = jnp.dot(chosen, source[...], preferred_element_type=jnp.float32)
        return (picked * root_of[j]).astype(bf16)

    def to_side(d, here, there):
        spot = rows.at[tensor, y_lo, lax.rem(x + NX - d, NX)]
        for r in range(2):
            pending.append(send(there, spot, ys.at[d, r], yr.at[d, r], sides[r]))
        pending.append(send(here, spot, ys.at[d, 2], yr.at[d, 2], far))

    def forward(d, r, l):
        x_s = lax.rem(x + NX - d, NX)
        spot = rows.at[lax.rem(y_hi + r, 2) * 2 + core, lax.rem(y_lo + l, 2), x_s]
        index = 2 * r + l
        pending.append(send(spot, spot, fs.at[d, index], fr.at[d, index], mate))

    def from_sides(d):
        x_s = lax.rem(x + NX - d, NX)
        for r in range(2):
            spot = rows.at[lax.rem(y_hi + r, 2) * 2 + core, other, x_s]
            arrived(spot, ys.at[d, r], yr.at[d, r], sides[r])
            forward(d, r, 1)
        spot = rows.at[(1 - y_hi) * 2 + core, y_lo, x_s]
        arrived(spot, ys.at[d, 2], yr.at[d, 2], far)
        forward(d, 1, 0)

    def from_mate(d):
        x_s = lax.rem(x + NX - d, NX)
        for r in range(2):
            for l in range(2):
                spot = rows.at[lax.rem(y_hi + r, 2) * 2 + 1 - core, lax.rem(y_lo + l, 2), x_s]
                arrived(spot, fs.at[d, 2 * r + l], fr.at[d, 2 * r + l], mate)

    units, real = down.shape[1], down_raw.shape[0]

    def run(d):
        x_s = lax.rem(x + NX - d, NX)
        total = jnp.zeros((2 * size, 2 * units), jnp.float32)
        for q in range(quarters):
            block = jnp.concatenate([rows[q, other, x_s], rows[q, y_lo, x_s]], axis=0)
            total += lax.dot_general(
                block, up[q], (((1,), (1,)), ((), ())), preferred_element_type=jnp.float32
            )
        gate, raised = total[:, :units], total[:, units:]
        active = (gate * jax.nn.sigmoid(1.702 * gate) * (raised + 1.0)).astype(bf16)
        for f in range(2):
            for h in range(2):
                half = lax.rem(y_hi + h, 2)
                for owner in range(2):
                    index = half * 2 + (core if owner else 1 - core)
                    value = jnp.dot(
                        active, down[index, :, cuts[f]], preferred_element_type=jnp.float32
                    ).astype(bf16)
                    into = mine[f] if owner else to_mate[f]
                    into[d, h] = value[:size]
                    into[d, 3 - h] = value[size:]
                    if not owner:
                        for kind in (h, 3 - h):
                            pending.append(
                                send(
                                    into.at[d, kind], core_in[f].at[d, kind],
                                    cs.at[f, d, kind], cr.at[f, d, kind], mate,
                                )
                            )

    def back_to_sides(f, d):
        for kind in range(4):
            arrived(core_in[f].at[d, kind], cs.at[f, d, kind], cr.at[f, d, kind], mate)
            both = f32(mine[f][d, kind]) + f32(core_in[f][d, kind])
            mine[f][d, kind] = both.astype(bf16)
            if kind < 3:
                to = far if kind == 2 else sides[kind]
                pending.append(
                    send(
                        mine[f].at[d, kind], side_in[f].at[d, kind],
                        bs.at[f, d, kind], br.at[f, d, kind], to,
                    )
                )

    def spot_of(f, owner, at_x):
        return back[f].at[owner * NX + at_x]

    def back_to_x(f, d):
        for kind in range(3):
            to = far if kind == 2 else sides[kind]
            arrived(side_in[f].at[d, kind], bs.at[f, d, kind], br.at[f, d, kind], to)
            if kind == 0:
                continue
            near = side_in[f][d, 0] if kind == 1 else mine[f][d, 3]
            both = (f32(near) + f32(side_in[f][d, kind])).astype(bf16)
            i = kind - 1
            owner = other if kind == 1 else y_lo
            if d == 0:
                back[f][owner * NX + x] = both
            else:
                e = NX - d - 1
                x_out[f][d - 1, i] = both
                pending.append(
                    send(
                        x_out[f].at[d - 1, i], spot_of(f, owner, x),
                        es.at[f, e, i], er.at[f, e, i], x_peers[e],
                    )
                )

    def from_x_back(f):
        for d in range(1, NX):
            x_e = lax.rem(x + NX - d, NX)
            for i in range(2):
                owner = other if i == 0 else y_lo
                arrived(
                    spot_of(f, owner, x_e), es.at[f, d - 1, i], er.at[f, d - 1, i], x_peers[d - 1]
                )

    half_rows, half = count // 2, NZ // 2

    def add_up(f, steps):
        value = jnp.dot(
            shares[steps],
            back[f][...].reshape(NY * NX * size, back[f].shape[2]),
            preferred_element_type=jnp.float32,
        )
        sums[f][steps] = value.astype(bf16)

    def reach(direction, piece):
        return half if direction == piece else half - 1

    def got(f, direction, steps, piece):
        index = 2 * steps + piece
        arrived(
            landed[f].at[direction, index], zs.at[f, direction, index], zr.at[f, direction, index],
            ring[direction],
        )
        return f32(landed[f][direction, index])

    def toward(f, steps):
        add_up(f, steps)
        if steps < half:
            add_up(f, NZ - steps)
        for piece in range(2):
            for direction in range(2):
                if steps > reach(direction, piece):
                    continue
                home = steps if direction == 0 else NZ - steps
                value = f32(sums[f][home, pl.ds(piece * half_rows, half_rows)])
                if steps < reach(direction, piece):
                    value = value + got(f, direction, steps, piece)
                index = 2 * (steps - 1) + piece
                staged[f][direction, index] = value.astype(bf16)
                pending.append(
                    send(
                        staged[f].at[direction, index], landed[f].at[direction, index],
                        zs.at[f, direction, index], zr.at[f, direction, index], ring[direction],
                    )
                )
        if steps == 1:
            add_up(f, 0)

    def arrive_home(f):
        for piece in range(2):
            span = pl.ds(piece * half_rows, half_rows)
            value = f32(sums[f][0, span])
            for direction in range(2):
                value = value + got(f, direction, 0, piece)
            out[span, cuts[f]] = (f32(hidden[span, cuts[f]]) + value).astype(bf16)

    sel[other, x] = pick(other, x)
    rows[tensor, y_lo, x] = pick(y_lo, x)
    to_side(0, rows.at[tensor, y_lo, x], sel.at[other, x])
    for d in (1, 3, 2):
        to = lax.rem(x + d, NX)
        for i in range(2):
            side = other if i == 0 else y_lo
            sel[side, to] = pick(side, to)
            dst = held.at[x] if i == 0 else rows.at[tensor, y_lo, x]
            pending.append(
                send(sel.at[side, to], dst, xs.at[d - 1, i], xr.at[d - 1, i], x_peers[d - 1])
            )
    forward(0, 0, 0)
    blank = jnp.zeros((units - real, width), bf16)
    for load in loads:
        load.wait()
    for q in range(quarters):
        span = slice(q * width, (q + 1) * width)
        for i in range(2):
            up[q, i * units : i * units + real, :] = up_raw[i, :, span]
            up[q, i * units + real : (i + 1) * units, :] = blank
        down[q, :real, :] = down_raw[:, span]
        down[q, real:, :] = blank

    def from_x(d):
        x_s = lax.rem(x + NX - d, NX)
        arrived(held.at[x_s], xs.at[d - 1, 0], xr.at[d - 1, 0], x_peers[d - 1])
        arrived(rows.at[tensor, y_lo, x_s], xs.at[d - 1, 1], xr.at[d - 1, 1], x_peers[d - 1])
        to_side(d, rows.at[tensor, y_lo, x_s], held.at[x_s])
        forward(d, 0, 0)

    from_x(1)
    from_x(3)
    from_sides(0)
    from_x(2)
    wide_lane = f32(lax.broadcasted_iota(jnp.int32, (size, count), 1))
    for steps in range(NZ):
        start = f32(jnp.full((size, count), lax.rem(z + steps, NZ) * count, jnp.int32))
        flipped = [
            jnp.where(wide_lane + start == slot_of[j], weight_of[j], 0.0) for j in range(NY * NX)
        ]
        shares[steps] = jnp.concatenate(flipped, axis=0).T.astype(bf16)
    for d in (0, 1, 3, 2):
        if d:
            from_sides(d)
        from_mate(d)
        run(d)
        if d in (1, 3):
            back_to_sides(0, d)
    back_to_sides(0, 2)
    back_to_sides(0, 0)
    for d in (1, 3, 2, 0):
        back_to_sides(1, d)
    for d in (1, 3, 2, 0):
        back_to_x(0, d)
    from_x_back(0)
    for steps, d in zip(range(half, 0, -1), (1, 3, 2, 0)):
        toward(0, steps)
        back_to_x(1, d)
    arrive_home(0)
    from_x_back(1)
    for steps in range(half, 0, -1):
        toward(1, steps)
    arrive_home(1)
    for copy in pending:
        copy.wait_send()


def run_experts(capacity, slab, source, roots, hidden, up, down):
    count, width = hidden.shape
    size = NZ * capacity
    quarters = down.shape[1] // width
    units = -(-down.shape[0] // 128) * 128
    vmem = pl.BlockSpec(memory_space=pltpu.VMEM)
    any_space = pl.BlockSpec(memory_space=pl.ANY)
    bf16, sem, wide = jnp.bfloat16, pltpu.SemaphoreType.DMA, jnp.float32
    cut = -(-width // 256) * 128
    parts = (cut, width - cut)
    groups = NY * NX

    def pair(*lead):
        return [pltpu.VMEM(lead + (part,), bf16) for part in parts]

    return pl.pallas_call(
        functools.partial(expert_kernel, capacity),
        out_shape=jax.ShapeDtypeStruct((count, width), bf16),
        in_specs=[vmem] * 4 + [any_space] * 2,
        out_specs=vmem,
        scratch_shapes=[
            pltpu.VMEM((quarters, NY, NX, size, width), bf16),
            pltpu.VMEM((NY, NX, size, width), bf16),
            pltpu.VMEM((NX, size, width), bf16),
            pltpu.VMEM(up.shape, bf16),
            pltpu.VMEM(down.shape, bf16),
            pltpu.VMEM((quarters, 2 * units, width), bf16),
            pltpu.VMEM((quarters, units, width), bf16),
            pltpu.VMEM((groups, size, 1), wide),
            pltpu.VMEM((groups, size, 1), wide),
            pltpu.VMEM((groups, size, 1), wide),
            pltpu.VMEM((NZ, count, groups * size), bf16),
            *pair(NX, 4, size),
            *pair(NX, 4, size),
            *pair(NX, 4, size),
            *pair(NX, 3, size),
            *pair(NX - 1, 2, size),
            *pair(groups, size),
            *pair(NZ, count),
            *pair(2, NZ, count // 2),
            *pair(2, NZ, count // 2),
            sem((2,)),
            sem((NX - 1, 2)),
            sem((NX - 1, 2)),
            sem((NX, 3)),
            sem((NX, 3)),
            sem((NX, 4)),
            sem((NX, 4)),
            sem((2, NX, 4)),
            sem((2, NX, 4)),
            sem((2, NX, 3)),
            sem((2, NX, 3)),
            sem((2, NX - 1, 2)),
            sem((2, NX - 1, 2)),
            sem((2, 2, NZ)),
            sem((2, 2, NZ)),
        ],
        compiler_params=pltpu.CompilerParams(
            collective_id=3, has_side_effects=True, vmem_limit_bytes=62 * 1024 * 1024
        ),
        name="run_experts",
    )(slab, source, roots, hidden, up, down)


def on_device(
    tokens,
    attn_gain,
    w_query,
    key_value_weight,
    w_out,
    cache_keyval,
    prefix_length,
    routed_experts,
    route_weights,
    expert_gain,
    w_gate_up,
    w_down,
):
    span_dev, seq_count, quarter = tokens.shape
    model_width = attn_gain.shape[0]
    row_count = span_dev * seq_count
    head_dim = key_value_weight.shape[2] // 2
    cache_rows = cache_keyval.shape[0]
    expert_rank = lax.axis_index("expert")
    quarters = model_width // quarter
    top_count = routed_experts.shape[2]
    expert_count = lax.axis_size("expert")
    capacity = min(row_count, max(2, 5 * row_count * top_count // (2 * expert_count)))
    half_dim = head_dim // 2
    steps_up = jnp.arange(half_dim, dtype=jnp.float32)
    frequency = jnp.exp(steps_up * (-math.log(ROPE_BASE) / half_dim))
    span_place = expert_rank * span_dev + jnp.arange(span_dev, dtype=jnp.int32)
    places = (prefix_length[:, None] + span_place[None, :]).reshape(row_count).astype(jnp.float32)
    angles = frequency[:, None] * places[None, :]
    own_tokens = tokens.transpose(1, 0, 2).reshape(row_count, quarter)
    fresh, hidden, spread, roots, slab_all = attention(
        head_dim ** (-0.5) * LOG2E,
        capacity,
        own_tokens,
        jnp.stack([attn_gain, expert_gain]).reshape(2, quarters, 1, quarter),
        jnp.cos(angles),
        jnp.sin(angles),
        cache_keyval[:, :, 0, :].transpose(1, 0, 2),
        routed_experts.transpose(1, 2, 0),
        route_weights.transpose(1, 2, 0),
        prefix_length,
        w_query,
        key_value_weight[:, 0, :],
        w_out.T,
    )
    new_key_value_rows = fresh.transpose(1, 0, 2)[:, :, None, :]
    layer_output = run_experts(
        capacity,
        slab_all,
        spread.reshape(NZ * row_count, quarter),
        roots,
        hidden,
        w_gate_up[0].transpose(1, 2, 0),
        w_down[0],
    )
    layer_output = layer_output.reshape(seq_count, span_dev, quarter).transpose(1, 0, 2)
    return (layer_output, new_key_value_rows)


def solution(mesh):
    return jax.shard_map(
        on_device,
        mesh=mesh,
        in_specs=(
            P("expert", None, "tensor"),
            P(),
            P(None, "tensor"),
            P(None, "tensor", None),
            P("tensor", None),
            P("expert", None, "tensor", None),
            P(),
            P("expert", None, None),
            P("expert", None, None),
            P(),
            P("expert", None, None, "tensor"),
            P("expert", "tensor", None),
        ),
        out_specs=(P("expert", None, "tensor"), P("expert", None, "tensor", None)),
        check_vma=False,
    )
```

```python
import functools
import math

import jax
import jax.numpy as jnp
from jax import lax
from jax.experimental import pallas as pl
from jax.experimental.pallas import tpu as pltpu
from jax.sharding import PartitionSpec as P

EPSILON = 1e-05
ROPE_BASE = 150000.0
NEG = -1e30
MESH = pl.DeviceIdType.MESH
NY, NX, NZ = 2, 4, 8
LOG2E = 1.4426950408889634


def place_of(expert_rank):
    return expert_rank // (NX * NZ), (expert_rank // NZ) % NX, expert_rank % NZ


def rank_of(y_lo, x, z):
    return (y_lo * NX + x) * NZ + z


def greet(devices):
    barrier = pltpu.get_barrier_semaphore()
    for device in devices:
        pl.semaphore_signal(barrier, inc=1, device_id=device, device_id_type=MESH)
    pl.semaphore_wait(barrier, len(devices))


def send(src, dst, send_sem, recv_sem, device):
    copy = pltpu.make_async_remote_copy(
        src_ref=src,
        dst_ref=dst,
        send_sem=send_sem,
        recv_sem=recv_sem,
        device_id=device,
        device_id_type=MESH,
    )
    copy.start()
    return copy


def arrived(dst, send_sem, recv_sem, device):
    pltpu.make_async_remote_copy(
        src_ref=dst,
        dst_ref=dst,
        send_sem=send_sem,
        recv_sem=recv_sem,
        device_id=device,
        device_id_type=MESH,
    ).wait_recv()


def swap_blocks(value):
    half = value.shape[0] // 2
    top, bottom = value[:half], value[half:]
    left = lax.broadcasted_iota(jnp.int32, top.shape, 1) < half
    return jnp.concatenate(
        [
            jnp.where(left, top, pltpu.roll(bottom, half, 1)),
            jnp.where(left, pltpu.roll(top, half, 1), bottom),
        ],
        axis=0,
    )


def turn(first, second, cosine, sine):
    return first * cosine - second * sine, second * cosine + first * sine


def corner(rank, tensor):
    y_lo, x, z = place_of(rank)
    y_hi, core = tensor // 2, lax.rem(tensor, 2)
    far = (rank, (1 - y_hi) * 2 + core)
    sides = [(rank_of(1 - y_lo, x, z), lax.rem(y_hi + r, 2) * 2 + core) for r in range(2)]
    mate = (rank, y_hi * 2 + 1 - core)
    return y_lo, x, z, y_hi, core, far, sides, mate


def f32(value):
    return value.astype(jnp.float32)


def route(capacity, routed, weights, slab):
    planes, groups, _ = slab.shape
    experts = planes * groups
    seqs, top_count, count = routed.shape
    row = lax.broadcasted_iota(jnp.int32, (experts, count), 0)
    lane = lax.broadcasted_iota(jnp.int32, (experts, count), 1)
    expert = lax.rem(row, groups) * planes + row // groups
    before = jnp.where(
        lax.broadcasted_iota(jnp.int32, (count, count), 0)
        < lax.broadcasted_iota(jnp.int32, (count, count), 1),
        1.0,
        0.0,
    ).astype(jnp.bfloat16)
    earlier = jnp.zeros((experts, 1), jnp.float32)
    named = []
    for s in range(seqs):
        for k in range(top_count):
            hit = jnp.where(expert == routed[s, k : k + 1, :], 1.0, 0.0)
            ahead = jnp.dot(hit.astype(jnp.bfloat16), before, preferred_element_type=jnp.float32)
            arrival = jnp.where(hit > 0.0, ahead + earlier, -1.0)
            named.append((arrival, f32(lane + s * count + 1), weights[s, k : k + 1, :]))
            earlier = earlier + jnp.sum(hit, axis=1, keepdims=True)
    slot = lax.broadcasted_iota(jnp.int32, (experts, 128), 1)

    def fill(place, carry):
        tokens, scales = carry
        token = jnp.zeros((experts, count), jnp.float32)
        scale = jnp.zeros((experts, count), jnp.float32)
        for arrival, number, share in named:
            here = arrival == f32(place)
            token = jnp.where(here, number, token)
            scale = jnp.where(here, share, scale)
        return (
            jnp.where(slot == place, jnp.sum(token, axis=1, keepdims=True) - 1.0, tokens),
            jnp.where(slot == place, jnp.sum(scale, axis=1, keepdims=True), scales),
        )

    empty = jnp.full((experts, 128), -1.0, jnp.float32)
    tokens, scales = lax.fori_loop(0, capacity, fill, (empty, jnp.zeros_like(empty)))
    slab[:, :, :128] = tokens.reshape(planes, groups, 128)
    slab[:, :, 128:] = scales.reshape(planes, groups, 128)


def attention_kernel(
    scale, capacity, own_tokens, gain, out_gain, cosine, sine, cache, routed, weights, prefix, w_query_hbm, w_keyval_hbm, w_out_hbm,
    fresh, hidden, spread, roots, slab_all,
    w_query, w_keyval, w_out, gathered, kv_old, kv_new, q_all, qa, tops, sums, o_out, stat_out,
    o_in, stat_in, to_core, core_in, keep, far_out, far_in, squares, squares_in,
    slab, gains, ws, gs, gr, xs, xr, ys, yr, zs, zr, ts, tr, os, orr, ss, sr, cs, cr, fs, fr, qs, qr, hs, hr, rs, rr,
):
    rank, tensor = lax.axis_index("expert"), lax.axis_index("tensor")
    y_lo, x, z, y_hi, core, far, sides, mate = corner(rank, tensor)
    other = 1 - y_lo
    rows, quarter = own_tokens.shape
    seqs, span, width = fresh.shape
    cache_rows, head = cache.shape[1], width // 2
    cols = q_all.shape[3]
    bf16 = jnp.bfloat16
    x_peers = [(rank_of(y_lo, lax.rem(x + d, NX), z), tensor) for d in range(1, NX)]
    y_peer = (rank_of(other, x, z), tensor)
    z_peers = [(rank_of(y_lo, x, lax.rem(z + d, NZ)), tensor) for d in range(1, NZ)]
    ring = [z_peers[0], z_peers[-1]]
    cross = (rank, (1 - y_hi) * 2 + 1 - core)
    greet(x_peers + [y_peer] + z_peers + [far, mate, cross])
    pending = []
    loads = [
        pltpu.make_async_copy(src, dst, ws.at[i])
        for i, (src, dst) in enumerate(
            [(w_query_hbm, w_query), (w_keyval_hbm, w_keyval), (w_out_hbm, w_out)]
        )
    ]
    for load in loads:
        load.start()
    half = NZ // 2
    stores = (kv_old, kv_new)

    def slot(part, direction, steps, piece):
        origin = lax.rem(z + (NZ - steps if direction == 0 else steps), NZ)
        return stores[part].at[origin * 2 + (y_lo if piece == 0 else other)]

    def sems(part, direction, step, piece):
        index = 2 * (step - 1) + piece
        return zs.at[part, direction, index], zr.at[part, direction, index]

    def pass_on(part, direction, step, piece):
        block = slot(part, direction, step - 1, piece)
        pending.append(send(block, block, *sems(part, direction, step, piece), ring[direction]))

    def got(part, direction, step, piece):
        arrived(
            slot(part, direction, step, piece), *sems(part, direction, step, piece), ring[direction]
        )

    def begin(part):
        block = slot(part, 0, 0, 0)
        pending.append(send(block, block, ys.at[part], yr.at[part], y_peer))
        for direction in range(2):
            pass_on(part, direction, 1, 0)

    def begin_other(part):
        arrived(slot(part, 0, 0, 1), ys.at[part], yr.at[part], y_peer)
        for direction in range(2):
            pass_on(part, direction, 1, 1)

    def step_on(part, step):
        for piece in range(2):
            for direction in range(2):
                got(part, direction, step - 1, piece)
                if step < half or direction == piece:
                    pass_on(part, direction, step, piece)

    mine = gathered.at[tensor]
    pending.append(send(own_tokens, mine, gs.at[0], gr.at[0], far))
    pending.append(send(own_tokens, mine, gs.at[1], gr.at[1], mate))
    kv_old[z * 2 + y_lo] = cache[...]
    begin(0)
    far_index, mate_index = (1 - y_hi) * 2 + core, y_hi * 2 + 1 - core
    cross_index = (1 - y_hi) * 2 + 1 - core

    for q in range(4):
        gains[0, q] = gain[:, q * quarter : (q + 1) * quarter]
        gains[1, q] = out_gain[:, q * quarter : (q + 1) * quarter]

    def rows_of(index):
        return pl.ds(pl.multiple_of(index * quarter, 16), quarter)

    def project(index, block):
        wide = f32(block)
        scaled = (wide * gains[0, index]).astype(bf16)
        return (
            jnp.dot(scaled, w_query[rows_of(index), :], preferred_element_type=jnp.float32),
            jnp.dot(scaled, w_keyval[rows_of(index), :], preferred_element_type=jnp.float32),
            jnp.sum(wide * wide, axis=1, keepdims=True),
        )

    loads[0].wait()
    loads[1].wait()
    def add_to(total, index):
        return [a + b for a, b in zip(total, project(index, gathered[index]))]

    total = project(tensor, own_tokens[...])
    arrived(gathered.at[mate_index], gs.at[1], gr.at[1], mate)
    total = add_to(total, mate_index)
    begin_other(0)
    route(capacity, routed, weights, slab)
    slab_all[z] = slab[z]
    arrived(gathered.at[far_index], gs.at[0], gr.at[0], far)
    block = gathered.at[far_index]
    pending.append(send(block, block, gs.at[2], gr.at[2], mate))
    for d in range(1, NZ):
        to = lax.rem(z + d, NZ)
        pending.append(
            send(slab.at[to], slab_all.at[z], ts.at[d - 1], tr.at[d - 1], z_peers[d - 1])
        )
    total = add_to(total, far_index)
    arrived(gathered.at[cross_index], gs.at[2], gr.at[2], mate)
    total = add_to(total, cross_index)
    root = lax.rsqrt(total[2] / (4 * quarter) + EPSILON)
    cos, sin = cosine[...], sine[...]
    flipped = (total[1] * root).T
    keys = turn(flipped[: head // 2], flipped[head // 2 : head], cos, sin)
    whole = jnp.concatenate([keys[0], keys[1], flipped[head:]], axis=0).T
    own_rows = whole.astype(bf16).reshape(fresh.shape)
    fresh[...] = own_rows
    kv_new[z * 2 + y_lo] = own_rows
    begin(1)
    step_on(0, 2)
    raw = total[0] * root
    for j in range(raw.shape[1] // width):
        pair = raw[:, j * width : (j + 1) * width].T
        turned = []
        for h in range(2):
            block = pair[h * head : (h + 1) * head]
            turned += turn(block[: head // 2], block[head // 2 :], cos, sin)
        first = swap_blocks(jnp.concatenate(turned, axis=0) * scale).astype(bf16)
        for s in range(seqs):
            q_all[0, s, :, j * width : (j + 1) * width] = first[s * head : (s + 1) * head]
    for s in range(seqs):
        for d in (1, 3, 2):
            src, dst = q_all.at[0, s], q_all.at[NX - d, s]
            pending.append(send(src, dst, xs.at[s, d - 1], xr.at[s, d - 1], x_peers[d - 1]))
    begin_other(1)

    row = lax.broadcasted_iota(jnp.int32, (width, cols), 0)
    lane = lax.broadcasted_iota(jnp.int32, (width, cols), 1)
    for k in range(NX):
        hot = (row == span + lax.rem(x + k, NX)) | (row == span + NX)
        if k == 0:
            hot = hot | (row == lax.rem(lane, span))
        for s in range(seqs):
            qa[s, k, head:width, :] = jnp.zeros((width - head, cols), bf16)
            qa[s, k, width:, :] = jnp.where(hot, 1.0, 0.0).astype(bf16)

    def old_chunk(s, offsets):
        values, masks = [], []
        old_row = lax.broadcasted_iota(jnp.int32, (cache_rows, width), 0)
        marked = lax.broadcasted_iota(jnp.int32, (cache_rows, width), 1) == span + NX
        for offset in offsets:
            origin = lax.rem(z + offset, NZ)
            for side in range(NY):
                values.append(kv_old[origin * 2 + side, s])
                place = old_row + rank_of(side, x, origin) * cache_rows
                masks.append(
                    jnp.where(marked & (place >= prefix[s]), NEG, 0.0).astype(bf16)
                )
        return jnp.concatenate(values, axis=0), jnp.concatenate(masks, axis=0)

    def new_chunk(s):
        masks = []
        new_row = lax.broadcasted_iota(jnp.int32, (span, width), 0)
        new_col = lax.broadcasted_iota(jnp.int32, (span, width), 1)
        in_block = (new_col >= span) & (new_col < span + NX)
        query_rank = rank_of(y_lo, new_col - span, z)
        later = (new_col < span) & (new_row > new_col)
        for shard in range(NY * NZ):
            key_rank = rank_of(shard % 2, x, shard // 2)
            late = in_block & (key_rank > query_rank)
            same = later & (jnp.full(later.shape, key_rank, jnp.int32) == rank)
            masks.append(jnp.where(late | same, NEG, 0.0).astype(bf16))
        return kv_new[:, s].reshape(NY * NZ * span, width), jnp.concatenate(masks, axis=0)

    def operands(keyval, mask):
        flipped = f32(keyval).T[head:].astype(bf16)
        ones = jnp.ones((16, keyval.shape[0]), bf16)
        return (
            jnp.concatenate([keyval, mask], axis=1),
            jnp.concatenate([ones, flipped], axis=0),
        )

    def attend(chunks, gates, ends):
        turns = [
            (s, c, k)
            for s in range(seqs)
            for c in range(len(chunks))
            for k in ((0, 1, 3, 2) if c == 0 else (2, 1, 3, 0))
        ]
        held = {}

        def score(turn):
            s, c, k = turn
            if (s, c) not in held:
                gates[s][c]()
                held[s, c] = operands(*chunks[c](s))
            if c == 0:
                if k:
                    e = NX - k - 1
                    arrived(q_all.at[k, s], xs.at[s, e], xr.at[s, e], x_peers[e])
                qa[s, k, :head, :] = q_all[k, s]
            return jnp.dot(held[s, c][0], qa[s, k], preferred_element_type=jnp.float32)

        ahead = score(turns[0])
        for at, (s, c, k) in enumerate(turns):
            scores = ahead
            if at + 1 < len(turns):
                ahead = score(turns[at + 1])
            top = jnp.max(scores, axis=0, keepdims=True)
            if c:
                top = jnp.maximum(top, tops[k])
            probs = jnp.exp2(scores - top).astype(bf16)
            part = jnp.dot(held[s, c][1], probs, preferred_element_type=jnp.float32)
            if c:
                part = part + sums[k] * jnp.exp2(tops[k] - top)
            sums[k] = part
            tops[k] = top
            if c == len(chunks) - 1:
                ends(s, k)

    def finish(s, k):
        value = sums[k]
        o_out[s, k] = (value[16:] / value[0:1]).astype(bf16)
        stat_out[s, k, 0:1, :] = tops[k]
        stat_out[s, k, 1:2, :] = value[0:1]
        stat_out[s, k, 2:, :] = jnp.zeros((6, cols), jnp.float32)
        if k:
            to, i = x_peers[k - 1], NX - k - 1
            pending.append(send(stat_out.at[s, k], stat_in.at[s, i], ss.at[s, i], sr.at[s, i], to))
            pending.append(send(o_out.at[s, k], o_in.at[s, i], os.at[s, i], orr.at[s, i], to))

    order = [1 - y_hi, y_hi]

    def combine(s):
        stats, values = [stat_out[s, 0]], [o_out[s, 0]]
        for i in (0, 2, 1):
            arrived(stat_in.at[s, i], ss.at[s, i], sr.at[s, i], x_peers[i])
            arrived(o_in.at[s, i], os.at[s, i], orr.at[s, i], x_peers[i])
            stats.append(stat_in[s, i])
            values.append(o_in[s, i])
        top = functools.reduce(jnp.maximum, [value[0:1] for value in stats])
        shares = [jnp.exp2(value[0:1] - top) * value[1:2] for value in stats]
        every = functools.reduce(jnp.add, shares)
        merged = functools.reduce(
            jnp.add, [f32(value) * (share / every) for value, share in zip(values, shares)]
        )
        blank = jnp.zeros((head, width), jnp.float32)
        attended = jnp.concatenate(
            [
                swap_blocks(
                    jnp.concatenate([merged[:, j * width : (j + 1) * width], blank], axis=0).T
                )[:span]
                for j in range(cols // width)
            ],
            axis=1,
        ).astype(bf16)

        def projected(index):
            return lax.dot_general(
                attended, w_out[rows_of(index), :], (((1,), (1,)), ((), ())),
                preferred_element_type=jnp.float32,
            )

        for i in range(2):
            to_core[s, i] = projected(order[i] * 2 + 1 - core).astype(bf16)
            pending.append(
                send(to_core.at[s, i], core_in.at[s, i], cs.at[s, i], cr.at[s, i], mate)
            )
        keep[s, 0] = projected(order[0] * 2 + core)
        keep[s, 1] = projected(order[1] * 2 + core)

    def across_core(s):
        arrived(core_in.at[s, 0], cs.at[s, 0], cr.at[s, 0], mate)
        far_out[s] = (keep[s, 0] + f32(core_in[s, 0])).astype(bf16)
        pending.append(send(far_out.at[s], far_in.at[s], fs.at[s], fr.at[s], far))

    trio = [mate, far, cross]

    def residual(s):
        mine = pl.ds(s * span, span)
        arrived(core_in.at[s, 1], cs.at[s, 1], cr.at[s, 1], mate)
        near = f32(own_tokens[mine]) + (keep[s, 1] + f32(core_in[s, 1]))
        arrived(far_in.at[s], fs.at[s], fr.at[s], far)
        rounded = (near + f32(far_in[s])).astype(bf16)
        hidden[mine] = rounded
        wide = f32(rounded)
        own = jnp.broadcast_to(jnp.sum(wide * wide, axis=1, keepdims=True), (span, width))
        blank = jnp.zeros((span, width), jnp.float32)
        squares[s] = jnp.concatenate([blank] * s + [own] + [blank] * (seqs - 1 - s), axis=0).T[:8]
        for i in range(3):
            pending.append(
                send(squares.at[s], squares_in.at[s, i], qs.at[s, i], qr.at[s, i], trio[i])
            )
        spread[z, mine] = (wide * gains[1, tensor]).astype(bf16)
        ring_on(s, 1)

    bits = 2
    fine = span // bits

    def ring_on(s, step):
        for bit in range(bits):
            for direction in range(2):
                if 1 < step <= half or (step > half and direction == s):
                    block = spot(direction, step - 1, s, bit)
                    index = bits * (step - 2) + bit
                    arrived(
                        block, hs.at[direction, index, s], hr.at[direction, index, s],
                        ring[direction],
                    )
                if step < half or (step == half and direction == s):
                    block = spot(direction, step - 1, s, bit)
                    index = bits * (step - 1) + bit
                    pending.append(
                        send(
                            block, block, hs.at[direction, index, s], hr.at[direction, index, s],
                            ring[direction],
                        )
                    )

    def spot(direction, steps, s, bit):
        origin = lax.rem(z + (NZ - steps if direction == 0 else steps), NZ)
        return spread.at[origin, pl.ds(s * span + bit * fine, fine)]

    def share_root(s):
        total = squares[s]
        for i in range(3):
            arrived(squares_in.at[s, i], qs.at[s, i], qr.at[s, i], trio[i])
            total = total + squares_in[s, i]
        lane = lax.broadcasted_iota(jnp.int32, total.shape, 1)
        ours = (lane >= s * span) & (lane < (s + 1) * span)
        roots[z, s] = jnp.where(ours, lax.rsqrt(total / (4 * quarter) + EPSILON), 0.0)
        block = roots.at[z, s]
        for d in range(1, NZ):
            pending.append(send(block, block, rs.at[s, d - 1], rr.at[s, d - 1], z_peers[d - 1]))

    near_first = [(0, NZ - 1), (1, NZ - 2), (2, NZ - 3), (3, 4)]
    def last(part):
        for direction in range(2):
            got(part, direction, half, direction)

    def second():
        step_on(0, 3)
        step_on(1, 2)

    def third():
        step_on(0, 4)
        step_on(1, 3)

    def fourth():
        last(0)
        step_on(1, 4)

    nothing = lambda: None
    chunks = [functools.partial(old_chunk, offsets=pair) for pair in near_first] + [new_chunk]
    gates = [
        [nothing, second, third, fourth, lambda: last(1)],
        [
            nothing,
            loads[2].wait,
            lambda: combine(0),
            lambda: across_core(0),
            lambda: residual(0),
        ],
    ]
    attend(chunks, gates, finish)
    ring_on(0, 2)
    combine(1)
    ring_on(0, 3)
    across_core(1)
    ring_on(0, 4)
    share_root(0)
    residual(1)
    ring_on(0, 5)
    for step in range(2, half + 2):
        ring_on(1, step)
        if step == 3:
            share_root(1)
    for s in range(seqs):
        for d in range(1, NZ):
            arrived(
                roots.at[lax.rem(z + NZ - d, NZ), s], rs.at[s, d - 1], rr.at[s, d - 1], z_peers[d - 1]
            )
    for d in range(1, NZ):
        arrived(
            slab_all.at[lax.rem(z + NZ - d, NZ)], ts.at[d - 1], tr.at[d - 1], z_peers[d - 1]
        )
    for copy in pending:
        copy.wait_send()


def attention(
    scale, capacity, own_tokens, gain, out_gain, cosine, sine, cache, routed, weights, prefix,
    w_query, w_keyval, w_out,
):
    seqs, cache_rows, width = cache.shape
    rows, quarter = own_tokens.shape
    span, head = rows // seqs, width // 2
    cols = w_query.shape[1] // head * span
    vmem = pl.BlockSpec(memory_space=pltpu.VMEM)
    any_space = pl.BlockSpec(memory_space=pl.ANY)
    bf16, wide, sem = jnp.bfloat16, jnp.float32, pltpu.SemaphoreType.DMA
    return pl.pallas_call(
        functools.partial(attention_kernel, scale, capacity),
        out_shape=(
            jax.ShapeDtypeStruct((seqs, span, width), bf16),
            jax.ShapeDtypeStruct((rows, quarter), bf16),
            jax.ShapeDtypeStruct((NZ, rows, quarter), bf16),
            jax.ShapeDtypeStruct((NZ, seqs, 8, rows), wide),
            jax.ShapeDtypeStruct((NZ, NY * NX, 256), wide),
        ),
        in_specs=[vmem] * 8 + [pl.BlockSpec(memory_space=pltpu.SMEM)] + [any_space] * 3,
        out_specs=(vmem,) * 5,
        scratch_shapes=[
            pltpu.VMEM(w_query.shape, bf16),
            pltpu.VMEM(w_keyval.shape, bf16),
            pltpu.VMEM(w_out.shape, bf16),
            pltpu.VMEM((4, rows, quarter), bf16),
            pltpu.VMEM((NY * NZ, seqs, cache_rows, width), bf16),
            pltpu.VMEM((NY * NZ, seqs, span, width), bf16),
            pltpu.VMEM((NX, seqs, head, cols), bf16),
            pltpu.VMEM((seqs, NX, 2 * width, cols), bf16),
            pltpu.VMEM((NX, 1, cols), wide),
            pltpu.VMEM((NX, 16 + head, cols), wide),
            pltpu.VMEM((seqs, NX, head, cols), bf16),
            pltpu.VMEM((seqs, NX, 8, cols), wide),
            pltpu.VMEM((seqs, NX - 1, head, cols), bf16),
            pltpu.VMEM((seqs, NX - 1, 8, cols), wide),
            pltpu.VMEM((seqs, 2, span, quarter), bf16),
            pltpu.VMEM((seqs, 2, span, quarter), bf16),
            pltpu.VMEM((seqs, 2, span, quarter), wide),
            pltpu.VMEM((seqs, span, quarter), bf16),
            pltpu.VMEM((seqs, span, quarter), bf16),
            pltpu.VMEM((seqs, 8, rows), wide),
            pltpu.VMEM((seqs, 3, 8, rows), wide),
            pltpu.VMEM((NZ, NY * NX, 256), wide),
            pltpu.VMEM((2, 4, 1, quarter), wide),
            sem((3,)),
            sem((3,)),
            sem((3,)),
            sem((seqs, NX - 1)),
            sem((seqs, NX - 1)),
            sem((2,)),
            sem((2,)),
            sem((2, 2, NZ)),
            sem((2, 2, NZ)),
            sem((NZ - 1,)),
            sem((NZ - 1,)),
            sem((seqs, NX - 1)),
            sem((seqs, NX - 1)),
            sem((seqs, NX - 1)),
            sem((seqs, NX - 1)),
            sem((seqs, 2)),
            sem((seqs, 2)),
            sem((seqs,)),
            sem((seqs,)),
            sem((seqs, 3)),
            sem((seqs, 3)),
            sem((2, NZ, seqs)),
            sem((2, NZ, seqs)),
            sem((seqs, NZ - 1)),
            sem((seqs, NZ - 1)),
        ],
        compiler_params=pltpu.CompilerParams(
            collective_id=0, has_side_effects=True, vmem_limit_bytes=60 * 1024 * 1024
        ),
        name="attention",
    )(
        own_tokens, gain, out_gain, cosine, sine, cache, routed, weights, prefix,
        w_query, w_keyval, w_out,
    )


def expert_kernel(
    capacity, slab, source, roots, hidden, up_hbm, down_hbm, out,
    rows, sel, held, up_raw, down_raw, up, down, slot_of, weight_of, root_of, shares,
    mine0, mine1, to_mate0, to_mate1, core_in0, core_in1, side_in0, side_in1, x_out0, x_out1,
    back0, back1, sums0, sums1, staged0, staged1, landed0, landed1,
    ws, xs, xr, ys, yr, fs, fr, cs, cr, bs, br, es, er, zs, zr,
):
    mine, to_mate, core_in = (mine0, mine1), (to_mate0, to_mate1), (core_in0, core_in1)
    side_in, x_out, back = (side_in0, side_in1), (x_out0, x_out1), (back0, back1)
    sums, staged, landed = (sums0, sums1), (staged0, staged1), (landed0, landed1)
    rank, tensor = lax.axis_index("expert"), lax.axis_index("tensor")
    y_lo, x, z, y_hi, core, far, sides, mate = corner(rank, tensor)
    other = 1 - y_lo
    x_peers = [(rank_of(y_lo, lax.rem(x + d, NX), z), tensor) for d in range(1, NX)]
    ring = [
        (rank_of(y_lo, x, lax.rem(z + 1, NZ)), tensor),
        (rank_of(y_lo, x, lax.rem(z + NZ - 1, NZ)), tensor),
    ]
    greet(x_peers + [far] + sides + [mate] + ring)
    pending = []
    loads = [
        pltpu.make_async_copy(up_hbm, up_raw, ws.at[0]),
        pltpu.make_async_copy(down_hbm, down_raw, ws.at[1]),
    ]
    for load in loads:
        load.start()
    size, width = sel.shape[2:]
    quarters = rows.shape[0]
    count = hidden.shape[0]
    bf16 = jnp.bfloat16
    cuts = (slice(0, mine0.shape[3]), slice(mine0.shape[3], width))

    at = lax.broadcasted_iota(jnp.int32, (size, count), 0)
    lane = lax.broadcasted_iota(jnp.int32, (size, count), 1)
    block_of = jnp.zeros((size, count), jnp.int32)
    for b in range(1, NZ):
        block_of = block_of + jnp.where(at >= b * capacity, 1, 0)
    ours = lane == at - block_of * capacity
    lane_f = f32(lane)

    def by_block(pieces):
        value = jnp.zeros((size, count), jnp.float32)
        for b in range(NZ):
            value = jnp.where(block_of == b, pieces[b], value)
        return value

    root_rows = by_block([roots[b, 0, 0:1, :] + roots[b, 1, 0:1, :] for b in range(NZ)])
    first = f32(block_of[:, 0:1] * count)

    def total_of(mask, value):
        return jnp.sum(jnp.where(mask, value, 0.0), axis=1, keepdims=True)

    group = lax.broadcasted_iota(jnp.int32, (NY * NX, count), 0)

    def pick_table(j):
        named = [
            jnp.sum(jnp.where(group == j, slab[b, :, :count], 0.0), axis=0, keepdims=True)
            for b in range(NZ)
        ]
        token = total_of(ours, by_block(named))
        root_of[j] = total_of(lane_f == token, root_rows)
        slot_of[j] = jnp.where(token >= 0.0, token + first, -1.0)

    lanes = f32(lax.broadcasted_iota(jnp.int32, (size, source.shape[0]), 1))

    def pick(side, to):
        j = side * NX + to
        pick_table(j)
        chosen = jnp.where(lanes == slot_of[j], 1.0, 0.0).astype(bf16)
        picked = jnp.dot(chosen, source[...], preferred_element_type=jnp.float32)
        return (picked * root_of[j]).astype(bf16)

    def to_side(d, here, there):
        spot = rows.at[tensor, y_lo, lax.rem(x + NX - d, NX)]
        if there is not None:
            for r in range(2):
                pending.append(send(there, spot, ys.at[d, r], yr.at[d, r], sides[r]))
        if here is not None:
            pending.append(send(here, spot, ys.at[d, 2], yr.at[d, 2], far))

    def forward(d, r, l):
        x_s = lax.rem(x + NX - d, NX)
        spot = rows.at[lax.rem(y_hi + r, 2) * 2 + core, lax.rem(y_lo + l, 2), x_s]
        index = 2 * r + l
        pending.append(send(spot, spot, fs.at[d, index], fr.at[d, index], mate))

    def from_sides(d):
        x_s = lax.rem(x + NX - d, NX)
        for r in range(2):
            spot = rows.at[lax.rem(y_hi + r, 2) * 2 + core, other, x_s]
            arrived(spot, ys.at[d, r], yr.at[d, r], sides[r])
            forward(d, r, 1)
        spot = rows.at[(1 - y_hi) * 2 + core, y_lo, x_s]
        arrived(spot, ys.at[d, 2], yr.at[d, 2], far)
        forward(d, 1, 0)

    def from_mate(d):
        x_s = lax.rem(x + NX - d, NX)
        for r in range(2):
            for l in range(2):
                spot = rows.at[lax.rem(y_hi + r, 2) * 2 + 1 - core, lax.rem(y_lo + l, 2), x_s]
                arrived(spot, fs.at[d, 2 * r + l], fr.at[d, 2 * r + l], mate)

    units, real = down.shape[1], down_raw.shape[0]

    def run(d):
        x_s = lax.rem(x + NX - d, NX)
        total = jnp.zeros((2 * size, 2 * units), jnp.float32)
        for q in range(quarters):
            block = jnp.concatenate([rows[q, other, x_s], rows[q, y_lo, x_s]], axis=0)
            total += lax.dot_general(
                block, up[q], (((1,), (1,)), ((), ())), preferred_element_type=jnp.float32
            )
        gate, raised = total[:, :units], total[:, units:]
        active = (gate * jax.nn.sigmoid(1.702 * gate) * (raised + 1.0)).astype(bf16)
        for f in range(2):
            for h in range(2):
                half = lax.rem(y_hi + h, 2)
                for owner in range(2):
                    index = half * 2 + (core if owner else 1 - core)
                    value = jnp.dot(
                        active, down[index, :, cuts[f]], preferred_element_type=jnp.float32
                    ).astype(bf16)
                    into = mine[f] if owner else to_mate[f]
                    into[d, h] = value[:size]
                    into[d, 3 - h] = value[size:]
                    if not owner:
                        for kind in (h, 3 - h):
                            pending.append(
                                send(
                                    into.at[d, kind], core_in[f].at[d, kind],
                                    cs.at[f, d, kind], cr.at[f, d, kind], mate,
                                )
                            )

    def back_to_sides(f, d):
        for kind in range(4):
            arrived(core_in[f].at[d, kind], cs.at[f, d, kind], cr.at[f, d, kind], mate)
            both = f32(mine[f][d, kind]) + f32(core_in[f][d, kind])
            mine[f][d, kind] = both.astype(bf16)
            if kind < 3:
                to = far if kind == 2 else sides[kind]
                pending.append(
                    send(
                        mine[f].at[d, kind], side_in[f].at[d, kind],
                        bs.at[f, d, kind], br.at[f, d, kind], to,
                    )
                )

    def spot_of(f, owner, at_x):
        return back[f].at[owner * NX + at_x]

    def back_to_x(f, d):
        for kind in range(3):
            to = far if kind == 2 else sides[kind]
            arrived(side_in[f].at[d, kind], bs.at[f, d, kind], br.at[f, d, kind], to)
            if kind == 0:
                continue
            near = side_in[f][d, 0] if kind == 1 else mine[f][d, 3]
            both = (f32(near) + f32(side_in[f][d, kind])).astype(bf16)
            i = kind - 1
            owner = other if kind == 1 else y_lo
            if d == 0:
                back[f][owner * NX + x] = both
            else:
                e = NX - d - 1
                x_out[f][d - 1, i] = both
                pending.append(
                    send(
                        x_out[f].at[d - 1, i], spot_of(f, owner, x),
                        es.at[f, e, i], er.at[f, e, i], x_peers[e],
                    )
                )

    def from_x_back(f):
        for d in range(1, NX):
            x_e = lax.rem(x + NX - d, NX)
            for i in range(2):
                owner = other if i == 0 else y_lo
                arrived(
                    spot_of(f, owner, x_e), es.at[f, d - 1, i], er.at[f, d - 1, i], x_peers[d - 1]
                )

    half_rows, half = count // 2, NZ // 2

    def add_up(f, steps):
        value = jnp.dot(
            shares[steps],
            back[f][...].reshape(NY * NX * size, back[f].shape[2]),
            preferred_element_type=jnp.float32,
        )
        sums[f][steps] = value.astype(bf16)

    def reach(direction, piece):
        return half if direction == piece else half - 1

    def got(f, direction, steps, piece):
        index = 2 * steps + piece
        arrived(
            landed[f].at[direction, index], zs.at[f, direction, index], zr.at[f, direction, index],
            ring[direction],
        )
        return f32(landed[f][direction, index])

    def toward(f, steps):
        add_up(f, steps)
        if steps < half:
            add_up(f, NZ - steps)
        for piece in range(2):
            for direction in range(2):
                if steps > reach(direction, piece):
                    continue
                home = steps if direction == 0 else NZ - steps
                value = f32(sums[f][home, pl.ds(piece * half_rows, half_rows)])
                if steps < reach(direction, piece):
                    value = value + got(f, direction, steps, piece)
                index = 2 * (steps - 1) + piece
                staged[f][direction, index] = value.astype(bf16)
                pending.append(
                    send(
                        staged[f].at[direction, index], landed[f].at[direction, index],
                        zs.at[f, direction, index], zr.at[f, direction, index], ring[direction],
                    )
                )
        if steps == 1:
            add_up(f, 0)

    def arrive_home(f):
        for piece in range(2):
            span = pl.ds(piece * half_rows, half_rows)
            value = f32(sums[f][0, span])
            for direction in range(2):
                value = value + got(f, direction, 0, piece)
            out[span, cuts[f]] = (f32(hidden[span, cuts[f]]) + value).astype(bf16)

    sel[other, x] = pick(other, x)
    rows[tensor, y_lo, x] = pick(y_lo, x)
    to_side(0, rows.at[tensor, y_lo, x], sel.at[other, x])
    for d in (1, 3, 2):
        to = lax.rem(x + d, NX)
        for i in range(2):
            side = other if i == 0 else y_lo
            sel[side, to] = pick(side, to)
            dst = held.at[x] if i == 0 else rows.at[tensor, y_lo, x]
            pending.append(
                send(sel.at[side, to], dst, xs.at[d - 1, i], xr.at[d - 1, i], x_peers[d - 1])
            )
    forward(0, 0, 0)
    def from_x(d, side):
        x_s = lax.rem(x + NX - d, NX)
        spot = held.at[x_s] if side else rows.at[tensor, y_lo, x_s]
        index = 0 if side else 1
        arrived(spot, xs.at[d - 1, index], xr.at[d - 1, index], x_peers[d - 1])
        if side:
            to_side(d, None, spot)
        else:
            to_side(d, spot, None)
            forward(d, 0, 0)

    from_x(1, True)
    from_x(3, True)
    from_x(1, False)
    from_x(3, False)
    blank = jnp.zeros((units - real, width), bf16)
    for load in loads:
        load.wait()
    for q in range(quarters):
        span = slice(q * width, (q + 1) * width)
        for i in range(2):
            up[q, i * units : i * units + real, :] = up_raw[i, :, span]
            up[q, i * units + real : (i + 1) * units, :] = blank
        down[q, :real, :] = down_raw[:, span]
        down[q, real:, :] = blank

    from_sides(0)
    from_x(2, True)
    from_x(2, False)
    wide_lane = f32(lax.broadcasted_iota(jnp.int32, (size, count), 1))
    for j in range(NY * NX):
        weight_of[j] = total_of(ours, by_block([slab[b, j : j + 1, count:] for b in range(NZ)]))
    for steps in range(NZ):
        start = f32(jnp.full((size, count), lax.rem(z + steps, NZ) * count, jnp.int32))
        flipped = [
            jnp.where(wide_lane + start == slot_of[j], weight_of[j], 0.0) for j in range(NY * NX)
        ]
        shares[steps] = jnp.concatenate(flipped, axis=0).T.astype(bf16)
    for d in (0, 1, 3, 2):
        if d:
            from_sides(d)
        from_mate(d)
        run(d)
        if d in (1, 3):
            back_to_sides(0, d)
    back_to_sides(0, 2)
    back_to_sides(0, 0)
    for d in (1, 3, 2, 0):
        back_to_sides(1, d)
    for d in (1, 3, 2, 0):
        back_to_x(0, d)
    from_x_back(0)
    for steps, d in zip(range(half, 0, -1), (1, 3, 2, 0)):
        toward(0, steps)
        back_to_x(1, d)
    arrive_home(0)
    from_x_back(1)
    for steps in range(half, 0, -1):
        toward(1, steps)
    arrive_home(1)
    for copy in pending:
        copy.wait_send()


def run_experts(capacity, slab, source, roots, hidden, up, down):
    count, width = hidden.shape
    size = NZ * capacity
    quarters = down.shape[1] // width
    units = -(-down.shape[0] // 128) * 128
    vmem = pl.BlockSpec(memory_space=pltpu.VMEM)
    any_space = pl.BlockSpec(memory_space=pl.ANY)
    bf16, sem, wide = jnp.bfloat16, pltpu.SemaphoreType.DMA, jnp.float32
    cut = -(-width // 256) * 128
    parts = (cut, width - cut)
    groups = NY * NX

    def pair(*lead):
        return [pltpu.VMEM(lead + (part,), bf16) for part in parts]

    return pl.pallas_call(
        functools.partial(expert_kernel, capacity),
        out_shape=jax.ShapeDtypeStruct((count, width), bf16),
        in_specs=[vmem] * 4 + [any_space] * 2,
        out_specs=vmem,
        scratch_shapes=[
            pltpu.VMEM((quarters, NY, NX, size, width), bf16),
            pltpu.VMEM((NY, NX, size, width), bf16),
            pltpu.VMEM((NX, size, width), bf16),
            pltpu.VMEM(up.shape, bf16),
            pltpu.VMEM(down.shape, bf16),
            pltpu.VMEM((quarters, 2 * units, width), bf16),
            pltpu.VMEM((quarters, units, width), bf16),
            pltpu.VMEM((groups, size, 1), wide),
            pltpu.VMEM((groups, size, 1), wide),
            pltpu.VMEM((groups, size, 1), wide),
            pltpu.VMEM((NZ, count, groups * size), bf16),
            *pair(NX, 4, size),
            *pair(NX, 4, size),
            *pair(NX, 4, size),
            *pair(NX, 3, size),
            *pair(NX - 1, 2, size),
            *pair(groups, size),
            *pair(NZ, count),
            *pair(2, NZ, count // 2),
            *pair(2, NZ, count // 2),
            sem((2,)),
            sem((NX - 1, 2)),
            sem((NX - 1, 2)),
            sem((NX, 3)),
            sem((NX, 3)),
            sem((NX, 4)),
            sem((NX, 4)),
            sem((2, NX, 4)),
            sem((2, NX, 4)),
            sem((2, NX, 3)),
            sem((2, NX, 3)),
            sem((2, NX - 1, 2)),
            sem((2, NX - 1, 2)),
            sem((2, 2, NZ)),
            sem((2, 2, NZ)),
        ],
        compiler_params=pltpu.CompilerParams(
            collective_id=3, has_side_effects=True, vmem_limit_bytes=62 * 1024 * 1024
        ),
        name="run_experts",
    )(slab, source, roots, hidden, up, down)


def on_device(
    tokens,
    attn_gain,
    w_query,
    key_value_weight,
    w_out,
    cache_keyval,
    prefix_length,
    routed_experts,
    route_weights,
    expert_gain,
    w_gate_up,
    w_down,
):
    span_dev, seq_count, quarter = tokens.shape
    model_width = attn_gain.shape[0]
    row_count = span_dev * seq_count
    head_dim = key_value_weight.shape[2] // 2
    cache_rows = cache_keyval.shape[0]
    expert_rank = lax.axis_index("expert")
    quarters = model_width // quarter
    top_count = routed_experts.shape[2]
    expert_count = lax.axis_size("expert")
    capacity = min(row_count, max(2, 5 * row_count * top_count // (2 * expert_count)))
    half_dim = head_dim // 2
    steps_up = jnp.arange(half_dim, dtype=jnp.float32)
    frequency = jnp.exp(steps_up * (-math.log(ROPE_BASE) / half_dim))
    span_place = expert_rank * span_dev + jnp.arange(span_dev, dtype=jnp.int32)
    places = (prefix_length[:, None] + span_place[None, :]).reshape(row_count).astype(jnp.float32)
    angles = frequency[:, None] * places[None, :]
    own_tokens = tokens.transpose(1, 0, 2).reshape(row_count, quarter)
    fresh, hidden, spread, roots, slab_all = attention(
        head_dim ** (-0.5) * LOG2E,
        capacity,
        own_tokens,
        attn_gain.reshape(1, model_width),
        expert_gain.reshape(1, model_width),
        jnp.cos(angles),
        jnp.sin(angles),
        cache_keyval[:, :, 0, :].transpose(1, 0, 2),
        routed_experts.transpose(1, 2, 0),
        route_weights.transpose(1, 2, 0),
        prefix_length,
        w_query,
        key_value_weight[:, 0, :],
        w_out.T,
    )
    new_key_value_rows = fresh.transpose(1, 0, 2)[:, :, None, :]
    layer_output = run_experts(
        capacity,
        slab_all,
        spread.reshape(NZ * row_count, quarter),
        roots,
        hidden,
        w_gate_up[0].transpose(1, 2, 0),
        w_down[0],
    )
    layer_output = layer_output.reshape(seq_count, span_dev, quarter).transpose(1, 0, 2)
    return (layer_output, new_key_value_rows)


def solution(mesh):
    return jax.shard_map(
        on_device,
        mesh=mesh,
        in_specs=(
            P("expert", None, "tensor"),
            P(),
            P(None, "tensor"),
            P(None, "tensor", None),
            P("tensor", None),
            P("expert", None, "tensor", None),
            P(),
            P("expert", None, None),
            P("expert", None, None),
            P(),
            P("expert", None, None, "tensor"),
            P("expert", "tensor", None),
        ),
        out_specs=(P("expert", None, "tensor"), P("expert", None, "tensor", None)),
        check_vma=False,
    )
```

```python
import functools
import math

import jax
import jax.numpy as jnp
from jax import lax
from jax.experimental import pallas as pl
from jax.experimental.pallas import tpu as pltpu
from jax.sharding import PartitionSpec as P

EPSILON = 1e-05
ROPE_BASE = 150000.0
NEG = -1e30
MESH = pl.DeviceIdType.MESH
NY, NX, NZ = 2, 4, 8
LOG2E = 1.4426950408889634


def place_of(expert_rank):
    return expert_rank // (NX * NZ), (expert_rank // NZ) % NX, expert_rank % NZ


def rank_of(y_lo, x, z):
    return (y_lo * NX + x) * NZ + z


def greet(devices):
    barrier = pltpu.get_barrier_semaphore()
    for device in devices:
        pl.semaphore_signal(barrier, inc=1, device_id=device, device_id_type=MESH)
    pl.semaphore_wait(barrier, len(devices))


def send(src, dst, send_sem, recv_sem, device):
    copy = pltpu.make_async_remote_copy(
        src_ref=src,
        dst_ref=dst,
        send_sem=send_sem,
        recv_sem=recv_sem,
        device_id=device,
        device_id_type=MESH,
    )
    copy.start()
    return copy


def arrived(dst, send_sem, recv_sem, device):
    pltpu.make_async_remote_copy(
        src_ref=dst,
        dst_ref=dst,
        send_sem=send_sem,
        recv_sem=recv_sem,
        device_id=device,
        device_id_type=MESH,
    ).wait_recv()


def swap_blocks(value):
    half = value.shape[0] // 2
    top, bottom = value[:half], value[half:]
    left = lax.broadcasted_iota(jnp.int32, top.shape, 1) < half
    return jnp.concatenate(
        [
            jnp.where(left, top, pltpu.roll(bottom, half, 1)),
            jnp.where(left, pltpu.roll(top, half, 1), bottom),
        ],
        axis=0,
    )


def turn(first, second, cosine, sine):
    return first * cosine - second * sine, second * cosine + first * sine


def corner(rank, tensor):
    y_lo, x, z = place_of(rank)
    y_hi, core = tensor // 2, lax.rem(tensor, 2)
    far = (rank, (1 - y_hi) * 2 + core)
    sides = [(rank_of(1 - y_lo, x, z), lax.rem(y_hi + r, 2) * 2 + core) for r in range(2)]
    mate = (rank, y_hi * 2 + 1 - core)
    return y_lo, x, z, y_hi, core, far, sides, mate


def f32(value):
    return value.astype(jnp.float32)


def route(capacity, routed, weights, slab):
    planes, groups, _ = slab.shape
    experts = planes * groups
    seqs, top_count, count = routed.shape
    row = lax.broadcasted_iota(jnp.int32, (experts, count), 0)
    lane = lax.broadcasted_iota(jnp.int32, (experts, count), 1)
    expert = lax.rem(row, groups) * planes + row // groups
    before = jnp.where(
        lax.broadcasted_iota(jnp.int32, (count, count), 0)
        < lax.broadcasted_iota(jnp.int32, (count, count), 1),
        1.0,
        0.0,
    ).astype(jnp.bfloat16)
    earlier = jnp.zeros((experts, 1), jnp.float32)
    named = []
    for s in range(seqs):
        for k in range(top_count):
            hit = jnp.where(expert == routed[s, k : k + 1, :], 1.0, 0.0)
            ahead = jnp.dot(hit.astype(jnp.bfloat16), before, preferred_element_type=jnp.float32)
            arrival = jnp.where(hit > 0.0, ahead + earlier, -1.0)
            named.append((arrival, f32(lane + s * count + 1), weights[s, k : k + 1, :]))
            earlier = earlier + jnp.sum(hit, axis=1, keepdims=True)
    slot = lax.broadcasted_iota(jnp.int32, (experts, 128), 1)

    def fill(place, carry):
        tokens, scales = carry
        token = jnp.zeros((experts, count), jnp.float32)
        scale = jnp.zeros((experts, count), jnp.float32)
        for arrival, number, share in named:
            here = arrival == f32(place)
            token = jnp.where(here, number, token)
            scale = jnp.where(here, share, scale)
        return (
            jnp.where(slot == place, jnp.sum(token, axis=1, keepdims=True) - 1.0, tokens),
            jnp.where(slot == place, jnp.sum(scale, axis=1, keepdims=True), scales),
        )

    empty = jnp.full((experts, 128), -1.0, jnp.float32)
    tokens, scales = lax.fori_loop(0, capacity, fill, (empty, jnp.zeros_like(empty)))
    slab[:, :, :128] = tokens.reshape(planes, groups, 128)
    slab[:, :, 128:] = scales.reshape(planes, groups, 128)


def attention_kernel(
    scale, capacity, own_tokens, gain, out_gain, cosine, sine, cache, routed, weights, prefix, w_query_hbm, w_keyval_hbm, w_out_hbm,
    fresh, hidden, spread, roots, slab_all,
    w_query, w_keyval, w_out, gathered, kv_old, kv_new, q_all, qa, tops, sums, o_out, stat_out,
    o_in, stat_in, to_core, core_in, keep, far_out, far_in, squares, squares_in,
    slab, gains, ws, gs, gr, xs, xr, ys, yr, zs, zr, ts, tr, os, orr, ss, sr, cs, cr, fs, fr, qs, qr, hs, hr, rs, rr,
):
    rank, tensor = lax.axis_index("expert"), lax.axis_index("tensor")
    y_lo, x, z, y_hi, core, far, sides, mate = corner(rank, tensor)
    other = 1 - y_lo
    rows, quarter = own_tokens.shape
    seqs, span, width = fresh.shape
    cache_rows, head = cache.shape[1], width // 2
    cols = q_all.shape[3]
    bf16 = jnp.bfloat16
    x_peers = [(rank_of(y_lo, lax.rem(x + d, NX), z), tensor) for d in range(1, NX)]
    y_peer = (rank_of(other, x, z), tensor)
    z_peers = [(rank_of(y_lo, x, lax.rem(z + d, NZ)), tensor) for d in range(1, NZ)]
    ring = [z_peers[0], z_peers[-1]]
    cross = (rank, (1 - y_hi) * 2 + 1 - core)
    greet(x_peers + [y_peer] + z_peers + [far, mate, cross])
    pending = []
    loads = [
        pltpu.make_async_copy(src, dst, ws.at[i])
        for i, (src, dst) in enumerate(
            [(w_query_hbm, w_query), (w_keyval_hbm, w_keyval), (w_out_hbm, w_out)]
        )
    ]
    for load in loads:
        load.start()
    half = NZ // 2
    stores = (kv_old, kv_new)

    def slot(part, direction, steps, piece):
        origin = lax.rem(z + (NZ - steps if direction == 0 else steps), NZ)
        return stores[part].at[origin * 2 + (y_lo if piece == 0 else other)]

    def sems(part, direction, step, piece):
        index = 2 * (step - 1) + piece
        return zs.at[part, direction, index], zr.at[part, direction, index]

    def pass_on(part, direction, step, piece):
        block = slot(part, direction, step - 1, piece)
        pending.append(send(block, block, *sems(part, direction, step, piece), ring[direction]))

    def got(part, direction, step, piece):
        arrived(
            slot(part, direction, step, piece), *sems(part, direction, step, piece), ring[direction]
        )

    def begin(part):
        block = slot(part, 0, 0, 0)
        pending.append(send(block, block, ys.at[part], yr.at[part], y_peer))
        for direction in range(2):
            pass_on(part, direction, 1, 0)

    def begin_other(part):
        arrived(slot(part, 0, 0, 1), ys.at[part], yr.at[part], y_peer)
        for direction in range(2):
            pass_on(part, direction, 1, 1)

    def step_on(part, step):
        for piece in range(2):
            for direction in range(2):
                got(part, direction, step - 1, piece)
                if step < half or direction == piece:
                    pass_on(part, direction, step, piece)

    mine = gathered.at[tensor]
    pending.append(send(own_tokens, mine, gs.at[0], gr.at[0], far))
    pending.append(send(own_tokens, mine, gs.at[1], gr.at[1], mate))
    kv_old[z * 2 + y_lo] = cache[...]
    begin(0)
    far_index, mate_index = (1 - y_hi) * 2 + core, y_hi * 2 + 1 - core
    cross_index = (1 - y_hi) * 2 + 1 - core

    for q in range(4):
        gains[0, q] = gain[:, q * quarter : (q + 1) * quarter]
        gains[1, q] = out_gain[:, q * quarter : (q + 1) * quarter]

    def rows_of(index):
        return pl.ds(pl.multiple_of(index * quarter, 16), quarter)

    def project(index, block):
        wide = f32(block)
        scaled = (wide * gains[0, index]).astype(bf16)
        return (
            jnp.dot(scaled, w_query[rows_of(index), :], preferred_element_type=jnp.float32),
            jnp.dot(scaled, w_keyval[rows_of(index), :], preferred_element_type=jnp.float32),
            jnp.sum(wide * wide, axis=1, keepdims=True),
        )

    loads[0].wait()
    loads[1].wait()
    def add_to(total, index):
        return [a + b for a, b in zip(total, project(index, gathered[index]))]

    total = project(tensor, own_tokens[...])
    arrived(gathered.at[mate_index], gs.at[1], gr.at[1], mate)
    total = add_to(total, mate_index)
    begin_other(0)
    route(capacity, routed, weights, slab)
    slab_all[z] = slab[z]
    arrived(gathered.at[far_index], gs.at[0], gr.at[0], far)
    block = gathered.at[far_index]
    pending.append(send(block, block, gs.at[2], gr.at[2], mate))
    for d in range(1, NZ):
        to = lax.rem(z + d, NZ)
        pending.append(
            send(slab.at[to], slab_all.at[z], ts.at[d - 1], tr.at[d - 1], z_peers[d - 1])
        )
    total = add_to(total, far_index)
    arrived(gathered.at[cross_index], gs.at[2], gr.at[2], mate)
    total = add_to(total, cross_index)
    root = lax.rsqrt(total[2] / (4 * quarter) + EPSILON)
    cos, sin = cosine[...], sine[...]
    flipped = (total[1] * root).T
    keys = turn(flipped[: head // 2], flipped[head // 2 : head], cos, sin)
    whole = jnp.concatenate([keys[0], keys[1], flipped[head:]], axis=0).T
    own_rows = whole.astype(bf16).reshape(fresh.shape)
    fresh[...] = own_rows
    kv_new[z * 2 + y_lo] = own_rows
    begin(1)
    step_on(0, 2)
    raw = total[0] * root
    for j in range(raw.shape[1] // width):
        pair = raw[:, j * width : (j + 1) * width].T
        turned = []
        for h in range(2):
            block = pair[h * head : (h + 1) * head]
            turned += turn(block[: head // 2], block[head // 2 :], cos, sin)
        first = swap_blocks(jnp.concatenate(turned, axis=0) * scale).astype(bf16)
        for s in range(seqs):
            q_all[0, s, :, j * width : (j + 1) * width] = first[s * head : (s + 1) * head]
    for s in range(seqs):
        for d in (1, 3, 2):
            src, dst = q_all.at[0, s], q_all.at[NX - d, s]
            pending.append(send(src, dst, xs.at[s, d - 1], xr.at[s, d - 1], x_peers[d - 1]))
    begin_other(1)

    row = lax.broadcasted_iota(jnp.int32, (width, cols), 0)
    lane = lax.broadcasted_iota(jnp.int32, (width, cols), 1)
    for k in range(NX):
        hot = (row == span + lax.rem(x + k, NX)) | (row == span + NX)
        if k == 0:
            hot = hot | (row == lax.rem(lane, span))
        for s in range(seqs):
            qa[s, k, head:width, :] = jnp.zeros((width - head, cols), bf16)
            qa[s, k, width:, :] = jnp.where(hot, 1.0, 0.0).astype(bf16)

    def old_chunk(s, offsets):
        values, masks = [], []
        old_row = lax.broadcasted_iota(jnp.int32, (cache_rows, width), 0)
        marked = lax.broadcasted_iota(jnp.int32, (cache_rows, width), 1) == span + NX
        for offset in offsets:
            origin = lax.rem(z + offset, NZ)
            for side in range(NY):
                values.append(kv_old[origin * 2 + side, s])
                place = old_row + rank_of(side, x, origin) * cache_rows
                masks.append(
                    jnp.where(marked & (place >= prefix[s]), NEG, 0.0).astype(bf16)
                )
        return jnp.concatenate(values, axis=0), jnp.concatenate(masks, axis=0)

    def new_chunk(s):
        masks = []
        new_row = lax.broadcasted_iota(jnp.int32, (span, width), 0)
        new_col = lax.broadcasted_iota(jnp.int32, (span, width), 1)
        in_block = (new_col >= span) & (new_col < span + NX)
        query_rank = rank_of(y_lo, new_col - span, z)
        later = (new_col < span) & (new_row > new_col)
        for shard in range(NY * NZ):
            key_rank = rank_of(shard % 2, x, shard // 2)
            late = in_block & (key_rank > query_rank)
            same = later & (jnp.full(later.shape, key_rank, jnp.int32) == rank)
            masks.append(jnp.where(late | same, NEG, 0.0).astype(bf16))
        return kv_new[:, s].reshape(NY * NZ * span, width), jnp.concatenate(masks, axis=0)

    def operands(keyval, mask):
        flipped = f32(keyval).T[head:].astype(bf16)
        ones = jnp.ones((16, keyval.shape[0]), bf16)
        return (
            jnp.concatenate([keyval, mask], axis=1),
            jnp.concatenate([ones, flipped], axis=0),
        )

    def attend(chunks, gates, ends):
        turns = [
            (s, c, k)
            for s in range(seqs)
            for c in range(len(chunks))
            for k in ((0, 1, 3, 2) if c == 0 else (2, 1, 3, 0))
        ]
        held = {}

        def score(turn):
            s, c, k = turn
            if (s, c) not in held:
                gates[s][c]()
                held[s, c] = operands(*chunks[c](s))
            if c == 0:
                if k:
                    e = NX - k - 1
                    arrived(q_all.at[k, s], xs.at[s, e], xr.at[s, e], x_peers[e])
                qa[s, k, :head, :] = q_all[k, s]
            return jnp.dot(held[s, c][0], qa[s, k], preferred_element_type=jnp.float32)

        ahead = score(turns[0])
        for at, (s, c, k) in enumerate(turns):
            scores = ahead
            if at + 1 < len(turns):
                ahead = score(turns[at + 1])
            top = jnp.max(scores, axis=0, keepdims=True)
            if c:
                top = jnp.maximum(top, tops[k])
            probs = jnp.exp2(scores - top).astype(bf16)
            part = jnp.dot(held[s, c][1], probs, preferred_element_type=jnp.float32)
            if c:
                part = part + sums[k] * jnp.exp2(tops[k] - top)
            sums[k] = part
            tops[k] = top
            if c == len(chunks) - 1:
                ends(s, k)

    def finish(s, k):
        value = sums[k]
        o_out[s, k] = (value[16:] / value[0:1]).astype(bf16)
        stat_out[s, k, 0:1, :] = tops[k]
        stat_out[s, k, 1:2, :] = value[0:1]
        stat_out[s, k, 2:, :] = jnp.zeros((6, cols), jnp.float32)
        if k:
            to, i = x_peers[k - 1], NX - k - 1
            pending.append(send(stat_out.at[s, k], stat_in.at[s, i], ss.at[s, i], sr.at[s, i], to))
            pending.append(send(o_out.at[s, k], o_in.at[s, i], os.at[s, i], orr.at[s, i], to))

    order = [1 - y_hi, y_hi]
    later = {}

    def combine(s):
        stats, values = [stat_out[s, 0]], [o_out[s, 0]]
        for i in (0, 2, 1):
            arrived(stat_in.at[s, i], ss.at[s, i], sr.at[s, i], x_peers[i])
            arrived(o_in.at[s, i], os.at[s, i], orr.at[s, i], x_peers[i])
            stats.append(stat_in[s, i])
            values.append(o_in[s, i])
        top = functools.reduce(jnp.maximum, [value[0:1] for value in stats])
        shares = [jnp.exp2(value[0:1] - top) * value[1:2] for value in stats]
        every = functools.reduce(jnp.add, shares)
        merged = functools.reduce(
            jnp.add, [f32(value) * (share / every) for value, share in zip(values, shares)]
        )
        blank = jnp.zeros((head, width), jnp.float32)
        attended = jnp.concatenate(
            [
                swap_blocks(
                    jnp.concatenate([merged[:, j * width : (j + 1) * width], blank], axis=0).T
                )[:span]
                for j in range(cols // width)
            ],
            axis=1,
        ).astype(bf16)

        def projected(index):
            return lax.dot_general(
                attended, w_out[rows_of(index), :], (((1,), (1,)), ((), ())),
                preferred_element_type=jnp.float32,
            )

        for i in range(2):
            to_core[s, i] = projected(order[i] * 2 + 1 - core).astype(bf16)
            pending.append(
                send(to_core.at[s, i], core_in.at[s, i], cs.at[s, i], cr.at[s, i], mate)
            )
        keep[s, 0] = projected(order[0] * 2 + core)
        later[s] = lambda: projected(order[1] * 2 + core)

    def across_core(s):
        arrived(core_in.at[s, 0], cs.at[s, 0], cr.at[s, 0], mate)
        far_out[s] = (keep[s, 0] + f32(core_in[s, 0])).astype(bf16)
        pending.append(send(far_out.at[s], far_in.at[s], fs.at[s], fr.at[s], far))
        keep[s, 1] = later[s]()

    trio = [mate, far, cross]

    def residual(s):
        mine = pl.ds(s * span, span)
        arrived(core_in.at[s, 1], cs.at[s, 1], cr.at[s, 1], mate)
        near = f32(own_tokens[mine]) + (keep[s, 1] + f32(core_in[s, 1]))
        arrived(far_in.at[s], fs.at[s], fr.at[s], far)
        rounded = (near + f32(far_in[s])).astype(bf16)
        hidden[mine] = rounded
        wide = f32(rounded)
        spread[z, mine] = (wide * gains[1, tensor]).astype(bf16)
        ring_on(s, 1)
        own = jnp.broadcast_to(jnp.sum(wide * wide, axis=1, keepdims=True), (span, width))
        blank = jnp.zeros((span, width), jnp.float32)
        squares[s] = jnp.concatenate([blank] * s + [own] + [blank] * (seqs - 1 - s), axis=0).T[:8]
        for i in range(3):
            pending.append(
                send(squares.at[s], squares_in.at[s, i], qs.at[s, i], qr.at[s, i], trio[i])
            )

    bits = 2
    fine = span // bits

    def ring_on(s, step):
        for bit in range(bits):
            for direction in range(2):
                if 1 < step <= half or (step > half and direction == s):
                    block = spot(direction, step - 1, s, bit)
                    index = bits * (step - 2) + bit
                    arrived(
                        block, hs.at[direction, index, s], hr.at[direction, index, s],
                        ring[direction],
                    )
                if step < half or (step == half and direction == s):
                    block = spot(direction, step - 1, s, bit)
                    index = bits * (step - 1) + bit
                    pending.append(
                        send(
                            block, block, hs.at[direction, index, s], hr.at[direction, index, s],
                            ring[direction],
                        )
                    )

    def spot(direction, steps, s, bit):
        origin = lax.rem(z + (NZ - steps if direction == 0 else steps), NZ)
        return spread.at[origin, pl.ds(s * span + bit * fine, fine)]

    def share_root(s):
        total = squares[s]
        for i in range(3):
            arrived(squares_in.at[s, i], qs.at[s, i], qr.at[s, i], trio[i])
            total = total + squares_in[s, i]
        lane = lax.broadcasted_iota(jnp.int32, total.shape, 1)
        ours = (lane >= s * span) & (lane < (s + 1) * span)
        roots[z, s] = jnp.where(ours, lax.rsqrt(total / (4 * quarter) + EPSILON), 0.0)
        block = roots.at[z, s]
        for d in range(1, NZ):
            pending.append(send(block, block, rs.at[s, d - 1], rr.at[s, d - 1], z_peers[d - 1]))

    near_first = [(0, NZ - 1), (1, NZ - 2), (2, NZ - 3), (3, 4)]
    def last(part):
        for direction in range(2):
            got(part, direction, half, direction)

    def second():
        step_on(0, 3)
        step_on(1, 2)

    def third():
        step_on(0, 4)
        step_on(1, 3)

    def fourth():
        last(0)
        step_on(1, 4)

    nothing = lambda: None
    chunks = [functools.partial(old_chunk, offsets=pair) for pair in near_first] + [new_chunk]
    gates = [
        [nothing, second, third, fourth, lambda: last(1)],
        [
            nothing,
            loads[2].wait,
            lambda: combine(0),
            lambda: across_core(0),
            lambda: residual(0),
        ],
    ]
    attend(chunks, gates, finish)
    ring_on(0, 2)
    combine(1)
    ring_on(0, 3)
    across_core(1)
    ring_on(0, 4)
    share_root(0)
    residual(1)
    ring_on(0, 5)
    for step in range(2, half + 2):
        ring_on(1, step)
        if step == 3:
            share_root(1)
    for s in range(seqs):
        for d in range(1, NZ):
            arrived(
                roots.at[lax.rem(z + NZ - d, NZ), s], rs.at[s, d - 1], rr.at[s, d - 1], z_peers[d - 1]
            )
    for d in range(1, NZ):
        arrived(
            slab_all.at[lax.rem(z + NZ - d, NZ)], ts.at[d - 1], tr.at[d - 1], z_peers[d - 1]
        )
    for copy in pending:
        copy.wait_send()


def attention(
    scale, capacity, own_tokens, gain, out_gain, cosine, sine, cache, routed, weights, prefix,
    w_query, w_keyval, w_out,
):
    seqs, cache_rows, width = cache.shape
    rows, quarter = own_tokens.shape
    span, head = rows // seqs, width // 2
    cols = w_query.shape[1] // head * span
    vmem = pl.BlockSpec(memory_space=pltpu.VMEM)
    any_space = pl.BlockSpec(memory_space=pl.ANY)
    bf16, wide, sem = jnp.bfloat16, jnp.float32, pltpu.SemaphoreType.DMA
    return pl.pallas_call(
        functools.partial(attention_kernel, scale, capacity),
        out_shape=(
            jax.ShapeDtypeStruct((seqs, span, width), bf16),
            jax.ShapeDtypeStruct((rows, quarter), bf16),
            jax.ShapeDtypeStruct((NZ, rows, quarter), bf16),
            jax.ShapeDtypeStruct((NZ, seqs, 8, rows), wide),
            jax.ShapeDtypeStruct((NZ, NY * NX, 256), wide),
        ),
        in_specs=[vmem] * 8 + [pl.BlockSpec(memory_space=pltpu.SMEM)] + [any_space] * 3,
        out_specs=(vmem,) * 5,
        scratch_shapes=[
            pltpu.VMEM(w_query.shape, bf16),
            pltpu.VMEM(w_keyval.shape, bf16),
            pltpu.VMEM(w_out.shape, bf16),
            pltpu.VMEM((4, rows, quarter), bf16),
            pltpu.VMEM((NY * NZ, seqs, cache_rows, width), bf16),
            pltpu.VMEM((NY * NZ, seqs, span, width), bf16),
            pltpu.VMEM((NX, seqs, head, cols), bf16),
            pltpu.VMEM((seqs, NX, 2 * width, cols), bf16),
            pltpu.VMEM((NX, 1, cols), wide),
            pltpu.VMEM((NX, 16 + head, cols), wide),
            pltpu.VMEM((seqs, NX, head, cols), bf16),
            pltpu.VMEM((seqs, NX, 8, cols), wide),
            pltpu.VMEM((seqs, NX - 1, head, cols), bf16),
            pltpu.VMEM((seqs, NX - 1, 8, cols), wide),
            pltpu.VMEM((seqs, 2, span, quarter), bf16),
            pltpu.VMEM((seqs, 2, span, quarter), bf16),
            pltpu.VMEM((seqs, 2, span, quarter), wide),
            pltpu.VMEM((seqs, span, quarter), bf16),
            pltpu.VMEM((seqs, span, quarter), bf16),
            pltpu.VMEM((seqs, 8, rows), wide),
            pltpu.VMEM((seqs, 3, 8, rows), wide),
            pltpu.VMEM((NZ, NY * NX, 256), wide),
            pltpu.VMEM((2, 4, 1, quarter), wide),
            sem((3,)),
            sem((3,)),
            sem((3,)),
            sem((seqs, NX - 1)),
            sem((seqs, NX - 1)),
            sem((2,)),
            sem((2,)),
            sem((2, 2, NZ)),
            sem((2, 2, NZ)),
            sem((NZ - 1,)),
            sem((NZ - 1,)),
            sem((seqs, NX - 1)),
            sem((seqs, NX - 1)),
            sem((seqs, NX - 1)),
            sem((seqs, NX - 1)),
            sem((seqs, 2)),
            sem((seqs, 2)),
            sem((seqs,)),
            sem((seqs,)),
            sem((seqs, 3)),
            sem((seqs, 3)),
            sem((2, NZ, seqs)),
            sem((2, NZ, seqs)),
            sem((seqs, NZ - 1)),
            sem((seqs, NZ - 1)),
        ],
        compiler_params=pltpu.CompilerParams(
            collective_id=0, has_side_effects=True, vmem_limit_bytes=60 * 1024 * 1024
        ),
        name="attention",
    )(
        own_tokens, gain, out_gain, cosine, sine, cache, routed, weights, prefix,
        w_query, w_keyval, w_out,
    )


def expert_kernel(
    capacity, slab, source, roots, hidden, up_hbm, down_hbm, out,
    rows, sel, held, up_raw, down_raw, up, down, slot_of, weight_of, root_of, shares,
    mine0, mine1, to_mate0, to_mate1, core_in0, core_in1, side_in0, side_in1, x_out0, x_out1,
    back0, back1, sums0, sums1, staged0, staged1, landed0, landed1,
    ws, xs, xr, ys, yr, fs, fr, cs, cr, bs, br, es, er, zs, zr,
):
    mine, to_mate, core_in = (mine0, mine1), (to_mate0, to_mate1), (core_in0, core_in1)
    side_in, x_out, back = (side_in0, side_in1), (x_out0, x_out1), (back0, back1)
    sums, staged, landed = (sums0, sums1), (staged0, staged1), (landed0, landed1)
    rank, tensor = lax.axis_index("expert"), lax.axis_index("tensor")
    y_lo, x, z, y_hi, core, far, sides, mate = corner(rank, tensor)
    other = 1 - y_lo
    x_peers = [(rank_of(y_lo, lax.rem(x + d, NX), z), tensor) for d in range(1, NX)]
    ring = [
        (rank_of(y_lo, x, lax.rem(z + 1, NZ)), tensor),
        (rank_of(y_lo, x, lax.rem(z + NZ - 1, NZ)), tensor),
    ]
    greet(x_peers + [far] + sides + [mate] + ring)
    pending = []
    loads = [
        pltpu.make_async_copy(up_hbm, up_raw, ws.at[0]),
        pltpu.make_async_copy(down_hbm, down_raw, ws.at[1]),
    ]
    for load in loads:
        load.start()
    size, width = sel.shape[2:]
    quarters = rows.shape[0]
    count = hidden.shape[0]
    bf16 = jnp.bfloat16
    cuts = (slice(0, mine0.shape[3]), slice(mine0.shape[3], width))

    at = lax.broadcasted_iota(jnp.int32, (size, count), 0)
    lane = lax.broadcasted_iota(jnp.int32, (size, count), 1)
    block_of = jnp.zeros((size, count), jnp.int32)
    for b in range(1, NZ):
        block_of = block_of + jnp.where(at >= b * capacity, 1, 0)
    ours = lane == at - block_of * capacity
    lane_f = f32(lane)

    def by_block(pieces):
        value = jnp.zeros((size, count), jnp.float32)
        for b in range(NZ):
            value = jnp.where(block_of == b, pieces[b], value)
        return value

    root_rows = by_block([roots[b, 0, 0:1, :] + roots[b, 1, 0:1, :] for b in range(NZ)])
    first = f32(block_of[:, 0:1] * count)

    def total_of(mask, value):
        return jnp.sum(jnp.where(mask, value, 0.0), axis=1, keepdims=True)

    group = lax.broadcasted_iota(jnp.int32, (NY * NX, count), 0)

    def pick_table(j):
        named = [
            jnp.sum(jnp.where(group == j, slab[b, :, :count], 0.0), axis=0, keepdims=True)
            for b in range(NZ)
        ]
        token = total_of(ours, by_block(named))
        root_of[j] = total_of(lane_f == token, root_rows)
        slot_of[j] = jnp.where(token >= 0.0, token + first, -1.0)

    lanes = f32(lax.broadcasted_iota(jnp.int32, (size, source.shape[0]), 1))

    def pick(side, to):
        j = side * NX + to
        pick_table(j)
        chosen = jnp.where(lanes == slot_of[j], 1.0, 0.0).astype(bf16)
        picked = jnp.dot(chosen, source[...], preferred_element_type=jnp.float32)
        return (picked * root_of[j]).astype(bf16)

    def to_side(d, here, there):
        spot = rows.at[tensor, y_lo, lax.rem(x + NX - d, NX)]
        if there is not None:
            for r in range(2):
                pending.append(send(there, spot, ys.at[d, r], yr.at[d, r], sides[r]))
        if here is not None:
            pending.append(send(here, spot, ys.at[d, 2], yr.at[d, 2], far))

    def forward(d, r, l):
        x_s = lax.rem(x + NX - d, NX)
        spot = rows.at[lax.rem(y_hi + r, 2) * 2 + core, lax.rem(y_lo + l, 2), x_s]
        index = 2 * r + l
        pending.append(send(spot, spot, fs.at[d, index], fr.at[d, index], mate))

    def from_sides(d):
        x_s = lax.rem(x + NX - d, NX)
        for r in range(2):
            spot = rows.at[lax.rem(y_hi + r, 2) * 2 + core, other, x_s]
            arrived(spot, ys.at[d, r], yr.at[d, r], sides[r])
            forward(d, r, 1)
        spot = rows.at[(1 - y_hi) * 2 + core, y_lo, x_s]
        arrived(spot, ys.at[d, 2], yr.at[d, 2], far)
        forward(d, 1, 0)

    def from_mate(d):
        x_s = lax.rem(x + NX - d, NX)
        for r in range(2):
            for l in range(2):
                spot = rows.at[lax.rem(y_hi + r, 2) * 2 + 1 - core, lax.rem(y_lo + l, 2), x_s]
                arrived(spot, fs.at[d, 2 * r + l], fr.at[d, 2 * r + l], mate)

    units, real = down.shape[1], down_raw.shape[0]

    def run(d):
        x_s = lax.rem(x + NX - d, NX)
        total = jnp.zeros((2 * size, 2 * units), jnp.float32)
        for q in range(quarters):
            block = jnp.concatenate([rows[q, other, x_s], rows[q, y_lo, x_s]], axis=0)
            total += lax.dot_general(
                block, up[q], (((1,), (1,)), ((), ())), preferred_element_type=jnp.float32
            )
        gate, raised = total[:, :units], total[:, units:]
        active = (gate * jax.nn.sigmoid(1.702 * gate) * (raised + 1.0)).astype(bf16)
        for f in range(2):
            for h in range(2):
                half = lax.rem(y_hi + h, 2)
                for owner in range(2):
                    index = half * 2 + (core if owner else 1 - core)
                    value = jnp.dot(
                        active, down[index, :, cuts[f]], preferred_element_type=jnp.float32
                    ).astype(bf16)
                    into = mine[f] if owner else to_mate[f]
                    into[d, h] = value[:size]
                    into[d, 3 - h] = value[size:]
                    if not owner:
                        for kind in (h, 3 - h):
                            pending.append(
                                send(
                                    into.at[d, kind], core_in[f].at[d, kind],
                                    cs.at[f, d, kind], cr.at[f, d, kind], mate,
                                )
                            )

    def back_to_sides(f, d):
        for kind in range(4):
            arrived(core_in[f].at[d, kind], cs.at[f, d, kind], cr.at[f, d, kind], mate)
            both = f32(mine[f][d, kind]) + f32(core_in[f][d, kind])
            mine[f][d, kind] = both.astype(bf16)
            if kind < 3:
                to = far if kind == 2 else sides[kind]
                pending.append(
                    send(
                        mine[f].at[d, kind], side_in[f].at[d, kind],
                        bs.at[f, d, kind], br.at[f, d, kind], to,
                    )
                )

    def spot_of(f, owner, at_x):
        return back[f].at[owner * NX + at_x]

    def back_to_x(f, d):
        for kind in range(3):
            to = far if kind == 2 else sides[kind]
            arrived(side_in[f].at[d, kind], bs.at[f, d, kind], br.at[f, d, kind], to)
            if kind == 0:
                continue
            near = side_in[f][d, 0] if kind == 1 else mine[f][d, 3]
            both = (f32(near) + f32(side_in[f][d, kind])).astype(bf16)
            i = kind - 1
            owner = other if kind == 1 else y_lo
            if d == 0:
                back[f][owner * NX + x] = both
            else:
                e = NX - d - 1
                x_out[f][d - 1, i] = both
                pending.append(
                    send(
                        x_out[f].at[d - 1, i], spot_of(f, owner, x),
                        es.at[f, e, i], er.at[f, e, i], x_peers[e],
                    )
                )

    def from_x_back(f):
        for d in range(1, NX):
            x_e = lax.rem(x + NX - d, NX)
            for i in range(2):
                owner = other if i == 0 else y_lo
                arrived(
                    spot_of(f, owner, x_e), es.at[f, d - 1, i], er.at[f, d - 1, i], x_peers[d - 1]
                )

    half_rows, half = count // 2, NZ // 2

    def add_up(f, steps):
        value = jnp.dot(
            shares[steps],
            back[f][...].reshape(NY * NX * size, back[f].shape[2]),
            preferred_element_type=jnp.float32,
        )
        sums[f][steps] = value.astype(bf16)

    def reach(direction, piece):
        return half if direction == piece else half - 1

    def got(f, direction, steps, piece):
        index = 2 * steps + piece
        arrived(
            landed[f].at[direction, index], zs.at[f, direction, index], zr.at[f, direction, index],
            ring[direction],
        )
        return f32(landed[f][direction, index])

    def toward(f, steps):
        add_up(f, steps)
        if steps < half:
            add_up(f, NZ - steps)
        for piece in range(2):
            for direction in range(2):
                if steps > reach(direction, piece):
                    continue
                home = steps if direction == 0 else NZ - steps
                value = f32(sums[f][home, pl.ds(piece * half_rows, half_rows)])
                if steps < reach(direction, piece):
                    value = value + got(f, direction, steps, piece)
                index = 2 * (steps - 1) + piece
                staged[f][direction, index] = value.astype(bf16)
                pending.append(
                    send(
                        staged[f].at[direction, index], landed[f].at[direction, index],
                        zs.at[f, direction, index], zr.at[f, direction, index], ring[direction],
                    )
                )
        if steps == 1:
            add_up(f, 0)

    def arrive_home(f):
        for piece in range(2):
            span = pl.ds(piece * half_rows, half_rows)
            value = f32(sums[f][0, span])
            for direction in range(2):
                value = value + got(f, direction, 0, piece)
            out[span, cuts[f]] = (f32(hidden[span, cuts[f]]) + value).astype(bf16)

    sel[other, x] = pick(other, x)
    rows[tensor, y_lo, x] = pick(y_lo, x)
    to_side(0, rows.at[tensor, y_lo, x], sel.at[other, x])
    for d in (1, 3, 2):
        to = lax.rem(x + d, NX)
        for i in range(2):
            side = other if i == 0 else y_lo
            sel[side, to] = pick(side, to)
            dst = held.at[x] if i == 0 else rows.at[tensor, y_lo, x]
            pending.append(
                send(sel.at[side, to], dst, xs.at[d - 1, i], xr.at[d - 1, i], x_peers[d - 1])
            )
    forward(0, 0, 0)
    def from_x(d, side):
        x_s = lax.rem(x + NX - d, NX)
        spot = held.at[x_s] if side else rows.at[tensor, y_lo, x_s]
        index = 0 if side else 1
        arrived(spot, xs.at[d - 1, index], xr.at[d - 1, index], x_peers[d - 1])
        if side:
            to_side(d, None, spot)
        else:
            to_side(d, spot, None)
            forward(d, 0, 0)

    from_x(1, True)
    from_x(3, True)
    from_x(1, False)
    from_x(3, False)
    blank = jnp.zeros((units - real, width), bf16)
    for load in loads:
        load.wait()
    for q in range(quarters):
        span = slice(q * width, (q + 1) * width)
        for i in range(2):
            up[q, i * units : i * units + real, :] = up_raw[i, :, span]
            up[q, i * units + real : (i + 1) * units, :] = blank
        down[q, :real, :] = down_raw[:, span]
        down[q, real:, :] = blank

    from_sides(0)
    from_x(2, True)
    from_x(2, False)
    wide_lane = f32(lax.broadcasted_iota(jnp.int32, (size, count), 1))
    for j in range(NY * NX):
        weight_of[j] = total_of(ours, by_block([slab[b, j : j + 1, count:] for b in range(NZ)]))
    for steps in range(NZ):
        start = f32(jnp.full((size, count), lax.rem(z + steps, NZ) * count, jnp.int32))
        flipped = [
            jnp.where(wide_lane + start == slot_of[j], weight_of[j], 0.0) for j in range(NY * NX)
        ]
        shares[steps] = jnp.concatenate(flipped, axis=0).T.astype(bf16)
    for d in (0, 1, 3, 2):
        if d:
            from_sides(d)
        from_mate(d)
        run(d)
        if d in (1, 3):
            back_to_sides(0, d)
    back_to_sides(0, 2)
    back_to_sides(0, 0)
    for d in (1, 3, 2, 0):
        back_to_sides(1, d)
    for d in (1, 3, 2, 0):
        back_to_x(0, d)
    from_x_back(0)
    for steps, d in zip(range(half, 0, -1), (1, 3, 2, 0)):
        toward(0, steps)
        back_to_x(1, d)
    arrive_home(0)
    from_x_back(1)
    for steps in range(half, 0, -1):
        toward(1, steps)
    arrive_home(1)
    for copy in pending:
        copy.wait_send()


def run_experts(capacity, slab, source, roots, hidden, up, down):
    count, width = hidden.shape
    size = NZ * capacity
    quarters = down.shape[1] // width
    units = -(-down.shape[0] // 128) * 128
    vmem = pl.BlockSpec(memory_space=pltpu.VMEM)
    any_space = pl.BlockSpec(memory_space=pl.ANY)
    bf16, sem, wide = jnp.bfloat16, pltpu.SemaphoreType.DMA, jnp.float32
    cut = -(-width // 256) * 128
    parts = (cut, width - cut)
    groups = NY * NX

    def pair(*lead):
        return [pltpu.VMEM(lead + (part,), bf16) for part in parts]

    return pl.pallas_call(
        functools.partial(expert_kernel, capacity),
        out_shape=jax.ShapeDtypeStruct((count, width), bf16),
        in_specs=[vmem] * 4 + [any_space] * 2,
        out_specs=vmem,
        scratch_shapes=[
            pltpu.VMEM((quarters, NY, NX, size, width), bf16),
            pltpu.VMEM((NY, NX, size, width), bf16),
            pltpu.VMEM((NX, size, width), bf16),
            pltpu.VMEM(up.shape, bf16),
            pltpu.VMEM(down.shape, bf16),
            pltpu.VMEM((quarters, 2 * units, width), bf16),
            pltpu.VMEM((quarters, units, width), bf16),
            pltpu.VMEM((groups, size, 1), wide),
            pltpu.VMEM((groups, size, 1), wide),
            pltpu.VMEM((groups, size, 1), wide),
            pltpu.VMEM((NZ, count, groups * size), bf16),
            *pair(NX, 4, size),
            *pair(NX, 4, size),
            *pair(NX, 4, size),
            *pair(NX, 3, size),
            *pair(NX - 1, 2, size),
            *pair(groups, size),
            *pair(NZ, count),
            *pair(2, NZ, count // 2),
            *pair(2, NZ, count // 2),
            sem((2,)),
            sem((NX - 1, 2)),
            sem((NX - 1, 2)),
            sem((NX, 3)),
            sem((NX, 3)),
            sem((NX, 4)),
            sem((NX, 4)),
            sem((2, NX, 4)),
            sem((2, NX, 4)),
            sem((2, NX, 3)),
            sem((2, NX, 3)),
            sem((2, NX - 1, 2)),
            sem((2, NX - 1, 2)),
            sem((2, 2, NZ)),
            sem((2, 2, NZ)),
        ],
        compiler_params=pltpu.CompilerParams(
            collective_id=3, has_side_effects=True, vmem_limit_bytes=62 * 1024 * 1024
        ),
        name="run_experts",
    )(slab, source, roots, hidden, up, down)


def on_device(
    tokens,
    attn_gain,
    w_query,
    key_value_weight,
    w_out,
    cache_keyval,
    prefix_length,
    routed_experts,
    route_weights,
    expert_gain,
    w_gate_up,
    w_down,
):
    span_dev, seq_count, quarter = tokens.shape
    model_width = attn_gain.shape[0]
    row_count = span_dev * seq_count
    head_dim = key_value_weight.shape[2] // 2
    cache_rows = cache_keyval.shape[0]
    expert_rank = lax.axis_index("expert")
    quarters = model_width // quarter
    top_count = routed_experts.shape[2]
    expert_count = lax.axis_size("expert")
    capacity = min(row_count, max(2, 5 * row_count * top_count // (2 * expert_count)))
    half_dim = head_dim // 2
    steps_up = jnp.arange(half_dim, dtype=jnp.float32)
    frequency = jnp.exp(steps_up * (-math.log(ROPE_BASE) / half_dim))
    span_place = expert_rank * span_dev + jnp.arange(span_dev, dtype=jnp.int32)
    places = (prefix_length[:, None] + span_place[None, :]).reshape(row_count).astype(jnp.float32)
    angles = frequency[:, None] * places[None, :]
    own_tokens = tokens.transpose(1, 0, 2).reshape(row_count, quarter)
    fresh, hidden, spread, roots, slab_all = attention(
        head_dim ** (-0.5) * LOG2E,
        capacity,
        own_tokens,
        attn_gain.reshape(1, model_width),
        expert_gain.reshape(1, model_width),
        jnp.cos(angles),
        jnp.sin(angles),
        cache_keyval[:, :, 0, :].transpose(1, 0, 2),
        routed_experts.transpose(1, 2, 0),
        route_weights.transpose(1, 2, 0),
        prefix_length,
        w_query,
        key_value_weight[:, 0, :],
        w_out.T,
    )
    new_key_value_rows = fresh.transpose(1, 0, 2)[:, :, None, :]
    layer_output = run_experts(
        capacity,
        slab_all,
        spread.reshape(NZ * row_count, quarter),
        roots,
        hidden,
        w_gate_up[0].transpose(1, 2, 0),
        w_down[0],
    )
    layer_output = layer_output.reshape(seq_count, span_dev, quarter).transpose(1, 0, 2)
    return (layer_output, new_key_value_rows)


def solution(mesh):
    return jax.shard_map(
        on_device,
        mesh=mesh,
        in_specs=(
            P("expert", None, "tensor"),
            P(),
            P(None, "tensor"),
            P(None, "tensor", None),
            P("tensor", None),
            P("expert", None, "tensor", None),
            P(),
            P("expert", None, None),
            P("expert", None, None),
            P(),
            P("expert", None, None, "tensor"),
            P("expert", "tensor", None),
        ),
        out_specs=(P("expert", None, "tensor"), P("expert", None, "tensor", None)),
        check_vma=False,
    )
```
